32 devices in a mesh: groups: 2 (over y), rows: 4 (over z), cols: 2 (over x), sub: 2 (over core).
Axes of the slice: x: 2, y: 2, z: 4, core: 2. Of those that a mesh axis runs over, the one named last changes fastest.
Arguments:
- elevation: float32 [256, 16384], P(('groups', 'rows', 'sub'), 'cols'), parts along dimension 0, may hold values from -6 to 6
- fill_depth: float32 [256, 16384], P(('groups', 'rows', 'sub'), 'cols'), parts along dimension 0, may hold values from 0.5 to 4
- edge_rows: int32 [4, 16384], P('groups', 'cols'), parts along dimension 0, may hold values 0 or 1
- edge_sides: int32 [4, 128], P('groups', ('rows', 'sub')), parts along dimension 0, may hold values 0 or 1
- adjacency: int32 [16, 6], P('groups'), parts along dimension 0, may hold values from 0 to 7
Outputs:
- filled: float32 [256, 16384], P(('groups', 'rows', 'sub'), 'cols'), parts along dimension 0
The draws below stay inside these ranges and needn't reach their ends.
There are 2 independent parts, one for each index of `groups`. The reference program is written for one: setup_inputs(seed, part) draws one part's arguments, and reference() takes and returns one part's arrays. A program takes and returns all parts, laid end to end along the dimension named above; each array names one. Nothing has to cross between parts.
Inputs may be any that keep to these rules, and one draw needn't show every extreme that they name: `adjacency`: tile numbers count tiles row by row.
All inputs are finite; a program needn't handle non-finite values. No bound on the sum of `edge_rows` or of `edge_sides` on one device may be relied on, other than what follows from the above.
Results may differ from the reference program's by a relative error of at most 0.00002.
Values sent between devices are 32-bit elements; how exact they have to be, the bound alone decides.
No kernel may reach another device: no remote copies, remote signals or barrier semaphores. Data moves between devices by JAX's collectives and lax.ppermute only.
A program may use at most 64 MiB of HBM per device.

```python
import math
import jax
import jax.numpy as jnp

PASSES = 8
FINAL = 4
ROUNDS = 4
DEG = 6
NR = 128
NC = 16384
TILES = 8
N_ROWS = 4
N_COLS = 2


def with_ends(drawn, own_key, smallest, largest):
    shape = drawn.shape
    place = [jax.random.randint(jax.random.fold_in(own_key, axis), (), 0, shape[axis]) for axis in range(len(shape))]
    drawn = drawn.at[tuple(place)].set(smallest)
    longest = shape.index(max(shape))
    place[longest] = (place[longest] + 1) % shape[longest]
    return drawn.at[tuple(place)].set(largest)


def steps_of(stream_key, shape, pieces, least, largest):
    def one(dim, blocks):
        draws = jax.random.uniform(jax.random.fold_in(jax.random.fold_in(stream_key, 6), dim), (blocks,), jnp.float32, least / len(pieces), largest / len(pieces))
        return jnp.repeat(jnp.exp(draws), shape[dim] // blocks).reshape((-1,) + (1,) * (len(shape) - dim - 1))

    factor_of = one(*pieces[0])
    for cut in pieces[1:]:
        factor_of = factor_of * one(*cut)
    return factor_of


def noise(key, shape, scale, limit, split=(), dtype=jnp.bfloat16):
    array = jax.random.normal(key, shape, jnp.float32) * scale
    if len(split) > 0:
        array = steps_of(key, shape, split, -0.22, 0.18) * array
    return jnp.clip(array, min=-limit, max=limit).astype(dtype)


def setup_inputs(seed: int = 0, part: int = 0) -> dict:
    seeds = jax.random.split(jax.random.key(seed), 6)
    part_keys = jax.random.split(jax.random.fold_in(seeds[5], part), 6)
    elevation = noise(part_keys[0], (NR, NC), 1.0, 6.0, ((0, 8), (1, 2)), jnp.float32)
    fill_depth = jnp.clip(jnp.exp(math.log(4.0) - 2.0794415 * jax.random.uniform(part_keys[1], (NR, NC), jnp.float32) ** steps_of(part_keys[1], (NR, NC), ((0, 8), (1, 2)), -0.2, 0.2)), 0.5, 4.0)
    edge_rows = with_ends((jax.random.randint(part_keys[2], (2, NC), 0, 8) < 1).astype(jnp.int32), jax.random.fold_in(part_keys[2], 1), 0, 1)
    edge_sides = with_ends((jax.random.randint(part_keys[3], (2, NR), 0, 8) < 1).astype(jnp.int32), jax.random.fold_in(part_keys[3], 1), 0, 1)
    adjacency = with_ends(jax.random.randint(part_keys[4], (TILES, DEG), 0, TILES), jax.random.fold_in(part_keys[4], 1), 0, TILES - 1).astype(jnp.int32)
    return dict(elevation=elevation, fill_depth=fill_depth, edge_rows=edge_rows, edge_sides=edge_sides, adjacency=adjacency)


unreached = 1.0e9
rise_step = 0.01
hop_rise = 0.05
spill_lift = 3.0


def neighbour_min(padded):
    height = padded.shape[0] - 2
    width = padded.shape[1] - 2
    lowest = None
    for shift_row in range(3):
        for shift_col in range(3):
            if shift_row == 1 and shift_col == 1:
                continue
            piece = padded[shift_row:shift_row + height, shift_col:shift_col + width]
            lowest = piece if lowest is None else jnp.minimum(lowest, piece)
    return lowest


def relax(surface, ground):
    padded = jnp.pad(surface, 1, constant_values=unreached)
    lowest = neighbour_min(padded)
    return jnp.maximum(ground, jnp.minimum(surface, lowest + rise_step))


def reference(elevation, fill_depth, edge_rows, edge_sides, adjacency):
    total_rows, total_cols = elevation.shape
    row_ids = jnp.arange(total_rows)[:, None]
    col_ids = jnp.arange(total_cols)[None, :]
    outlet = ((row_ids == 0) & (edge_rows[0][None, :] == 1)) | ((row_ids == total_rows - 1) & (edge_rows[1][None, :] == 1))
    outlet = outlet | ((col_ids == 0) & (edge_sides[0][:, None] == 1)) | ((col_ids == total_cols - 1) & (edge_sides[1][:, None] == 1))
    surface = jnp.where(outlet, elevation, elevation + fill_depth)
    for step in range(PASSES):
        surface = relax(surface, elevation)
    tile_rows = total_rows // N_ROWS
    tile_cols = total_cols // N_COLS
    blocks = surface.reshape(N_ROWS, tile_rows, N_COLS, tile_cols)
    floors = jnp.minimum(jnp.min(blocks[:, 0, :, :], axis=-1), jnp.min(blocks[:, -1, :, :], axis=-1))
    floors = jnp.minimum(floors, jnp.min(blocks[:, :, :, 0], axis=1))
    floors = jnp.minimum(floors, jnp.min(blocks[:, :, :, -1], axis=1))
    level = floors.reshape(N_ROWS * N_COLS)
    for step in range(ROUNDS):
        level = jnp.minimum(level, jnp.min(level[adjacency], axis=1) + hop_rise)
    ceiling = (level + spill_lift).reshape(N_ROWS, 1, N_COLS, 1)
    blocks = jnp.maximum(elevation.reshape(N_ROWS, tile_rows, N_COLS, tile_cols), jnp.minimum(blocks, ceiling))
    surface = blocks.reshape(total_rows, total_cols)
    for step in range(FINAL):
        surface = relax(surface, elevation)
    return surface
```

```python
import functools

import jax
import jax.numpy as jnp
from jax import lax
from jax.experimental import pallas as pl
from jax.experimental.pallas import tpu as pltpu
from jax.sharding import PartitionSpec as P

PASSES = 8
FINAL = 4
ROUNDS = 4
HALO = PASSES + FINAL
SUBS = 8
LANES = 128
BLOCK = 4

unreached = 1000000000.0
rise_step = 0.01
hop_rise = 0.05
spill_lift = 3.0


def matching(count, first):
    pairs = []
    for low in range(first, count - 1, 2):
        pairs += [(low, low + 1), (low + 1, low)]
    return pairs


def cross(row_pairs, col_pairs, cols, subs):
    def device(place, col):
        return (place // subs * cols + col) * subs + place % subs

    return [
        (device(row, col), device(row_to, col_to))
        for row, row_to in row_pairs
        for col, col_to in col_pairs
    ]


def chain_place():
    subs = lax.axis_size("sub")
    return lax.axis_index("rows") * subs + lax.axis_index("sub"), lax.axis_size("rows") * subs


def position():
    sub = lax.broadcasted_iota(jnp.int32, (SUBS, LANES), 0)
    lane = lax.broadcasted_iota(jnp.int32, (SUBS, LANES), 1)
    return sub, lane


def pack_kernel(
    ground_hbm, depth_hbm, rows_ref, sides_ref, own_ref, far_ref, near_ref, even_ref, odd_ref,
    ground_ref, depth_ref, sems,
):
    height, width = ground_hbm.shape
    groups = height // SUBS
    tiles = width // (SUBS * LANES)
    part = width // 4
    copies = []
    for group in range(groups):
        for piece in range(4):
            where = (pl.ds(group * SUBS, SUBS), pl.ds(piece * part, part))
            number = group * 4 + piece
            pair = (
                pltpu.make_async_copy(ground_hbm.at[where], ground_ref.at[where], sems.at[0, number]),
                pltpu.make_async_copy(depth_hbm.at[where], depth_ref.at[where], sems.at[1, number]),
            )
            for copy in pair:
                copy.start()
            copies.append(pair)
    place, places = chain_place()
    col, cols = lax.axis_index("cols"), lax.axis_size("cols")
    sub, lane = position()
    square = (height, height)
    diagonal = lax.broadcasted_iota(jnp.int32, square, 0) == lax.broadcasted_iota(jnp.int32, square, 1)
    marks = sides_ref[...].astype(jnp.float32)
    side_marks = [
        jnp.sum(jnp.where(diagonal, marks[side : side + 1, :], 0.0), axis=1, keepdims=True)
        for side in range(2)
    ]
    row_size = tiles * SUBS
    surface_base = height * row_size
    last_tile = width // LANES - 1
    corner = {}
    for group in range(groups):
        for tile in range(last_tile + 1):
            if tile * LANES % part == 0:
                for copy in copies[group * 4 + tile * LANES // part]:
                    copy.wait()
            rows = pl.ds(group * SUBS, SUBS)
            columns = pl.ds(tile * LANES, LANES)
            ground = ground_ref[rows, columns]
            surface = ground + depth_ref[rows, columns]
            outlets = []
            if group == 0:
                outlets.append((rows_ref[0:1, columns] == 1) & (sub == 0) & (place == 0))
            if group == groups - 1:
                outlets.append(
                    (rows_ref[1:2, columns] == 1) & (sub == SUBS - 1) & (place == places - 1)
                )
            if tile == 0:
                outlets.append(
                    (side_marks[0][group * SUBS : (group + 1) * SUBS] > 0.5) & (lane == 0) & (col == 0)
                )
            if tile == last_tile:
                outlets.append(
                    (side_marks[1][group * SUBS : (group + 1) * SUBS] > 0.5)
                    & (lane == LANES - 1)
                    & (col == cols - 1)
                )
            for outlet in outlets:
                surface = jnp.where(outlet, ground, surface)
            chunk, slot = tile // tiles, tile % tiles
            start = group * SUBS * row_size + slot * SUBS + chunk
            own_ref[pl.ds(start, SUBS, stride=row_size), :] = ground
            own_ref[pl.ds(surface_base + start, SUBS, stride=row_size), :] = surface
            if tile == 0 or tile == last_tile:
                corner[group, tile] = (ground, surface)
    for group in range(groups):
        for kind in range(2):
            first = corner[group, 0][kind]
            last = corner[group, last_tile][kind]
            rows = pl.ds(kind * height + group * SUBS, SUBS)
            rightward = col % 2 == 0
            even_ref[rows, :] = jnp.where(rightward, last, first)
            odd_ref[rows, :] = jnp.where(rightward, first, last)
    top = place % 2 == 0
    span = HALO * row_size
    for out_ref, is_top in ((far_ref, top), (near_ref, jnp.logical_not(top))):
        offset = jnp.where(is_top, 0, (height - HALO) * row_size)
        for kind in range(2):
            for row in range(HALO):
                source = pl.multiple_of(kind * surface_base + offset + row * row_size, SUBS)
                target = kind * span + row * row_size
                out_ref[pl.ds(target, row_size), :] = own_ref[pl.ds(source, row_size), :]


def relax_pass(source, target, ground, first, count, ring):
    size = ring * SUBS
    _, lane = position()
    at_first = lane == 0
    at_last = lane == LANES - 1

    def body(step, carry):
        base = first + step * BLOCK

        def load(ref, row, slot):
            return ref[pl.ds(pl.multiple_of((base + row) * size + slot * SUBS, SUBS), SUBS), :]

        for row in range(0, BLOCK, 2):
            center = [[], []]
            column = [[], []]
            for slot in range(ring):
                high = load(source, row, slot)
                low = load(source, row + 1, slot)
                both = jnp.minimum(high, low)
                center[0].append(high)
                center[1].append(low)
                column[0].append(jnp.minimum(load(source, row - 1, slot), both))
                column[1].append(jnp.minimum(load(source, row + 2, slot), both))
            for one in range(2):
                left = [pltpu.roll(value, 1, 1) for value in column[one]]
                right = [pltpu.roll(value, LANES - 1, 1) for value in column[one]]
                for slot in range(ring):
                    from_left = jnp.where(at_first, left[slot - 1], left[slot])
                    from_right = jnp.where(at_last, right[(slot + 1) % ring], right[slot])
                    lowest = jnp.minimum(jnp.minimum(from_left, from_right), column[one][slot])
                    raised = jnp.minimum(center[one][slot], lowest + rise_step)
                    result = jnp.maximum(load(ground, row + one, slot), raised)
                    where = pl.multiple_of((base + row + one) * size + slot * SUBS, SUBS)
                    target[pl.ds(where, SUBS), :] = result
        return carry

    lax.fori_loop(0, -(-count // BLOCK), body, 0)


def hop_counts(links_ref, hops_ref, needed):
    tiles, degree = links_ref.shape
    links = links_ref[...]
    number = lax.broadcasted_iota(jnp.int32, (tiles, tiles), 1)
    linked = links[:, 0:1] == number
    for edge in range(1, degree):
        linked = linked | (links[:, edge : edge + 1] == number)
    linked = linked.astype(jnp.float32)
    tile = lax.broadcasted_iota(jnp.int32, (tiles, LANES), 0)
    lane = lax.broadcasted_iota(jnp.int32, (tiles, LANES), 1)
    reached = jnp.zeros((tiles, LANES), jnp.float32)
    for index, wanted in enumerate(needed):
        reached = jnp.where((lane == index) & (tile == wanted), 1.0, reached)
    hops = jnp.where(reached > 0.5, 0.0, float(ROUNDS + 1))
    for hop in range(1, ROUNDS + 1):
        reached = lax.dot_general(
            linked, reached, (((0,), (0,)), ((), ())), preferred_element_type=jnp.float32
        )
        reached = jnp.where(reached > 0.5, 1.0, 0.0)
        hops = jnp.minimum(hops, jnp.where(reached > 0.5, float(hop), float(ROUNDS + 1)))
    for index in range(len(needed)):
        hops_ref[pl.ds(index * tiles, tiles), :] = jnp.broadcast_to(
            hops[:, index : index + 1], (tiles, LANES)
        )


def needed_tiles():
    row, rows = lax.axis_index("rows"), lax.axis_size("rows")
    col, cols = lax.axis_index("cols"), lax.axis_size("cols")
    sub, subs = lax.axis_index("sub"), lax.axis_size("sub")
    above = jnp.maximum(jnp.where(sub == 0, row - 1, row), 0)
    below = jnp.minimum(jnp.where(sub == subs - 1, row + 1, row), rows - 1)
    left = jnp.maximum(col - 1, 0)
    right = jnp.minimum(col + 1, cols - 1)
    return [r * cols + c for r in (above, row, below) for c in (left, col, right)]


def early_kernel(
    height, tiles, own_ref, far_ref, near_ref, strips_refs, links_ref,
    ground_ref, surface_ref, floor_ref, hops_ref, other_ref,
):
    ring = tiles + 1
    size = ring * SUBS
    place, places = chain_place()
    col, cols = lax.axis_index("cols"), lax.axis_size("cols")
    sub, lane = position()
    hop_counts(links_ref, hops_ref, needed_tiles())
    top = place % 2 == 0
    has_far = jnp.where(top, place > 0, place < places - 1)
    has_near = jnp.where(top, place < places - 1, place > 0)
    low, high = 0, HALO + height
    rightward = col % 2 == 0
    regions = (
        (own_ref, height, HALO, None, 0),
        (far_ref, HALO, jnp.where(top, low, high), has_far, jnp.where(top, height - HALO, 0)),
        (near_ref, HALO, jnp.where(top, high, low), has_near, jnp.where(top, 0, height - HALO)),
    )
    for region, (ref, count, first, present, strip_first) in enumerate(regions):
        even_ref, odd_ref = strips_refs[region]
        for kind, out_ref in ((0, ground_ref), (1, surface_ref)):

            def body(row, carry):
                def keep(value, exists):
                    return jnp.where(exists, value, unreached) if exists is not None else value

                source = (kind * count + row) * tiles * SUBS
                target = (first + row) * size
                values = [
                    keep(
                        ref[pl.ds(pl.multiple_of(source + slot * SUBS, SUBS), SUBS), :], present
                    )
                    for slot in range(tiles)
                ]
                for slot in range(tiles):
                    out_ref[pl.ds(pl.multiple_of(target + slot * SUBS, SUBS), SUBS), :] = values[slot]
                strip_row = kind * height + strip_first + row
                even = even_ref[pl.ds(strip_row, 1), :]
                odd = odd_ref[pl.ds(strip_row, 1), :]
                after = jnp.where(rightward, even, odd)
                before = jnp.where(rightward, odd, even)
                after = keep(jnp.where(col < cols - 1, after, unreached), present)
                before = keep(jnp.where(col > 0, before, unreached), present)
                after = jnp.where(sub == SUBS - 1, after, pltpu.roll(values[0], SUBS - 1, 0))
                before = jnp.where(sub == 0, before, pltpu.roll(values[-1], 1, 0))
                seam = jnp.where(lane < LANES // 2, after, before)
                out_ref[pl.ds(pl.multiple_of(target + tiles * SUBS, SUBS), SUBS), :] = seam
                return carry

            lax.fori_loop(0, count, body, 0, unroll=4)
    total = height + 2 * HALO
    for step in range(PASSES):
        source, target = (surface_ref, other_ref) if step % 2 == 0 else (other_ref, surface_ref)
        relax_pass(source, target, ground_ref, step + 1, total - 2 * (step + 1), ring)
    final_ref = surface_ref if PASSES % 2 == 0 else other_ref
    band, bands = lax.axis_index("sub"), lax.axis_size("sub")
    lowest = jnp.full((SUBS, LANES), unreached, jnp.float32)

    def at(row, slot):
        return final_ref[pl.ds((HALO + row) * size + slot * SUBS, SUBS), :]

    for slot in range(tiles):
        lowest = jnp.minimum(lowest, jnp.where(band == 0, at(0, slot), unreached))
        lowest = jnp.minimum(lowest, jnp.where(band == bands - 1, at(height - 1, slot), unreached))
    first_cell = (sub == 0) & (lane == 0)
    last_cell = (sub == SUBS - 1) & (lane == LANES - 1)
    for row in range(height):
        lowest = jnp.minimum(lowest, jnp.where(first_cell, at(row, 0), unreached))
        lowest = jnp.minimum(lowest, jnp.where(last_cell, at(row, tiles - 1), unreached))
    lowest = jnp.min(jnp.min(lowest, axis=0, keepdims=True), axis=1, keepdims=True)
    floor_ref[...] = jnp.broadcast_to(lowest, floor_ref.shape)


def late_kernel(
    height, tiles, ground_ref, surface_ref, floors_ref, hops_ref, out_hbm,
    one_ref, two_ref, out_ref, sems,
):
    ring = tiles + 1
    size = ring * SUBS
    sub, lane = position()
    bands = lax.axis_size("sub")
    count = floors_ref.shape[0] // bands
    level = floors_ref[pl.ds(0, count, stride=bands), :]
    for band in range(1, bands):
        level = jnp.minimum(level, floors_ref[pl.ds(band, count, stride=bands), :])
    raised = [level]
    for hop in range(ROUNDS):
        raised.append(raised[-1] + hop_rise)
    ceilings = []
    for index in range(9):
        hops = hops_ref[pl.ds(index * count, count), :]
        lowest = jnp.full((count, LANES), unreached, jnp.float32)
        for hop in range(ROUNDS + 1):
            lowest = jnp.where(hops == float(hop), raised[hop], lowest)
        lowest = jnp.min(lowest, axis=0, keepdims=True) + spill_lift
        ceilings.append(jnp.broadcast_to(lowest, (SUBS, LANES)))
    start = HALO - FINAL
    spans = ((start, FINAL), (HALO, height), (HALO + height, FINAL))
    for region, (first, rows) in enumerate(spans):
        left, middle, right = ceilings[3 * region : 3 * region + 3]
        seam = jnp.where(
            lane < LANES // 2,
            jnp.where(sub == SUBS - 1, right, middle),
            jnp.where(sub == 0, left, middle),
        )

        def body(row, carry):
            for slot in range(ring):
                where = pl.ds(pl.multiple_of((first + row) * size + slot * SUBS, SUBS), SUBS)
                value = jnp.minimum(surface_ref[where, :], seam if slot == tiles else middle)
                one_ref[where, :] = jnp.maximum(ground_ref[where, :], value)
            return carry

        lax.fori_loop(0, rows, body, 0, unroll=4)
    for step in range(FINAL):
        source, target = (one_ref, two_ref) if step % 2 == 0 else (two_ref, one_ref)
        first = start + step + 1
        relax_pass(source, target, ground_ref, first, 2 * HALO + height - 2 * first, ring)
    final_ref = one_ref if FINAL % 2 == 0 else two_ref
    copies = []
    for group in range(height // SUBS):
        for tile in range(tiles * SUBS):
            chunk, slot = tile // tiles, tile % tiles
            source = (HALO + group * SUBS) * size + slot * SUBS + chunk
            out_ref[pl.ds(group * SUBS, SUBS), pl.ds(tile * LANES, LANES)] = final_ref[
                pl.ds(source, SUBS, stride=size), :
            ]
        where = (pl.ds(group * SUBS, SUBS), slice(None))
        copies.append(pltpu.make_async_copy(out_ref.at[where], out_hbm.at[where], sems.at[group]))
        copies[-1].start()
    for copy in copies:
        copy.wait()


def in_vmem(count):
    return [pl.BlockSpec(memory_space=pltpu.VMEM)] * count


def in_hbm(count):
    return [pl.BlockSpec(memory_space=pltpu.HBM)] * count


def per_device(elevation, fill_depth, edge_rows, edge_sides, adjacency):
    height, width = elevation.shape
    tiles = width // (SUBS * LANES)
    groups = height // SUBS
    f32 = jnp.float32
    row_size = tiles * SUBS
    limit = pltpu.CompilerParams(vmem_limit_bytes=24 << 20)
    own, far, near, even, odd = pl.pallas_call(
        pack_kernel,
        out_shape=[
            pltpu.VMEM((2 * height * row_size, LANES), f32),
            pltpu.VMEM((2 * HALO * row_size, LANES), f32),
            pltpu.VMEM((2 * HALO * row_size, LANES), f32),
            pltpu.VMEM((2 * height, LANES), f32),
            pltpu.VMEM((2 * height, LANES), f32),
        ],
        in_specs=in_hbm(2) + in_vmem(2),
        out_specs=in_vmem(5),
        scratch_shapes=[
            pltpu.VMEM((height, width), f32),
            pltpu.VMEM((height, width), f32),
            pltpu.SemaphoreType.DMA((2, 4 * groups)),
        ],
        compiler_params=limit,
    )(elevation, fill_depth, edge_rows, edge_sides)

    places = lax.axis_size(("rows", "sub"))
    cols = lax.axis_size("cols")
    near_pairs, far_pairs = matching(places, 0), matching(places, 1)
    stay = [(place, place) for place in range(places)]
    far_rows = lax.ppermute(far, ("rows", "sub"), far_pairs)
    near_rows = lax.ppermute(near, ("rows", "sub"), near_pairs)
    strips = []
    for row_pairs in (stay, far_pairs, near_pairs):
        for piece, col_pairs in ((even, matching(cols, 0)), (odd, matching(cols, 1))):
            pairs = cross(row_pairs, col_pairs, cols, lax.axis_size("sub"))
            strips.append(lax.ppermute(piece, ("rows", "cols", "sub"), pairs) if pairs else piece)

    def early(own_ref, far_ref, near_ref, *refs):
        strip_refs = [refs[0:2], refs[2:4], refs[4:6]]
        early_kernel(height, tiles, own_ref, far_ref, near_ref, strip_refs, *refs[6:])

    total = height + 2 * HALO + BLOCK
    work = (total * (tiles + 1) * SUBS, LANES)
    devices = lax.axis_size(("rows", "cols", "sub"))
    tile_count = adjacency.shape[0]
    ground, surface, floors, hops = pl.pallas_call(
        early,
        out_shape=[
            pltpu.VMEM(work, f32),
            pltpu.VMEM(work, f32),
            pltpu.VMEM((devices, LANES), f32),
            pltpu.VMEM((9 * tile_count, LANES), f32),
        ],
        in_specs=in_vmem(10),
        out_specs=in_vmem(4),
        scratch_shapes=[pltpu.VMEM(work, f32)],
        compiler_params=limit,
    )(own, far_rows, near_rows, *strips, adjacency)

    floors = lax.all_to_all(floors, ("rows", "cols", "sub"), 0, 0, tiled=True)

    return pl.pallas_call(
        functools.partial(late_kernel, height, tiles),
        out_shape=jax.ShapeDtypeStruct((height, width), f32),
        in_specs=in_vmem(4),
        out_specs=pl.BlockSpec(memory_space=pltpu.HBM),
        scratch_shapes=[
            pltpu.VMEM(work, f32),
            pltpu.VMEM(work, f32),
            pltpu.VMEM((height, width), f32),
            pltpu.SemaphoreType.DMA((groups,)),
        ],
        compiler_params=limit,
    )(ground, surface, floors, hops)


def solution(mesh):
    placed = (
        P(("groups", "rows", "sub"), "cols"),
        P(("groups", "rows", "sub"), "cols"),
        P("groups", "cols"),
        P("groups", ("rows", "sub")),
        P("groups", None),
    )
    return jax.shard_map(
        per_device,
        mesh=mesh,
        in_specs=placed,
        out_specs=P(("groups", "rows", "sub"), "cols"),
        check_vma=False,
    )
```

```python
import functools

import jax
import jax.numpy as jnp
from jax import lax
from jax.experimental import pallas as pl
from jax.experimental.pallas import tpu as pltpu
from jax.sharding import PartitionSpec as P

PASSES = 8
FINAL = 4
ROUNDS = 4
HALO = PASSES + FINAL
SUBS = 8
LANES = 128
BLOCK = 8

unreached = 1000000000.0
rise_step = 0.01
hop_rise = 0.05
spill_lift = 3.0


def matching(count, first):
    pairs = []
    for low in range(first, count - 1, 2):
        pairs += [(low, low + 1), (low + 1, low)]
    return pairs


def cross(row_pairs, col_pairs, cols, subs):
    def device(place, col):
        return (place // subs * cols + col) * subs + place % subs

    return [
        (device(row, col), device(row_to, col_to))
        for row, row_to in row_pairs
        for col, col_to in col_pairs
    ]


def chain_place():
    subs = lax.axis_size("sub")
    return lax.axis_index("rows") * subs + lax.axis_index("sub"), lax.axis_size("rows") * subs


def position():
    sub = lax.broadcasted_iota(jnp.int32, (SUBS, LANES), 0)
    lane = lax.broadcasted_iota(jnp.int32, (SUBS, LANES), 1)
    return sub, lane


def pack_kernel(
    ground_hbm, depth_hbm, rows_hbm, sides_hbm, links_hbm,
    own_ref, far_ref, near_ref, even_ref, odd_ref, hops_ref,
    ground_ref, depth_ref, rows_ref, sides_ref, links_ref, sems, small_sems,
):
    small = [
        pltpu.make_async_copy(source, target, small_sems.at[number])
        for number, (source, target) in enumerate(
            ((rows_hbm, rows_ref), (sides_hbm, sides_ref), (links_hbm, links_ref))
        )
    ]
    for copy in small:
        copy.start()
    height, width = ground_hbm.shape
    groups = height // SUBS
    tiles = width // (SUBS * LANES)
    part = width // 4
    copies = []
    for group in range(groups):
        for piece in range(4):
            where = (pl.ds(group * SUBS, SUBS), pl.ds(piece * part, part))
            number = group * 4 + piece
            pair = (
                pltpu.make_async_copy(ground_hbm.at[where], ground_ref.at[where], sems.at[0, number]),
                pltpu.make_async_copy(depth_hbm.at[where], depth_ref.at[where], sems.at[1, number]),
            )
            for copy in pair:
                copy.start()
            copies.append(pair)
    for copy in small:
        copy.wait()
    hop_counts(links_ref, hops_ref, needed_tiles())
    place, places = chain_place()
    col, cols = lax.axis_index("cols"), lax.axis_size("cols")
    sub, lane = position()
    square = (height, height)
    diagonal = lax.broadcasted_iota(jnp.int32, square, 0) == lax.broadcasted_iota(jnp.int32, square, 1)
    marks = sides_ref[...].astype(jnp.float32)
    side_marks = [
        jnp.sum(jnp.where(diagonal, marks[side : side + 1, :], 0.0), axis=1, keepdims=True)
        for side in range(2)
    ]
    row_size = tiles * SUBS
    surface_base = height * row_size
    last_tile = width // LANES - 1
    corner = {}
    for group in range(groups):
        for tile in range(last_tile + 1):
            if tile * LANES % part == 0:
                for copy in copies[group * 4 + tile * LANES // part]:
                    copy.wait()
            rows = pl.ds(group * SUBS, SUBS)
            columns = pl.ds(tile * LANES, LANES)
            ground = ground_ref[rows, columns]
            surface = ground + depth_ref[rows, columns]
            outlets = []
            if group == 0:
                outlets.append((rows_ref[0:1, columns] == 1) & (sub == 0) & (place == 0))
            if group == groups - 1:
                outlets.append(
                    (rows_ref[1:2, columns] == 1) & (sub == SUBS - 1) & (place == places - 1)
                )
            if tile == 0:
                outlets.append(
                    (side_marks[0][group * SUBS : (group + 1) * SUBS] > 0.5) & (lane == 0) & (col == 0)
                )
            if tile == last_tile:
                outlets.append(
                    (side_marks[1][group * SUBS : (group + 1) * SUBS] > 0.5)
                    & (lane == LANES - 1)
                    & (col == cols - 1)
                )
            for outlet in outlets:
                surface = jnp.where(outlet, ground, surface)
            chunk, slot = tile // tiles, tile % tiles
            start = group * SUBS * row_size + slot * SUBS + chunk
            own_ref[pl.ds(start, SUBS, stride=row_size), :] = ground
            own_ref[pl.ds(surface_base + start, SUBS, stride=row_size), :] = surface
            if tile == 0 or tile == last_tile:
                corner[group, tile] = (ground, surface)
    for group in range(groups):
        for kind in range(2):
            first = corner[group, 0][kind]
            last = corner[group, last_tile][kind]
            rows = pl.ds(kind * height + group * SUBS, SUBS)
            rightward = col % 2 == 0
            even_ref[rows, :] = jnp.where(rightward, last, first)
            odd_ref[rows, :] = jnp.where(rightward, first, last)
    top = place % 2 == 0
    span = HALO * row_size
    for out_ref, is_top in ((far_ref, top), (near_ref, jnp.logical_not(top))):
        offset = jnp.where(is_top, 0, (height - HALO) * row_size)
        for kind in range(2):
            for row in range(HALO):
                source = pl.multiple_of(kind * surface_base + offset + row * row_size, SUBS)
                target = kind * span + row * row_size
                out_ref[pl.ds(target, row_size), :] = own_ref[pl.ds(source, row_size), :]


def relax_pass(source, target, ground, first, count, ring):
    size = ring * SUBS
    _, lane = position()
    at_first = lane == 0
    at_last = lane == LANES - 1

    def body(step, carry):
        base = first + step * BLOCK

        def load(ref, row, slot):
            return ref[pl.ds(pl.multiple_of((base + row) * size + slot * SUBS, SUBS), SUBS), :]

        for row in range(0, BLOCK, 2):
            center = [[], []]
            column = [[], []]
            for slot in range(ring):
                high = load(source, row, slot)
                low = load(source, row + 1, slot)
                both = jnp.minimum(high, low)
                center[0].append(high)
                center[1].append(low)
                column[0].append(jnp.minimum(load(source, row - 1, slot), both))
                column[1].append(jnp.minimum(load(source, row + 2, slot), both))
            for one in range(2):
                left = [pltpu.roll(value, 1, 1) for value in column[one]]
                right = [pltpu.roll(value, LANES - 1, 1) for value in column[one]]
                for slot in range(ring):
                    from_left = jnp.where(at_first, left[slot - 1], left[slot])
                    from_right = jnp.where(at_last, right[(slot + 1) % ring], right[slot])
                    lowest = jnp.minimum(jnp.minimum(from_left, from_right), column[one][slot])
                    raised = jnp.minimum(center[one][slot], lowest + rise_step)
                    result = jnp.maximum(load(ground, row + one, slot), raised)
                    where = pl.multiple_of((base + row + one) * size + slot * SUBS, SUBS)
                    target[pl.ds(where, SUBS), :] = result
        return carry

    lax.fori_loop(0, -(-count // BLOCK), body, 0)


def hop_counts(links_ref, hops_ref, needed):
    tiles, degree = links_ref.shape
    links = links_ref[...]
    number = lax.broadcasted_iota(jnp.int32, (tiles, tiles), 1)
    linked = links[:, 0:1] == number
    for edge in range(1, degree):
        linked = linked | (links[:, edge : edge + 1] == number)
    linked = linked.astype(jnp.float32)
    tile = lax.broadcasted_iota(jnp.int32, (tiles, LANES), 0)
    lane = lax.broadcasted_iota(jnp.int32, (tiles, LANES), 1)
    reached = jnp.zeros((tiles, LANES), jnp.float32)
    for index, wanted in enumerate(needed):
        reached = jnp.where((lane == index) & (tile == wanted), 1.0, reached)
    hops = jnp.where(reached > 0.5, 0.0, float(ROUNDS + 1))
    for hop in range(1, ROUNDS + 1):
        reached = lax.dot_general(
            linked, reached, (((0,), (0,)), ((), ())), preferred_element_type=jnp.float32
        )
        reached = jnp.where(reached > 0.5, 1.0, 0.0)
        hops = jnp.minimum(hops, jnp.where(reached > 0.5, float(hop), float(ROUNDS + 1)))
    for index in range(len(needed)):
        hops_ref[pl.ds(index * tiles, tiles), :] = jnp.broadcast_to(
            hops[:, index : index + 1], (tiles, LANES)
        )


def needed_tiles():
    row, rows = lax.axis_index("rows"), lax.axis_size("rows")
    col, cols = lax.axis_index("cols"), lax.axis_size("cols")
    sub, subs = lax.axis_index("sub"), lax.axis_size("sub")
    above = jnp.maximum(jnp.where(sub == 0, row - 1, row), 0)
    below = jnp.minimum(jnp.where(sub == subs - 1, row + 1, row), rows - 1)
    left = jnp.maximum(col - 1, 0)
    right = jnp.minimum(col + 1, cols - 1)
    return [r * cols + c for r in (above, row, below) for c in (left, col, right)]


def early_kernel(
    height, tiles, own_ref, far_ref, near_ref, strips_refs,
    ground_ref, surface_ref, floor_ref, other_ref,
):
    ring = tiles + 1
    size = ring * SUBS
    place, places = chain_place()
    col, cols = lax.axis_index("cols"), lax.axis_size("cols")
    sub, lane = position()
    top = place % 2 == 0
    has_far = jnp.where(top, place > 0, place < places - 1)
    has_near = jnp.where(top, place < places - 1, place > 0)
    low, high = 0, HALO + height
    rightward = col % 2 == 0
    regions = (
        (own_ref, height, HALO, None, 0),
        (far_ref, HALO, jnp.where(top, low, high), has_far, jnp.where(top, height - HALO, 0)),
        (near_ref, HALO, jnp.where(top, high, low), has_near, jnp.where(top, 0, height - HALO)),
    )
    for region, (ref, count, first, present, strip_first) in enumerate(regions):
        even_ref, odd_ref = strips_refs[region]
        for kind, out_ref in ((0, ground_ref), (1, surface_ref)):

            def body(row, carry):
                def keep(value, exists):
                    return jnp.where(exists, value, unreached) if exists is not None else value

                source = (kind * count + row) * tiles * SUBS
                target = (first + row) * size
                values = [
                    keep(
                        ref[pl.ds(pl.multiple_of(source + slot * SUBS, SUBS), SUBS), :], present
                    )
                    for slot in range(tiles)
                ]
                for slot in range(tiles):
                    out_ref[pl.ds(pl.multiple_of(target + slot * SUBS, SUBS), SUBS), :] = values[slot]
                strip_row = kind * height + strip_first + row
                even = even_ref[pl.ds(strip_row, 1), :]
                odd = odd_ref[pl.ds(strip_row, 1), :]
                after = jnp.where(rightward, even, odd)
                before = jnp.where(rightward, odd, even)
                after = keep(jnp.where(col < cols - 1, after, unreached), present)
                before = keep(jnp.where(col > 0, before, unreached), present)
                after = jnp.where(sub == SUBS - 1, after, pltpu.roll(values[0], SUBS - 1, 0))
                before = jnp.where(sub == 0, before, pltpu.roll(values[-1], 1, 0))
                seam = jnp.where(lane < LANES // 2, after, before)
                out_ref[pl.ds(pl.multiple_of(target + tiles * SUBS, SUBS), SUBS), :] = seam
                return carry

            lax.fori_loop(0, count, body, 0, unroll=4)
    total = height + 2 * HALO
    for step in range(PASSES):
        source, target = (surface_ref, other_ref) if step % 2 == 0 else (other_ref, surface_ref)
        relax_pass(source, target, ground_ref, step + 1, total - 2 * (step + 1), ring)
    final_ref = surface_ref if PASSES % 2 == 0 else other_ref
    band, bands = lax.axis_index("sub"), lax.axis_size("sub")
    lowest = jnp.full((SUBS, LANES), unreached, jnp.float32)

    def at(row, slot):
        return final_ref[pl.ds((HALO + row) * size + slot * SUBS, SUBS), :]

    for slot in range(tiles):
        lowest = jnp.minimum(lowest, jnp.where(band == 0, at(0, slot), unreached))
        lowest = jnp.minimum(lowest, jnp.where(band == bands - 1, at(height - 1, slot), unreached))
    first_cell = (sub == 0) & (lane == 0)
    last_cell = (sub == SUBS - 1) & (lane == LANES - 1)
    for row in range(height):
        lowest = jnp.minimum(lowest, jnp.where(first_cell, at(row, 0), unreached))
        lowest = jnp.minimum(lowest, jnp.where(last_cell, at(row, tiles - 1), unreached))
    lowest = jnp.min(jnp.min(lowest, axis=0, keepdims=True), axis=1, keepdims=True)
    floor_ref[...] = jnp.broadcast_to(lowest, floor_ref.shape)


def late_kernel(
    height, tiles, ground_ref, surface_ref, floors_ref, hops_ref, out_hbm,
    one_ref, two_ref, out_ref, sems,
):
    ring = tiles + 1
    size = ring * SUBS
    sub, lane = position()
    bands = lax.axis_size("sub")
    count = floors_ref.shape[0] // bands
    level = floors_ref[pl.ds(0, count, stride=bands), :]
    for band in range(1, bands):
        level = jnp.minimum(level, floors_ref[pl.ds(band, count, stride=bands), :])
    raised = [level]
    for hop in range(ROUNDS):
        raised.append(raised[-1] + hop_rise)
    ceilings = []
    for index in range(9):
        hops = hops_ref[pl.ds(index * count, count), :]
        lowest = jnp.full((count, LANES), unreached, jnp.float32)
        for hop in range(ROUNDS + 1):
            lowest = jnp.where(hops == float(hop), raised[hop], lowest)
        lowest = jnp.min(lowest, axis=0, keepdims=True) + spill_lift
        ceilings.append(jnp.broadcast_to(lowest, (SUBS, LANES)))
    start = HALO - FINAL
    spans = ((start, FINAL), (HALO, height), (HALO + height, FINAL))
    for region, (first, rows) in enumerate(spans):
        left, middle, right = ceilings[3 * region : 3 * region + 3]
        seam = jnp.where(
            lane < LANES // 2,
            jnp.where(sub == SUBS - 1, right, middle),
            jnp.where(sub == 0, left, middle),
        )

        def body(row, carry):
            for slot in range(ring):
                where = pl.ds(pl.multiple_of((first + row) * size + slot * SUBS, SUBS), SUBS)
                value = jnp.minimum(surface_ref[where, :], seam if slot == tiles else middle)
                one_ref[where, :] = jnp.maximum(ground_ref[where, :], value)
            return carry

        lax.fori_loop(0, rows, body, 0, unroll=4)
    for step in range(FINAL):
        source, target = (one_ref, two_ref) if step % 2 == 0 else (two_ref, one_ref)
        first = start + step + 1
        relax_pass(source, target, ground_ref, first, 2 * HALO + height - 2 * first, ring)
    final_ref = one_ref if FINAL % 2 == 0 else two_ref
    copies = []
    for group in range(height // SUBS):
        for tile in range(tiles * SUBS):
            chunk, slot = tile // tiles, tile % tiles
            source = (HALO + group * SUBS) * size + slot * SUBS + chunk
            out_ref[pl.ds(group * SUBS, SUBS), pl.ds(tile * LANES, LANES)] = final_ref[
                pl.ds(source, SUBS, stride=size), :
            ]
        where = (pl.ds(group * SUBS, SUBS), slice(None))
        copies.append(pltpu.make_async_copy(out_ref.at[where], out_hbm.at[where], sems.at[group]))
        copies[-1].start()
    for copy in copies:
        copy.wait()


def in_vmem(count):
    return [pl.BlockSpec(memory_space=pltpu.VMEM)] * count


def in_hbm(count):
    return [pl.BlockSpec(memory_space=pltpu.HBM)] * count


def per_device(elevation, fill_depth, edge_rows, edge_sides, adjacency):
    height, width = elevation.shape
    tiles = width // (SUBS * LANES)
    groups = height // SUBS
    f32 = jnp.float32
    row_size = tiles * SUBS
    limit = pltpu.CompilerParams(vmem_limit_bytes=24 << 20)
    tile_count = adjacency.shape[0]
    arguments = [
        pltpu.with_memory_space_constraint(value, pltpu.HBM)
        for value in (elevation, fill_depth, edge_rows, edge_sides, adjacency)
    ]
    own, far, near, even, odd, hops = pl.pallas_call(
        pack_kernel,
        out_shape=[
            pltpu.VMEM((2 * height * row_size, LANES), f32),
            pltpu.VMEM((2 * HALO * row_size, LANES), f32),
            pltpu.VMEM((2 * HALO * row_size, LANES), f32),
            pltpu.VMEM((2 * height, LANES), f32),
            pltpu.VMEM((2 * height, LANES), f32),
            pltpu.VMEM((9 * tile_count, LANES), f32),
        ],
        in_specs=in_hbm(5),
        out_specs=in_vmem(6),
        scratch_shapes=[
            pltpu.VMEM((height, width), f32),
            pltpu.VMEM((height, width), f32),
            pltpu.VMEM(edge_rows.shape, jnp.int32),
            pltpu.VMEM(edge_sides.shape, jnp.int32),
            pltpu.VMEM(adjacency.shape, jnp.int32),
            pltpu.SemaphoreType.DMA((2, 4 * groups)),
            pltpu.SemaphoreType.DMA((3,)),
        ],
        compiler_params=limit,
    )(*arguments)

    places = lax.axis_size(("rows", "sub"))
    cols = lax.axis_size("cols")
    near_pairs, far_pairs = matching(places, 0), matching(places, 1)
    stay = [(place, place) for place in range(places)]
    far_rows = lax.ppermute(far, ("rows", "sub"), far_pairs)
    near_rows = lax.ppermute(near, ("rows", "sub"), near_pairs)
    strips = []
    for row_pairs in (stay, far_pairs, near_pairs):
        for piece, col_pairs in ((even, matching(cols, 0)), (odd, matching(cols, 1))):
            pairs = cross(row_pairs, col_pairs, cols, lax.axis_size("sub"))
            strips.append(lax.ppermute(piece, ("rows", "cols", "sub"), pairs) if pairs else piece)

    def early(own_ref, far_ref, near_ref, *refs):
        strip_refs = [refs[0:2], refs[2:4], refs[4:6]]
        early_kernel(height, tiles, own_ref, far_ref, near_ref, strip_refs, *refs[6:])

    total = height + 2 * HALO + BLOCK
    work = (total * (tiles + 1) * SUBS, LANES)
    devices = lax.axis_size(("rows", "cols", "sub"))
    ground, surface, floors = pl.pallas_call(
        early,
        out_shape=[
            pltpu.VMEM(work, f32),
            pltpu.VMEM(work, f32),
            pltpu.VMEM((devices, LANES), f32),
        ],
        in_specs=in_vmem(9),
        out_specs=in_vmem(3),
        scratch_shapes=[pltpu.VMEM(work, f32)],
        compiler_params=limit,
    )(own, far_rows, near_rows, *strips)

    floors = lax.all_to_all(floors, ("rows", "cols", "sub"), 0, 0, tiled=True)

    return pl.pallas_call(
        functools.partial(late_kernel, height, tiles),
        out_shape=jax.ShapeDtypeStruct((height, width), f32),
        in_specs=in_vmem(4),
        out_specs=pl.BlockSpec(memory_space=pltpu.HBM),
        scratch_shapes=[
            pltpu.VMEM(work, f32),
            pltpu.VMEM(work, f32),
            pltpu.VMEM((height, width), f32),
            pltpu.SemaphoreType.DMA((groups,)),
        ],
        compiler_params=limit,
    )(ground, surface, floors, hops)


def solution(mesh):
    placed = (
        P(("groups", "rows", "sub"), "cols"),
        P(("groups", "rows", "sub"), "cols"),
        P("groups", "cols"),
        P("groups", ("rows", "sub")),
        P("groups", None),
    )
    return jax.shard_map(
        per_device,
        mesh=mesh,
        in_specs=placed,
        out_specs=P(("groups", "rows", "sub"), "cols"),
        check_vma=False,
    )
```

```python
import jax
import jax.numpy as jnp
from jax import lax
from jax.experimental import pallas as pl
from jax.experimental.pallas import tpu as pltpu
from jax.sharding import PartitionSpec as P

PASSES = 8
FINAL = 4
ROUNDS = 4
SUBS = 8
LANES = 128
AHEAD = 5

unreached = 1000000000.0
rise_step = 0.01
hop_rise = 0.05
spill_lift = 3.0


def matching(count, first):
    pairs = []
    for low in range(first, count - 1, 2):
        pairs += [(low, low + 1), (low + 1, low)]
    return pairs


def cross(row_pairs, col_pairs, cols, subs):
    def device(place, col):
        return (place // subs * cols + col) * subs + place % subs

    return [
        (device(row, col), device(row_to, col_to))
        for row, row_to in row_pairs
        for col, col_to in col_pairs
    ]


def chain_place():
    subs = lax.axis_size("sub")
    return lax.axis_index("rows") * subs + lax.axis_index("sub"), lax.axis_size("rows") * subs


def position():
    sub = lax.broadcasted_iota(jnp.int32, (SUBS, LANES), 0)
    lane = lax.broadcasted_iota(jnp.int32, (SUBS, LANES), 1)
    return sub, lane


def aligned(start):
    return start if isinstance(start, int) else pl.multiple_of(start, SUBS)


def rows_at(first, count, size):
    return pl.ds(aligned(first * size), count * size)


def register(row, slot, size):
    return pl.ds(aligned(row * size + slot * SUBS), SUBS)


def side_marks(sides_ref):
    height = sides_ref.shape[1]
    square = (height, height)
    diagonal = lax.broadcasted_iota(jnp.int32, square, 0) == lax.broadcasted_iota(jnp.int32, square, 1)
    marks = sides_ref[...].astype(jnp.float32)
    return [
        jnp.sum(jnp.where(diagonal, marks[side : side + 1, :], 0.0), axis=1, keepdims=True)
        for side in range(2)
    ]


def start_all(copies):
    for copy in copies:
        copy.start()
    return copies


def wait_all(copies):
    for copy in copies:
        copy.wait()


def far_kernel(
    ground_hbm, depth_hbm, rows_hbm, sides_hbm,
    far_ref, far_even_ref, far_odd_ref, even_ref, odd_ref,
    ground_ref, depth_ref, edge_ref, marks_ref, sides_ref, sems, small_sems,
):
    height, width = ground_hbm.shape
    groups = height // SUBS
    tiles = width // (SUBS * LANES)
    last_tile = width // LANES - 1
    pieces = sems.shape[1]
    part = width // pieces
    place, places = chain_place()
    col, cols = lax.axis_index("cols"), lax.axis_size("cols")
    top = place % 2 == 0
    far_first = aligned(jnp.where(top, 0, height - SUBS))
    small = [pltpu.make_async_copy(sides_hbm, sides_ref, small_sems.at[0])]
    for side, tile in enumerate((0, last_tile)):
        columns = pl.ds(tile * LANES, LANES)
        for number, (source, target) in enumerate(
            (
                (ground_hbm.at[:, columns], edge_ref.at[side, 0]),
                (depth_hbm.at[:, columns], edge_ref.at[side, 1]),
                (rows_hbm.at[:, columns], marks_ref.at[side]),
            )
        ):
            small.append(pltpu.make_async_copy(source, target, small_sems.at[1 + side * 3 + number]))
    copies = []
    for piece in range(pieces):
        columns = pl.ds(piece * part, part)
        copies.append(
            [
                pltpu.make_async_copy(
                    source.at[pl.ds(far_first, SUBS), columns], target.at[:, columns], sems.at[kind, piece]
                )
                for kind, (source, target) in enumerate(((ground_hbm, ground_ref), (depth_hbm, depth_ref)))
            ]
        )
    start_all(copies[0])
    start_all(small)
    for pair in copies[1:]:
        start_all(pair)
    sub, lane = position()
    size = tiles * SUBS
    ground_base = jnp.where(top, 0, (SUBS - 1) * size)
    surface_base = jnp.where(top, (SUBS - 1) * size, 0)
    wait_all(copies[0])
    wait_all(small)
    marks = side_marks(sides_ref)
    shown = []
    for side in range(2):
        chosen = jnp.where(top, marks[side][:SUBS], marks[side][height - SUBS :])
        shown.append(
            (chosen > 0.5)
            & (lane == (0 if side == 0 else LANES - 1))
            & (col == (0 if side == 0 else cols - 1))
        )
    for tile in range(last_tile + 1):
        if tile and tile * LANES % part == 0:
            wait_all(copies[tile * LANES // part])
        columns = pl.ds(tile * LANES, LANES)
        ground = ground_ref[:, columns]
        surface = ground + depth_ref[:, columns]
        if tile == 0:
            surface = jnp.where(shown[0], ground, surface)
        if tile == last_tile:
            surface = jnp.where(shown[1], ground, surface)
        chunk, slot = tile // tiles, tile % tiles
        start = slot * SUBS + chunk
        far_ref[pl.ds(ground_base + start, SUBS, stride=size), :] = ground
        far_ref[pl.ds(surface_base + start, SUBS, stride=size), :] = surface
    rightward = col % 2 == 0
    strips = []
    for group in range(groups):
        rows = pl.ds(group * SUBS, SUBS)
        values = []
        for side in range(2):
            ground = edge_ref[side, 0, rows, :]
            surface = ground + edge_ref[side, 1, rows, :]
            outlet = (
                (marks[side][group * SUBS : (group + 1) * SUBS] > 0.5)
                & (lane == (0 if side == 0 else LANES - 1))
                & (col == (0 if side == 0 else cols - 1))
            )
            if group == 0:
                outlet = outlet | (marks_ref[side, 0:1] == 1) & (sub == 0) & (place == 0)
            if group == groups - 1:
                outlet = outlet | (marks_ref[side, 1:2] == 1) & (sub == SUBS - 1) & (place == places - 1)
            values.append((ground, jnp.where(outlet, ground, surface)))
        strips.append(values)
        for kind in range(2):
            rows = pl.ds(kind * height + group * SUBS, SUBS)
            even_ref[rows, :] = jnp.where(rightward, values[1][kind], values[0][kind])
            odd_ref[rows, :] = jnp.where(rightward, values[0][kind], values[1][kind])
    for kind in range(2):
        rows = pl.ds(kind * SUBS, SUBS)
        first, last = [jnp.where(top, strips[0][side][kind], strips[-1][side][kind]) for side in range(2)]
        far_even_ref[rows, :] = jnp.where(rightward, last, first)
        far_odd_ref[rows, :] = jnp.where(rightward, first, last)


def own_kernel(
    ground_hbm, depth_hbm, rows_hbm, sides_hbm, links_hbm, after_ref,
    ground_out, surface_out, near_ref, hops_ref,
    ground_ref, depth_ref, rows_ref, sides_ref, links_ref, sems, small_sems,
):
    height, width = ground_hbm.shape
    groups = height // SUBS
    tiles = width // (SUBS * LANES)
    last_tile = width // LANES - 1
    pieces = sems.shape[1] // groups
    part = width // pieces
    size = (tiles + 1) * SUBS
    copies = []
    for group in range(groups):
        for piece in range(pieces):
            where = (pl.ds(group * SUBS, SUBS), pl.ds(piece * part, part))
            number = group * pieces + piece
            copies.append(
                start_all(
                    [
                        pltpu.make_async_copy(ground_hbm.at[where], ground_ref.at[where], sems.at[0, number]),
                        pltpu.make_async_copy(depth_hbm.at[where], depth_ref.at[where], sems.at[1, number]),
                    ]
                )
            )
    small = start_all(
        [
            pltpu.make_async_copy(source, target, small_sems.at[number])
            for number, (source, target) in enumerate(
                ((rows_hbm, rows_ref), (sides_hbm, sides_ref), (links_hbm, links_ref))
            )
        ]
    )
    wait_all(small)
    hop_counts(links_ref, hops_ref, needed_tiles())
    place, places = chain_place()
    col, cols = lax.axis_index("cols"), lax.axis_size("cols")
    sub, lane = position()
    marks = side_marks(sides_ref)
    for group in range(groups):
        rows = pl.ds(group * SUBS, SUBS)
        for tile in range(last_tile + 1):
            if tile * LANES % part == 0:
                wait_all(copies[group * pieces + tile * LANES // part])
            columns = pl.ds(tile * LANES, LANES)
            ground = ground_ref[rows, columns]
            surface = ground + depth_ref[rows, columns]
            outlets = []
            if group == 0:
                outlets.append((rows_ref[0:1, columns] == 1) & (sub == 0) & (place == 0))
            if group == groups - 1:
                outlets.append(
                    (rows_ref[1:2, columns] == 1) & (sub == SUBS - 1) & (place == places - 1)
                )
            if tile == 0:
                outlets.append(
                    (marks[0][group * SUBS : (group + 1) * SUBS] > 0.5) & (lane == 0) & (col == 0)
                )
            if tile == last_tile:
                outlets.append(
                    (marks[1][group * SUBS : (group + 1) * SUBS] > 0.5)
                    & (lane == LANES - 1)
                    & (col == cols - 1)
                )
            for outlet in outlets:
                surface = jnp.where(outlet, ground, surface)
            chunk, slot = tile // tiles, tile % tiles
            start = (PASSES + group * SUBS) * size + slot * SUBS + chunk
            ground_out[pl.ds(start, SUBS, stride=size), :] = ground
            surface_out[pl.ds(start, SUBS, stride=size), :] = surface
    top = place % 2 == 0
    first = PASSES + jnp.where(top, height - SUBS, 0)
    packed = tiles * SUBS
    ground_base = jnp.where(top, SUBS - 1, 0)
    surface_base = jnp.where(top, 0, SUBS - 1)
    for source, base in ((ground_out, ground_base), (surface_out, surface_base)):
        for row in range(SUBS):
            for slot in range(tiles):
                near_ref[register(base + row, slot, packed), :] = source[register(first + row, slot, size), :]


def unpack_rows(rows_ref, first, is_top, present, strip_refs, strip_rows, ground_ref, surface_ref, tiles):
    packed = tiles * SUBS
    size = packed + SUBS
    bases = (jnp.where(is_top, SUBS - 1, 0), jnp.where(is_top, 0, SUBS - 1))
    for base, out_ref, strip_row in zip(bases, (ground_ref, surface_ref), strip_rows):

        def body(row, carry):
            values = [
                jnp.where(present, rows_ref[register(base + row, slot, packed), :], unreached)
                for slot in range(tiles)
            ]
            for slot in range(tiles):
                out_ref[register(first + row, slot, size), :] = values[slot]
            fill_seam(out_ref, first + row, values[0], values[-1], strip_refs, strip_row + row, present, tiles)
            return carry

        lax.fori_loop(0, PASSES, body, 0, unroll=4)


def fill_seam(out_ref, row, first_tile, last_tile, strip_refs, strip_row, present, tiles):
    col, cols = lax.axis_index("cols"), lax.axis_size("cols")
    sub, lane = position()
    rightward = col % 2 == 0
    even, odd = [ref[pl.ds(strip_row, 1), :] for ref in strip_refs]
    after = jnp.where(present & (col < cols - 1), jnp.where(rightward, even, odd), unreached)
    before = jnp.where(present & (col > 0), jnp.where(rightward, odd, even), unreached)
    after = jnp.where(sub == SUBS - 1, after, pltpu.roll(first_tile, SUBS - 1, 0))
    before = jnp.where(sub == 0, before, pltpu.roll(last_tile, 1, 0))
    out_ref[register(row, tiles, (tiles + 1) * SUBS), :] = jnp.where(lane < LANES // 2, after, before)


def relax_rows(source, target, ground, first, count, ring):
    size = ring * SUBS
    _, lane = position()
    at_first = lane == 0
    at_last = lane == LANES - 1
    order = [ring - 1] + list(range(ring - 1))
    made = {}

    def make(pair, slot):
        row = first + 2 * pair
        values = [source[register(row + step, slot, size), :] for step in range(-1, 3)]
        both = jnp.minimum(values[1], values[2])
        for one, column in enumerate((jnp.minimum(values[0], both), jnp.minimum(both, values[3]))):
            made[pair, one, slot] = (column, pltpu.roll(column, 1, 1), pltpu.roll(column, LANES - 1, 1))

    def finish(pair, slot):
        for one in range(2):
            row = first + 2 * pair + one
            before, here, after = [made[pair, one, (slot + step) % ring] for step in (-1, 0, 1)]
            from_left = jnp.where(at_first, before[1], here[1])
            from_right = jnp.where(at_last, after[2], here[2])
            lowest = jnp.minimum(jnp.minimum(from_left, from_right), here[0])
            where = register(row, slot, size)
            raised = jnp.minimum(source[where, :], lowest + rise_step)
            target[where, :] = jnp.maximum(ground[where, :], raised)

    makes = [(pair, slot) for pair in range(count // 2) for slot in order]
    finishes = [(pair, slot) for pair in range(count // 2) for slot in range(ring)]
    done = 0
    for number, item in enumerate(makes):
        make(*item)
        if number >= AHEAD:
            finish(*finishes[done])
            done += 1
    for item in finishes[done:]:
        finish(*item)


def hop_counts(links_ref, hops_ref, needed):
    tiles, degree = links_ref.shape
    links = links_ref[...]
    number = lax.broadcasted_iota(jnp.int32, (tiles, tiles), 1)
    linked = links[:, 0:1] == number
    for edge in range(1, degree):
        linked = linked | (links[:, edge : edge + 1] == number)
    linked = linked.astype(jnp.float32)
    tile = lax.broadcasted_iota(jnp.int32, (tiles, LANES), 0)
    lane = lax.broadcasted_iota(jnp.int32, (tiles, LANES), 1)
    reached = jnp.zeros((tiles, LANES), jnp.float32)
    for index, wanted in enumerate(needed):
        reached = jnp.where((lane == index) & (tile == wanted), 1.0, reached)
    hops = jnp.where(reached > 0.5, 0.0, float(ROUNDS + 1))
    for hop in range(1, ROUNDS + 1):
        reached = lax.dot_general(
            linked, reached, (((0,), (0,)), ((), ())), preferred_element_type=jnp.float32
        )
        reached = jnp.where(reached > 0.5, 1.0, 0.0)
        hops = jnp.minimum(hops, jnp.where(reached > 0.5, float(hop), float(ROUNDS + 1)))
    for index in range(len(needed)):
        hops_ref[pl.ds(index * tiles, tiles), :] = jnp.broadcast_to(
            hops[:, index : index + 1], (tiles, LANES)
        )


def needed_tiles():
    row, rows = lax.axis_index("rows"), lax.axis_size("rows")
    col, cols = lax.axis_index("cols"), lax.axis_size("cols")
    sub, subs = lax.axis_index("sub"), lax.axis_size("sub")
    above = jnp.maximum(jnp.where(sub == 0, row - 1, row), 0)
    below = jnp.minimum(jnp.where(sub == subs - 1, row + 1, row), rows - 1)
    left = jnp.maximum(col - 1, 0)
    right = jnp.minimum(col + 1, cols - 1)
    return [r * cols + c for r in (above, row, below) for c in (left, col, right)]


def inner_kernel(height, tiles, near_ref, *refs):
    own_strips, near_strips = refs[0:2], refs[2:4]
    ground_ref, surface_ref, other_ref = refs[6:9]
    ring = tiles + 1
    size = ring * SUBS
    place, places = chain_place()
    top = place % 2 == 0
    has_near = jnp.where(top, place < places - 1, place > 0)
    unpack_rows(
        near_ref,
        jnp.where(top, PASSES + height, 0),
        jnp.logical_not(top),
        has_near,
        near_strips,
        [kind * height + jnp.where(top, 0, height - SUBS) for kind in range(2)],
        ground_ref,
        surface_ref,
        tiles,
    )
    for kind, out_ref in enumerate((ground_ref, surface_ref)):

        def body(row, carry):
            first_tile = out_ref[register(PASSES + row, 0, size), :]
            last_tile = out_ref[register(PASSES + row, tiles - 1, size), :]
            fill_seam(
                out_ref, PASSES + row, first_tile, last_tile, own_strips, kind * height + row, place >= 0, tiles
            )
            return carry

        lax.fori_loop(0, height, body, 0, unroll=4)
    buffers = (surface_ref, other_ref)
    for step in range(1, PASSES + 1):
        first = step + jnp.where(top, PASSES, 0)
        count = height + PASSES - 2 * step
        relax_rows(buffers[(step + 1) % 2], buffers[step % 2], ground_ref, first, count, ring)


def outer_kernel(height, tiles, far_ref, even_ref, odd_ref, *refs):
    ground_ref, surface_ref, other_ref, level_ref, far_out, near_out = refs[3:9]
    ring = tiles + 1
    size = ring * SUBS
    place, places = chain_place()
    top = place % 2 == 0
    has_far = jnp.where(top, place > 0, place < places - 1)
    unpack_rows(
        far_ref,
        jnp.where(top, 0, PASSES + height),
        top,
        has_far,
        (even_ref, odd_ref),
        [0, SUBS],
        ground_ref,
        surface_ref,
        tiles,
    )
    buffers = (surface_ref, other_ref)
    for step in range(1, PASSES + 1):
        first = jnp.where(top, step, PASSES + height - step)
        relax_rows(buffers[(step + 1) % 2], buffers[step % 2], ground_ref, first, PASSES, ring)
    low, high = PASSES, PASSES + height - FINAL
    far_out[...] = surface_ref[rows_at(jnp.where(top, low, high), FINAL, size), :]
    near_out[...] = surface_ref[rows_at(jnp.where(top, high, low), FINAL, size), :]
    band, bands = lax.axis_index("sub"), lax.axis_size("sub")
    sub, lane = position()

    def at(row, slot):
        return surface_ref[register(PASSES + row, slot, size), :]

    first_cell = (sub == 0) & (lane == 0)
    last_cell = (sub == SUBS - 1) & (lane == LANES - 1)
    first_lows, last_lows, row_lows = [], [], []
    for row in range(height):
        first_lows.append(at(row, 0))
        last_lows.append(at(row, tiles - 1))
    for slot in range(tiles):
        row_lows.append(jnp.where(band == 0, at(0, slot), unreached))
        row_lows.append(jnp.where(band == bands - 1, at(height - 1, slot), unreached))
    lowest = jnp.minimum(
        least(row_lows),
        jnp.minimum(
            jnp.where(first_cell, least(first_lows), unreached),
            jnp.where(last_cell, least(last_lows), unreached),
        ),
    )
    lowest = jnp.min(jnp.min(lowest, axis=0, keepdims=True), axis=1, keepdims=True)
    tile_id = lax.axis_index("rows") * lax.axis_size("cols") + lax.axis_index("cols")
    number = lax.broadcasted_iota(jnp.int32, level_ref.shape, 0)
    level_ref[...] = jnp.where(number == tile_id, lowest, unreached)


def least(values):
    values = list(values)
    while len(values) > 1:
        values = [
            jnp.minimum(*values[number : number + 2]) if number + 1 < len(values) else values[number]
            for number in range(0, len(values), 2)
        ]
    return values[0]


def late_kernel(
    height, tiles, ground_ref, surface_ref, far_ref, near_ref, level_ref, hops_ref, out_hbm,
    one_ref, two_ref, out_ref, sems,
):
    ring = tiles + 1
    size = ring * SUBS
    sub, lane = position()
    place, _ = chain_place()
    top = place % 2 == 0
    level = level_ref[...]
    count = level.shape[0]
    raised = [level]
    for hop in range(ROUNDS):
        raised.append(raised[-1] + hop_rise)
    ceilings = []
    for index in range(9):
        hops = hops_ref[pl.ds(index * count, count), :]
        lowest = jnp.full((count, LANES), unreached, jnp.float32)
        for hop in range(ROUNDS + 1):
            lowest = jnp.where(hops == float(hop), raised[hop], lowest)
        lowest = jnp.min(lowest, axis=0, keepdims=True) + spill_lift
        ceilings.append(jnp.broadcast_to(lowest, (SUBS, LANES)))
    pairs = []
    for region in range(3):
        left, middle, right = ceilings[3 * region : 3 * region + 3]
        seam = jnp.where(
            lane < LANES // 2,
            jnp.where(sub == SUBS - 1, right, middle),
            jnp.where(sub == 0, left, middle),
        )
        pairs.append((middle, seam))
    low, high = PASSES - FINAL, PASSES + height
    far_pair = [jnp.where(top, above, below) for above, below in zip(pairs[0], pairs[2])]
    near_pair = [jnp.where(top, below, above) for above, below in zip(pairs[0], pairs[2])]
    spans = (
        (far_ref, 0, jnp.where(top, low, high), FINAL, far_pair),
        (near_ref, 0, jnp.where(top, high, low), FINAL, near_pair),
        (surface_ref, PASSES, PASSES, height, pairs[1]),
    )
    for source, source_first, first, rows, (middle, seam) in spans:

        def body(row, carry):
            for slot in range(ring):
                value = source[register(source_first + row, slot, size), :]
                value = jnp.minimum(value, seam if slot == tiles else middle)
                where = register(first + row, slot, size)
                one_ref[where, :] = jnp.maximum(ground_ref[where, :], value)
            return carry

        lax.fori_loop(0, rows, body, 0, unroll=4)
    buffers = (one_ref, two_ref)
    for step in range(1, FINAL):
        first = PASSES - FINAL + step
        relax_rows(
            buffers[(step + 1) % 2], buffers[step % 2], ground_ref, first, 2 * PASSES + height - 2 * first, ring
        )
    source, target = buffers[(FINAL + 1) % 2], buffers[FINAL % 2]
    copies = []
    for group in range(height // SUBS):
        first = PASSES + group * SUBS
        relax_rows(source, target, ground_ref, first, SUBS, ring)
        for tile in range(tiles * SUBS):
            chunk, slot = tile // tiles, tile % tiles
            out_ref[pl.ds(group * SUBS, SUBS), pl.ds(tile * LANES, LANES)] = target[
                pl.ds(first * size + slot * SUBS + chunk, SUBS, stride=size), :
            ]
        where = (pl.ds(group * SUBS, SUBS), slice(None))
        copies += start_all([pltpu.make_async_copy(out_ref.at[where], out_hbm.at[where], sems.at[group])])
    wait_all(copies)


def in_vmem(count):
    return [pl.BlockSpec(memory_space=pltpu.VMEM)] * count


def in_hbm(count):
    return [pl.BlockSpec(memory_space=pltpu.HBM)] * count


def exchange_stages(rows, cols, subs):
    bits = []
    for axis, count in enumerate((rows, cols, subs)):
        bit = 1
        while bit < count:
            bits.append((axis, bit))
            bit *= 2
    bits.reverse()
    stages = []
    for first in range(0, len(bits), 2):
        group = bits[first : first + 2]
        shifts = []
        for chosen in range(1, 2 ** len(group)):
            shift = [0, 0, 0]
            for number, (axis, bit) in enumerate(group):
                if chosen >> number & 1:
                    shift[axis] ^= bit
            shifts.append(shift)
        stages.append(shifts)
    return stages


def share_levels(level):
    rows, cols, subs = [lax.axis_size(axis) for axis in ("rows", "cols", "sub")]
    if any(count & (count - 1) for count in (rows, cols, subs)):
        return lax.pmin(level, ("rows", "cols", "sub"))
    for shifts in exchange_stages(rows, cols, subs):
        arrived = [level]
        for down, across, core in shifts:
            pairs = [
                (
                    (row * cols + col) * subs + sub,
                    ((row ^ down) * cols + (col ^ across)) * subs + (sub ^ core),
                )
                for row in range(rows)
                for col in range(cols)
                for sub in range(subs)
            ]
            arrived.append(lax.ppermute(level, ("rows", "cols", "sub"), pairs))
        level = least(arrived)
    return level


def per_device(elevation, fill_depth, edge_rows, edge_sides, adjacency):
    height, width = elevation.shape
    tiles = width // (SUBS * LANES)
    groups = height // SUBS
    f32 = jnp.float32
    packed = tiles * SUBS
    size = packed + SUBS
    tile_count = adjacency.shape[0]
    places = lax.axis_size(("rows", "sub"))
    cols, subs = lax.axis_size("cols"), lax.axis_size("sub")
    short = pl.CostEstimate(flops=1024, bytes_accessed=1024, transcendentals=0)
    limit = pltpu.CompilerParams(vmem_limit_bytes=24 << 20)
    arguments = [
        pltpu.with_memory_space_constraint(value, pltpu.HBM)
        for value in (elevation, fill_depth, edge_rows, edge_sides, adjacency)
    ]
    sent = pltpu.VMEM(((2 * PASSES - 1) * packed, LANES), f32)
    strip = pltpu.VMEM((2 * height, LANES), f32)
    far_strip = pltpu.VMEM((2 * SUBS, LANES), f32)
    far, far_even, far_odd, even, odd = pl.pallas_call(
        far_kernel,
        out_shape=[sent, far_strip, far_strip, strip, strip],
        in_specs=in_hbm(4),
        out_specs=in_vmem(5),
        scratch_shapes=[
            pltpu.VMEM((SUBS, width), f32),
            pltpu.VMEM((SUBS, width), f32),
            pltpu.VMEM((2, 2, height, LANES), f32),
            pltpu.VMEM((2, 2, LANES), jnp.int32),
            pltpu.VMEM(edge_sides.shape, jnp.int32),
            pltpu.SemaphoreType.DMA((2, 4)),
            pltpu.SemaphoreType.DMA((7,)),
        ],
        compiler_params=limit,
        cost_estimate=short,
        name="far_rows",
    )(*arguments[:4])

    near_pairs, far_pairs = matching(places, 0), matching(places, 1)
    stay = [(place, place) for place in range(places)]
    device_axes = ("rows", "cols", "sub")

    def swap_strips(pieces, row_pairs):
        arrived = []
        for first, piece in enumerate(pieces):
            pairs = cross(row_pairs, matching(cols, first), cols, subs)
            arrived.append(lax.ppermute(piece, device_axes, pairs) if pairs else piece)
        return arrived

    far_strips = swap_strips((far_even, far_odd), far_pairs)
    far_rows = lax.ppermute(far, ("rows", "sub"), far_pairs)

    work = pltpu.VMEM(((height + 2 * PASSES) * size, LANES), f32)
    ground, surface, near, hops = pl.pallas_call(
        own_kernel,
        out_shape=[work, work, sent, pltpu.VMEM((9 * tile_count, LANES), f32)],
        in_specs=in_hbm(5) + in_vmem(1),
        out_specs=in_vmem(4),
        scratch_shapes=[
            pltpu.VMEM((height, width), f32),
            pltpu.VMEM((height, width), f32),
            pltpu.VMEM(edge_rows.shape, jnp.int32),
            pltpu.VMEM(edge_sides.shape, jnp.int32),
            pltpu.VMEM(adjacency.shape, jnp.int32),
            pltpu.SemaphoreType.DMA((2, 4 * groups)),
            pltpu.SemaphoreType.DMA((3,)),
        ],
        compiler_params=limit,
        cost_estimate=short,
        name="own_rows",
    )(*arguments, far_even)

    near_rows = lax.ppermute(near, ("rows", "sub"), near_pairs)
    strips = swap_strips((even, odd), stay) + swap_strips((even, odd), near_pairs)

    def inner(near_ref, *refs):
        inner_kernel(height, tiles, near_ref, *refs)

    ground, surface, other = pl.pallas_call(
        inner,
        out_shape=[work, work, work],
        in_specs=in_vmem(7),
        out_specs=in_vmem(3),
        input_output_aliases={5: 0, 6: 1},
        compiler_params=limit,
        cost_estimate=short,
        name="inner_passes",
    )(near_rows, *strips, ground, surface)

    def outer(far_ref, *refs):
        outer_kernel(height, tiles, far_ref, *refs)

    again = pltpu.VMEM((FINAL * size, LANES), f32)
    ground, surface, other, level, far, near = pl.pallas_call(
        outer,
        out_shape=[work, work, work, pltpu.VMEM((tile_count, LANES), f32), again, again],
        in_specs=in_vmem(6),
        out_specs=in_vmem(6),
        input_output_aliases={3: 0, 4: 1, 5: 2},
        compiler_params=limit,
        cost_estimate=short,
        name="outer_passes",
    )(far_rows, *far_strips, ground, surface, other)

    far_rows = lax.ppermute(far, ("rows", "sub"), far_pairs)
    near_rows = lax.ppermute(near, ("rows", "sub"), near_pairs)
    level = share_levels(level)

    def late(*refs):
        late_kernel(height, tiles, *refs)

    return pl.pallas_call(
        late,
        out_shape=jax.ShapeDtypeStruct((height, width), f32),
        in_specs=in_vmem(6),
        out_specs=pl.BlockSpec(memory_space=pltpu.HBM),
        scratch_shapes=[
            pltpu.VMEM(((height + 2 * PASSES) * size, LANES), f32),
            pltpu.VMEM(((height + 2 * PASSES) * size, LANES), f32),
            pltpu.VMEM((height, width), f32),
            pltpu.SemaphoreType.DMA((groups,)),
        ],
        compiler_params=limit,
        cost_estimate=short,
        name="final_passes",
    )(ground, surface, far_rows, near_rows, level, hops)


def solution(mesh):
    placed = (
        P(("groups", "rows", "sub"), "cols"),
        P(("groups", "rows", "sub"), "cols"),
        P("groups", "cols"),
        P("groups", ("rows", "sub")),
        P("groups", None),
    )
    return jax.shard_map(
        per_device,
        mesh=mesh,
        in_specs=placed,
        out_specs=P(("groups", "rows", "sub"), "cols"),
        check_vma=False,
    )
```

```python
import jax
import jax.numpy as jnp
from jax import lax
from jax.experimental import pallas as pl
from jax.experimental.pallas import tpu as pltpu
from jax.sharding import PartitionSpec as P

PASSES = 8
FINAL = 4
ROUNDS = 4
SUBS = 8
LANES = 128
AHEAD = 5

unreached = 1000000000.0
rise_step = 0.01
hop_rise = 0.05
spill_lift = 3.0


def matching(count, first):
    pairs = []
    for low in range(first, count - 1, 2):
        pairs += [(low, low + 1), (low + 1, low)]
    return pairs


def cross(row_pairs, col_pairs, cols, subs):
    def device(place, col):
        return (place // subs * cols + col) * subs + place % subs

    return [
        (device(row, col), device(row_to, col_to))
        for row, row_to in row_pairs
        for col, col_to in col_pairs
    ]


def chain_place():
    subs = lax.axis_size("sub")
    return lax.axis_index("rows") * subs + lax.axis_index("sub"), lax.axis_size("rows") * subs


def position():
    sub = lax.broadcasted_iota(jnp.int32, (SUBS, LANES), 0)
    lane = lax.broadcasted_iota(jnp.int32, (SUBS, LANES), 1)
    return sub, lane


def aligned(start):
    return start if isinstance(start, int) else pl.multiple_of(start, SUBS)


def rows_at(first, count, size):
    return pl.ds(aligned(first * size), count * size)


def register(row, slot, size):
    return pl.ds(aligned(row * size + slot * SUBS), SUBS)


def side_marks(sides_ref):
    height = sides_ref.shape[1]
    square = (height, height)
    diagonal = lax.broadcasted_iota(jnp.int32, square, 0) == lax.broadcasted_iota(jnp.int32, square, 1)
    marks = sides_ref[...].astype(jnp.float32)
    return [
        jnp.sum(jnp.where(diagonal, marks[side : side + 1, :], 0.0), axis=1, keepdims=True)
        for side in range(2)
    ]


def start_all(copies):
    for copy in copies:
        copy.start()
    return copies


def wait_all(copies):
    for copy in copies:
        copy.wait()


def edge_kernel(
    ground_hbm, depth_hbm, rows_hbm, sides_hbm,
    far_ref, near_ref, far_even_ref, far_odd_ref, even_ref, odd_ref,
    ground_ref, depth_ref, edge_ref, marks_ref, sides_ref, sems, small_sems,
):
    height, width = ground_hbm.shape
    groups = height // SUBS
    tiles = width // (SUBS * LANES)
    last_tile = width // LANES - 1
    pieces = sems.shape[2]
    part = width // pieces
    place, places = chain_place()
    col, cols = lax.axis_index("cols"), lax.axis_size("cols")
    top = place % 2 == 0
    firsts = [aligned(jnp.where(is_top, 0, height - SUBS)) for is_top in (top, jnp.logical_not(top))]
    small = [pltpu.make_async_copy(sides_hbm, sides_ref, small_sems.at[0])]
    for side, tile in enumerate((0, last_tile)):
        columns = pl.ds(tile * LANES, LANES)
        for number, (source, target) in enumerate(
            (
                (ground_hbm.at[:, columns], edge_ref.at[side, 0]),
                (depth_hbm.at[:, columns], edge_ref.at[side, 1]),
                (rows_hbm.at[:, columns], marks_ref.at[side]),
            )
        ):
            small.append(pltpu.make_async_copy(source, target, small_sems.at[1 + side * 3 + number]))
    copies = [
        [
            [
                pltpu.make_async_copy(
                    source.at[pl.ds(first, SUBS), pl.ds(piece * part, part)],
                    target.at[where, :, pl.ds(piece * part, part)],
                    sems.at[where, kind, piece],
                )
                for kind, (source, target) in enumerate(((ground_hbm, ground_ref), (depth_hbm, depth_ref)))
            ]
            for piece in range(pieces)
        ]
        for where, first in enumerate(firsts)
    ]
    start_all(copies[0][0])
    start_all(small)
    for pair in copies[0][1:] + copies[1]:
        start_all(pair)
    sub, lane = position()
    size = tiles * SUBS
    wait_all(small)
    marks = side_marks(sides_ref)
    at_edges = [(lane == 0) & (col == 0), (lane == LANES - 1) & (col == cols - 1)]
    for where, (out_ref, is_top) in enumerate(((far_ref, top), (near_ref, jnp.logical_not(top)))):
        ground_base = jnp.where(is_top, 0, (SUBS - 1) * size)
        surface_base = jnp.where(is_top, (SUBS - 1) * size, 0)
        for tile in range(last_tile + 1):
            if tile * LANES % part == 0:
                wait_all(copies[where][tile * LANES // part])
            columns = pl.ds(tile * LANES, LANES)
            ground = ground_ref[where, :, columns]
            surface = ground + depth_ref[where, :, columns]
            if tile in (0, last_tile):
                side = 0 if tile == 0 else 1
                chosen = jnp.where(is_top, marks[side][:SUBS], marks[side][height - SUBS :])
                surface = jnp.where((chosen > 0.5) & at_edges[side], ground, surface)
            chunk, slot = tile // tiles, tile % tiles
            start = slot * SUBS + chunk
            out_ref[pl.ds(ground_base + start, SUBS, stride=size), :] = ground
            out_ref[pl.ds(surface_base + start, SUBS, stride=size), :] = surface
    rightward = col % 2 == 0
    strips = []
    for group in range(groups):
        rows = pl.ds(group * SUBS, SUBS)
        values = []
        for side in range(2):
            ground = edge_ref[side, 0, rows, :]
            surface = ground + edge_ref[side, 1, rows, :]
            outlet = (marks[side][group * SUBS : (group + 1) * SUBS] > 0.5) & at_edges[side]
            if group == 0:
                outlet = outlet | (marks_ref[side, 0:1] == 1) & (sub == 0) & (place == 0)
            if group == groups - 1:
                outlet = outlet | (marks_ref[side, 1:2] == 1) & (sub == SUBS - 1) & (place == places - 1)
            values.append((ground, jnp.where(outlet, ground, surface)))
        strips.append(values)
        for kind in range(2):
            rows = pl.ds(kind * height + group * SUBS, SUBS)
            even_ref[rows, :] = jnp.where(rightward, values[1][kind], values[0][kind])
            odd_ref[rows, :] = jnp.where(rightward, values[0][kind], values[1][kind])
    for kind in range(2):
        rows = pl.ds(kind * SUBS, SUBS)
        first, last = [jnp.where(top, strips[0][side][kind], strips[-1][side][kind]) for side in range(2)]
        far_even_ref[rows, :] = jnp.where(rightward, last, first)
        far_odd_ref[rows, :] = jnp.where(rightward, first, last)


def start_own(ground_hbm, depth_hbm, ground_ref, depth_ref, sems):
    height, width = ground_hbm.shape
    groups = height // SUBS
    pieces = sems.shape[1] // groups
    part = width // pieces
    copies = []
    for group in range(groups):
        for piece in range(pieces):
            where = (pl.ds(group * SUBS, SUBS), pl.ds(piece * part, part))
            number = group * pieces + piece
            copies.append(
                start_all(
                    [
                        pltpu.make_async_copy(ground_hbm.at[where], ground_ref.at[where], sems.at[0, number]),
                        pltpu.make_async_copy(depth_hbm.at[where], depth_ref.at[where], sems.at[1, number]),
                    ]
                )
            )
    return copies


def fold_own(copies, ground_ref, depth_ref, rows_ref, sides_ref, ground_out, surface_out):
    height, width = ground_ref.shape
    groups = height // SUBS
    tiles = width // (SUBS * LANES)
    last_tile = width // LANES - 1
    pieces = len(copies) // groups
    part = width // pieces
    size = (tiles + 1) * SUBS
    place, places = chain_place()
    col, cols = lax.axis_index("cols"), lax.axis_size("cols")
    sub, lane = position()
    marks = side_marks(sides_ref)
    for group in range(groups):
        rows = pl.ds(group * SUBS, SUBS)
        for tile in range(last_tile + 1):
            if tile * LANES % part == 0:
                wait_all(copies[group * pieces + tile * LANES // part])
            columns = pl.ds(tile * LANES, LANES)
            ground = ground_ref[rows, columns]
            surface = ground + depth_ref[rows, columns]
            outlets = []
            if group == 0:
                outlets.append((rows_ref[0:1, columns] == 1) & (sub == 0) & (place == 0))
            if group == groups - 1:
                outlets.append(
                    (rows_ref[1:2, columns] == 1) & (sub == SUBS - 1) & (place == places - 1)
                )
            if tile == 0:
                outlets.append(
                    (marks[0][group * SUBS : (group + 1) * SUBS] > 0.5) & (lane == 0) & (col == 0)
                )
            if tile == last_tile:
                outlets.append(
                    (marks[1][group * SUBS : (group + 1) * SUBS] > 0.5)
                    & (lane == LANES - 1)
                    & (col == cols - 1)
                )
            for outlet in outlets:
                surface = jnp.where(outlet, ground, surface)
            chunk, slot = tile // tiles, tile % tiles
            start = (PASSES + group * SUBS) * size + slot * SUBS + chunk
            ground_out[pl.ds(start, SUBS, stride=size), :] = ground
            surface_out[pl.ds(start, SUBS, stride=size), :] = surface


def unpack_rows(rows_ref, first, is_top, present, strip_refs, strip_rows, ground_ref, surface_ref, tiles):
    packed = tiles * SUBS
    size = packed + SUBS
    bases = (jnp.where(is_top, SUBS - 1, 0), jnp.where(is_top, 0, SUBS - 1))
    for base, out_ref, strip_row in zip(bases, (ground_ref, surface_ref), strip_rows):

        def body(row, carry):
            values = [
                jnp.where(present, rows_ref[register(base + row, slot, packed), :], unreached)
                for slot in range(tiles)
            ]
            for slot in range(tiles):
                out_ref[register(first + row, slot, size), :] = values[slot]
            fill_seam(out_ref, first + row, values[0], values[-1], strip_refs, strip_row + row, present, tiles)
            return carry

        lax.fori_loop(0, PASSES, body, 0, unroll=4)


def fill_seam(out_ref, row, first_tile, last_tile, strip_refs, strip_row, present, tiles):
    col, cols = lax.axis_index("cols"), lax.axis_size("cols")
    sub, lane = position()
    rightward = col % 2 == 0
    even, odd = [ref[pl.ds(strip_row, 1), :] for ref in strip_refs]
    after = jnp.where(present & (col < cols - 1), jnp.where(rightward, even, odd), unreached)
    before = jnp.where(present & (col > 0), jnp.where(rightward, odd, even), unreached)
    after = jnp.where(sub == SUBS - 1, after, pltpu.roll(first_tile, SUBS - 1, 0))
    before = jnp.where(sub == 0, before, pltpu.roll(last_tile, 1, 0))
    out_ref[register(row, tiles, (tiles + 1) * SUBS), :] = jnp.where(lane < LANES // 2, after, before)


def relax_rows(source, target, ground, first, count, ring):
    size = ring * SUBS
    _, lane = position()
    at_first = lane == 0
    at_last = lane == LANES - 1
    order = [ring - 1] + list(range(ring - 1))
    made = {}

    def make(pair, slot):
        row = first + 2 * pair
        values = [source[register(row + step, slot, size), :] for step in range(-1, 3)]
        both = jnp.minimum(values[1], values[2])
        for one, column in enumerate((jnp.minimum(values[0], both), jnp.minimum(both, values[3]))):
            made[pair, one, slot] = (column, pltpu.roll(column, 1, 1), pltpu.roll(column, LANES - 1, 1))

    def finish(pair, slot):
        for one in range(2):
            row = first + 2 * pair + one
            before, here, after = [made[pair, one, (slot + step) % ring] for step in (-1, 0, 1)]
            from_left = jnp.where(at_first, before[1], here[1])
            from_right = jnp.where(at_last, after[2], here[2])
            lowest = jnp.minimum(jnp.minimum(from_left, from_right), here[0])
            where = register(row, slot, size)
            raised = jnp.minimum(source[where, :], lowest + rise_step)
            target[where, :] = jnp.maximum(ground[where, :], raised)

    makes = [(pair, slot) for pair in range(count // 2) for slot in order]
    finishes = [(pair, slot) for pair in range(count // 2) for slot in range(ring)]
    done = 0
    for number, item in enumerate(makes):
        make(*item)
        if number >= AHEAD:
            finish(*finishes[done])
            done += 1
    for item in finishes[done:]:
        finish(*item)


def hop_counts(links_ref, hops_ref, needed):
    tiles, degree = links_ref.shape
    links = links_ref[...]
    number = lax.broadcasted_iota(jnp.int32, (tiles, tiles), 1)
    linked = links[:, 0:1] == number
    for edge in range(1, degree):
        linked = linked | (links[:, edge : edge + 1] == number)
    linked = linked.astype(jnp.float32)
    tile = lax.broadcasted_iota(jnp.int32, (tiles, LANES), 0)
    lane = lax.broadcasted_iota(jnp.int32, (tiles, LANES), 1)
    reached = jnp.zeros((tiles, LANES), jnp.float32)
    for index, wanted in enumerate(needed):
        reached = jnp.where((lane == index) & (tile == wanted), 1.0, reached)
    hops = jnp.where(reached > 0.5, 0.0, float(ROUNDS + 1))
    for hop in range(1, ROUNDS + 1):
        reached = lax.dot_general(
            linked, reached, (((0,), (0,)), ((), ())), preferred_element_type=jnp.float32
        )
        reached = jnp.where(reached > 0.5, 1.0, 0.0)
        hops = jnp.minimum(hops, jnp.where(reached > 0.5, float(hop), float(ROUNDS + 1)))
    for index in range(len(needed)):
        hops_ref[pl.ds(index * tiles, tiles), :] = jnp.broadcast_to(
            hops[:, index : index + 1], (tiles, LANES)
        )


def needed_tiles():
    row, rows = lax.axis_index("rows"), lax.axis_size("rows")
    col, cols = lax.axis_index("cols"), lax.axis_size("cols")
    sub, subs = lax.axis_index("sub"), lax.axis_size("sub")
    above = jnp.maximum(jnp.where(sub == 0, row - 1, row), 0)
    below = jnp.minimum(jnp.where(sub == subs - 1, row + 1, row), rows - 1)
    left = jnp.maximum(col - 1, 0)
    right = jnp.minimum(col + 1, cols - 1)
    return [r * cols + c for r in (above, row, below) for c in (left, col, right)]


def inner_kernel(
    ground_hbm, depth_hbm, rows_hbm, sides_hbm, links_hbm,
    near_ref, own_even_ref, own_odd_ref, near_even_ref, near_odd_ref,
    ground_ref, surface_ref, other_ref, hops_ref,
    raw_ground_ref, raw_depth_ref, rows_ref, sides_ref, links_ref, sems, small_sems,
):
    height, width = ground_hbm.shape
    tiles = width // (SUBS * LANES)
    small = start_all(
        [
            pltpu.make_async_copy(source, target, small_sems.at[number])
            for number, (source, target) in enumerate(
                ((rows_hbm, rows_ref), (sides_hbm, sides_ref), (links_hbm, links_ref))
            )
        ]
    )
    copies = start_own(ground_hbm, depth_hbm, raw_ground_ref, raw_depth_ref, sems)
    own_strips, near_strips = (own_even_ref, own_odd_ref), (near_even_ref, near_odd_ref)
    ring = tiles + 1
    size = ring * SUBS
    place, places = chain_place()
    top = place % 2 == 0
    has_near = jnp.where(top, place < places - 1, place > 0)
    unpack_rows(
        near_ref,
        jnp.where(top, PASSES + height, 0),
        jnp.logical_not(top),
        has_near,
        near_strips,
        [kind * height + jnp.where(top, 0, height - SUBS) for kind in range(2)],
        ground_ref,
        surface_ref,
        tiles,
    )
    wait_all(small)
    hop_counts(links_ref, hops_ref, needed_tiles())
    fold_own(copies, raw_ground_ref, raw_depth_ref, rows_ref, sides_ref, ground_ref, surface_ref)
    for kind, out_ref in enumerate((ground_ref, surface_ref)):

        def body(row, carry):
            first_tile = out_ref[register(PASSES + row, 0, size), :]
            last_tile = out_ref[register(PASSES + row, tiles - 1, size), :]
            fill_seam(
                out_ref, PASSES + row, first_tile, last_tile, own_strips, kind * height + row, place >= 0, tiles
            )
            return carry

        lax.fori_loop(0, height, body, 0, unroll=4)
    buffers = (surface_ref, other_ref)
    for step in range(1, PASSES + 1):
        first = step + jnp.where(top, PASSES, 0)
        count = height + PASSES - 2 * step
        relax_rows(buffers[(step + 1) % 2], buffers[step % 2], ground_ref, first, count, ring)


def outer_kernel(height, tiles, far_ref, even_ref, odd_ref, *refs):
    ground_ref, surface_ref, other_ref, level_ref, far_out, near_out = refs[3:9]
    ring = tiles + 1
    size = ring * SUBS
    place, places = chain_place()
    top = place % 2 == 0
    has_far = jnp.where(top, place > 0, place < places - 1)
    unpack_rows(
        far_ref,
        jnp.where(top, 0, PASSES + height),
        top,
        has_far,
        (even_ref, odd_ref),
        [0, SUBS],
        ground_ref,
        surface_ref,
        tiles,
    )
    buffers = (surface_ref, other_ref)
    for step in range(1, PASSES + 1):
        first = jnp.where(top, step, PASSES + height - step)
        relax_rows(buffers[(step + 1) % 2], buffers[step % 2], ground_ref, first, PASSES, ring)
    low, high = PASSES, PASSES + height - FINAL
    far_out[...] = surface_ref[rows_at(jnp.where(top, low, high), FINAL, size), :]
    near_out[...] = surface_ref[rows_at(jnp.where(top, high, low), FINAL, size), :]
    band, bands = lax.axis_index("sub"), lax.axis_size("sub")
    sub, lane = position()

    def at(row, slot):
        return surface_ref[register(PASSES + row, slot, size), :]

    first_cell = (sub == 0) & (lane == 0)
    last_cell = (sub == SUBS - 1) & (lane == LANES - 1)
    first_lows, last_lows, row_lows = [], [], []
    for row in range(height):
        first_lows.append(at(row, 0))
        last_lows.append(at(row, tiles - 1))
    for slot in range(tiles):
        row_lows.append(jnp.where(band == 0, at(0, slot), unreached))
        row_lows.append(jnp.where(band == bands - 1, at(height - 1, slot), unreached))
    lowest = jnp.minimum(
        least(row_lows),
        jnp.minimum(
            jnp.where(first_cell, least(first_lows), unreached),
            jnp.where(last_cell, least(last_lows), unreached),
        ),
    )
    lowest = jnp.min(jnp.min(lowest, axis=0, keepdims=True), axis=1, keepdims=True)
    level_ref[...] = jnp.broadcast_to(lowest, level_ref.shape)


def least(values):
    values = list(values)
    while len(values) > 1:
        values = [
            jnp.minimum(*values[number : number + 2]) if number + 1 < len(values) else values[number]
            for number in range(0, len(values), 2)
        ]
    return values[0]


def late_kernel(
    height, tiles, ground_ref, surface_ref, far_ref, near_ref, floors_ref, hops_ref, out_hbm,
    one_ref, two_ref, out_ref, sems,
):
    ring = tiles + 1
    size = ring * SUBS
    sub, lane = position()
    place, _ = chain_place()
    top = place % 2 == 0
    bands = lax.axis_size("sub")
    count = floors_ref.shape[0] // (bands * SUBS)
    level = least(floors_ref[pl.ds(band * SUBS, count, stride=bands * SUBS), :] for band in range(bands))
    raised = [level]
    for hop in range(ROUNDS):
        raised.append(raised[-1] + hop_rise)
    ceilings = []
    for index in range(9):
        hops = hops_ref[pl.ds(index * count, count), :]
        lowest = jnp.full((count, LANES), unreached, jnp.float32)
        for hop in range(ROUNDS + 1):
            lowest = jnp.where(hops == float(hop), raised[hop], lowest)
        lowest = jnp.min(lowest, axis=0, keepdims=True) + spill_lift
        ceilings.append(jnp.broadcast_to(lowest, (SUBS, LANES)))
    pairs = []
    for region in range(3):
        left, middle, right = ceilings[3 * region : 3 * region + 3]
        seam = jnp.where(
            lane < LANES // 2,
            jnp.where(sub == SUBS - 1, right, middle),
            jnp.where(sub == 0, left, middle),
        )
        pairs.append((middle, seam))
    low, high = PASSES - FINAL, PASSES + height
    far_pair = [jnp.where(top, above, below) for above, below in zip(pairs[0], pairs[2])]
    near_pair = [jnp.where(top, below, above) for above, below in zip(pairs[0], pairs[2])]
    spans = (
        (far_ref, 0, jnp.where(top, low, high), FINAL, far_pair),
        (near_ref, 0, jnp.where(top, high, low), FINAL, near_pair),
        (surface_ref, PASSES, PASSES, height, pairs[1]),
    )
    for source, source_first, first, rows, (middle, seam) in spans:

        def body(row, carry):
            for slot in range(ring):
                value = source[register(source_first + row, slot, size), :]
                value = jnp.minimum(value, seam if slot == tiles else middle)
                where = register(first + row, slot, size)
                one_ref[where, :] = jnp.maximum(ground_ref[where, :], value)
            return carry

        lax.fori_loop(0, rows, body, 0, unroll=4)
    buffers = (one_ref, two_ref)
    for step in range(1, FINAL):
        first = PASSES - FINAL + step
        relax_rows(
            buffers[(step + 1) % 2], buffers[step % 2], ground_ref, first, 2 * PASSES + height - 2 * first, ring
        )
    source, target = buffers[(FINAL + 1) % 2], buffers[FINAL % 2]
    copies = []
    for group in range(height // SUBS):
        first = PASSES + group * SUBS
        relax_rows(source, target, ground_ref, first, SUBS, ring)
        for tile in range(tiles * SUBS):
            chunk, slot = tile // tiles, tile % tiles
            out_ref[pl.ds(group * SUBS, SUBS), pl.ds(tile * LANES, LANES)] = target[
                pl.ds(first * size + slot * SUBS + chunk, SUBS, stride=size), :
            ]
        where = (pl.ds(group * SUBS, SUBS), slice(None))
        copies += start_all([pltpu.make_async_copy(out_ref.at[where], out_hbm.at[where], sems.at[group])])
    wait_all(copies)


def in_vmem(count):
    return [pl.BlockSpec(memory_space=pltpu.VMEM)] * count


def in_hbm(count):
    return [pl.BlockSpec(memory_space=pltpu.HBM)] * count


def per_device(elevation, fill_depth, edge_rows, edge_sides, adjacency):
    height, width = elevation.shape
    tiles = width // (SUBS * LANES)
    groups = height // SUBS
    f32 = jnp.float32
    packed = tiles * SUBS
    size = packed + SUBS
    tile_count = adjacency.shape[0]
    places = lax.axis_size(("rows", "sub"))
    cols, subs = lax.axis_size("cols"), lax.axis_size("sub")
    short = pl.CostEstimate(flops=1024, bytes_accessed=1024, transcendentals=0)
    limit = pltpu.CompilerParams(vmem_limit_bytes=24 << 20)
    arguments = [
        pltpu.with_memory_space_constraint(value, pltpu.HBM)
        for value in (elevation, fill_depth, edge_rows, edge_sides, adjacency)
    ]
    sent = pltpu.VMEM(((2 * PASSES - 1) * packed, LANES), f32)
    strip = pltpu.VMEM((2 * height, LANES), f32)
    far_strip = pltpu.VMEM((2 * SUBS, LANES), f32)
    far, near, far_even, far_odd, even, odd = pl.pallas_call(
        edge_kernel,
        out_shape=[sent, sent, far_strip, far_strip, strip, strip],
        in_specs=in_hbm(4),
        out_specs=in_vmem(6),
        scratch_shapes=[
            pltpu.VMEM((2, SUBS, width), f32),
            pltpu.VMEM((2, SUBS, width), f32),
            pltpu.VMEM((2, 2, height, LANES), f32),
            pltpu.VMEM((2, 2, LANES), jnp.int32),
            pltpu.VMEM(edge_sides.shape, jnp.int32),
            pltpu.SemaphoreType.DMA((2, 2, 4)),
            pltpu.SemaphoreType.DMA((7,)),
        ],
        compiler_params=limit,
        cost_estimate=short,
        name="edge_rows",
    )(*arguments[:4])

    near_pairs, far_pairs = matching(places, 0), matching(places, 1)
    stay = [(place, place) for place in range(places)]
    device_axes = ("rows", "cols", "sub")

    def swap_strips(pieces, row_pairs):
        arrived = []
        for first, piece in enumerate(pieces):
            pairs = cross(row_pairs, matching(cols, first), cols, subs)
            arrived.append(lax.ppermute(piece, device_axes, pairs) if pairs else piece)
        return arrived

    far_strips = swap_strips((far_even, far_odd), far_pairs)
    far_rows = lax.ppermute(far, ("rows", "sub"), far_pairs)
    near_rows = lax.ppermute(near, ("rows", "sub"), near_pairs)
    strips = swap_strips((even, odd), stay) + swap_strips((even, odd), near_pairs)

    work = pltpu.VMEM(((height + 2 * PASSES) * size, LANES), f32)
    ground, surface, other, hops = pl.pallas_call(
        inner_kernel,
        out_shape=[work, work, work, pltpu.VMEM((9 * tile_count, LANES), f32)],
        in_specs=in_hbm(5) + in_vmem(5),
        out_specs=in_vmem(4),
        scratch_shapes=[
            pltpu.VMEM((height, width), f32),
            pltpu.VMEM((height, width), f32),
            pltpu.VMEM(edge_rows.shape, jnp.int32),
            pltpu.VMEM(edge_sides.shape, jnp.int32),
            pltpu.VMEM(adjacency.shape, jnp.int32),
            pltpu.SemaphoreType.DMA((2, 4 * groups)),
            pltpu.SemaphoreType.DMA((3,)),
        ],
        compiler_params=limit,
        cost_estimate=short,
        name="inner_passes",
    )(*arguments, near_rows, *strips)

    def outer(far_ref, *refs):
        outer_kernel(height, tiles, far_ref, *refs)

    again = pltpu.VMEM((FINAL * size, LANES), f32)
    ground, surface, other, level, far, near = pl.pallas_call(
        outer,
        out_shape=[work, work, work, pltpu.VMEM((SUBS, LANES), f32), again, again],
        in_specs=in_vmem(6),
        out_specs=in_vmem(6),
        input_output_aliases={3: 0, 4: 1, 5: 2},
        compiler_params=limit,
        cost_estimate=short,
        name="outer_passes",
    )(far_rows, *far_strips, ground, surface, other)

    floors = lax.all_gather(level, device_axes, axis=0, tiled=True)
    far_rows = lax.ppermute(far, ("rows", "sub"), far_pairs)
    near_rows = lax.ppermute(near, ("rows", "sub"), near_pairs)

    def late(*refs):
        late_kernel(height, tiles, *refs)

    return pl.pallas_call(
        late,
        out_shape=jax.ShapeDtypeStruct((height, width), f32),
        in_specs=in_vmem(6),
        out_specs=pl.BlockSpec(memory_space=pltpu.HBM),
        scratch_shapes=[
            pltpu.VMEM(((height + 2 * PASSES) * size, LANES), f32),
            pltpu.VMEM(((height + 2 * PASSES) * size, LANES), f32),
            pltpu.VMEM((height, width), f32),
            pltpu.SemaphoreType.DMA((groups,)),
        ],
        compiler_params=limit,
        cost_estimate=short,
        name="final_passes",
    )(ground, surface, far_rows, near_rows, floors, hops)


def solution(mesh):
    placed = (
        P(("groups", "rows", "sub"), "cols"),
        P(("groups", "rows", "sub"), "cols"),
        P("groups", "cols"),
        P("groups", ("rows", "sub")),
        P("groups", None),
    )
    return jax.shard_map(
        per_device,
        mesh=mesh,
        in_specs=placed,
        out_specs=P(("groups", "rows", "sub"), "cols"),
        check_vma=False,
    )
```

```python
import jax
import jax.numpy as jnp
from jax import lax
from jax.experimental import pallas as pl
from jax.experimental.pallas import tpu as pltpu
from jax.sharding import PartitionSpec as P

PASSES = 8
FINAL = 4
ROUNDS = 4
SUBS = 8
LANES = 128
AHEAD = 5

unreached = 1000000000.0
rise_step = 0.01
hop_rise = 0.05
spill_lift = 3.0


def matching(count, first):
    pairs = []
    for low in range(first, count - 1, 2):
        pairs += [(low, low + 1), (low + 1, low)]
    return pairs


def closed(pairs, count):
    used = {source for source, _ in pairs}
    return pairs + [(place, place) for place in range(count) if place not in used]


def cross(row_pairs, col_pairs, cols, subs):
    def device(place, col):
        return (place // subs * cols + col) * subs + place % subs

    return [
        (device(row, col), device(row_to, col_to))
        for row, row_to in row_pairs
        for col, col_to in col_pairs
    ]


def chain_place():
    subs = lax.axis_size("sub")
    return lax.axis_index("rows") * subs + lax.axis_index("sub"), lax.axis_size("rows") * subs


def position():
    sub = lax.broadcasted_iota(jnp.int32, (SUBS, LANES), 0)
    lane = lax.broadcasted_iota(jnp.int32, (SUBS, LANES), 1)
    return sub, lane


def aligned(start):
    return start if isinstance(start, int) else pl.multiple_of(start, SUBS)


def rows_at(first, count, size):
    return pl.ds(aligned(first * size), count * size)


def register(row, slot, size):
    return pl.ds(aligned(row * size + slot * SUBS), SUBS)


def side_marks(sides_ref):
    height = sides_ref.shape[1]
    square = (height, height)
    diagonal = lax.broadcasted_iota(jnp.int32, square, 0) == lax.broadcasted_iota(jnp.int32, square, 1)
    marks = sides_ref[...].astype(jnp.float32)
    return [
        jnp.sum(jnp.where(diagonal, marks[side : side + 1, :], 0.0), axis=1, keepdims=True)
        for side in range(2)
    ]


def start_all(copies):
    for copy in copies:
        copy.start()
    return copies


def wait_all(copies):
    for copy in copies:
        copy.wait()


def edge_kernel(
    ground_hbm, depth_hbm, rows_hbm, sides_hbm,
    far_ref, near_ref, far_even_ref, far_odd_ref, even_ref, odd_ref,
    ground_ref, depth_ref, edge_ref, marks_ref, sides_ref, sems, small_sems,
):
    height, width = ground_hbm.shape
    groups = height // SUBS
    tiles = width // (SUBS * LANES)
    last_tile = width // LANES - 1
    pieces = sems.shape[2]
    part = width // pieces
    place, places = chain_place()
    col, cols = lax.axis_index("cols"), lax.axis_size("cols")
    top = place % 2 == 0
    firsts = [aligned(jnp.where(is_top, 0, height - SUBS)) for is_top in (top, jnp.logical_not(top))]
    small = [pltpu.make_async_copy(sides_hbm, sides_ref, small_sems.at[0])]
    for side, tile in enumerate((0, last_tile)):
        columns = pl.ds(tile * LANES, LANES)
        for number, (source, target) in enumerate(
            (
                (ground_hbm.at[:, columns], edge_ref.at[side, 0]),
                (depth_hbm.at[:, columns], edge_ref.at[side, 1]),
                (rows_hbm.at[:, columns], marks_ref.at[side]),
            )
        ):
            small.append(pltpu.make_async_copy(source, target, small_sems.at[1 + side * 3 + number]))
    copies = [
        [
            [
                pltpu.make_async_copy(
                    source.at[pl.ds(first, SUBS), pl.ds(piece * part, part)],
                    target.at[where, :, pl.ds(piece * part, part)],
                    sems.at[where, kind, piece],
                )
                for kind, (source, target) in enumerate(((ground_hbm, ground_ref), (depth_hbm, depth_ref)))
            ]
            for piece in range(pieces)
        ]
        for where, first in enumerate(firsts)
    ]
    start_all(copies[0][0])
    start_all(small)
    for pair in copies[0][1:] + copies[1]:
        start_all(pair)
    sub, lane = position()
    size = tiles * SUBS
    wait_all(small)
    marks = side_marks(sides_ref)
    at_edges = [(lane == 0) & (col == 0), (lane == LANES - 1) & (col == cols - 1)]
    for where, (out_ref, is_top) in enumerate(((far_ref, top), (near_ref, jnp.logical_not(top)))):
        ground_base = jnp.where(is_top, 0, (SUBS - 1) * size)
        surface_base = jnp.where(is_top, (SUBS - 1) * size, 0)
        for tile in range(last_tile + 1):
            if tile * LANES % part == 0:
                wait_all(copies[where][tile * LANES // part])
            columns = pl.ds(tile * LANES, LANES)
            ground = ground_ref[where, :, columns]
            surface = ground + depth_ref[where, :, columns]
            if tile in (0, last_tile):
                side = 0 if tile == 0 else 1
                chosen = jnp.where(is_top, marks[side][:SUBS], marks[side][height - SUBS :])
                surface = jnp.where((chosen > 0.5) & at_edges[side], ground, surface)
            chunk, slot = tile // tiles, tile % tiles
            start = slot * SUBS + chunk
            out_ref[pl.ds(ground_base + start, SUBS, stride=size), :] = ground
            out_ref[pl.ds(surface_base + start, SUBS, stride=size), :] = surface
    rightward = col % 2 == 0
    strips = []
    for group in range(groups):
        rows = pl.ds(group * SUBS, SUBS)
        values = []
        for side in range(2):
            ground = edge_ref[side, 0, rows, :]
            surface = ground + edge_ref[side, 1, rows, :]
            outlet = (marks[side][group * SUBS : (group + 1) * SUBS] > 0.5) & at_edges[side]
            if group == 0:
                outlet = outlet | (marks_ref[side, 0:1] == 1) & (sub == 0) & (place == 0)
            if group == groups - 1:
                outlet = outlet | (marks_ref[side, 1:2] == 1) & (sub == SUBS - 1) & (place == places - 1)
            values.append((ground, jnp.where(outlet, ground, surface)))
        strips.append(values)
        for kind in range(2):
            rows = pl.ds(kind * height + group * SUBS, SUBS)
            even_ref[rows, :] = jnp.where(rightward, values[1][kind], values[0][kind])
            odd_ref[rows, :] = jnp.where(rightward, values[0][kind], values[1][kind])
    for kind in range(2):
        rows = pl.ds(kind * SUBS, SUBS)
        first, last = [jnp.where(top, strips[0][side][kind], strips[-1][side][kind]) for side in range(2)]
        far_even_ref[rows, :] = jnp.where(rightward, last, first)
        far_odd_ref[rows, :] = jnp.where(rightward, first, last)


def start_own(ground_hbm, depth_hbm, ground_ref, depth_ref, sems):
    height, width = ground_hbm.shape
    groups = height // SUBS
    pieces = sems.shape[1] // groups
    part = width // pieces
    copies = []
    for group in range(groups):
        for piece in range(pieces):
            where = (pl.ds(group * SUBS, SUBS), pl.ds(piece * part, part))
            number = group * pieces + piece
            copies.append(
                start_all(
                    [
                        pltpu.make_async_copy(ground_hbm.at[where], ground_ref.at[where], sems.at[0, number]),
                        pltpu.make_async_copy(depth_hbm.at[where], depth_ref.at[where], sems.at[1, number]),
                    ]
                )
            )
    return copies


def fold_own(copies, ground_ref, depth_ref, rows_ref, sides_ref, ground_out, surface_out):
    height, width = ground_ref.shape
    groups = height // SUBS
    tiles = width // (SUBS * LANES)
    last_tile = width // LANES - 1
    pieces = len(copies) // groups
    part = width // pieces
    size = (tiles + 1) * SUBS
    place, places = chain_place()
    col, cols = lax.axis_index("cols"), lax.axis_size("cols")
    sub, lane = position()
    marks = side_marks(sides_ref)
    for group in range(groups):
        rows = pl.ds(group * SUBS, SUBS)
        for tile in range(last_tile + 1):
            if tile * LANES % part == 0:
                wait_all(copies[group * pieces + tile * LANES // part])
            columns = pl.ds(tile * LANES, LANES)
            ground = ground_ref[rows, columns]
            surface = ground + depth_ref[rows, columns]
            outlets = []
            if group == 0:
                outlets.append((rows_ref[0:1, columns] == 1) & (sub == 0) & (place == 0))
            if group == groups - 1:
                outlets.append(
                    (rows_ref[1:2, columns] == 1) & (sub == SUBS - 1) & (place == places - 1)
                )
            if tile == 0:
                outlets.append(
                    (marks[0][group * SUBS : (group + 1) * SUBS] > 0.5) & (lane == 0) & (col == 0)
                )
            if tile == last_tile:
                outlets.append(
                    (marks[1][group * SUBS : (group + 1) * SUBS] > 0.5)
                    & (lane == LANES - 1)
                    & (col == cols - 1)
                )
            for outlet in outlets:
                surface = jnp.where(outlet, ground, surface)
            chunk, slot = tile // tiles, tile % tiles
            start = (PASSES + group * SUBS) * size + slot * SUBS + chunk
            ground_out[pl.ds(start, SUBS, stride=size), :] = ground
            surface_out[pl.ds(start, SUBS, stride=size), :] = surface


def unpack_rows(rows_ref, first, is_top, present, strip_refs, strip_rows, ground_ref, surface_ref, tiles):
    packed = tiles * SUBS
    size = packed + SUBS
    bases = (jnp.where(is_top, SUBS - 1, 0), jnp.where(is_top, 0, SUBS - 1))
    for base, out_ref, strip_row in zip(bases, (ground_ref, surface_ref), strip_rows):

        def body(row, carry):
            values = [
                jnp.where(present, rows_ref[register(base + row, slot, packed), :], unreached)
                for slot in range(tiles)
            ]
            for slot in range(tiles):
                out_ref[register(first + row, slot, size), :] = values[slot]
            fill_seam(out_ref, first + row, values[0], values[-1], strip_refs, strip_row + row, present, tiles)
            return carry

        lax.fori_loop(0, PASSES, body, 0, unroll=4)


def fill_seam(out_ref, row, first_tile, last_tile, strip_refs, strip_row, present, tiles):
    col, cols = lax.axis_index("cols"), lax.axis_size("cols")
    sub, lane = position()
    rightward = col % 2 == 0
    even, odd = [ref[pl.ds(strip_row, 1), :] for ref in strip_refs]
    after = jnp.where(present & (col < cols - 1), jnp.where(rightward, even, odd), unreached)
    before = jnp.where(present & (col > 0), jnp.where(rightward, odd, even), unreached)
    after = jnp.where(sub == SUBS - 1, after, pltpu.roll(first_tile, SUBS - 1, 0))
    before = jnp.where(sub == 0, before, pltpu.roll(last_tile, 1, 0))
    out_ref[register(row, tiles, (tiles + 1) * SUBS), :] = jnp.where(lane < LANES // 2, after, before)


def relax_rows(source, target, ground, first, count, ring):
    size = ring * SUBS
    _, lane = position()
    at_first = lane == 0
    at_last = lane == LANES - 1
    order = [ring - 1] + list(range(ring - 1))
    made = {}

    def make(pair, slot):
        row = first + 2 * pair
        values = [source[register(row + step, slot, size), :] for step in range(-1, 3)]
        both = jnp.minimum(values[1], values[2])
        for one, column in enumerate((jnp.minimum(values[0], both), jnp.minimum(both, values[3]))):
            made[pair, one, slot] = (column, pltpu.roll(column, 1, 1), pltpu.roll(column, LANES - 1, 1))

    def finish(pair, slot):
        for one in range(2):
            row = first + 2 * pair + one
            before, here, after = [made[pair, one, (slot + step) % ring] for step in (-1, 0, 1)]
            from_left = jnp.where(at_first, before[1], here[1])
            from_right = jnp.where(at_last, after[2], here[2])
            lowest = jnp.minimum(jnp.minimum(from_left, from_right), here[0])
            where = register(row, slot, size)
            raised = jnp.minimum(source[where, :], lowest + rise_step)
            target[where, :] = jnp.maximum(ground[where, :], raised)

    makes = [(pair, slot) for pair in range(count // 2) for slot in order]
    finishes = [(pair, slot) for pair in range(count // 2) for slot in range(ring)]
    done = 0
    for number, item in enumerate(makes):
        make(*item)
        if number >= AHEAD:
            finish(*finishes[done])
            done += 1
    for item in finishes[done:]:
        finish(*item)


def hop_counts(links_ref, hops_ref, needed):
    tiles, degree = links_ref.shape
    links = links_ref[...]
    number = lax.broadcasted_iota(jnp.int32, (tiles, tiles), 1)
    linked = links[:, 0:1] == number
    for edge in range(1, degree):
        linked = linked | (links[:, edge : edge + 1] == number)
    linked = linked.astype(jnp.float32)
    tile = lax.broadcasted_iota(jnp.int32, (tiles, LANES), 0)
    lane = lax.broadcasted_iota(jnp.int32, (tiles, LANES), 1)
    reached = jnp.zeros((tiles, LANES), jnp.float32)
    for index, wanted in enumerate(needed):
        reached = jnp.where((lane == index) & (tile == wanted), 1.0, reached)
    hops = jnp.where(reached > 0.5, 0.0, float(ROUNDS + 1))
    for hop in range(1, ROUNDS + 1):
        reached = lax.dot_general(
            linked, reached, (((0,), (0,)), ((), ())), preferred_element_type=jnp.float32
        )
        reached = jnp.where(reached > 0.5, 1.0, 0.0)
        hops = jnp.minimum(hops, jnp.where(reached > 0.5, float(hop), float(ROUNDS + 1)))
    for index in range(len(needed)):
        hops_ref[pl.ds(index * tiles, tiles), :] = jnp.broadcast_to(
            hops[:, index : index + 1], (tiles, LANES)
        )


def needed_tiles():
    row, rows = lax.axis_index("rows"), lax.axis_size("rows")
    col, cols = lax.axis_index("cols"), lax.axis_size("cols")
    sub, subs = lax.axis_index("sub"), lax.axis_size("sub")
    above = jnp.maximum(jnp.where(sub == 0, row - 1, row), 0)
    below = jnp.minimum(jnp.where(sub == subs - 1, row + 1, row), rows - 1)
    left = jnp.maximum(col - 1, 0)
    right = jnp.minimum(col + 1, cols - 1)
    return [r * cols + c for r in (above, row, below) for c in (left, col, right)]


def inner_kernel(
    ground_hbm, depth_hbm, rows_hbm, sides_hbm, links_hbm,
    near_ref, own_even_ref, own_odd_ref, near_even_ref, near_odd_ref,
    ground_ref, surface_ref, other_ref, hops_ref,
    raw_ground_ref, raw_depth_ref, rows_ref, sides_ref, links_ref, sems, small_sems,
):
    height, width = ground_hbm.shape
    tiles = width // (SUBS * LANES)
    small = start_all(
        [
            pltpu.make_async_copy(source, target, small_sems.at[number])
            for number, (source, target) in enumerate(
                ((rows_hbm, rows_ref), (sides_hbm, sides_ref), (links_hbm, links_ref))
            )
        ]
    )
    copies = start_own(ground_hbm, depth_hbm, raw_ground_ref, raw_depth_ref, sems)
    own_strips, near_strips = (own_even_ref, own_odd_ref), (near_even_ref, near_odd_ref)
    ring = tiles + 1
    size = ring * SUBS
    place, places = chain_place()
    top = place % 2 == 0
    has_near = jnp.where(top, place < places - 1, place > 0)
    unpack_rows(
        near_ref,
        jnp.where(top, PASSES + height, 0),
        jnp.logical_not(top),
        has_near,
        near_strips,
        [kind * height + jnp.where(top, 0, height - SUBS) for kind in range(2)],
        ground_ref,
        surface_ref,
        tiles,
    )
    wait_all(small)
    hop_counts(links_ref, hops_ref, needed_tiles())
    fold_own(copies, raw_ground_ref, raw_depth_ref, rows_ref, sides_ref, ground_ref, surface_ref)
    for kind, out_ref in enumerate((ground_ref, surface_ref)):

        def body(row, carry):
            first_tile = out_ref[register(PASSES + row, 0, size), :]
            last_tile = out_ref[register(PASSES + row, tiles - 1, size), :]
            fill_seam(
                out_ref, PASSES + row, first_tile, last_tile, own_strips, kind * height + row, place >= 0, tiles
            )
            return carry

        lax.fori_loop(0, height, body, 0, unroll=4)
    buffers = (surface_ref, other_ref)
    for step in range(1, PASSES + 1):
        first = step + jnp.where(top, PASSES, 0)
        count = height + PASSES - 2 * step
        relax_rows(buffers[(step + 1) % 2], buffers[step % 2], ground_ref, first, count, ring)


def outer_kernel(height, tiles, far_ref, even_ref, odd_ref, *refs):
    ground_ref, surface_ref, other_ref, level_ref, far_out, near_out = refs[3:9]
    ring = tiles + 1
    size = ring * SUBS
    place, places = chain_place()
    top = place % 2 == 0
    has_far = jnp.where(top, place > 0, place < places - 1)
    unpack_rows(
        far_ref,
        jnp.where(top, 0, PASSES + height),
        top,
        has_far,
        (even_ref, odd_ref),
        [0, SUBS],
        ground_ref,
        surface_ref,
        tiles,
    )
    buffers = (surface_ref, other_ref)
    for step in range(1, PASSES + 1):
        first = jnp.where(top, step, PASSES + height - step)
        relax_rows(buffers[(step + 1) % 2], buffers[step % 2], ground_ref, first, PASSES, ring)
    low, high = PASSES, PASSES + height - FINAL
    far_out[...] = surface_ref[rows_at(jnp.where(top, low, high), FINAL, size), :]
    near_out[...] = surface_ref[rows_at(jnp.where(top, high, low), FINAL, size), :]
    band, bands = lax.axis_index("sub"), lax.axis_size("sub")
    sub, lane = position()

    def at(row, slot):
        return surface_ref[register(PASSES + row, slot, size), :]

    first_cell = (sub == 0) & (lane == 0)
    last_cell = (sub == SUBS - 1) & (lane == LANES - 1)
    first_lows, last_lows, row_lows = [], [], []
    for row in range(height):
        first_lows.append(at(row, 0))
        last_lows.append(at(row, tiles - 1))
    for slot in range(tiles):
        row_lows.append(jnp.where(band == 0, at(0, slot), unreached))
        row_lows.append(jnp.where(band == bands - 1, at(height - 1, slot), unreached))
    lowest = jnp.minimum(
        least(row_lows),
        jnp.minimum(
            jnp.where(first_cell, least(first_lows), unreached),
            jnp.where(last_cell, least(last_lows), unreached),
        ),
    )
    lowest = jnp.min(jnp.min(lowest, axis=0, keepdims=True), axis=1, keepdims=True)
    tile_id = lax.axis_index("rows") * lax.axis_size("cols") + lax.axis_index("cols")
    number = lax.broadcasted_iota(jnp.int32, level_ref.shape, 0)
    level_ref[...] = jnp.where(number == tile_id, lowest, unreached)


def least(values):
    values = list(values)
    while len(values) > 1:
        values = [
            jnp.minimum(*values[number : number + 2]) if number + 1 < len(values) else values[number]
            for number in range(0, len(values), 2)
        ]
    return values[0]


def late_kernel(
    height, tiles, ground_ref, surface_ref, far_ref, near_ref, level_ref, hops_ref, out_hbm,
    one_ref, two_ref, out_ref, sems,
):
    ring = tiles + 1
    size = ring * SUBS
    sub, lane = position()
    place, _ = chain_place()
    top = place % 2 == 0
    level = level_ref[...]
    count = level.shape[0]
    raised = [level]
    for hop in range(ROUNDS):
        raised.append(raised[-1] + hop_rise)
    ceilings = []
    for index in range(9):
        hops = hops_ref[pl.ds(index * count, count), :]
        lowest = jnp.full((count, LANES), unreached, jnp.float32)
        for hop in range(ROUNDS + 1):
            lowest = jnp.where(hops == float(hop), raised[hop], lowest)
        lowest = jnp.min(lowest, axis=0, keepdims=True) + spill_lift
        ceilings.append(jnp.broadcast_to(lowest, (SUBS, LANES)))
    pairs = []
    for region in range(3):
        left, middle, right = ceilings[3 * region : 3 * region + 3]
        seam = jnp.where(
            lane < LANES // 2,
            jnp.where(sub == SUBS - 1, right, middle),
            jnp.where(sub == 0, left, middle),
        )
        pairs.append((middle, seam))
    low, high = PASSES - FINAL, PASSES + height
    far_pair = [jnp.where(top, above, below) for above, below in zip(pairs[0], pairs[2])]
    near_pair = [jnp.where(top, below, above) for above, below in zip(pairs[0], pairs[2])]
    spans = (
        (far_ref, 0, jnp.where(top, low, high), FINAL, far_pair),
        (near_ref, 0, jnp.where(top, high, low), FINAL, near_pair),
        (surface_ref, PASSES, PASSES, height, pairs[1]),
    )
    for source, source_first, first, rows, (middle, seam) in spans:

        def body(row, carry):
            for slot in range(ring):
                value = source[register(source_first + row, slot, size), :]
                value = jnp.minimum(value, seam if slot == tiles else middle)
                where = register(first + row, slot, size)
                one_ref[where, :] = jnp.maximum(ground_ref[where, :], value)
            return carry

        lax.fori_loop(0, rows, body, 0, unroll=4)
    buffers = (one_ref, two_ref)
    for step in range(1, FINAL):
        first = PASSES - FINAL + step
        relax_rows(
            buffers[(step + 1) % 2], buffers[step % 2], ground_ref, first, 2 * PASSES + height - 2 * first, ring
        )
    source, target = buffers[(FINAL + 1) % 2], buffers[FINAL % 2]
    copies = []
    for group in range(height // SUBS):
        first = PASSES + group * SUBS
        relax_rows(source, target, ground_ref, first, SUBS, ring)
        for tile in range(tiles * SUBS):
            chunk, slot = tile // tiles, tile % tiles
            out_ref[pl.ds(group * SUBS, SUBS), pl.ds(tile * LANES, LANES)] = target[
                pl.ds(first * size + slot * SUBS + chunk, SUBS, stride=size), :
            ]
        where = (pl.ds(group * SUBS, SUBS), slice(None))
        copies += start_all([pltpu.make_async_copy(out_ref.at[where], out_hbm.at[where], sems.at[group])])
    wait_all(copies)


def in_vmem(count):
    return [pl.BlockSpec(memory_space=pltpu.VMEM)] * count


def in_hbm(count):
    return [pl.BlockSpec(memory_space=pltpu.HBM)] * count


def exchange_stages(rows, cols, subs):
    bits = []
    for axis, count in enumerate((rows, cols, subs)):
        bit = 1
        while bit < count:
            bits.append((axis, bit))
            bit *= 2
    bits.reverse()
    stages = []
    for first in range(0, len(bits), 2):
        group = bits[first : first + 2]
        shifts = []
        for chosen in range(1, 2 ** len(group)):
            shift = [0, 0, 0]
            for number, (axis, bit) in enumerate(group):
                if chosen >> number & 1:
                    shift[axis] ^= bit
            shifts.append(shift)
        stages.append(shifts)
    return stages


def share_levels(level, rows_arriving):
    rows, cols, subs = [lax.axis_size(axis) for axis in ("rows", "cols", "sub")]
    if any(count & (count - 1) for count in (rows, cols, subs)):
        return lax.pmin(level, ("rows", "cols", "sub")), rows_arriving
    for number, shifts in enumerate(exchange_stages(rows, cols, subs)):
        arrived = [level]
        for down, across, core in shifts:
            pairs = [
                (
                    (row * cols + col) * subs + sub,
                    ((row ^ down) * cols + (col ^ across)) * subs + (sub ^ core),
                )
                for row in range(rows)
                for col in range(cols)
                for sub in range(subs)
            ]
            arrived.append(lax.ppermute(level, ("rows", "cols", "sub"), pairs))
        level = least(arrived)
        if number == 0:
            level, *rows_arriving = lax.optimization_barrier((level, *rows_arriving))
    return level, rows_arriving


def per_device(elevation, fill_depth, edge_rows, edge_sides, adjacency):
    height, width = elevation.shape
    tiles = width // (SUBS * LANES)
    groups = height // SUBS
    f32 = jnp.float32
    packed = tiles * SUBS
    size = packed + SUBS
    tile_count = adjacency.shape[0]
    places = lax.axis_size(("rows", "sub"))
    cols, subs = lax.axis_size("cols"), lax.axis_size("sub")
    short = pl.CostEstimate(flops=1024, bytes_accessed=1024, transcendentals=0)
    limit = pltpu.CompilerParams(vmem_limit_bytes=24 << 20)
    arguments = [
        pltpu.with_memory_space_constraint(value, pltpu.HBM)
        for value in (elevation, fill_depth, edge_rows, edge_sides, adjacency)
    ]
    sent = pltpu.VMEM(((2 * PASSES - 1) * packed, LANES), f32)
    strip = pltpu.VMEM((2 * height, LANES), f32)
    far_strip = pltpu.VMEM((2 * SUBS, LANES), f32)
    far, near, far_even, far_odd, even, odd = pl.pallas_call(
        edge_kernel,
        out_shape=[sent, sent, far_strip, far_strip, strip, strip],
        in_specs=in_hbm(4),
        out_specs=in_vmem(6),
        scratch_shapes=[
            pltpu.VMEM((2, SUBS, width), f32),
            pltpu.VMEM((2, SUBS, width), f32),
            pltpu.VMEM((2, 2, height, LANES), f32),
            pltpu.VMEM((2, 2, LANES), jnp.int32),
            pltpu.VMEM(edge_sides.shape, jnp.int32),
            pltpu.SemaphoreType.DMA((2, 2, 4)),
            pltpu.SemaphoreType.DMA((7,)),
        ],
        compiler_params=limit,
        cost_estimate=short,
        name="edge_rows",
    )(*arguments[:4])

    near_pairs, far_pairs = [closed(matching(places, first), places) for first in range(2)]
    stay = [(place, place) for place in range(places)]
    device_axes = ("rows", "cols", "sub")

    def swap_strips(pieces, row_pairs):
        arrived = []
        for first, piece in enumerate(pieces):
            pairs = cross(row_pairs, matching(cols, first), cols, subs)
            arrived.append(lax.ppermute(piece, device_axes, pairs) if pairs else piece)
        return arrived

    far_strips = swap_strips((far_even, far_odd), far_pairs)
    far_rows = lax.ppermute(far, ("rows", "sub"), far_pairs)
    near_rows = lax.ppermute(near, ("rows", "sub"), near_pairs)
    strips = swap_strips((even, odd), stay) + swap_strips((even, odd), near_pairs)

    work = pltpu.VMEM(((height + 2 * PASSES) * size, LANES), f32)
    ground, surface, other, hops = pl.pallas_call(
        inner_kernel,
        out_shape=[work, work, work, pltpu.VMEM((9 * tile_count, LANES), f32)],
        in_specs=in_hbm(5) + in_vmem(5),
        out_specs=in_vmem(4),
        scratch_shapes=[
            pltpu.VMEM((height, width), f32),
            pltpu.VMEM((height, width), f32),
            pltpu.VMEM(edge_rows.shape, jnp.int32),
            pltpu.VMEM(edge_sides.shape, jnp.int32),
            pltpu.VMEM(adjacency.shape, jnp.int32),
            pltpu.SemaphoreType.DMA((2, 4 * groups)),
            pltpu.SemaphoreType.DMA((3,)),
        ],
        compiler_params=limit,
        cost_estimate=short,
        name="inner_passes",
    )(*arguments, near_rows, *strips)

    def outer(far_ref, *refs):
        outer_kernel(height, tiles, far_ref, *refs)

    again = pltpu.VMEM((FINAL * size, LANES), f32)
    ground, surface, other, level, far, near = pl.pallas_call(
        outer,
        out_shape=[work, work, work, pltpu.VMEM((tile_count, LANES), f32), again, again],
        in_specs=in_vmem(6),
        out_specs=in_vmem(6),
        input_output_aliases={3: 0, 4: 1, 5: 2},
        compiler_params=limit,
        cost_estimate=short,
        name="outer_passes",
    )(far_rows, *far_strips, ground, surface, other)

    far_rows = lax.ppermute(far, ("rows", "sub"), far_pairs)
    near_rows = lax.ppermute(near, ("rows", "sub"), near_pairs)
    level, (far_rows, near_rows) = share_levels(level, (far_rows, near_rows))

    def late(*refs):
        late_kernel(height, tiles, *refs)

    return pl.pallas_call(
        late,
        out_shape=jax.ShapeDtypeStruct((height, width), f32),
        in_specs=in_vmem(6),
        out_specs=pl.BlockSpec(memory_space=pltpu.HBM),
        scratch_shapes=[
            pltpu.VMEM(((height + 2 * PASSES) * size, LANES), f32),
            pltpu.VMEM(((height + 2 * PASSES) * size, LANES), f32),
            pltpu.VMEM((height, width), f32),
            pltpu.SemaphoreType.DMA((groups,)),
        ],
        compiler_params=limit,
        cost_estimate=short,
        name="final_passes",
    )(ground, surface, far_rows, near_rows, level, hops)


def solution(mesh):
    placed = (
        P(("groups", "rows", "sub"), "cols"),
        P(("groups", "rows", "sub"), "cols"),
        P("groups", "cols"),
        P("groups", ("rows", "sub")),
        P("groups", None),
    )
    return jax.shard_map(
        per_device,
        mesh=mesh,
        in_specs=placed,
        out_specs=P(("groups", "rows", "sub"), "cols"),
        check_vma=False,
    )
```

```python
import jax
import jax.numpy as jnp
from jax import lax
from jax.experimental import pallas as pl
from jax.experimental.pallas import tpu as pltpu
from jax.sharding import PartitionSpec as P

PASSES = 8
FINAL = 4
ROUNDS = 4
HALO = PASSES + FINAL
SUBS = 8
LANES = 128
AHEAD = 5

unreached = 1000000000.0
rise_step = 0.01
hop_rise = 0.05
spill_lift = 3.0


def matching(count, first):
    pairs = []
    for low in range(first, count - 1, 2):
        pairs += [(low, low + 1), (low + 1, low)]
    return pairs


def closed(pairs, count):
    used = {source for source, _ in pairs}
    return pairs + [(place, place) for place in range(count) if place not in used]


def cross(row_pairs, col_pairs, cols, subs):
    def device(place, col):
        return (place // subs * cols + col) * subs + place % subs

    return [
        (device(row, col), device(row_to, col_to))
        for row, row_to in row_pairs
        for col, col_to in col_pairs
    ]


def chain_place():
    subs = lax.axis_size("sub")
    return lax.axis_index("rows") * subs + lax.axis_index("sub"), lax.axis_size("rows") * subs


def position():
    sub = lax.broadcasted_iota(jnp.int32, (SUBS, LANES), 0)
    lane = lax.broadcasted_iota(jnp.int32, (SUBS, LANES), 1)
    return sub, lane


def aligned(start):
    return start if isinstance(start, int) else pl.multiple_of(start, SUBS)


def rows_at(first, count, size):
    return pl.ds(aligned(first * size), count * size)


def register(row, slot, size):
    return pl.ds(aligned(row * size + slot * SUBS), SUBS)


def side_marks(sides_ref):
    height = sides_ref.shape[1]
    square = (height, height)
    diagonal = lax.broadcasted_iota(jnp.int32, square, 0) == lax.broadcasted_iota(jnp.int32, square, 1)
    marks = sides_ref[...].astype(jnp.float32)
    return [
        jnp.sum(jnp.where(diagonal, marks[side : side + 1, :], 0.0), axis=1, keepdims=True)
        for side in range(2)
    ]


def start_all(copies):
    for copy in copies:
        copy.start()
    return copies


def wait_all(copies):
    for copy in copies:
        copy.wait()


def edge_kernel(
    ground_hbm, depth_hbm, rows_hbm, sides_hbm,
    far_ref, near_ref, even_ref, odd_ref,
    ground_ref, depth_ref, marks_ref, sides_ref, sems, small_sems,
):
    height, width = ground_hbm.shape
    groups = height // SUBS
    last_tile = width // LANES - 1
    place, places = chain_place()
    col, cols = lax.axis_index("cols"), lax.axis_size("cols")
    small = [pltpu.make_async_copy(sides_hbm, sides_ref, small_sems.at[0])]
    for side, tile in enumerate((0, last_tile)):
        columns = pl.ds(tile * LANES, LANES)
        small.append(pltpu.make_async_copy(rows_hbm.at[:, columns], marks_ref.at[side], small_sems.at[1 + side]))
    copies = start_own(ground_hbm, depth_hbm, ground_ref, depth_ref, sems)
    start_all(small)
    sub, lane = position()
    wait_all(small)
    marks = side_marks(sides_ref)
    at_edges = [(lane == 0) & (col == 0), (lane == LANES - 1) & (col == cols - 1)]
    for copy in copies:
        wait_all(copy)

    def raised(group, tile):
        rows, columns = pl.ds(group * SUBS, SUBS), pl.ds(tile * LANES, LANES)
        ground = ground_ref[rows, columns]
        surface = ground + depth_ref[rows, columns]
        if tile in (0, last_tile):
            side = 0 if tile == 0 else 1
            chosen = marks[side][group * SUBS : (group + 1) * SUBS]
            surface = jnp.where((chosen > 0.5) & at_edges[side], ground, surface)
        return ground, surface

    def pack(up_ref, down_ref):
        tiles = width // (SUBS * LANES)
        size = tiles * SUBS
        skipped = height - HALO
        for tile in range(last_tile + 1):
            start = tile % tiles * SUBS + tile // tiles
            for out_ref, ground_slot, surface_slot, shift, keep in (
                (up_ref, 0, HALO - 1, 0, range(0, HALO)),
                (down_ref, HALO - 1, 0, skipped, range(skipped, height)),
            ):
                values = [raised(group, tile) for group in range(groups)]
                for kind, slot in enumerate((ground_slot, surface_slot)):
                    for group in range(groups):
                        inside = [row for row in range(group * SUBS, (group + 1) * SUBS) if row in keep]
                        first, count = inside[0], len(inside)
                        offset = first - group * SUBS
                        row = slot + first - shift
                        out_ref[pl.ds(row * size + start, count, stride=size), :] = values[group][kind][
                            offset : offset + count
                        ]

    top = place % 2 == 0
    pl.when(top)(lambda: pack(far_ref, near_ref))
    pl.when(jnp.logical_not(top))(lambda: pack(near_ref, far_ref))
    rightward = col % 2 == 0
    for group in range(groups):
        values = []
        for side, tile in enumerate((0, last_tile)):
            ground, surface = raised(group, tile)
            if group == 0:
                outlet = (marks_ref[side, 0:1] == 1) & (sub == 0) & (place == 0)
                surface = jnp.where(outlet, ground, surface)
            if group == groups - 1:
                outlet = (marks_ref[side, 1:2] == 1) & (sub == SUBS - 1) & (place == places - 1)
                surface = jnp.where(outlet, ground, surface)
            values.append((ground, surface))
        for kind in range(2):
            rows = pl.ds(kind * height + group * SUBS, SUBS)
            even_ref[rows, :] = jnp.where(rightward, values[1][kind], values[0][kind])
            odd_ref[rows, :] = jnp.where(rightward, values[0][kind], values[1][kind])


def start_own(ground_hbm, depth_hbm, ground_ref, depth_ref, sems):
    height, width = ground_hbm.shape
    groups = height // SUBS
    pieces = sems.shape[1] // groups
    part = width // pieces
    copies = []
    for group in range(groups):
        for piece in range(pieces):
            where = (pl.ds(group * SUBS, SUBS), pl.ds(piece * part, part))
            number = group * pieces + piece
            copies.append(
                start_all(
                    [
                        pltpu.make_async_copy(ground_hbm.at[where], ground_ref.at[where], sems.at[0, number]),
                        pltpu.make_async_copy(depth_hbm.at[where], depth_ref.at[where], sems.at[1, number]),
                    ]
                )
            )
    return copies


def fold_own(copies, ground_ref, depth_ref, rows_ref, sides_ref, ground_out, surface_out):
    height, width = ground_ref.shape
    groups = height // SUBS
    tiles = width // (SUBS * LANES)
    last_tile = width // LANES - 1
    pieces = len(copies) // groups
    part = width // pieces
    size = (tiles + 1) * SUBS
    place, places = chain_place()
    col, cols = lax.axis_index("cols"), lax.axis_size("cols")
    sub, lane = position()
    marks = side_marks(sides_ref)
    for group in range(groups):
        rows = pl.ds(group * SUBS, SUBS)
        for tile in range(last_tile + 1):
            if tile * LANES % part == 0:
                wait_all(copies[group * pieces + tile * LANES // part])
            columns = pl.ds(tile * LANES, LANES)
            ground = ground_ref[rows, columns]
            surface = ground + depth_ref[rows, columns]
            outlets = []
            if group == 0:
                outlets.append((rows_ref[0:1, columns] == 1) & (sub == 0) & (place == 0))
            if group == groups - 1:
                outlets.append(
                    (rows_ref[1:2, columns] == 1) & (sub == SUBS - 1) & (place == places - 1)
                )
            if tile == 0:
                outlets.append(
                    (marks[0][group * SUBS : (group + 1) * SUBS] > 0.5) & (lane == 0) & (col == 0)
                )
            if tile == last_tile:
                outlets.append(
                    (marks[1][group * SUBS : (group + 1) * SUBS] > 0.5)
                    & (lane == LANES - 1)
                    & (col == cols - 1)
                )
            for outlet in outlets:
                surface = jnp.where(outlet, ground, surface)
            chunk, slot = tile // tiles, tile % tiles
            start = (HALO + group * SUBS) * size + slot * SUBS + chunk
            ground_out[pl.ds(start, SUBS, stride=size), :] = ground
            surface_out[pl.ds(start, SUBS, stride=size), :] = surface


def unpack_rows(rows_ref, first, is_top, present, strip_refs, strip_rows, ground_ref, surface_ref, tiles):
    packed = tiles * SUBS
    size = packed + SUBS
    bases = (jnp.where(is_top, HALO - 1, 0), jnp.where(is_top, 0, HALO - 1))
    for base, out_ref, strip_row in zip(bases, (ground_ref, surface_ref), strip_rows):

        def body(row, carry):
            values = [
                jnp.where(present, rows_ref[register(base + row, slot, packed), :], unreached)
                for slot in range(tiles)
            ]
            for slot in range(tiles):
                out_ref[register(first + row, slot, size), :] = values[slot]
            fill_seam(out_ref, first + row, values[0], values[-1], strip_refs, strip_row + row, present, tiles)
            return carry

        lax.fori_loop(0, HALO, body, 0, unroll=4)


def fill_seam(out_ref, row, first_tile, last_tile, strip_refs, strip_row, present, tiles):
    col, cols = lax.axis_index("cols"), lax.axis_size("cols")
    sub, lane = position()
    rightward = col % 2 == 0
    even, odd = [ref[pl.ds(strip_row, 1), :] for ref in strip_refs]
    after = jnp.where(present & (col < cols - 1), jnp.where(rightward, even, odd), unreached)
    before = jnp.where(present & (col > 0), jnp.where(rightward, odd, even), unreached)
    after = jnp.where(sub == SUBS - 1, after, pltpu.roll(first_tile, SUBS - 1, 0))
    before = jnp.where(sub == 0, before, pltpu.roll(last_tile, 1, 0))
    out_ref[register(row, tiles, (tiles + 1) * SUBS), :] = jnp.where(lane < LANES // 2, after, before)


def relax_rows(source, target, ground, first, count, ring):
    size = ring * SUBS
    _, lane = position()
    at_first = lane == 0
    at_last = lane == LANES - 1
    order = [ring - 1] + list(range(ring - 1))
    made = {}

    def make(pair, slot):
        row = first + 2 * pair
        values = [source[register(row + step, slot, size), :] for step in range(-1, 3)]
        both = jnp.minimum(values[1], values[2])
        for one, column in enumerate((jnp.minimum(values[0], both), jnp.minimum(both, values[3]))):
            made[pair, one, slot] = (column, pltpu.roll(column, 1, 1), pltpu.roll(column, LANES - 1, 1))

    def finish(pair, slot):
        for one in range(2):
            row = first + 2 * pair + one
            before, here, after = [made[pair, one, (slot + step) % ring] for step in (-1, 0, 1)]
            from_left = jnp.where(at_first, before[1], here[1])
            from_right = jnp.where(at_last, after[2], here[2])
            lowest = jnp.minimum(jnp.minimum(from_left, from_right), here[0])
            where = register(row, slot, size)
            raised = jnp.minimum(source[where, :], lowest + rise_step)
            target[where, :] = jnp.maximum(ground[where, :], raised)

    makes = [(pair, slot) for pair in range(count // 2) for slot in order]
    finishes = [(pair, slot) for pair in range(count // 2) for slot in range(ring)]
    done = 0
    for number, item in enumerate(makes):
        make(*item)
        if number >= AHEAD:
            finish(*finishes[done])
            done += 1
    for item in finishes[done:]:
        finish(*item)


def hop_counts(links_ref, hops_ref, needed):
    tiles, degree = links_ref.shape
    links = links_ref[...]
    number = lax.broadcasted_iota(jnp.int32, (tiles, tiles), 1)
    linked = links[:, 0:1] == number
    for edge in range(1, degree):
        linked = linked | (links[:, edge : edge + 1] == number)
    linked = linked.astype(jnp.float32)
    tile = lax.broadcasted_iota(jnp.int32, (tiles, LANES), 0)
    lane = lax.broadcasted_iota(jnp.int32, (tiles, LANES), 1)
    reached = jnp.zeros((tiles, LANES), jnp.float32)
    for index, wanted in enumerate(needed):
        reached = jnp.where((lane == index) & (tile == wanted), 1.0, reached)
    hops = jnp.where(reached > 0.5, 0.0, float(ROUNDS + 1))
    for hop in range(1, ROUNDS + 1):
        reached = lax.dot_general(
            linked, reached, (((0,), (0,)), ((), ())), preferred_element_type=jnp.float32
        )
        reached = jnp.where(reached > 0.5, 1.0, 0.0)
        hops = jnp.minimum(hops, jnp.where(reached > 0.5, float(hop), float(ROUNDS + 1)))
    for index in range(len(needed)):
        hops_ref[pl.ds(index * tiles, tiles), :] = jnp.broadcast_to(
            hops[:, index : index + 1], (tiles, LANES)
        )


def needed_tiles():
    row, rows = lax.axis_index("rows"), lax.axis_size("rows")
    col, cols = lax.axis_index("cols"), lax.axis_size("cols")
    sub, subs = lax.axis_index("sub"), lax.axis_size("sub")
    above = jnp.maximum(jnp.where(sub == 0, row - 1, row), 0)
    below = jnp.minimum(jnp.where(sub == subs - 1, row + 1, row), rows - 1)
    left = jnp.maximum(col - 1, 0)
    right = jnp.minimum(col + 1, cols - 1)
    return [r * cols + c for r in (above, row, below) for c in (left, col, right)]


def inner_kernel(
    ground_hbm, depth_hbm, rows_hbm, sides_hbm, links_hbm,
    near_ref, own_even_ref, own_odd_ref, near_even_ref, near_odd_ref,
    ground_ref, surface_ref, other_ref, hops_ref,
    raw_ground_ref, raw_depth_ref, rows_ref, sides_ref, links_ref, sems, small_sems,
):
    height, width = ground_hbm.shape
    tiles = width // (SUBS * LANES)
    small = start_all(
        [
            pltpu.make_async_copy(source, target, small_sems.at[number])
            for number, (source, target) in enumerate(
                ((rows_hbm, rows_ref), (sides_hbm, sides_ref), (links_hbm, links_ref))
            )
        ]
    )
    copies = start_own(ground_hbm, depth_hbm, raw_ground_ref, raw_depth_ref, sems)
    own_strips, near_strips = (own_even_ref, own_odd_ref), (near_even_ref, near_odd_ref)
    ring = tiles + 1
    size = ring * SUBS
    place, places = chain_place()
    top = place % 2 == 0
    has_near = jnp.where(top, place < places - 1, place > 0)
    unpack_rows(
        near_ref,
        jnp.where(top, HALO + height, 0),
        jnp.logical_not(top),
        has_near,
        near_strips,
        [kind * height + jnp.where(top, 0, height - HALO) for kind in range(2)],
        ground_ref,
        surface_ref,
        tiles,
    )
    wait_all(small)
    hop_counts(links_ref, hops_ref, needed_tiles())
    fold_own(copies, raw_ground_ref, raw_depth_ref, rows_ref, sides_ref, ground_ref, surface_ref)
    for kind, out_ref in enumerate((ground_ref, surface_ref)):

        def body(row, carry):
            first_tile = out_ref[register(HALO + row, 0, size), :]
            last_tile = out_ref[register(HALO + row, tiles - 1, size), :]
            fill_seam(
                out_ref, HALO + row, first_tile, last_tile, own_strips, kind * height + row, place >= 0, tiles
            )
            return carry

        lax.fori_loop(0, height, body, 0, unroll=4)
    buffers = (surface_ref, other_ref)
    for step in range(1, PASSES + 1):
        first = step + jnp.where(top, HALO, 0)
        count = height + HALO - 2 * step
        relax_rows(buffers[(step + 1) % 2], buffers[step % 2], ground_ref, first, count, ring)


def outer_kernel(height, tiles, far_ref, even_ref, odd_ref, *refs):
    ground_ref, surface_ref, other_ref, level_ref = refs[3:7]
    ring = tiles + 1
    size = ring * SUBS
    place, places = chain_place()
    top = place % 2 == 0
    has_far = jnp.where(top, place > 0, place < places - 1)
    unpack_rows(
        far_ref,
        jnp.where(top, 0, HALO + height),
        top,
        has_far,
        (even_ref, odd_ref),
        [kind * height + jnp.where(top, height - HALO, 0) for kind in range(2)],
        ground_ref,
        surface_ref,
        tiles,
    )
    buffers = (surface_ref, other_ref)
    for step in range(1, PASSES + 1):
        first = jnp.where(top, step, HALO + height - step)
        relax_rows(buffers[(step + 1) % 2], buffers[step % 2], ground_ref, first, HALO, ring)
    band, bands = lax.axis_index("sub"), lax.axis_size("sub")
    sub, lane = position()

    def at(row, slot):
        return surface_ref[register(HALO + row, slot, size), :]

    first_cell = (sub == 0) & (lane == 0)
    last_cell = (sub == SUBS - 1) & (lane == LANES - 1)
    first_lows, last_lows, row_lows = [], [], []
    for row in range(height):
        first_lows.append(at(row, 0))
        last_lows.append(at(row, tiles - 1))
    for slot in range(tiles):
        row_lows.append(jnp.where(band == 0, at(0, slot), unreached))
        row_lows.append(jnp.where(band == bands - 1, at(height - 1, slot), unreached))
    lowest = jnp.minimum(
        least(row_lows),
        jnp.minimum(
            jnp.where(first_cell, least(first_lows), unreached),
            jnp.where(last_cell, least(last_lows), unreached),
        ),
    )
    lowest = jnp.min(jnp.min(lowest, axis=0, keepdims=True), axis=1, keepdims=True)
    level_ref[...] = jnp.broadcast_to(lowest, level_ref.shape)


def least(values):
    values = list(values)
    while len(values) > 1:
        values = [
            jnp.minimum(*values[number : number + 2]) if number + 1 < len(values) else values[number]
            for number in range(0, len(values), 2)
        ]
    return values[0]


def late_kernel(
    height, tiles, ground_ref, surface_ref, floors_ref, hops_ref, out_hbm,
    one_ref, two_ref, out_ref, sems,
):
    ring = tiles + 1
    size = ring * SUBS
    sub, lane = position()
    bands = lax.axis_size("sub")
    count = floors_ref.shape[0] // bands
    level = least(floors_ref[pl.ds(band, count, stride=bands), :] for band in range(bands))
    raised = [level]
    for hop in range(ROUNDS):
        raised.append(raised[-1] + hop_rise)
    ceilings = []
    for index in range(9):
        hops = hops_ref[pl.ds(index * count, count), :]
        lowest = jnp.full((count, LANES), unreached, jnp.float32)
        for hop in range(ROUNDS + 1):
            lowest = jnp.where(hops == float(hop), raised[hop], lowest)
        lowest = jnp.min(lowest, axis=0, keepdims=True) + spill_lift
        ceilings.append(jnp.broadcast_to(lowest, (SUBS, LANES)))
    pairs = []
    for region in range(3):
        left, middle, right = ceilings[3 * region : 3 * region + 3]
        seam = jnp.where(
            lane < LANES // 2,
            jnp.where(sub == SUBS - 1, right, middle),
            jnp.where(sub == 0, left, middle),
        )
        pairs.append((middle, seam))
    spans = ((HALO - FINAL, FINAL), (HALO, height), (HALO + height, FINAL))
    for (first, rows), (middle, seam) in zip(spans, pairs):

        def body(row, carry):
            for slot in range(ring):
                where = register(first + row, slot, size)
                value = jnp.minimum(surface_ref[where, :], seam if slot == tiles else middle)
                one_ref[where, :] = jnp.maximum(ground_ref[where, :], value)
            return carry

        lax.fori_loop(0, rows, body, 0, unroll=4)
    buffers = (one_ref, two_ref)
    for step in range(1, FINAL):
        first = HALO - FINAL + step
        relax_rows(
            buffers[(step + 1) % 2], buffers[step % 2], ground_ref, first, 2 * HALO + height - 2 * first, ring
        )
    source, target = buffers[(FINAL + 1) % 2], buffers[FINAL % 2]
    copies = []
    for group in range(height // SUBS):
        first = HALO + group * SUBS
        relax_rows(source, target, ground_ref, first, SUBS, ring)
        for tile in range(tiles * SUBS):
            chunk, slot = tile // tiles, tile % tiles
            out_ref[pl.ds(group * SUBS, SUBS), pl.ds(tile * LANES, LANES)] = target[
                pl.ds(first * size + slot * SUBS + chunk, SUBS, stride=size), :
            ]
        where = (pl.ds(group * SUBS, SUBS), slice(None))
        copies += start_all([pltpu.make_async_copy(out_ref.at[where], out_hbm.at[where], sems.at[group])])
    wait_all(copies)


def in_vmem(count):
    return [pl.BlockSpec(memory_space=pltpu.VMEM)] * count


def in_hbm(count):
    return [pl.BlockSpec(memory_space=pltpu.HBM)] * count


def per_device(elevation, fill_depth, edge_rows, edge_sides, adjacency):
    height, width = elevation.shape
    tiles = width // (SUBS * LANES)
    groups = height // SUBS
    f32 = jnp.float32
    packed = tiles * SUBS
    size = packed + SUBS
    tile_count = adjacency.shape[0]
    places = lax.axis_size(("rows", "sub"))
    cols, subs = lax.axis_size("cols"), lax.axis_size("sub")
    short = pl.CostEstimate(flops=1024, bytes_accessed=1024, transcendentals=0)
    limit = pltpu.CompilerParams(vmem_limit_bytes=24 << 20)
    arguments = [
        pltpu.with_memory_space_constraint(value, pltpu.HBM)
        for value in (elevation, fill_depth, edge_rows, edge_sides, adjacency)
    ]
    sent = pltpu.VMEM(((2 * HALO - 1) * packed, LANES), f32)
    strip = pltpu.VMEM((2 * height, LANES), f32)
    far, near, even, odd = pl.pallas_call(
        edge_kernel,
        out_shape=[sent, sent, strip, strip],
        in_specs=in_hbm(4),
        out_specs=in_vmem(4),
        scratch_shapes=[
            pltpu.VMEM((height, width), f32),
            pltpu.VMEM((height, width), f32),
            pltpu.VMEM((2, 2, LANES), jnp.int32),
            pltpu.VMEM(edge_sides.shape, jnp.int32),
            pltpu.SemaphoreType.DMA((2, 4 * groups)),
            pltpu.SemaphoreType.DMA((3,)),
        ],
        compiler_params=limit,
        cost_estimate=short,
        name="edge_rows",
    )(*arguments[:4])

    near_pairs, far_pairs = [closed(matching(places, first), places) for first in range(2)]
    stay = [(place, place) for place in range(places)]
    device_axes = ("rows", "cols", "sub")

    def swap_strips(pieces, row_pairs):
        arrived = []
        for first, piece in enumerate(pieces):
            pairs = cross(row_pairs, matching(cols, first), cols, subs)
            arrived.append(lax.ppermute(piece, device_axes, pairs) if pairs else piece)
        return arrived

    far_strips = swap_strips((even, odd), far_pairs)
    far_rows = lax.ppermute(far, ("rows", "sub"), far_pairs)
    near_rows = lax.ppermute(near, ("rows", "sub"), near_pairs)
    strips = swap_strips((even, odd), stay) + swap_strips((even, odd), near_pairs)

    work = pltpu.VMEM(((height + 2 * HALO) * size, LANES), f32)
    work_scratch = pltpu.VMEM(((height + 2 * HALO) * size, LANES), f32)
    ground, surface, other, hops = pl.pallas_call(
        inner_kernel,
        out_shape=[work, work, work, pltpu.VMEM((9 * tile_count, LANES), f32)],
        in_specs=in_hbm(5) + in_vmem(5),
        out_specs=in_vmem(4),
        scratch_shapes=[
            pltpu.VMEM((height, width), f32),
            pltpu.VMEM((height, width), f32),
            pltpu.VMEM(edge_rows.shape, jnp.int32),
            pltpu.VMEM(edge_sides.shape, jnp.int32),
            pltpu.VMEM(adjacency.shape, jnp.int32),
            pltpu.SemaphoreType.DMA((2, 4 * groups)),
            pltpu.SemaphoreType.DMA((3,)),
        ],
        compiler_params=limit,
        cost_estimate=short,
        name="inner_passes",
    )(*arguments, near_rows, *strips)

    def outer(far_ref, *refs):
        outer_kernel(height, tiles, far_ref, *refs)

    devices = lax.axis_size(device_axes)
    ground, surface, other, floors = pl.pallas_call(
        outer,
        out_shape=[work, work, work, pltpu.VMEM((devices, LANES), f32)],
        in_specs=in_vmem(6),
        out_specs=in_vmem(4),
        input_output_aliases={3: 0, 4: 1, 5: 2},
        compiler_params=limit,
        cost_estimate=short,
        name="outer_passes",
    )(far_rows, *far_strips, ground, surface, other)

    floors = lax.all_to_all(floors, device_axes, 0, 0, tiled=True)

    def late(*refs):
        late_kernel(height, tiles, *refs)

    return pl.pallas_call(
        late,
        out_shape=jax.ShapeDtypeStruct((height, width), f32),
        in_specs=in_vmem(4),
        out_specs=pl.BlockSpec(memory_space=pltpu.HBM),
        scratch_shapes=[
            work_scratch,
            work_scratch,
            pltpu.VMEM((height, width), f32),
            pltpu.SemaphoreType.DMA((groups,)),
        ],
        compiler_params=limit,
        cost_estimate=short,
        name="final_passes",
    )(ground, surface, floors, hops)


def solution(mesh):
    placed = (
        P(("groups", "rows", "sub"), "cols"),
        P(("groups", "rows", "sub"), "cols"),
        P("groups", "cols"),
        P("groups", ("rows", "sub")),
        P("groups", None),
    )
    return jax.shard_map(
        per_device,
        mesh=mesh,
        in_specs=placed,
        out_specs=P(("groups", "rows", "sub"), "cols"),
        check_vma=False,
    )
```

```python
import jax
import jax.numpy as jnp
from jax import lax
from jax.experimental import pallas as pl
from jax.experimental.pallas import tpu as pltpu
from jax.sharding import PartitionSpec as P

PASSES = 8
FINAL = 4
ROUNDS = 4
HALO = PASSES + FINAL
SUBS = 8
LANES = 128
AHEAD = 5

unreached = 1000000000.0
rise_step = 0.01
hop_rise = 0.05
spill_lift = 3.0


def matching(count, first):
    pairs = []
    for low in range(first, count - 1, 2):
        pairs += [(low, low + 1), (low + 1, low)]
    return pairs


def closed(pairs, count):
    used = {source for source, _ in pairs}
    return pairs + [(place, place) for place in range(count) if place not in used]


def cross(row_pairs, col_pairs, cols, subs):
    def device(place, col):
        return (place // subs * cols + col) * subs + place % subs

    return [
        (device(row, col), device(row_to, col_to))
        for row, row_to in row_pairs
        for col, col_to in col_pairs
    ]


def chain_place():
    subs = lax.axis_size("sub")
    return lax.axis_index("rows") * subs + lax.axis_index("sub"), lax.axis_size("rows") * subs


def position():
    sub = lax.broadcasted_iota(jnp.int32, (SUBS, LANES), 0)
    lane = lax.broadcasted_iota(jnp.int32, (SUBS, LANES), 1)
    return sub, lane


def aligned(start):
    return start if isinstance(start, int) else pl.multiple_of(start, SUBS)


def rows_at(first, count, size):
    return pl.ds(aligned(first * size), count * size)


def register(row, slot, size):
    return pl.ds(aligned(row * size + slot * SUBS), SUBS)


def side_marks(sides_ref):
    height = sides_ref.shape[1]
    square = (height, height)
    diagonal = lax.broadcasted_iota(jnp.int32, square, 0) == lax.broadcasted_iota(jnp.int32, square, 1)
    marks = sides_ref[...].astype(jnp.float32)
    return [
        jnp.sum(jnp.where(diagonal, marks[side : side + 1, :], 0.0), axis=1, keepdims=True)
        for side in range(2)
    ]


def start_all(copies):
    for copy in copies:
        copy.start()
    return copies


def wait_all(copies):
    for copy in copies:
        copy.wait()


def edge_kernel(
    ground_hbm, depth_hbm, rows_hbm, sides_hbm,
    far_ref, near_ref, even_ref, odd_ref,
    ground_ref, depth_ref, marks_ref, sides_ref, sems, small_sems,
):
    height, width = ground_hbm.shape
    groups = height // SUBS
    last_tile = width // LANES - 1
    place, places = chain_place()
    col, cols = lax.axis_index("cols"), lax.axis_size("cols")
    small = [pltpu.make_async_copy(sides_hbm, sides_ref, small_sems.at[0])]
    for side, tile in enumerate((0, last_tile)):
        columns = pl.ds(tile * LANES, LANES)
        small.append(pltpu.make_async_copy(rows_hbm.at[:, columns], marks_ref.at[side], small_sems.at[1 + side]))
    copies = start_own(ground_hbm, depth_hbm, ground_ref, depth_ref, sems)
    start_all(small)
    sub, lane = position()
    wait_all(small)
    marks = side_marks(sides_ref)
    at_edges = [(lane == 0) & (col == 0), (lane == LANES - 1) & (col == cols - 1)]
    for copy in copies:
        wait_all(copy)

    def raised(group, tile):
        rows, columns = pl.ds(group * SUBS, SUBS), pl.ds(tile * LANES, LANES)
        ground = ground_ref[rows, columns]
        surface = ground + depth_ref[rows, columns]
        if tile in (0, last_tile):
            side = 0 if tile == 0 else 1
            chosen = marks[side][group * SUBS : (group + 1) * SUBS]
            surface = jnp.where((chosen > 0.5) & at_edges[side], ground, surface)
        return ground, surface

    def pack(up_ref, down_ref):
        tiles = width // (SUBS * LANES)
        size = tiles * SUBS
        skipped = height - HALO
        for tile in range(last_tile + 1):
            start = tile % tiles * SUBS + tile // tiles
            for out_ref, ground_slot, surface_slot, shift, keep in (
                (up_ref, 0, HALO - 1, 0, range(0, HALO)),
                (down_ref, HALO - 1, 0, skipped, range(skipped, height)),
            ):
                values = [raised(group, tile) for group in range(groups)]
                for kind, slot in enumerate((ground_slot, surface_slot)):
                    for group in range(groups):
                        inside = [row for row in range(group * SUBS, (group + 1) * SUBS) if row in keep]
                        first, count = inside[0], len(inside)
                        offset = first - group * SUBS
                        row = slot + first - shift
                        out_ref[pl.ds(row * size + start, count, stride=size), :] = values[group][kind][
                            offset : offset + count
                        ]

    top = place % 2 == 0
    pl.when(top)(lambda: pack(far_ref, near_ref))
    pl.when(jnp.logical_not(top))(lambda: pack(near_ref, far_ref))
    rightward = col % 2 == 0
    for group in range(groups):
        values = []
        for side, tile in enumerate((0, last_tile)):
            ground, surface = raised(group, tile)
            if group == 0:
                outlet = (marks_ref[side, 0:1] == 1) & (sub == 0) & (place == 0)
                surface = jnp.where(outlet, ground, surface)
            if group == groups - 1:
                outlet = (marks_ref[side, 1:2] == 1) & (sub == SUBS - 1) & (place == places - 1)
                surface = jnp.where(outlet, ground, surface)
            values.append((ground, surface))
        for kind in range(2):
            rows = pl.ds(kind * height + group * SUBS, SUBS)
            even_ref[rows, :] = jnp.where(rightward, values[1][kind], values[0][kind])
            odd_ref[rows, :] = jnp.where(rightward, values[0][kind], values[1][kind])


def start_own(ground_hbm, depth_hbm, ground_ref, depth_ref, sems):
    height, width = ground_hbm.shape
    groups = height // SUBS
    pieces = sems.shape[1] // groups
    part = width // pieces
    copies = []
    for group in range(groups):
        for piece in range(pieces):
            where = (pl.ds(group * SUBS, SUBS), pl.ds(piece * part, part))
            number = group * pieces + piece
            copies.append(
                start_all(
                    [
                        pltpu.make_async_copy(ground_hbm.at[where], ground_ref.at[where], sems.at[0, number]),
                        pltpu.make_async_copy(depth_hbm.at[where], depth_ref.at[where], sems.at[1, number]),
                    ]
                )
            )
    return copies


def fold_own(copies, ground_ref, depth_ref, rows_ref, sides_ref, ground_out, surface_out):
    height, width = ground_ref.shape
    groups = height // SUBS
    tiles = width // (SUBS * LANES)
    last_tile = width // LANES - 1
    pieces = len(copies) // groups
    part = width // pieces
    size = (tiles + 1) * SUBS
    place, places = chain_place()
    col, cols = lax.axis_index("cols"), lax.axis_size("cols")
    sub, lane = position()
    marks = side_marks(sides_ref)
    for group in range(groups):
        rows = pl.ds(group * SUBS, SUBS)
        for tile in range(last_tile + 1):
            if tile * LANES % part == 0:
                wait_all(copies[group * pieces + tile * LANES // part])
            columns = pl.ds(tile * LANES, LANES)
            ground = ground_ref[rows, columns]
            surface = ground + depth_ref[rows, columns]
            outlets = []
            if group == 0:
                outlets.append((rows_ref[0:1, columns] == 1) & (sub == 0) & (place == 0))
            if group == groups - 1:
                outlets.append(
                    (rows_ref[1:2, columns] == 1) & (sub == SUBS - 1) & (place == places - 1)
                )
            if tile == 0:
                outlets.append(
                    (marks[0][group * SUBS : (group + 1) * SUBS] > 0.5) & (lane == 0) & (col == 0)
                )
            if tile == last_tile:
                outlets.append(
                    (marks[1][group * SUBS : (group + 1) * SUBS] > 0.5)
                    & (lane == LANES - 1)
                    & (col == cols - 1)
                )
            for outlet in outlets:
                surface = jnp.where(outlet, ground, surface)
            chunk, slot = tile // tiles, tile % tiles
            start = (HALO + group * SUBS) * size + slot * SUBS + chunk
            ground_out[pl.ds(start, SUBS, stride=size), :] = ground
            surface_out[pl.ds(start, SUBS, stride=size), :] = surface


def unpack_rows(rows_ref, first, is_top, present, strip_refs, strip_rows, ground_ref, surface_ref, tiles):
    packed = tiles * SUBS
    size = packed + SUBS
    bases = (jnp.where(is_top, HALO - 1, 0), jnp.where(is_top, 0, HALO - 1))
    for base, out_ref, strip_row in zip(bases, (ground_ref, surface_ref), strip_rows):

        def body(row, carry):
            values = [
                jnp.where(present, rows_ref[register(base + row, slot, packed), :], unreached)
                for slot in range(tiles)
            ]
            for slot in range(tiles):
                out_ref[register(first + row, slot, size), :] = values[slot]
            fill_seam(out_ref, first + row, values[0], values[-1], strip_refs, strip_row + row, present, tiles)
            return carry

        lax.fori_loop(0, HALO, body, 0, unroll=4)


def fill_seam(out_ref, row, first_tile, last_tile, strip_refs, strip_row, present, tiles):
    col, cols = lax.axis_index("cols"), lax.axis_size("cols")
    sub, lane = position()
    rightward = col % 2 == 0
    even, odd = [ref[pl.ds(strip_row, 1), :] for ref in strip_refs]
    after = jnp.where(present & (col < cols - 1), jnp.where(rightward, even, odd), unreached)
    before = jnp.where(present & (col > 0), jnp.where(rightward, odd, even), unreached)
    after = jnp.where(sub == SUBS - 1, after, pltpu.roll(first_tile, SUBS - 1, 0))
    before = jnp.where(sub == 0, before, pltpu.roll(last_tile, 1, 0))
    out_ref[register(row, tiles, (tiles + 1) * SUBS), :] = jnp.where(lane < LANES // 2, after, before)


def relax_rows(source, target, ground, first, count, ring):
    size = ring * SUBS
    _, lane = position()
    at_first = lane == 0
    at_last = lane == LANES - 1
    order = [ring - 1] + list(range(ring - 1))
    made = {}

    def make(pair, slot):
        row = first + 2 * pair
        values = [source[register(row + step, slot, size), :] for step in range(-1, 3)]
        both = jnp.minimum(values[1], values[2])
        for one, column in enumerate((jnp.minimum(values[0], both), jnp.minimum(both, values[3]))):
            made[pair, one, slot] = (column, pltpu.roll(column, 1, 1), pltpu.roll(column, LANES - 1, 1))

    def finish(pair, slot):
        for one in range(2):
            row = first + 2 * pair + one
            before, here, after = [made[pair, one, (slot + step) % ring] for step in (-1, 0, 1)]
            from_left = jnp.where(at_first, before[1], here[1])
            from_right = jnp.where(at_last, after[2], here[2])
            lowest = jnp.minimum(jnp.minimum(from_left, from_right), here[0])
            where = register(row, slot, size)
            raised = jnp.minimum(source[where, :], lowest + rise_step)
            target[where, :] = jnp.maximum(ground[where, :], raised)

    makes = [(pair, slot) for pair in range(count // 2) for slot in order]
    finishes = [(pair, slot) for pair in range(count // 2) for slot in range(ring)]
    done = 0
    for number, item in enumerate(makes):
        make(*item)
        if number >= AHEAD:
            finish(*finishes[done])
            done += 1
    for item in finishes[done:]:
        finish(*item)


def hop_counts(links_ref, hops_ref, needed):
    tiles, degree = links_ref.shape
    links = links_ref[...]
    number = lax.broadcasted_iota(jnp.int32, (tiles, tiles), 1)
    linked = links[:, 0:1] == number
    for edge in range(1, degree):
        linked = linked | (links[:, edge : edge + 1] == number)
    linked = linked.astype(jnp.float32)
    tile = lax.broadcasted_iota(jnp.int32, (tiles, LANES), 0)
    lane = lax.broadcasted_iota(jnp.int32, (tiles, LANES), 1)
    reached = jnp.zeros((tiles, LANES), jnp.float32)
    for index, wanted in enumerate(needed):
        reached = jnp.where((lane == index) & (tile == wanted), 1.0, reached)
    hops = jnp.where(reached > 0.5, 0.0, float(ROUNDS + 1))
    for hop in range(1, ROUNDS + 1):
        reached = lax.dot_general(
            linked, reached, (((0,), (0,)), ((), ())), preferred_element_type=jnp.float32
        )
        reached = jnp.where(reached > 0.5, 1.0, 0.0)
        hops = jnp.minimum(hops, jnp.where(reached > 0.5, float(hop), float(ROUNDS + 1)))
    for index in range(len(needed)):
        hops_ref[pl.ds(index * tiles, tiles), :] = jnp.broadcast_to(
            hops[:, index : index + 1], (tiles, LANES)
        )


def needed_tiles():
    row, rows = lax.axis_index("rows"), lax.axis_size("rows")
    col, cols = lax.axis_index("cols"), lax.axis_size("cols")
    sub, subs = lax.axis_index("sub"), lax.axis_size("sub")
    above = jnp.maximum(jnp.where(sub == 0, row - 1, row), 0)
    below = jnp.minimum(jnp.where(sub == subs - 1, row + 1, row), rows - 1)
    left = jnp.maximum(col - 1, 0)
    right = jnp.minimum(col + 1, cols - 1)
    return [r * cols + c for r in (above, row, below) for c in (left, col, right)]


def inner_kernel(
    ground_hbm, depth_hbm, rows_hbm, sides_hbm, links_hbm,
    near_ref, own_even_ref, own_odd_ref, near_even_ref, near_odd_ref,
    ground_ref, surface_ref, other_ref, hops_ref,
    raw_ground_ref, raw_depth_ref, rows_ref, sides_ref, links_ref, sems, small_sems,
):
    height, width = ground_hbm.shape
    tiles = width // (SUBS * LANES)
    small = start_all(
        [
            pltpu.make_async_copy(source, target, small_sems.at[number])
            for number, (source, target) in enumerate(
                ((rows_hbm, rows_ref), (sides_hbm, sides_ref), (links_hbm, links_ref))
            )
        ]
    )
    copies = start_own(ground_hbm, depth_hbm, raw_ground_ref, raw_depth_ref, sems)
    own_strips, near_strips = (own_even_ref, own_odd_ref), (near_even_ref, near_odd_ref)
    ring = tiles + 1
    size = ring * SUBS
    place, places = chain_place()
    top = place % 2 == 0
    has_near = jnp.where(top, place < places - 1, place > 0)
    unpack_rows(
        near_ref,
        jnp.where(top, HALO + height, 0),
        jnp.logical_not(top),
        has_near,
        near_strips,
        [kind * height + jnp.where(top, 0, height - HALO) for kind in range(2)],
        ground_ref,
        surface_ref,
        tiles,
    )
    wait_all(small)
    hop_counts(links_ref, hops_ref, needed_tiles())
    fold_own(copies, raw_ground_ref, raw_depth_ref, rows_ref, sides_ref, ground_ref, surface_ref)
    for kind, out_ref in enumerate((ground_ref, surface_ref)):

        def body(row, carry):
            first_tile = out_ref[register(HALO + row, 0, size), :]
            last_tile = out_ref[register(HALO + row, tiles - 1, size), :]
            fill_seam(
                out_ref, HALO + row, first_tile, last_tile, own_strips, kind * height + row, place >= 0, tiles
            )
            return carry

        lax.fori_loop(0, height, body, 0, unroll=4)
    buffers = (surface_ref, other_ref)
    for step in range(1, PASSES + 1):
        first = step + jnp.where(top, HALO, 0)
        count = height + HALO - 2 * step
        relax_rows(buffers[(step + 1) % 2], buffers[step % 2], ground_ref, first, count, ring)


def outer_kernel(height, tiles, far_ref, even_ref, odd_ref, *refs):
    ground_ref, surface_ref, other_ref, level_ref = refs[3:7]
    ring = tiles + 1
    size = ring * SUBS
    place, places = chain_place()
    top = place % 2 == 0
    has_far = jnp.where(top, place > 0, place < places - 1)
    unpack_rows(
        far_ref,
        jnp.where(top, 0, HALO + height),
        top,
        has_far,
        (even_ref, odd_ref),
        [kind * height + jnp.where(top, height - HALO, 0) for kind in range(2)],
        ground_ref,
        surface_ref,
        tiles,
    )
    buffers = (surface_ref, other_ref)
    for step in range(1, PASSES + 1):
        first = jnp.where(top, step, HALO + height - step)
        relax_rows(buffers[(step + 1) % 2], buffers[step % 2], ground_ref, first, HALO, ring)
    band, bands = lax.axis_index("sub"), lax.axis_size("sub")
    sub, lane = position()

    def at(row, slot):
        return surface_ref[register(HALO + row, slot, size), :]

    first_cell = (sub == 0) & (lane == 0)
    last_cell = (sub == SUBS - 1) & (lane == LANES - 1)
    first_lows, last_lows, row_lows = [], [], []
    for row in range(height):
        first_lows.append(at(row, 0))
        last_lows.append(at(row, tiles - 1))
    for slot in range(tiles):
        row_lows.append(jnp.where(band == 0, at(0, slot), unreached))
        row_lows.append(jnp.where(band == bands - 1, at(height - 1, slot), unreached))
    lowest = jnp.minimum(
        least(row_lows),
        jnp.minimum(
            jnp.where(first_cell, least(first_lows), unreached),
            jnp.where(last_cell, least(last_lows), unreached),
        ),
    )
    lowest = jnp.min(jnp.min(lowest, axis=0, keepdims=True), axis=1, keepdims=True)
    level_ref[...] = jnp.broadcast_to(lowest, level_ref.shape)


def least(values):
    values = list(values)
    while len(values) > 1:
        values = [
            jnp.minimum(*values[number : number + 2]) if number + 1 < len(values) else values[number]
            for number in range(0, len(values), 2)
        ]
    return values[0]


def late_kernel(
    height, tiles, ground_ref, surface_ref, floors_ref, hops_ref, out_hbm,
    one_ref, two_ref, out_ref, sems,
):
    ring = tiles + 1
    size = ring * SUBS
    sub, lane = position()
    bands = lax.axis_size("sub")
    count = floors_ref.shape[0] // bands
    level = least(floors_ref[pl.ds(band, count, stride=bands), :] for band in range(bands))
    raised = [level]
    for hop in range(ROUNDS):
        raised.append(raised[-1] + hop_rise)
    ceilings = []
    for index in range(9):
        hops = hops_ref[pl.ds(index * count, count), :]
        lowest = jnp.full((count, LANES), unreached, jnp.float32)
        for hop in range(ROUNDS + 1):
            lowest = jnp.where(hops == float(hop), raised[hop], lowest)
        lowest = jnp.min(lowest, axis=0, keepdims=True) + spill_lift
        ceilings.append(jnp.broadcast_to(lowest, (SUBS, LANES)))
    pairs = []
    for region in range(3):
        left, middle, right = ceilings[3 * region : 3 * region + 3]
        seam = jnp.where(
            lane < LANES // 2,
            jnp.where(sub == SUBS - 1, right, middle),
            jnp.where(sub == 0, left, middle),
        )
        pairs.append((middle, seam))
    spans = ((HALO - FINAL, FINAL), (HALO, height), (HALO + height, FINAL))
    for (first, rows), (middle, seam) in zip(spans, pairs):

        def body(row, carry):
            for slot in range(ring):
                where = register(first + row, slot, size)
                value = jnp.minimum(surface_ref[where, :], seam if slot == tiles else middle)
                one_ref[where, :] = jnp.maximum(ground_ref[where, :], value)
            return carry

        lax.fori_loop(0, rows, body, 0, unroll=4)
    buffers = (one_ref, two_ref)
    for step in range(1, FINAL):
        first = HALO - FINAL + step
        relax_rows(
            buffers[(step + 1) % 2], buffers[step % 2], ground_ref, first, 2 * HALO + height - 2 * first, ring
        )
    source, target = buffers[(FINAL + 1) % 2], buffers[FINAL % 2]
    copies = []
    for group in range(height // SUBS):
        first = HALO + group * SUBS
        relax_rows(source, target, ground_ref, first, SUBS, ring)
        for tile in range(tiles * SUBS):
            chunk, slot = tile // tiles, tile % tiles
            out_ref[pl.ds(group * SUBS, SUBS), pl.ds(tile * LANES, LANES)] = target[
                pl.ds(first * size + slot * SUBS + chunk, SUBS, stride=size), :
            ]
        where = (pl.ds(group * SUBS, SUBS), slice(None))
        copies += start_all([pltpu.make_async_copy(out_ref.at[where], out_hbm.at[where], sems.at[group])])
    wait_all(copies)


def in_vmem(count):
    return [pl.BlockSpec(memory_space=pltpu.VMEM)] * count


def in_hbm(count):
    return [pl.BlockSpec(memory_space=pltpu.HBM)] * count


def per_device(elevation, fill_depth, edge_rows, edge_sides, adjacency):
    height, width = elevation.shape
    tiles = width // (SUBS * LANES)
    groups = height // SUBS
    f32 = jnp.float32
    packed = tiles * SUBS
    size = packed + SUBS
    tile_count = adjacency.shape[0]
    places = lax.axis_size(("rows", "sub"))
    cols, subs = lax.axis_size("cols"), lax.axis_size("sub")
    short = pl.CostEstimate(flops=1024, bytes_accessed=1024, transcendentals=0)
    limit = pltpu.CompilerParams(vmem_limit_bytes=24 << 20)
    arguments = [
        pltpu.with_memory_space_constraint(value, pltpu.HBM)
        for value in (elevation, fill_depth, edge_rows, edge_sides, adjacency)
    ]
    sent = pltpu.VMEM(((2 * HALO - 1) * packed, LANES), f32)
    strip = pltpu.VMEM((2 * height, LANES), f32)
    far, near, even, odd = pl.pallas_call(
        edge_kernel,
        out_shape=[sent, sent, strip, strip],
        in_specs=in_hbm(4),
        out_specs=in_vmem(4),
        scratch_shapes=[
            pltpu.VMEM((height, width), f32),
            pltpu.VMEM((height, width), f32),
            pltpu.VMEM((2, 2, LANES), jnp.int32),
            pltpu.VMEM(edge_sides.shape, jnp.int32),
            pltpu.SemaphoreType.DMA((2, 4 * groups)),
            pltpu.SemaphoreType.DMA((3,)),
        ],
        compiler_params=limit,
        cost_estimate=short,
        name="edge_rows",
    )(*arguments[:4])

    near_pairs, far_pairs = [matching(places, first) for first in range(2)]
    col_pairs = closed(matching(cols, 0), cols)
    ends = [(place, place) for place in range(places) if place not in dict(far_pairs)]
    same_col = [(col, col) for col in range(cols)]
    far_all = cross(far_pairs, same_col, cols, subs) + cross(ends, col_pairs, cols, subs)
    stay = [(place, place) for place in range(places)]
    device_axes = ("rows", "cols", "sub")

    def swap_strips(pieces, row_pairs):
        arrived = []
        for first, piece in enumerate(pieces):
            pairs = cross(row_pairs, matching(cols, first), cols, subs)
            arrived.append(lax.ppermute(piece, device_axes, pairs) if pairs else piece)
        return arrived

    far_strips = swap_strips((even, odd), far_pairs + ends)
    far_rows = lax.ppermute(far, device_axes, far_all)
    near_rows = lax.ppermute(near, ("rows", "sub"), near_pairs)
    strips = swap_strips((even, odd), stay) + swap_strips((even, odd), near_pairs)

    work = pltpu.VMEM(((height + 2 * HALO) * size, LANES), f32)
    work_scratch = pltpu.VMEM(((height + 2 * HALO) * size, LANES), f32)
    ground, surface, other, hops = pl.pallas_call(
        inner_kernel,
        out_shape=[work, work, work, pltpu.VMEM((9 * tile_count, LANES), f32)],
        in_specs=in_hbm(5) + in_vmem(5),
        out_specs=in_vmem(4),
        scratch_shapes=[
            pltpu.VMEM((height, width), f32),
            pltpu.VMEM((height, width), f32),
            pltpu.VMEM(edge_rows.shape, jnp.int32),
            pltpu.VMEM(edge_sides.shape, jnp.int32),
            pltpu.VMEM(adjacency.shape, jnp.int32),
            pltpu.SemaphoreType.DMA((2, 4 * groups)),
            pltpu.SemaphoreType.DMA((3,)),
        ],
        compiler_params=limit,
        cost_estimate=short,
        name="inner_passes",
    )(*arguments, near_rows, *strips)

    def outer(far_ref, *refs):
        outer_kernel(height, tiles, far_ref, *refs)

    devices = lax.axis_size(device_axes)
    ground, surface, other, floors = pl.pallas_call(
        outer,
        out_shape=[work, work, work, pltpu.VMEM((devices, LANES), f32)],
        in_specs=in_vmem(6),
        out_specs=in_vmem(4),
        input_output_aliases={3: 0, 4: 1, 5: 2},
        compiler_params=limit,
        cost_estimate=short,
        name="outer_passes",
    )(far_rows, *far_strips, ground, surface, other)

    floors = lax.all_to_all(floors, device_axes, 0, 0, tiled=True)

    def late(*refs):
        late_kernel(height, tiles, *refs)

    return pl.pallas_call(
        late,
        out_shape=jax.ShapeDtypeStruct((height, width), f32),
        in_specs=in_vmem(4),
        out_specs=pl.BlockSpec(memory_space=pltpu.HBM),
        scratch_shapes=[
            work_scratch,
            work_scratch,
            pltpu.VMEM((height, width), f32),
            pltpu.SemaphoreType.DMA((groups,)),
        ],
        compiler_params=limit,
        cost_estimate=short,
        name="final_passes",
    )(ground, surface, floors, hops)


def solution(mesh):
    placed = (
        P(("groups", "rows", "sub"), "cols"),
        P(("groups", "rows", "sub"), "cols"),
        P("groups", "cols"),
        P("groups", ("rows", "sub")),
        P("groups", None),
    )
    return jax.shard_map(
        per_device,
        mesh=mesh,
        in_specs=placed,
        out_specs=P(("groups", "rows", "sub"), "cols"),
        check_vma=False,
    )
```

```python
import jax
import jax.numpy as jnp
from jax import lax
from jax.experimental import pallas as pl
from jax.experimental.pallas import tpu as pltpu
from jax.sharding import PartitionSpec as P

PASSES = 8
FINAL = 4
ROUNDS = 4
HALO = PASSES + FINAL
SUBS = 8
LANES = 128
AHEAD = 5

unreached = 1000000000.0
rise_step = 0.01
hop_rise = 0.05
spill_lift = 3.0


def matching(count, first):
    pairs = []
    for low in range(first, count - 1, 2):
        pairs += [(low, low + 1), (low + 1, low)]
    return pairs


def closed(pairs, count):
    used = {source for source, _ in pairs}
    return pairs + [(place, place) for place in range(count) if place not in used]


def cross(row_pairs, col_pairs, cols, subs):
    def device(place, col):
        return (place // subs * cols + col) * subs + place % subs

    return [
        (device(row, col), device(row_to, col_to))
        for row, row_to in row_pairs
        for col, col_to in col_pairs
    ]


def chain_place():
    subs = lax.axis_size("sub")
    return lax.axis_index("rows") * subs + lax.axis_index("sub"), lax.axis_size("rows") * subs


def position():
    sub = lax.broadcasted_iota(jnp.int32, (SUBS, LANES), 0)
    lane = lax.broadcasted_iota(jnp.int32, (SUBS, LANES), 1)
    return sub, lane


def aligned(start):
    return start if isinstance(start, int) else pl.multiple_of(start, SUBS)


def rows_at(first, count, size):
    return pl.ds(aligned(first * size), count * size)


def register(row, slot, size):
    return pl.ds(aligned(row * size + slot * SUBS), SUBS)


def side_marks(sides_ref):
    height = sides_ref.shape[1]
    square = (height, height)
    diagonal = lax.broadcasted_iota(jnp.int32, square, 0) == lax.broadcasted_iota(jnp.int32, square, 1)
    marks = sides_ref[...].astype(jnp.float32)
    return [
        jnp.sum(jnp.where(diagonal, marks[side : side + 1, :], 0.0), axis=1, keepdims=True)
        for side in range(2)
    ]


def start_all(copies):
    for copy in copies:
        copy.start()
    return copies


def wait_all(copies):
    for copy in copies:
        copy.wait()


def edge_kernel(
    ground_hbm, depth_hbm, rows_hbm, sides_hbm,
    far_ref, near_ref, even_ref, odd_ref,
    ground_ref, depth_ref, marks_ref, sides_ref, sems, small_sems,
):
    height, width = ground_hbm.shape
    groups = height // SUBS
    last_tile = width // LANES - 1
    place, places = chain_place()
    col, cols = lax.axis_index("cols"), lax.axis_size("cols")
    small = [pltpu.make_async_copy(sides_hbm, sides_ref, small_sems.at[0])]
    for side, tile in enumerate((0, last_tile)):
        columns = pl.ds(tile * LANES, LANES)
        small.append(pltpu.make_async_copy(rows_hbm.at[:, columns], marks_ref.at[side], small_sems.at[1 + side]))
    copies = start_own(ground_hbm, depth_hbm, ground_ref, depth_ref, sems)
    start_all(small)
    sub, lane = position()
    wait_all(small)
    marks = side_marks(sides_ref)
    at_edges = [(lane == 0) & (col == 0), (lane == LANES - 1) & (col == cols - 1)]
    for copy in copies:
        wait_all(copy)

    def raised(group, tile):
        rows, columns = pl.ds(group * SUBS, SUBS), pl.ds(tile * LANES, LANES)
        ground = ground_ref[rows, columns]
        surface = ground + depth_ref[rows, columns]
        if tile in (0, last_tile):
            side = 0 if tile == 0 else 1
            chosen = marks[side][group * SUBS : (group + 1) * SUBS]
            surface = jnp.where((chosen > 0.5) & at_edges[side], ground, surface)
        return ground, surface

    def pack(up_ref, down_ref):
        tiles = width // (SUBS * LANES)
        size = tiles * SUBS
        skipped = height - HALO
        for tile in range(last_tile + 1):
            start = tile % tiles * SUBS + tile // tiles
            for out_ref, ground_slot, surface_slot, shift, keep in (
                (up_ref, 0, HALO - 1, 0, range(0, HALO)),
                (down_ref, HALO - 1, 0, skipped, range(skipped, height)),
            ):
                values = [raised(group, tile) for group in range(groups)]
                for kind, slot in enumerate((ground_slot, surface_slot)):
                    for group in range(groups):
                        inside = [row for row in range(group * SUBS, (group + 1) * SUBS) if row in keep]
                        first, count = inside[0], len(inside)
                        offset = first - group * SUBS
                        row = slot + first - shift
                        out_ref[pl.ds(row * size + start, count, stride=size), :] = values[group][kind][
                            offset : offset + count
                        ]

    top = place % 2 == 0
    pl.when(top)(lambda: pack(far_ref, near_ref))
    pl.when(jnp.logical_not(top))(lambda: pack(near_ref, far_ref))
    rightward = col % 2 == 0
    for group in range(groups):
        values = []
        for side, tile in enumerate((0, last_tile)):
            ground, surface = raised(group, tile)
            if group == 0:
                outlet = (marks_ref[side, 0:1] == 1) & (sub == 0) & (place == 0)
                surface = jnp.where(outlet, ground, surface)
            if group == groups - 1:
                outlet = (marks_ref[side, 1:2] == 1) & (sub == SUBS - 1) & (place == places - 1)
                surface = jnp.where(outlet, ground, surface)
            values.append((ground, surface))
        for kind in range(2):
            rows = pl.ds(kind * height + group * SUBS, SUBS)
            even_ref[rows, :] = jnp.where(rightward, values[1][kind], values[0][kind])
            odd_ref[rows, :] = jnp.where(rightward, values[0][kind], values[1][kind])


def start_own(ground_hbm, depth_hbm, ground_ref, depth_ref, sems):
    height, width = ground_hbm.shape
    groups = height // SUBS
    pieces = sems.shape[1] // groups
    part = width // pieces
    copies = []
    for group in range(groups):
        for piece in range(pieces):
            where = (pl.ds(group * SUBS, SUBS), pl.ds(piece * part, part))
            number = group * pieces + piece
            copies.append(
                start_all(
                    [
                        pltpu.make_async_copy(ground_hbm.at[where], ground_ref.at[where], sems.at[0, number]),
                        pltpu.make_async_copy(depth_hbm.at[where], depth_ref.at[where], sems.at[1, number]),
                    ]
                )
            )
    return copies


def fold_own(copies, ground_ref, depth_ref, rows_ref, sides_ref, ground_out, surface_out):
    height, width = ground_ref.shape
    groups = height // SUBS
    tiles = width // (SUBS * LANES)
    last_tile = width // LANES - 1
    pieces = len(copies) // groups
    part = width // pieces
    size = (tiles + 1) * SUBS
    place, places = chain_place()
    col, cols = lax.axis_index("cols"), lax.axis_size("cols")
    sub, lane = position()
    marks = side_marks(sides_ref)
    for group in range(groups):
        rows = pl.ds(group * SUBS, SUBS)
        for tile in range(last_tile + 1):
            if tile * LANES % part == 0:
                wait_all(copies[group * pieces + tile * LANES // part])
            columns = pl.ds(tile * LANES, LANES)
            ground = ground_ref[rows, columns]
            surface = ground + depth_ref[rows, columns]
            outlets = []
            if group == 0:
                outlets.append((rows_ref[0:1, columns] == 1) & (sub == 0) & (place == 0))
            if group == groups - 1:
                outlets.append(
                    (rows_ref[1:2, columns] == 1) & (sub == SUBS - 1) & (place == places - 1)
                )
            if tile == 0:
                outlets.append(
                    (marks[0][group * SUBS : (group + 1) * SUBS] > 0.5) & (lane == 0) & (col == 0)
                )
            if tile == last_tile:
                outlets.append(
                    (marks[1][group * SUBS : (group + 1) * SUBS] > 0.5)
                    & (lane == LANES - 1)
                    & (col == cols - 1)
                )
            for outlet in outlets:
                surface = jnp.where(outlet, ground, surface)
            chunk, slot = tile // tiles, tile % tiles
            start = (HALO + group * SUBS) * size + slot * SUBS + chunk
            ground_out[pl.ds(start, SUBS, stride=size), :] = ground
            surface_out[pl.ds(start, SUBS, stride=size), :] = surface


def unpack_rows(rows_ref, first, is_top, present, strip_refs, strip_rows, ground_ref, surface_ref, tiles):
    packed = tiles * SUBS
    size = packed + SUBS
    bases = (jnp.where(is_top, HALO - 1, 0), jnp.where(is_top, 0, HALO - 1))
    for base, out_ref, strip_row in zip(bases, (ground_ref, surface_ref), strip_rows):

        def body(row, carry):
            values = [
                jnp.where(present, rows_ref[register(base + row, slot, packed), :], unreached)
                for slot in range(tiles)
            ]
            for slot in range(tiles):
                out_ref[register(first + row, slot, size), :] = values[slot]
            fill_seam(out_ref, first + row, values[0], values[-1], strip_refs, strip_row + row, present, tiles)
            return carry

        lax.fori_loop(0, HALO, body, 0, unroll=4)


def fill_seam(out_ref, row, first_tile, last_tile, strip_refs, strip_row, present, tiles):
    col, cols = lax.axis_index("cols"), lax.axis_size("cols")
    sub, lane = position()
    rightward = col % 2 == 0
    even, odd = [ref[pl.ds(strip_row, 1), :] for ref in strip_refs]
    after = jnp.where(present & (col < cols - 1), jnp.where(rightward, even, odd), unreached)
    before = jnp.where(present & (col > 0), jnp.where(rightward, odd, even), unreached)
    after = jnp.where(sub == SUBS - 1, after, pltpu.roll(first_tile, SUBS - 1, 0))
    before = jnp.where(sub == 0, before, pltpu.roll(last_tile, 1, 0))
    out_ref[register(row, tiles, (tiles + 1) * SUBS), :] = jnp.where(lane < LANES // 2, after, before)


def relax_rows(source, target, ground, first, count, ring):
    size = ring * SUBS
    _, lane = position()
    at_first = lane == 0
    at_last = lane == LANES - 1
    order = [ring - 1] + list(range(ring - 1))
    made = {}

    def make(pair, slot):
        row = first + 2 * pair
        values = [source[register(row + step, slot, size), :] for step in range(-1, 3)]
        both = jnp.minimum(values[1], values[2])
        for one, column in enumerate((jnp.minimum(values[0], both), jnp.minimum(both, values[3]))):
            made[pair, one, slot] = (column, pltpu.roll(column, 1, 1), pltpu.roll(column, LANES - 1, 1))

    def finish(pair, slot):
        for one in range(2):
            row = first + 2 * pair + one
            before, here, after = [made[pair, one, (slot + step) % ring] for step in (-1, 0, 1)]
            from_left = jnp.where(at_first, before[1], here[1])
            from_right = jnp.where(at_last, after[2], here[2])
            lowest = jnp.minimum(jnp.minimum(from_left, from_right), here[0])
            where = register(row, slot, size)
            raised = jnp.minimum(source[where, :], lowest + rise_step)
            target[where, :] = jnp.maximum(ground[where, :], raised)

    makes = [(pair, slot) for pair in range(count // 2) for slot in order]
    finishes = [(pair, slot) for pair in range(count // 2) for slot in range(ring)]
    done = 0
    for number, item in enumerate(makes):
        make(*item)
        if number >= AHEAD:
            finish(*finishes[done])
            done += 1
    for item in finishes[done:]:
        finish(*item)


def hop_counts(links_ref, hops_ref, needed):
    tiles, degree = links_ref.shape
    links = links_ref[...]
    number = lax.broadcasted_iota(jnp.int32, (tiles, tiles), 1)
    linked = links[:, 0:1] == number
    for edge in range(1, degree):
        linked = linked | (links[:, edge : edge + 1] == number)
    linked = linked.astype(jnp.float32)
    tile = lax.broadcasted_iota(jnp.int32, (tiles, LANES), 0)
    lane = lax.broadcasted_iota(jnp.int32, (tiles, LANES), 1)
    reached = jnp.zeros((tiles, LANES), jnp.float32)
    for index, wanted in enumerate(needed):
        reached = jnp.where((lane == index) & (tile == wanted), 1.0, reached)
    hops = jnp.where(reached > 0.5, 0.0, float(ROUNDS + 1))
    for hop in range(1, ROUNDS + 1):
        reached = lax.dot_general(
            linked, reached, (((0,), (0,)), ((), ())), preferred_element_type=jnp.float32
        )
        reached = jnp.where(reached > 0.5, 1.0, 0.0)
        hops = jnp.minimum(hops, jnp.where(reached > 0.5, float(hop), float(ROUNDS + 1)))
    for index in range(len(needed)):
        hops_ref[pl.ds(index * tiles, tiles), :] = jnp.broadcast_to(
            hops[:, index : index + 1], (tiles, LANES)
        )


def needed_tiles():
    row, rows = lax.axis_index("rows"), lax.axis_size("rows")
    col, cols = lax.axis_index("cols"), lax.axis_size("cols")
    sub, subs = lax.axis_index("sub"), lax.axis_size("sub")
    above = jnp.maximum(jnp.where(sub == 0, row - 1, row), 0)
    below = jnp.minimum(jnp.where(sub == subs - 1, row + 1, row), rows - 1)
    left = jnp.maximum(col - 1, 0)
    right = jnp.minimum(col + 1, cols - 1)
    return [r * cols + c for r in (above, row, below) for c in (left, col, right)]


def inner_kernel(
    ground_hbm, depth_hbm, rows_hbm, sides_hbm, links_hbm,
    near_ref, own_even_ref, own_odd_ref, near_even_ref, near_odd_ref,
    ground_ref, surface_ref, other_ref, hops_ref,
    raw_ground_ref, raw_depth_ref, rows_ref, sides_ref, links_ref, sems, small_sems,
):
    height, width = ground_hbm.shape
    tiles = width // (SUBS * LANES)
    small = start_all(
        [
            pltpu.make_async_copy(source, target, small_sems.at[number])
            for number, (source, target) in enumerate(
                ((rows_hbm, rows_ref), (sides_hbm, sides_ref), (links_hbm, links_ref))
            )
        ]
    )
    copies = start_own(ground_hbm, depth_hbm, raw_ground_ref, raw_depth_ref, sems)
    own_strips, near_strips = (own_even_ref, own_odd_ref), (near_even_ref, near_odd_ref)
    ring = tiles + 1
    size = ring * SUBS
    place, places = chain_place()
    top = place % 2 == 0
    has_near = jnp.where(top, place < places - 1, place > 0)
    unpack_rows(
        near_ref,
        jnp.where(top, HALO + height, 0),
        jnp.logical_not(top),
        has_near,
        near_strips,
        [kind * height + jnp.where(top, 0, height - HALO) for kind in range(2)],
        ground_ref,
        surface_ref,
        tiles,
    )
    wait_all(small)
    hop_counts(links_ref, hops_ref, needed_tiles())
    fold_own(copies, raw_ground_ref, raw_depth_ref, rows_ref, sides_ref, ground_ref, surface_ref)
    for kind, out_ref in enumerate((ground_ref, surface_ref)):

        def body(row, carry):
            first_tile = out_ref[register(HALO + row, 0, size), :]
            last_tile = out_ref[register(HALO + row, tiles - 1, size), :]
            fill_seam(
                out_ref, HALO + row, first_tile, last_tile, own_strips, kind * height + row, place >= 0, tiles
            )
            return carry

        lax.fori_loop(0, height, body, 0, unroll=4)
    buffers = (surface_ref, other_ref)
    for step in range(1, PASSES + 1):
        first = step + jnp.where(top, HALO, 0)
        count = height + HALO - 2 * step
        relax_rows(buffers[(step + 1) % 2], buffers[step % 2], ground_ref, first, count, ring)


def outer_kernel(height, tiles, far_ref, even_ref, odd_ref, *refs):
    ground_ref, surface_ref, other_ref, level_ref = refs[3:7]
    ring = tiles + 1
    size = ring * SUBS
    place, places = chain_place()
    top = place % 2 == 0
    has_far = jnp.where(top, place > 0, place < places - 1)
    unpack_rows(
        far_ref,
        jnp.where(top, 0, HALO + height),
        top,
        has_far,
        (even_ref, odd_ref),
        [kind * height + jnp.where(top, height - HALO, 0) for kind in range(2)],
        ground_ref,
        surface_ref,
        tiles,
    )
    buffers = (surface_ref, other_ref)
    for step in range(1, PASSES + 1):
        first = jnp.where(top, step, HALO + height - step)
        relax_rows(buffers[(step + 1) % 2], buffers[step % 2], ground_ref, first, HALO, ring)
    band, bands = lax.axis_index("sub"), lax.axis_size("sub")
    sub, lane = position()

    def at(row, slot):
        return surface_ref[register(HALO + row, slot, size), :]

    first_cell = (sub == 0) & (lane == 0)
    last_cell = (sub == SUBS - 1) & (lane == LANES - 1)
    first_lows, last_lows, row_lows = [], [], []
    for row in range(height):
        first_lows.append(at(row, 0))
        last_lows.append(at(row, tiles - 1))
    for slot in range(tiles):
        row_lows.append(jnp.where(band == 0, at(0, slot), unreached))
        row_lows.append(jnp.where(band == bands - 1, at(height - 1, slot), unreached))
    lowest = jnp.minimum(
        least(row_lows),
        jnp.minimum(
            jnp.where(first_cell, least(first_lows), unreached),
            jnp.where(last_cell, least(last_lows), unreached),
        ),
    )
    lowest = jnp.min(jnp.min(lowest, axis=0, keepdims=True), axis=1, keepdims=True)
    level_ref[...] = jnp.broadcast_to(lowest, level_ref.shape)


def least(values):
    values = list(values)
    while len(values) > 1:
        values = [
            jnp.minimum(*values[number : number + 2]) if number + 1 < len(values) else values[number]
            for number in range(0, len(values), 2)
        ]
    return values[0]


def late_kernel(
    height, tiles, ground_ref, surface_ref, floors_ref, hops_ref, out_hbm,
    one_ref, two_ref, out_ref, sems,
):
    ring = tiles + 1
    size = ring * SUBS
    sub, lane = position()
    bands = lax.axis_size("sub")
    count = floors_ref.shape[0] // bands
    level = least(floors_ref[pl.ds(band, count, stride=bands), :] for band in range(bands))
    raised = [level]
    for hop in range(ROUNDS):
        raised.append(raised[-1] + hop_rise)
    ceilings = []
    for index in range(9):
        hops = hops_ref[pl.ds(index * count, count), :]
        lowest = jnp.full((count, LANES), unreached, jnp.float32)
        for hop in range(ROUNDS + 1):
            lowest = jnp.where(hops == float(hop), raised[hop], lowest)
        lowest = jnp.min(lowest, axis=0, keepdims=True) + spill_lift
        ceilings.append(jnp.broadcast_to(lowest, (SUBS, LANES)))
    pairs = []
    for region in range(3):
        left, middle, right = ceilings[3 * region : 3 * region + 3]
        seam = jnp.where(
            lane < LANES // 2,
            jnp.where(sub == SUBS - 1, right, middle),
            jnp.where(sub == 0, left, middle),
        )
        pairs.append((middle, seam))
    spans = ((HALO - FINAL, FINAL), (HALO, height), (HALO + height, FINAL))
    for (first, rows), (middle, seam) in zip(spans, pairs):

        def body(row, carry):
            for slot in range(ring):
                where = register(first + row, slot, size)
                value = jnp.minimum(surface_ref[where, :], seam if slot == tiles else middle)
                one_ref[where, :] = jnp.maximum(ground_ref[where, :], value)
            return carry

        lax.fori_loop(0, rows, body, 0, unroll=4)
    buffers = (one_ref, two_ref)
    for step in range(1, FINAL):
        first = HALO - FINAL + step
        relax_rows(
            buffers[(step + 1) % 2], buffers[step % 2], ground_ref, first, 2 * HALO + height - 2 * first, ring
        )
    source, target = buffers[(FINAL + 1) % 2], buffers[FINAL % 2]
    copies = []
    for group in range(height // SUBS):
        first = HALO + group * SUBS
        relax_rows(source, target, ground_ref, first, SUBS, ring)
        for tile in range(tiles * SUBS):
            chunk, slot = tile // tiles, tile % tiles
            out_ref[pl.ds(group * SUBS, SUBS), pl.ds(tile * LANES, LANES)] = target[
                pl.ds(first * size + slot * SUBS + chunk, SUBS, stride=size), :
            ]
        where = (pl.ds(group * SUBS, SUBS), slice(None))
        copies += start_all([pltpu.make_async_copy(out_ref.at[where], out_hbm.at[where], sems.at[group])])
    wait_all(copies)


def in_vmem(count):
    return [pl.BlockSpec(memory_space=pltpu.VMEM)] * count


def in_hbm(count):
    return [pl.BlockSpec(memory_space=pltpu.HBM)] * count


def per_device(elevation, fill_depth, edge_rows, edge_sides, adjacency):
    height, width = elevation.shape
    tiles = width // (SUBS * LANES)
    groups = height // SUBS
    f32 = jnp.float32
    packed = tiles * SUBS
    size = packed + SUBS
    tile_count = adjacency.shape[0]
    places = lax.axis_size(("rows", "sub"))
    cols, subs = lax.axis_size("cols"), lax.axis_size("sub")
    short = pl.CostEstimate(flops=1024, bytes_accessed=1024, transcendentals=0)
    limit = pltpu.CompilerParams(vmem_limit_bytes=24 << 20)
    arguments = [
        pltpu.with_memory_space_constraint(value, pltpu.HBM)
        for value in (elevation, fill_depth, edge_rows, edge_sides, adjacency)
    ]
    sent = pltpu.VMEM(((2 * HALO - 1) * packed, LANES), f32)
    strip = pltpu.VMEM((2 * height, LANES), f32)
    far, near, even, odd = pl.pallas_call(
        edge_kernel,
        out_shape=[sent, sent, strip, strip],
        in_specs=in_hbm(4),
        out_specs=in_vmem(4),
        scratch_shapes=[
            pltpu.VMEM((height, width), f32),
            pltpu.VMEM((height, width), f32),
            pltpu.VMEM((2, 2, LANES), jnp.int32),
            pltpu.VMEM(edge_sides.shape, jnp.int32),
            pltpu.SemaphoreType.DMA((2, 4 * groups)),
            pltpu.SemaphoreType.DMA((3,)),
        ],
        compiler_params=limit,
        cost_estimate=short,
        name="edge_rows",
    )(*arguments[:4])

    near_pairs, far_pairs = [matching(places, first) for first in range(2)]
    stay = [(place, place) for place in range(places)]
    ends = [(place, place) for place in range(places) if place not in dict(far_pairs)]
    groups_count = lax.axis_size("groups")
    part = places * cols
    far_all = []
    for group, other in closed(matching(groups_count, 0), groups_count):
        for chosen, target in ((far_pairs, group), (ends, other)):
            for source, arrival in cross(chosen, [(col, col) for col in range(cols)], cols, subs):
                far_all.append((group * part + source, target * part + arrival))
    device_axes = ("rows", "cols", "sub")

    def swap_strips(pieces, row_pairs):
        arrived = []
        for first, piece in enumerate(pieces):
            pairs = cross(row_pairs, matching(cols, first), cols, subs)
            arrived.append(lax.ppermute(piece, device_axes, pairs) if pairs else piece)
        return arrived

    far_strips = swap_strips((even, odd), far_pairs + ends)
    far_rows = lax.ppermute(far, ("groups",) + device_axes, far_all)
    near_rows = lax.ppermute(near, ("rows", "sub"), near_pairs)
    strips = swap_strips((even, odd), stay) + swap_strips((even, odd), near_pairs)

    work = pltpu.VMEM(((height + 2 * HALO) * size, LANES), f32)
    work_scratch = pltpu.VMEM(((height + 2 * HALO) * size, LANES), f32)
    ground, surface, other, hops = pl.pallas_call(
        inner_kernel,
        out_shape=[work, work, work, pltpu.VMEM((9 * tile_count, LANES), f32)],
        in_specs=in_hbm(5) + in_vmem(5),
        out_specs=in_vmem(4),
        scratch_shapes=[
            pltpu.VMEM((height, width), f32),
            pltpu.VMEM((height, width), f32),
            pltpu.VMEM(edge_rows.shape, jnp.int32),
            pltpu.VMEM(edge_sides.shape, jnp.int32),
            pltpu.VMEM(adjacency.shape, jnp.int32),
            pltpu.SemaphoreType.DMA((2, 4 * groups)),
            pltpu.SemaphoreType.DMA((3,)),
        ],
        compiler_params=limit,
        cost_estimate=short,
        name="inner_passes",
    )(*arguments, near_rows, *strips)

    def outer(far_ref, *refs):
        outer_kernel(height, tiles, far_ref, *refs)

    devices = lax.axis_size(device_axes)
    ground, surface, other, floors = pl.pallas_call(
        outer,
        out_shape=[work, work, work, pltpu.VMEM((devices, LANES), f32)],
        in_specs=in_vmem(6),
        out_specs=in_vmem(4),
        input_output_aliases={3: 0, 4: 1, 5: 2},
        compiler_params=limit,
        cost_estimate=short,
        name="outer_passes",
    )(far_rows, *far_strips, ground, surface, other)

    floors = lax.all_to_all(floors, device_axes, 0, 0, tiled=True)

    def late(*refs):
        late_kernel(height, tiles, *refs)

    return pl.pallas_call(
        late,
        out_shape=jax.ShapeDtypeStruct((height, width), f32),
        in_specs=in_vmem(4),
        out_specs=pl.BlockSpec(memory_space=pltpu.HBM),
        scratch_shapes=[
            work_scratch,
            work_scratch,
            pltpu.VMEM((height, width), f32),
            pltpu.SemaphoreType.DMA((groups,)),
        ],
        compiler_params=limit,
        cost_estimate=short,
        name="final_passes",
    )(ground, surface, floors, hops)


def solution(mesh):
    placed = (
        P(("groups", "rows", "sub"), "cols"),
        P(("groups", "rows", "sub"), "cols"),
        P("groups", "cols"),
        P("groups", ("rows", "sub")),
        P("groups", None),
    )
    return jax.shard_map(
        per_device,
        mesh=mesh,
        in_specs=placed,
        out_specs=P(("groups", "rows", "sub"), "cols"),
        check_vma=False,
    )
```

```python
import jax
import jax.numpy as jnp
from jax import lax
from jax.experimental import pallas as pl
from jax.experimental.pallas import tpu as pltpu
from jax.sharding import PartitionSpec as P

PASSES = 8
FINAL = 4
ROUNDS = 4
HALO = PASSES + FINAL
SUBS = 8
LANES = 128
AHEAD = 5

unreached = 1000000000.0
rise_step = 0.01
hop_rise = 0.05
spill_lift = 3.0


def matching(count, first):
    pairs = []
    for low in range(first, count - 1, 2):
        pairs += [(low, low + 1), (low + 1, low)]
    return pairs


def closed(pairs, count):
    used = {source for source, _ in pairs}
    return pairs + [(place, place) for place in range(count) if place not in used]


def cross(row_pairs, col_pairs, cols, subs):
    def device(place, col):
        return (place // subs * cols + col) * subs + place % subs

    return [
        (device(row, col), device(row_to, col_to))
        for row, row_to in row_pairs
        for col, col_to in col_pairs
    ]


def chain_place():
    subs = lax.axis_size("sub")
    return lax.axis_index("rows") * subs + lax.axis_index("sub"), lax.axis_size("rows") * subs


def position():
    sub = lax.broadcasted_iota(jnp.int32, (SUBS, LANES), 0)
    lane = lax.broadcasted_iota(jnp.int32, (SUBS, LANES), 1)
    return sub, lane


def aligned(start):
    return start if isinstance(start, int) else pl.multiple_of(start, SUBS)


def rows_at(first, count, size):
    return pl.ds(aligned(first * size), count * size)


def register(row, slot, size):
    return pl.ds(aligned(row * size + slot * SUBS), SUBS)


def side_marks(sides_ref):
    height = sides_ref.shape[1]
    square = (height, height)
    diagonal = lax.broadcasted_iota(jnp.int32, square, 0) == lax.broadcasted_iota(jnp.int32, square, 1)
    marks = sides_ref[...].astype(jnp.float32)
    return [
        jnp.sum(jnp.where(diagonal, marks[side : side + 1, :], 0.0), axis=1, keepdims=True)
        for side in range(2)
    ]


def start_all(copies):
    for copy in copies:
        copy.start()
    return copies


def wait_all(copies):
    for copy in copies:
        copy.wait()


def edge_kernel(
    ground_hbm, depth_hbm, rows_hbm, sides_hbm,
    far_ref, near_ref, even_ref, odd_ref,
    ground_ref, depth_ref, marks_ref, sides_ref, sems, small_sems,
):
    height, width = ground_hbm.shape
    groups = height // SUBS
    last_tile = width // LANES - 1
    place, places = chain_place()
    col, cols = lax.axis_index("cols"), lax.axis_size("cols")
    small = [pltpu.make_async_copy(sides_hbm, sides_ref, small_sems.at[0])]
    for side, tile in enumerate((0, last_tile)):
        columns = pl.ds(tile * LANES, LANES)
        small.append(pltpu.make_async_copy(rows_hbm.at[:, columns], marks_ref.at[side], small_sems.at[1 + side]))
    copies = start_own(ground_hbm, depth_hbm, ground_ref, depth_ref, sems)
    start_all(small)
    sub, lane = position()
    wait_all(small)
    marks = side_marks(sides_ref)
    at_edges = [(lane == 0) & (col == 0), (lane == LANES - 1) & (col == cols - 1)]
    for copy in copies:
        wait_all(copy)

    def raised(group, tile):
        rows, columns = pl.ds(group * SUBS, SUBS), pl.ds(tile * LANES, LANES)
        ground = ground_ref[rows, columns]
        surface = ground + depth_ref[rows, columns]
        if tile in (0, last_tile):
            side = 0 if tile == 0 else 1
            chosen = marks[side][group * SUBS : (group + 1) * SUBS]
            surface = jnp.where((chosen > 0.5) & at_edges[side], ground, surface)
        return ground, surface

    def pack(up_ref, down_ref):
        tiles = width // (SUBS * LANES)
        size = tiles * SUBS
        skipped = height - HALO
        for tile in range(last_tile + 1):
            start = tile % tiles * SUBS + tile // tiles
            for out_ref, ground_slot, surface_slot, shift, keep in (
                (up_ref, 0, HALO - 1, 0, range(0, HALO)),
                (down_ref, HALO - 1, 0, skipped, range(skipped, height)),
            ):
                values = [raised(group, tile) for group in range(groups)]
                for kind, slot in enumerate((ground_slot, surface_slot)):
                    for group in range(groups):
                        inside = [row for row in range(group * SUBS, (group + 1) * SUBS) if row in keep]
                        first, count = inside[0], len(inside)
                        offset = first - group * SUBS
                        row = slot + first - shift
                        out_ref[pl.ds(row * size + start, count, stride=size), :] = values[group][kind][
                            offset : offset + count
                        ]

    top = place % 2 == 0
    pl.when(top)(lambda: pack(far_ref, near_ref))
    pl.when(jnp.logical_not(top))(lambda: pack(near_ref, far_ref))
    rightward = col % 2 == 0
    for group in range(groups):
        values = []
        for side, tile in enumerate((0, last_tile)):
            ground, surface = raised(group, tile)
            if group == 0:
                outlet = (marks_ref[side, 0:1] == 1) & (sub == 0) & (place == 0)
                surface = jnp.where(outlet, ground, surface)
            if group == groups - 1:
                outlet = (marks_ref[side, 1:2] == 1) & (sub == SUBS - 1) & (place == places - 1)
                surface = jnp.where(outlet, ground, surface)
            values.append((ground, surface))
        for kind in range(2):
            rows = pl.ds(kind * height + group * SUBS, SUBS)
            even_ref[rows, :] = jnp.where(rightward, values[1][kind], values[0][kind])
            odd_ref[rows, :] = jnp.where(rightward, values[0][kind], values[1][kind])


def start_own(ground_hbm, depth_hbm, ground_ref, depth_ref, sems):
    height, width = ground_hbm.shape
    groups = height // SUBS
    pieces = sems.shape[1] // groups
    part = width // pieces
    copies = []
    for group in range(groups):
        for piece in range(pieces):
            where = (pl.ds(group * SUBS, SUBS), pl.ds(piece * part, part))
            number = group * pieces + piece
            copies.append(
                start_all(
                    [
                        pltpu.make_async_copy(ground_hbm.at[where], ground_ref.at[where], sems.at[0, number]),
                        pltpu.make_async_copy(depth_hbm.at[where], depth_ref.at[where], sems.at[1, number]),
                    ]
                )
            )
    return copies


def fold_own(copies, ground_ref, depth_ref, rows_ref, sides_ref, ground_out, surface_out):
    height, width = ground_ref.shape
    groups = height // SUBS
    tiles = width // (SUBS * LANES)
    last_tile = width // LANES - 1
    pieces = len(copies) // groups
    part = width // pieces
    size = (tiles + 1) * SUBS
    place, places = chain_place()
    col, cols = lax.axis_index("cols"), lax.axis_size("cols")
    sub, lane = position()
    marks = side_marks(sides_ref)
    for group in range(groups):
        rows = pl.ds(group * SUBS, SUBS)
        for tile in range(last_tile + 1):
            if tile * LANES % part == 0:
                wait_all(copies[group * pieces + tile * LANES // part])
            columns = pl.ds(tile * LANES, LANES)
            ground = ground_ref[rows, columns]
            surface = ground + depth_ref[rows, columns]
            outlets = []
            if group == 0:
                outlets.append((rows_ref[0:1, columns] == 1) & (sub == 0) & (place == 0))
            if group == groups - 1:
                outlets.append(
                    (rows_ref[1:2, columns] == 1) & (sub == SUBS - 1) & (place == places - 1)
                )
            if tile == 0:
                outlets.append(
                    (marks[0][group * SUBS : (group + 1) * SUBS] > 0.5) & (lane == 0) & (col == 0)
                )
            if tile == last_tile:
                outlets.append(
                    (marks[1][group * SUBS : (group + 1) * SUBS] > 0.5)
                    & (lane == LANES - 1)
                    & (col == cols - 1)
                )
            for outlet in outlets:
                surface = jnp.where(outlet, ground, surface)
            chunk, slot = tile // tiles, tile % tiles
            start = (HALO + group * SUBS) * size + slot * SUBS + chunk
            ground_out[pl.ds(start, SUBS, stride=size), :] = ground
            surface_out[pl.ds(start, SUBS, stride=size), :] = surface


def unpack_rows(rows_ref, first, is_top, present, strip_refs, strip_rows, ground_ref, surface_ref, tiles):
    packed = tiles * SUBS
    size = packed + SUBS
    bases = (jnp.where(is_top, HALO - 1, 0), jnp.where(is_top, 0, HALO - 1))
    for base, out_ref, strip_row in zip(bases, (ground_ref, surface_ref), strip_rows):

        def body(row, carry):
            values = [
                jnp.where(present, rows_ref[register(base + row, slot, packed), :], unreached)
                for slot in range(tiles)
            ]
            for slot in range(tiles):
                out_ref[register(first + row, slot, size), :] = values[slot]
            fill_seam(out_ref, first + row, values[0], values[-1], strip_refs, strip_row + row, present, tiles)
            return carry

        lax.fori_loop(0, HALO, body, 0, unroll=4)


def fill_seam(out_ref, row, first_tile, last_tile, strip_refs, strip_row, present, tiles):
    col, cols = lax.axis_index("cols"), lax.axis_size("cols")
    sub, lane = position()
    rightward = col % 2 == 0
    even, odd = [ref[pl.ds(strip_row, 1), :] for ref in strip_refs]
    after = jnp.where(present & (col < cols - 1), jnp.where(rightward, even, odd), unreached)
    before = jnp.where(present & (col > 0), jnp.where(rightward, odd, even), unreached)
    after = jnp.where(sub == SUBS - 1, after, pltpu.roll(first_tile, SUBS - 1, 0))
    before = jnp.where(sub == 0, before, pltpu.roll(last_tile, 1, 0))
    out_ref[register(row, tiles, (tiles + 1) * SUBS), :] = jnp.where(lane < LANES // 2, after, before)


def relax_rows(source, target, ground, first, count, ring):
    size = ring * SUBS
    _, lane = position()
    at_first = lane == 0
    at_last = lane == LANES - 1
    order = [ring - 1] + list(range(ring - 1))
    made = {}

    def make(pair, slot):
        row = first + 2 * pair
        values = [source[register(row + step, slot, size), :] for step in range(-1, 3)]
        both = jnp.minimum(values[1], values[2])
        for one, column in enumerate((jnp.minimum(values[0], both), jnp.minimum(both, values[3]))):
            made[pair, one, slot] = (column, pltpu.roll(column, 1, 1), pltpu.roll(column, LANES - 1, 1))

    def finish(pair, slot):
        for one in range(2):
            row = first + 2 * pair + one
            before, here, after = [made[pair, one, (slot + step) % ring] for step in (-1, 0, 1)]
            from_left = jnp.where(at_first, before[1], here[1])
            from_right = jnp.where(at_last, after[2], here[2])
            lowest = jnp.minimum(jnp.minimum(from_left, from_right), here[0])
            where = register(row, slot, size)
            raised = jnp.minimum(source[where, :], lowest + rise_step)
            target[where, :] = jnp.maximum(ground[where, :], raised)

    makes = [(pair, slot) for pair in range(count // 2) for slot in order]
    finishes = [(pair, slot) for pair in range(count // 2) for slot in range(ring)]
    done = 0
    for number, item in enumerate(makes):
        make(*item)
        if number >= AHEAD:
            finish(*finishes[done])
            done += 1
    for item in finishes[done:]:
        finish(*item)


def hop_counts(links_ref, hops_ref, needed):
    tiles, degree = links_ref.shape
    links = links_ref[...]
    number = lax.broadcasted_iota(jnp.int32, (tiles, tiles), 1)
    linked = links[:, 0:1] == number
    for edge in range(1, degree):
        linked = linked | (links[:, edge : edge + 1] == number)
    linked = linked.astype(jnp.float32)
    tile = lax.broadcasted_iota(jnp.int32, (tiles, LANES), 0)
    lane = lax.broadcasted_iota(jnp.int32, (tiles, LANES), 1)
    reached = jnp.zeros((tiles, LANES), jnp.float32)
    for index, wanted in enumerate(needed):
        reached = jnp.where((lane == index) & (tile == wanted), 1.0, reached)
    hops = jnp.where(reached > 0.5, 0.0, float(ROUNDS + 1))
    for hop in range(1, ROUNDS + 1):
        reached = lax.dot_general(
            linked, reached, (((0,), (0,)), ((), ())), preferred_element_type=jnp.float32
        )
        reached = jnp.where(reached > 0.5, 1.0, 0.0)
        hops = jnp.minimum(hops, jnp.where(reached > 0.5, float(hop), float(ROUNDS + 1)))
    for index in range(len(needed)):
        hops_ref[pl.ds(index * tiles, tiles), :] = jnp.broadcast_to(
            hops[:, index : index + 1], (tiles, LANES)
        )


def needed_tiles():
    row, rows = lax.axis_index("rows"), lax.axis_size("rows")
    col, cols = lax.axis_index("cols"), lax.axis_size("cols")
    sub, subs = lax.axis_index("sub"), lax.axis_size("sub")
    above = jnp.maximum(jnp.where(sub == 0, row - 1, row), 0)
    below = jnp.minimum(jnp.where(sub == subs - 1, row + 1, row), rows - 1)
    left = jnp.maximum(col - 1, 0)
    right = jnp.minimum(col + 1, cols - 1)
    return [r * cols + c for r in (above, row, below) for c in (left, col, right)]


def inner_kernel(
    ground_hbm, depth_hbm, rows_hbm, sides_hbm, links_hbm,
    near_ref, own_even_ref, own_odd_ref, near_even_ref, near_odd_ref,
    ground_ref, surface_ref, other_ref, hops_ref,
    raw_ground_ref, raw_depth_ref, rows_ref, sides_ref, links_ref, sems, small_sems,
):
    height, width = ground_hbm.shape
    tiles = width // (SUBS * LANES)
    small = start_all(
        [
            pltpu.make_async_copy(source, target, small_sems.at[number])
            for number, (source, target) in enumerate(
                ((rows_hbm, rows_ref), (sides_hbm, sides_ref), (links_hbm, links_ref))
            )
        ]
    )
    copies = start_own(ground_hbm, depth_hbm, raw_ground_ref, raw_depth_ref, sems)
    own_strips, near_strips = (own_even_ref, own_odd_ref), (near_even_ref, near_odd_ref)
    ring = tiles + 1
    size = ring * SUBS
    place, places = chain_place()
    top = place % 2 == 0
    has_near = jnp.where(top, place < places - 1, place > 0)
    unpack_rows(
        near_ref,
        jnp.where(top, HALO + height, 0),
        jnp.logical_not(top),
        has_near,
        near_strips,
        [kind * height + jnp.where(top, 0, height - HALO) for kind in range(2)],
        ground_ref,
        surface_ref,
        tiles,
    )
    wait_all(small)
    hop_counts(links_ref, hops_ref, needed_tiles())
    fold_own(copies, raw_ground_ref, raw_depth_ref, rows_ref, sides_ref, ground_ref, surface_ref)
    for kind, out_ref in enumerate((ground_ref, surface_ref)):

        def body(row, carry):
            first_tile = out_ref[register(HALO + row, 0, size), :]
            last_tile = out_ref[register(HALO + row, tiles - 1, size), :]
            fill_seam(
                out_ref, HALO + row, first_tile, last_tile, own_strips, kind * height + row, place >= 0, tiles
            )
            return carry

        lax.fori_loop(0, height, body, 0, unroll=4)
    buffers = (surface_ref, other_ref)
    for step in range(1, PASSES + 1):
        first = step + jnp.where(top, HALO, 0)
        count = height + HALO - 2 * step
        relax_rows(buffers[(step + 1) % 2], buffers[step % 2], ground_ref, first, count, ring)


def outer_kernel(height, tiles, far_ref, even_ref, odd_ref, *refs):
    ground_ref, surface_ref, other_ref, level_ref = refs[3:7]
    ring = tiles + 1
    size = ring * SUBS
    place, places = chain_place()
    top = place % 2 == 0
    has_far = jnp.where(top, place > 0, place < places - 1)
    unpack_rows(
        far_ref,
        jnp.where(top, 0, HALO + height),
        top,
        has_far,
        (even_ref, odd_ref),
        [kind * height + jnp.where(top, height - HALO, 0) for kind in range(2)],
        ground_ref,
        surface_ref,
        tiles,
    )
    buffers = (surface_ref, other_ref)
    for step in range(1, PASSES + 1):
        first = jnp.where(top, step, HALO + height - step)
        relax_rows(buffers[(step + 1) % 2], buffers[step % 2], ground_ref, first, HALO, ring)
    band, bands = lax.axis_index("sub"), lax.axis_size("sub")
    sub, lane = position()

    def at(row, slot):
        return surface_ref[register(HALO + row, slot, size), :]

    first_cell = (sub == 0) & (lane == 0)
    last_cell = (sub == SUBS - 1) & (lane == LANES - 1)
    first_lows, last_lows, row_lows = [], [], []
    for row in range(height):
        first_lows.append(at(row, 0))
        last_lows.append(at(row, tiles - 1))
    for slot in range(tiles):
        row_lows.append(jnp.where(band == 0, at(0, slot), unreached))
        row_lows.append(jnp.where(band == bands - 1, at(height - 1, slot), unreached))
    lowest = jnp.minimum(
        least(row_lows),
        jnp.minimum(
            jnp.where(first_cell, least(first_lows), unreached),
            jnp.where(last_cell, least(last_lows), unreached),
        ),
    )
    lowest = jnp.min(jnp.min(lowest, axis=0, keepdims=True), axis=1, keepdims=True)
    level_ref[...] = jnp.broadcast_to(lowest, level_ref.shape)


def least(values):
    values = list(values)
    while len(values) > 1:
        values = [
            jnp.minimum(*values[number : number + 2]) if number + 1 < len(values) else values[number]
            for number in range(0, len(values), 2)
        ]
    return values[0]


def late_kernel(
    height, tiles, ground_ref, surface_ref, floors_ref, hops_ref, out_hbm,
    one_ref, two_ref, out_ref, sems,
):
    ring = tiles + 1
    size = ring * SUBS
    sub, lane = position()
    level = floors_ref[...]
    count = level.shape[0]
    raised = [level]
    for hop in range(ROUNDS):
        raised.append(raised[-1] + hop_rise)
    ceilings = []
    for index in range(9):
        hops = hops_ref[pl.ds(index * count, count), :]
        lowest = jnp.full((count, LANES), unreached, jnp.float32)
        for hop in range(ROUNDS + 1):
            lowest = jnp.where(hops == float(hop), raised[hop], lowest)
        lowest = jnp.min(lowest, axis=0, keepdims=True) + spill_lift
        ceilings.append(jnp.broadcast_to(lowest, (SUBS, LANES)))
    pairs = []
    for region in range(3):
        left, middle, right = ceilings[3 * region : 3 * region + 3]
        seam = jnp.where(
            lane < LANES // 2,
            jnp.where(sub == SUBS - 1, right, middle),
            jnp.where(sub == 0, left, middle),
        )
        pairs.append((middle, seam))
    spans = ((HALO - FINAL, FINAL), (HALO, height), (HALO + height, FINAL))
    for (first, rows), (middle, seam) in zip(spans, pairs):

        def body(row, carry):
            for slot in range(ring):
                where = register(first + row, slot, size)
                value = jnp.minimum(surface_ref[where, :], seam if slot == tiles else middle)
                one_ref[where, :] = jnp.maximum(ground_ref[where, :], value)
            return carry

        lax.fori_loop(0, rows, body, 0, unroll=4)
    buffers = (one_ref, two_ref)
    for step in range(1, FINAL):
        first = HALO - FINAL + step
        relax_rows(
            buffers[(step + 1) % 2], buffers[step % 2], ground_ref, first, 2 * HALO + height - 2 * first, ring
        )
    source, target = buffers[(FINAL + 1) % 2], buffers[FINAL % 2]
    copies = []
    for group in range(height // SUBS):
        first = HALO + group * SUBS
        relax_rows(source, target, ground_ref, first, SUBS, ring)
        for tile in range(tiles * SUBS):
            chunk, slot = tile // tiles, tile % tiles
            out_ref[pl.ds(group * SUBS, SUBS), pl.ds(tile * LANES, LANES)] = target[
                pl.ds(first * size + slot * SUBS + chunk, SUBS, stride=size), :
            ]
        where = (pl.ds(group * SUBS, SUBS), slice(None))
        copies += start_all([pltpu.make_async_copy(out_ref.at[where], out_hbm.at[where], sems.at[group])])
    wait_all(copies)


def in_vmem(count):
    return [pl.BlockSpec(memory_space=pltpu.VMEM)] * count


def in_hbm(count):
    return [pl.BlockSpec(memory_space=pltpu.HBM)] * count


def per_device(elevation, fill_depth, edge_rows, edge_sides, adjacency):
    height, width = elevation.shape
    tiles = width // (SUBS * LANES)
    groups = height // SUBS
    f32 = jnp.float32
    packed = tiles * SUBS
    size = packed + SUBS
    tile_count = adjacency.shape[0]
    places = lax.axis_size(("rows", "sub"))
    cols, subs = lax.axis_size("cols"), lax.axis_size("sub")
    short = pl.CostEstimate(flops=1024, bytes_accessed=1024, transcendentals=0)
    limit = pltpu.CompilerParams(vmem_limit_bytes=24 << 20)
    arguments = [
        pltpu.with_memory_space_constraint(value, pltpu.HBM)
        for value in (elevation, fill_depth, edge_rows, edge_sides, adjacency)
    ]
    sent = pltpu.VMEM(((2 * HALO - 1) * packed, LANES), f32)
    strip = pltpu.VMEM((2 * height, LANES), f32)
    far, near, even, odd = pl.pallas_call(
        edge_kernel,
        out_shape=[sent, sent, strip, strip],
        in_specs=in_hbm(4),
        out_specs=in_vmem(4),
        scratch_shapes=[
            pltpu.VMEM((height, width), f32),
            pltpu.VMEM((height, width), f32),
            pltpu.VMEM((2, 2, LANES), jnp.int32),
            pltpu.VMEM(edge_sides.shape, jnp.int32),
            pltpu.SemaphoreType.DMA((2, 4 * groups)),
            pltpu.SemaphoreType.DMA((3,)),
        ],
        compiler_params=limit,
        cost_estimate=short,
        name="edge_rows",
    )(*arguments[:4])

    near_pairs, far_pairs = [matching(places, first) for first in range(2)]
    stay = [(place, place) for place in range(places)]
    ends = [(place, place) for place in range(places) if place not in dict(far_pairs)]
    groups_count = lax.axis_size("groups")
    part = places * cols
    far_all = []
    for group, other in closed(matching(groups_count, 0), groups_count):
        for chosen, target in ((far_pairs, group), (ends, other)):
            for source, arrival in cross(chosen, [(col, col) for col in range(cols)], cols, subs):
                far_all.append((group * part + source, target * part + arrival))
    device_axes = ("rows", "cols", "sub")

    def swap_strips(pieces, row_pairs):
        arrived = []
        for first, piece in enumerate(pieces):
            pairs = cross(row_pairs, matching(cols, first), cols, subs)
            arrived.append(lax.ppermute(piece, device_axes, pairs) if pairs else piece)
        return arrived

    far_strips = swap_strips((even, odd), far_pairs + ends)
    far_rows = lax.ppermute(far, ("groups",) + device_axes, far_all)
    near_rows = lax.ppermute(near, ("rows", "sub"), near_pairs)
    strips = swap_strips((even, odd), stay) + swap_strips((even, odd), near_pairs)

    work = pltpu.VMEM(((height + 2 * HALO) * size, LANES), f32)
    work_scratch = pltpu.VMEM(((height + 2 * HALO) * size, LANES), f32)
    ground, surface, other, hops = pl.pallas_call(
        inner_kernel,
        out_shape=[work, work, work, pltpu.VMEM((9 * tile_count, LANES), f32)],
        in_specs=in_hbm(5) + in_vmem(5),
        out_specs=in_vmem(4),
        scratch_shapes=[
            pltpu.VMEM((height, width), f32),
            pltpu.VMEM((height, width), f32),
            pltpu.VMEM(edge_rows.shape, jnp.int32),
            pltpu.VMEM(edge_sides.shape, jnp.int32),
            pltpu.VMEM(adjacency.shape, jnp.int32),
            pltpu.SemaphoreType.DMA((2, 4 * groups)),
            pltpu.SemaphoreType.DMA((3,)),
        ],
        compiler_params=limit,
        cost_estimate=short,
        name="inner_passes",
    )(*arguments, near_rows, *strips)

    def outer(far_ref, *refs):
        outer_kernel(height, tiles, far_ref, *refs)

    ground, surface, other, floors = pl.pallas_call(
        outer,
        out_shape=[work, work, work, pltpu.VMEM((tile_count, LANES), f32)],
        in_specs=in_vmem(6),
        out_specs=in_vmem(4),
        input_output_aliases={3: 0, 4: 1, 5: 2},
        compiler_params=limit,
        cost_estimate=short,
        name="outer_passes",
    )(far_rows, *far_strips, ground, surface, other)

    for shift in range(1, subs):
        pairs = [(sub, (sub + shift) % subs) for sub in range(subs)]
        floors = jnp.minimum(floors, lax.ppermute(floors, "sub", pairs))
    floors = lax.all_to_all(floors, ("rows", "cols"), 0, 0, tiled=True)

    def late(*refs):
        late_kernel(height, tiles, *refs)

    return pl.pallas_call(
        late,
        out_shape=jax.ShapeDtypeStruct((height, width), f32),
        in_specs=in_vmem(4),
        out_specs=pl.BlockSpec(memory_space=pltpu.HBM),
        scratch_shapes=[
            work_scratch,
            work_scratch,
            pltpu.VMEM((height, width), f32),
            pltpu.SemaphoreType.DMA((groups,)),
        ],
        compiler_params=limit,
        cost_estimate=short,
        name="final_passes",
    )(ground, surface, floors, hops)


def solution(mesh):
    placed = (
        P(("groups", "rows", "sub"), "cols"),
        P(("groups", "rows", "sub"), "cols"),
        P("groups", "cols"),
        P("groups", ("rows", "sub")),
        P("groups", None),
    )
    return jax.shard_map(
        per_device,
        mesh=mesh,
        in_specs=placed,
        out_specs=P(("groups", "rows", "sub"), "cols"),
        check_vma=False,
    )
```

```python
import jax
import jax.numpy as jnp
from jax import lax
from jax.experimental import pallas as pl
from jax.experimental.pallas import tpu as pltpu
from jax.sharding import PartitionSpec as P

PASSES = 8
FINAL = 4
ROUNDS = 4
HALO = PASSES
SUBS = 8
LANES = 128
AHEAD = 5

unreached = 1000000000.0
rise_step = 0.01
hop_rise = 0.05
spill_lift = 3.0


def matching(count, first):
    pairs = []
    for low in range(first, count - 1, 2):
        pairs += [(low, low + 1), (low + 1, low)]
    return pairs


def closed(pairs, count):
    used = {source for source, _ in pairs}
    return pairs + [(place, place) for place in range(count) if place not in used]


def cross(row_pairs, col_pairs, cols, subs):
    def device(place, col):
        return (place // subs * cols + col) * subs + place % subs

    return [
        (device(row, col), device(row_to, col_to))
        for row, row_to in row_pairs
        for col, col_to in col_pairs
    ]


def chain_place():
    subs = lax.axis_size("sub")
    return lax.axis_index("rows") * subs + lax.axis_index("sub"), lax.axis_size("rows") * subs


def position():
    sub = lax.broadcasted_iota(jnp.int32, (SUBS, LANES), 0)
    lane = lax.broadcasted_iota(jnp.int32, (SUBS, LANES), 1)
    return sub, lane


def aligned(start):
    return start if isinstance(start, int) else pl.multiple_of(start, SUBS)


def rows_at(first, count, size):
    return pl.ds(aligned(first * size), count * size)


def register(row, slot, size):
    return pl.ds(aligned(row * size + slot * SUBS), SUBS)


def side_marks(sides_ref):
    height = sides_ref.shape[1]
    square = (height, height)
    diagonal = lax.broadcasted_iota(jnp.int32, square, 0) == lax.broadcasted_iota(jnp.int32, square, 1)
    marks = sides_ref[...].astype(jnp.float32)
    return [
        jnp.sum(jnp.where(diagonal, marks[side : side + 1, :], 0.0), axis=1, keepdims=True)
        for side in range(2)
    ]


def start_all(copies):
    for copy in copies:
        copy.start()
    return copies


def wait_all(copies):
    for copy in copies:
        copy.wait()


def edge_kernel(
    ground_hbm, depth_hbm, rows_hbm, sides_hbm,
    far_ref, near_ref, even_ref, odd_ref, ground_out, surface_out,
    ground_ref, depth_ref, rows_ref, sides_ref, sems, small_sems,
):
    height, width = ground_hbm.shape
    tiles = width // (SUBS * LANES)
    small = [
        pltpu.make_async_copy(rows_hbm, rows_ref, small_sems.at[0]),
        pltpu.make_async_copy(sides_hbm, sides_ref, small_sems.at[1]),
    ]
    start_all(small[1:])
    copies = start_own(ground_hbm, depth_hbm, ground_ref, depth_ref, sems)
    start_all(small[:1])
    wait_all(small)
    edges = fold_own(copies, ground_ref, depth_ref, rows_ref, sides_ref, ground_out, surface_out)
    place, _ = chain_place()
    top = place % 2 == 0
    size, packed = (tiles + 1) * SUBS, tiles * SUBS
    for out_ref, is_top in ((far_ref, top), (near_ref, jnp.logical_not(top))):
        first = HALO + jnp.where(is_top, 0, height - HALO)
        bases = (jnp.where(is_top, 0, HALO - 1), jnp.where(is_top, HALO - 1, 0))
        for source, base in zip((ground_out, surface_out), bases):
            for row in range(HALO):
                for slot in range(tiles):
                    out_ref[register(base + row, slot, packed), :] = source[register(first + row, slot, size), :]
    rightward = lax.axis_index("cols") % 2 == 0
    for group, values in enumerate(edges):
        for kind in range(2):
            rows = pl.ds(kind * height + group * SUBS, SUBS)
            even_ref[rows, :] = jnp.where(rightward, values[1][kind], values[0][kind])
            odd_ref[rows, :] = jnp.where(rightward, values[0][kind], values[1][kind])


def start_own(ground_hbm, depth_hbm, ground_ref, depth_ref, sems):
    height, width = ground_hbm.shape
    groups = height // SUBS
    pieces = sems.shape[1] // groups
    part = width // pieces
    copies = []
    for group in range(groups):
        for piece in range(pieces):
            where = (pl.ds(group * SUBS, SUBS), pl.ds(piece * part, part))
            number = group * pieces + piece
            copies.append(
                start_all(
                    [
                        pltpu.make_async_copy(ground_hbm.at[where], ground_ref.at[where], sems.at[0, number]),
                        pltpu.make_async_copy(depth_hbm.at[where], depth_ref.at[where], sems.at[1, number]),
                    ]
                )
            )
    return copies


def fold_own(copies, ground_ref, depth_ref, rows_ref, sides_ref, ground_out, surface_out):
    height, width = ground_ref.shape
    groups = height // SUBS
    tiles = width // (SUBS * LANES)
    last_tile = width // LANES - 1
    pieces = len(copies) // groups
    part = width // pieces
    size = (tiles + 1) * SUBS
    place, places = chain_place()
    col, cols = lax.axis_index("cols"), lax.axis_size("cols")
    sub, lane = position()
    marks = side_marks(sides_ref)
    edges = [[] for _ in range(groups)]
    for group in range(groups):
        rows = pl.ds(group * SUBS, SUBS)
        for tile in range(last_tile + 1):
            if tile * LANES % part == 0:
                wait_all(copies[group * pieces + tile * LANES // part])
            columns = pl.ds(tile * LANES, LANES)
            ground = ground_ref[rows, columns]
            surface = ground + depth_ref[rows, columns]
            outlets = []
            if group == 0:
                outlets.append((rows_ref[0:1, columns] == 1) & (sub == 0) & (place == 0))
            if group == groups - 1:
                outlets.append(
                    (rows_ref[1:2, columns] == 1) & (sub == SUBS - 1) & (place == places - 1)
                )
            if tile == 0:
                outlets.append(
                    (marks[0][group * SUBS : (group + 1) * SUBS] > 0.5) & (lane == 0) & (col == 0)
                )
            if tile == last_tile:
                outlets.append(
                    (marks[1][group * SUBS : (group + 1) * SUBS] > 0.5)
                    & (lane == LANES - 1)
                    & (col == cols - 1)
                )
            for outlet in outlets:
                surface = jnp.where(outlet, ground, surface)
            chunk, slot = tile // tiles, tile % tiles
            start = (HALO + group * SUBS) * size + slot * SUBS + chunk
            ground_out[pl.ds(start, SUBS, stride=size), :] = ground
            surface_out[pl.ds(start, SUBS, stride=size), :] = surface
            if tile in (0, last_tile):
                edges[group].append((ground, surface))
    return edges


def unpack_rows(rows_ref, first, is_top, present, strip_refs, strip_rows, ground_ref, surface_ref, tiles):
    packed = tiles * SUBS
    size = packed + SUBS
    bases = (jnp.where(is_top, HALO - 1, 0), jnp.where(is_top, 0, HALO - 1))
    for base, out_ref, strip_row in zip(bases, (ground_ref, surface_ref), strip_rows):

        def body(row, carry):
            values = [
                jnp.where(present, rows_ref[register(base + row, slot, packed), :], unreached)
                for slot in range(tiles)
            ]
            for slot in range(tiles):
                out_ref[register(first + row, slot, size), :] = values[slot]
            fill_seam(out_ref, first + row, values[0], values[-1], strip_refs, strip_row + row, present, tiles)
            return carry

        lax.fori_loop(0, HALO, body, 0, unroll=4)


def fill_seam(out_ref, row, first_tile, last_tile, strip_refs, strip_row, present, tiles):
    col, cols = lax.axis_index("cols"), lax.axis_size("cols")
    sub, lane = position()
    rightward = col % 2 == 0
    even, odd = [ref[pl.ds(strip_row, 1), :] for ref in strip_refs]
    after = jnp.where(present & (col < cols - 1), jnp.where(rightward, even, odd), unreached)
    before = jnp.where(present & (col > 0), jnp.where(rightward, odd, even), unreached)
    after = jnp.where(sub == SUBS - 1, after, pltpu.roll(first_tile, SUBS - 1, 0))
    before = jnp.where(sub == 0, before, pltpu.roll(last_tile, 1, 0))
    out_ref[register(row, tiles, (tiles + 1) * SUBS), :] = jnp.where(lane < LANES // 2, after, before)


def relax_rows(source, target, ground, first, count, ring):
    size = ring * SUBS
    _, lane = position()
    at_first = lane == 0
    at_last = lane == LANES - 1
    order = [ring - 1] + list(range(ring - 1))
    made = {}

    def make(pair, slot):
        row = first + 2 * pair
        values = [source[register(row + step, slot, size), :] for step in range(-1, 3)]
        both = jnp.minimum(values[1], values[2])
        for one, column in enumerate((jnp.minimum(values[0], both), jnp.minimum(both, values[3]))):
            made[pair, one, slot] = (column, pltpu.roll(column, 1, 1), pltpu.roll(column, LANES - 1, 1))

    def finish(pair, slot):
        for one in range(2):
            row = first + 2 * pair + one
            before, here, after = [made[pair, one, (slot + step) % ring] for step in (-1, 0, 1)]
            from_left = jnp.where(at_first, before[1], here[1])
            from_right = jnp.where(at_last, after[2], here[2])
            lowest = jnp.minimum(jnp.minimum(from_left, from_right), here[0])
            where = register(row, slot, size)
            raised = jnp.minimum(source[where, :], lowest + rise_step)
            target[where, :] = jnp.maximum(ground[where, :], raised)

    makes = [(pair, slot) for pair in range(count // 2) for slot in order]
    finishes = [(pair, slot) for pair in range(count // 2) for slot in range(ring)]
    done = 0
    for number, item in enumerate(makes):
        make(*item)
        if number >= AHEAD:
            finish(*finishes[done])
            done += 1
    for item in finishes[done:]:
        finish(*item)


def hop_counts(links_ref, hops_ref, needed):
    tiles, degree = links_ref.shape
    links = links_ref[...]
    number = lax.broadcasted_iota(jnp.int32, (tiles, tiles), 1)
    linked = links[:, 0:1] == number
    for edge in range(1, degree):
        linked = linked | (links[:, edge : edge + 1] == number)
    linked = linked.astype(jnp.float32)
    tile = lax.broadcasted_iota(jnp.int32, (tiles, LANES), 0)
    lane = lax.broadcasted_iota(jnp.int32, (tiles, LANES), 1)
    reached = jnp.zeros((tiles, LANES), jnp.float32)
    for index, wanted in enumerate(needed):
        reached = jnp.where((lane == index) & (tile == wanted), 1.0, reached)
    hops = jnp.where(reached > 0.5, 0.0, float(ROUNDS + 1))
    for hop in range(1, ROUNDS + 1):
        reached = lax.dot_general(
            linked, reached, (((0,), (0,)), ((), ())), preferred_element_type=jnp.float32
        )
        reached = jnp.where(reached > 0.5, 1.0, 0.0)
        hops = jnp.minimum(hops, jnp.where(reached > 0.5, float(hop), float(ROUNDS + 1)))
    for index in range(len(needed)):
        hops_ref[pl.ds(index * tiles, tiles), :] = jnp.broadcast_to(
            hops[:, index : index + 1], (tiles, LANES)
        )


def needed_tiles():
    row, rows = lax.axis_index("rows"), lax.axis_size("rows")
    col, cols = lax.axis_index("cols"), lax.axis_size("cols")
    sub, subs = lax.axis_index("sub"), lax.axis_size("sub")
    above = jnp.maximum(jnp.where(sub == 0, row - 1, row), 0)
    below = jnp.minimum(jnp.where(sub == subs - 1, row + 1, row), rows - 1)
    left = jnp.maximum(col - 1, 0)
    right = jnp.minimum(col + 1, cols - 1)
    return [r * cols + c for r in (above, row, below) for c in (left, col, right)]


def inner_kernel(
    height, tiles, links_hbm, near_ref, own_even_ref, own_odd_ref, near_even_ref, near_odd_ref, *refs
):
    ground_ref, surface_ref, other_ref, hops_ref, links_ref, sem = refs[2:]
    links = pltpu.make_async_copy(links_hbm, links_ref, sem)
    links.start()
    own_strips, near_strips = (own_even_ref, own_odd_ref), (near_even_ref, near_odd_ref)
    ring = tiles + 1
    size = ring * SUBS
    place, places = chain_place()
    top = place % 2 == 0
    has_near = jnp.where(top, place < places - 1, place > 0)
    unpack_rows(
        near_ref,
        jnp.where(top, HALO + height, 0),
        jnp.logical_not(top),
        has_near,
        near_strips,
        [kind * height + jnp.where(top, 0, height - HALO) for kind in range(2)],
        ground_ref,
        surface_ref,
        tiles,
    )
    links.wait()
    hop_counts(links_ref, hops_ref, needed_tiles())
    for kind, out_ref in enumerate((ground_ref, surface_ref)):

        def body(row, carry):
            first_tile = out_ref[register(HALO + row, 0, size), :]
            last_tile = out_ref[register(HALO + row, tiles - 1, size), :]
            fill_seam(
                out_ref, HALO + row, first_tile, last_tile, own_strips, kind * height + row, place >= 0, tiles
            )
            return carry

        lax.fori_loop(0, height, body, 0, unroll=4)
    buffers = (surface_ref, other_ref)
    for step in range(1, PASSES + 1):
        first = step + jnp.where(top, HALO, 0)
        count = height + HALO - 2 * step
        relax_rows(buffers[(step + 1) % 2], buffers[step % 2], ground_ref, first, count, ring)


def outer_kernel(height, tiles, far_ref, even_ref, odd_ref, *refs):
    ground_ref, surface_ref, other_ref, level_ref, far_out, near_out = refs[3:9]
    ring = tiles + 1
    size = ring * SUBS
    place, places = chain_place()
    top = place % 2 == 0
    has_far = jnp.where(top, place > 0, place < places - 1)
    unpack_rows(
        far_ref,
        jnp.where(top, 0, HALO + height),
        top,
        has_far,
        (even_ref, odd_ref),
        [kind * height + jnp.where(top, height - HALO, 0) for kind in range(2)],
        ground_ref,
        surface_ref,
        tiles,
    )
    buffers = (surface_ref, other_ref)
    for step in range(1, PASSES + 1):
        first = jnp.where(top, step, HALO + height - step)
        relax_rows(buffers[(step + 1) % 2], buffers[step % 2], ground_ref, first, HALO, ring)
    low, high = HALO, HALO + height - FINAL
    for row in range(FINAL):
        for slot in range(ring):
            where = register(row, slot, size)
            far_out[where, :] = surface_ref[register(jnp.where(top, low, high) + row, slot, size), :]
            near_out[where, :] = surface_ref[register(jnp.where(top, high, low) + row, slot, size), :]
    band, bands = lax.axis_index("sub"), lax.axis_size("sub")
    sub, lane = position()

    def at(row, slot):
        return surface_ref[register(HALO + row, slot, size), :]

    first_cell = (sub == 0) & (lane == 0)
    last_cell = (sub == SUBS - 1) & (lane == LANES - 1)
    first_lows, last_lows, row_lows = [], [], []
    for row in range(height):
        first_lows.append(at(row, 0))
        last_lows.append(at(row, tiles - 1))
    for slot in range(tiles):
        row_lows.append(jnp.where(band == 0, at(0, slot), unreached))
        row_lows.append(jnp.where(band == bands - 1, at(height - 1, slot), unreached))
    lowest = jnp.minimum(
        least(row_lows),
        jnp.minimum(
            jnp.where(first_cell, least(first_lows), unreached),
            jnp.where(last_cell, least(last_lows), unreached),
        ),
    )
    lowest = jnp.min(jnp.min(lowest, axis=0, keepdims=True), axis=1, keepdims=True)
    level_ref[...] = jnp.broadcast_to(lowest, level_ref.shape)


def least(values):
    values = list(values)
    while len(values) > 1:
        values = [
            jnp.minimum(*values[number : number + 2]) if number + 1 < len(values) else values[number]
            for number in range(0, len(values), 2)
        ]
    return values[0]


def late_kernel(
    height, tiles, ground_ref, surface_ref, far_ref, near_ref, floors_ref, hops_ref, out_hbm,
    one_ref, two_ref, out_ref, sems,
):
    ring = tiles + 1
    size = ring * SUBS
    sub, lane = position()
    bands = lax.axis_size("sub")
    count = floors_ref.shape[0] // bands
    level = least(floors_ref[pl.ds(band, count, stride=bands), :] for band in range(bands))
    raised = [level]
    for hop in range(ROUNDS):
        raised.append(raised[-1] + hop_rise)
    ceilings = []
    for index in range(9):
        hops = hops_ref[pl.ds(index * count, count), :]
        lowest = jnp.full((count, LANES), unreached, jnp.float32)
        for hop in range(ROUNDS + 1):
            lowest = jnp.where(hops == float(hop), raised[hop], lowest)
        lowest = jnp.min(lowest, axis=0, keepdims=True) + spill_lift
        ceilings.append(jnp.broadcast_to(lowest, (SUBS, LANES)))
    pairs = []
    for region in range(3):
        left, middle, right = ceilings[3 * region : 3 * region + 3]
        seam = jnp.where(
            lane < LANES // 2,
            jnp.where(sub == SUBS - 1, right, middle),
            jnp.where(sub == 0, left, middle),
        )
        pairs.append((middle, seam))
    place, _ = chain_place()
    top = place % 2 == 0
    low, high = HALO - FINAL, HALO + height
    far_pair = [jnp.where(top, above, below) for above, below in zip(pairs[0], pairs[2])]
    near_pair = [jnp.where(top, below, above) for above, below in zip(pairs[0], pairs[2])]
    spans = (
        (surface_ref, HALO, HALO, height, pairs[1]),
        (near_ref, 0, jnp.where(top, high, low), FINAL, near_pair),
        (far_ref, 0, jnp.where(top, low, high), FINAL, far_pair),
    )
    for source, source_first, first, rows, (middle, seam) in spans:

        def body(row, carry):
            for slot in range(ring):
                value = source[register(source_first + row, slot, size), :]
                value = jnp.minimum(value, seam if slot == tiles else middle)
                where = register(first + row, slot, size)
                one_ref[where, :] = jnp.maximum(ground_ref[where, :], value)
            return carry

        lax.fori_loop(0, rows, body, 0, unroll=4)
    buffers = (one_ref, two_ref)
    for step in range(1, FINAL):
        first = HALO - FINAL + step
        relax_rows(
            buffers[(step + 1) % 2], buffers[step % 2], ground_ref, first, 2 * HALO + height - 2 * first, ring
        )
    source, target = buffers[(FINAL + 1) % 2], buffers[FINAL % 2]
    copies = []
    for group in range(height // SUBS):
        first = HALO + group * SUBS
        relax_rows(source, target, ground_ref, first, SUBS, ring)
        for tile in range(tiles * SUBS):
            chunk, slot = tile // tiles, tile % tiles
            out_ref[pl.ds(group * SUBS, SUBS), pl.ds(tile * LANES, LANES)] = target[
                pl.ds(first * size + slot * SUBS + chunk, SUBS, stride=size), :
            ]
        where = (pl.ds(group * SUBS, SUBS), slice(None))
        copies += start_all([pltpu.make_async_copy(out_ref.at[where], out_hbm.at[where], sems.at[group])])
    wait_all(copies)


def in_vmem(count):
    return [pl.BlockSpec(memory_space=pltpu.VMEM)] * count


def in_hbm(count):
    return [pl.BlockSpec(memory_space=pltpu.HBM)] * count


def per_device(elevation, fill_depth, edge_rows, edge_sides, adjacency):
    height, width = elevation.shape
    tiles = width // (SUBS * LANES)
    groups = height // SUBS
    f32 = jnp.float32
    packed = tiles * SUBS
    size = packed + SUBS
    tile_count = adjacency.shape[0]
    places = lax.axis_size(("rows", "sub"))
    cols, subs = lax.axis_size("cols"), lax.axis_size("sub")
    short = pl.CostEstimate(flops=1024, bytes_accessed=1024, transcendentals=0)
    limit = pltpu.CompilerParams(vmem_limit_bytes=24 << 20)
    arguments = [
        pltpu.with_memory_space_constraint(value, pltpu.HBM)
        for value in (elevation, fill_depth, edge_rows, edge_sides, adjacency)
    ]
    sent = pltpu.VMEM(((2 * HALO - 1) * packed, LANES), f32)
    strip = pltpu.VMEM((2 * height, LANES), f32)
    work = pltpu.VMEM(((height + 2 * HALO) * size, LANES), f32)
    far, near, even, odd, ground, surface = pl.pallas_call(
        edge_kernel,
        out_shape=[sent, sent, strip, strip, work, work],
        in_specs=in_hbm(4),
        out_specs=in_vmem(6),
        scratch_shapes=[
            pltpu.VMEM((height, width), f32),
            pltpu.VMEM((height, width), f32),
            pltpu.VMEM(edge_rows.shape, jnp.int32),
            pltpu.VMEM(edge_sides.shape, jnp.int32),
            pltpu.SemaphoreType.DMA((2, 4 * groups)),
            pltpu.SemaphoreType.DMA((2,)),
        ],
        compiler_params=limit,
        cost_estimate=short,
        name="edge_rows",
    )(*arguments[:4])

    near_pairs, far_pairs = [matching(places, first) for first in range(2)]
    stay = [(place, place) for place in range(places)]
    ends = [(place, place) for place in range(places) if place not in dict(far_pairs)]
    groups_count = lax.axis_size("groups")
    part = places * cols
    far_all = []
    for group, other in closed(matching(groups_count, 0), groups_count):
        for chosen, target in ((far_pairs, group), (ends, other)):
            for source, arrival in cross(chosen, [(col, col) for col in range(cols)], cols, subs):
                far_all.append((group * part + source, target * part + arrival))
    device_axes = ("rows", "cols", "sub")

    def swap_strips(pieces, row_pairs):
        arrived = []
        for first, piece in enumerate(pieces):
            pairs = cross(row_pairs, matching(cols, first), cols, subs)
            arrived.append(lax.ppermute(piece, device_axes, pairs) if pairs else piece)
        return arrived

    far_strips = swap_strips((even, odd), far_pairs + ends)
    far_rows = lax.ppermute(far, ("groups",) + device_axes, far_all)
    near_rows = lax.ppermute(near, ("rows", "sub"), near_pairs)
    strips = swap_strips((even, odd), stay) + swap_strips((even, odd), near_pairs)

    def inner(*refs):
        inner_kernel(height, tiles, *refs)

    ground, surface, other, hops = pl.pallas_call(
        inner,
        out_shape=[work, work, work, pltpu.VMEM((9 * tile_count, LANES), f32)],
        in_specs=in_hbm(1) + in_vmem(7),
        out_specs=in_vmem(4),
        scratch_shapes=[pltpu.VMEM(adjacency.shape, jnp.int32), pltpu.SemaphoreType.DMA],
        input_output_aliases={6: 0, 7: 1},
        compiler_params=limit,
        cost_estimate=short,
        name="inner_passes",
    )(arguments[4], near_rows, *strips, ground, surface)

    def outer(far_ref, *refs):
        outer_kernel(height, tiles, far_ref, *refs)

    devices = lax.axis_size(device_axes)
    again = pltpu.VMEM((FINAL * size, LANES), f32)
    ground, surface, other, floors, far, near = pl.pallas_call(
        outer,
        out_shape=[work, work, work, pltpu.VMEM((devices, LANES), f32), again, again],
        in_specs=in_vmem(6),
        out_specs=in_vmem(6),
        input_output_aliases={3: 0, 4: 1, 5: 2},
        compiler_params=limit,
        cost_estimate=short,
        name="outer_passes",
    )(far_rows, *far_strips, ground, surface, other)

    far_rows = lax.ppermute(far, ("groups",) + device_axes, far_all)
    near_rows = lax.ppermute(near, ("rows", "sub"), near_pairs)
    floors = lax.all_to_all(floors, device_axes, 0, 0, tiled=True)

    def late(*refs):
        late_kernel(height, tiles, *refs)

    return pl.pallas_call(
        late,
        out_shape=jax.ShapeDtypeStruct((height, width), f32),
        in_specs=in_vmem(6),
        out_specs=pl.BlockSpec(memory_space=pltpu.HBM),
        scratch_shapes=[
            work,
            work,
            pltpu.VMEM((height, width), f32),
            pltpu.SemaphoreType.DMA((groups,)),
        ],
        compiler_params=limit,
        cost_estimate=short,
        name="final_passes",
    )(ground, surface, far_rows, near_rows, floors, hops)


def solution(mesh):
    placed = (
        P(("groups", "rows", "sub"), "cols"),
        P(("groups", "rows", "sub"), "cols"),
        P("groups", "cols"),
        P("groups", ("rows", "sub")),
        P("groups", None),
    )
    return jax.shard_map(
        per_device,
        mesh=mesh,
        in_specs=placed,
        out_specs=P(("groups", "rows", "sub"), "cols"),
        check_vma=False,
    )
```

```python
import jax
import jax.numpy as jnp
from jax import lax
from jax.experimental import pallas as pl
from jax.experimental.pallas import tpu as pltpu
from jax.sharding import PartitionSpec as P

PASSES = 8
FINAL = 4
ROUNDS = 4
HALO = PASSES
SUBS = 8
LANES = 128
AHEAD = 5

unreached = 1000000000.0
rise_step = 0.01
hop_rise = 0.05
spill_lift = 3.0


def matching(count, first):
    pairs = []
    for low in range(first, count - 1, 2):
        pairs += [(low, low + 1), (low + 1, low)]
    return pairs


def closed(pairs, count):
    used = {source for source, _ in pairs}
    return pairs + [(place, place) for place in range(count) if place not in used]


def cross(row_pairs, col_pairs, cols, subs):
    def device(place, col):
        return (place // subs * cols + col) * subs + place % subs

    return [
        (device(row, col), device(row_to, col_to))
        for row, row_to in row_pairs
        for col, col_to in col_pairs
    ]


def chain_place():
    subs = lax.axis_size("sub")
    return lax.axis_index("rows") * subs + lax.axis_index("sub"), lax.axis_size("rows") * subs


def position():
    sub = lax.broadcasted_iota(jnp.int32, (SUBS, LANES), 0)
    lane = lax.broadcasted_iota(jnp.int32, (SUBS, LANES), 1)
    return sub, lane


def aligned(start):
    return start if isinstance(start, int) else pl.multiple_of(start, SUBS)


def rows_at(first, count, size):
    return pl.ds(aligned(first * size), count * size)


def register(row, slot, size):
    return pl.ds(aligned(row * size + slot * SUBS), SUBS)


def side_marks(sides_ref):
    height = sides_ref.shape[1]
    square = (height, height)
    diagonal = lax.broadcasted_iota(jnp.int32, square, 0) == lax.broadcasted_iota(jnp.int32, square, 1)
    marks = sides_ref[...].astype(jnp.float32)
    return [
        jnp.sum(jnp.where(diagonal, marks[side : side + 1, :], 0.0), axis=1, keepdims=True)
        for side in range(2)
    ]


def start_all(copies):
    for copy in copies:
        copy.start()
    return copies


def wait_all(copies):
    for copy in copies:
        copy.wait()


def edge_kernel(
    ground_hbm, depth_hbm, rows_hbm, sides_hbm,
    far_ref, near_ref, even_ref, odd_ref, ground_out, surface_out,
    ground_ref, depth_ref, rows_ref, sides_ref, sems, small_sems,
):
    height, width = ground_hbm.shape
    tiles = width // (SUBS * LANES)
    small = [
        pltpu.make_async_copy(rows_hbm, rows_ref, small_sems.at[0]),
        pltpu.make_async_copy(sides_hbm, sides_ref, small_sems.at[1]),
    ]
    start_all(small[1:])
    copies = start_own(ground_hbm, depth_hbm, ground_ref, depth_ref, sems)
    start_all(small[:1])
    wait_all(small)
    edges = fold_own(copies, ground_ref, depth_ref, rows_ref, sides_ref, ground_out, surface_out)
    place, _ = chain_place()
    top = place % 2 == 0
    size, packed = (tiles + 1) * SUBS, tiles * SUBS
    for out_ref, is_top in ((far_ref, top), (near_ref, jnp.logical_not(top))):
        first = HALO + jnp.where(is_top, 0, height - HALO)
        bases = (jnp.where(is_top, 0, HALO - 1), jnp.where(is_top, HALO - 1, 0))
        for source, base in zip((ground_out, surface_out), bases):
            for row in range(HALO):
                for slot in range(tiles):
                    out_ref[register(base + row, slot, packed), :] = source[register(first + row, slot, size), :]
    rightward = lax.axis_index("cols") % 2 == 0
    for group, values in enumerate(edges):
        for kind in range(2):
            rows = pl.ds(kind * height + group * SUBS, SUBS)
            even_ref[rows, :] = jnp.where(rightward, values[1][kind], values[0][kind])
            odd_ref[rows, :] = jnp.where(rightward, values[0][kind], values[1][kind])


def start_own(ground_hbm, depth_hbm, ground_ref, depth_ref, sems):
    height, width = ground_hbm.shape
    groups = height // SUBS
    pieces = sems.shape[1] // groups
    part = width // pieces
    copies = []
    for group in range(groups):
        for piece in range(pieces):
            where = (pl.ds(group * SUBS, SUBS), pl.ds(piece * part, part))
            number = group * pieces + piece
            copies.append(
                start_all(
                    [
                        pltpu.make_async_copy(ground_hbm.at[where], ground_ref.at[where], sems.at[0, number]),
                        pltpu.make_async_copy(depth_hbm.at[where], depth_ref.at[where], sems.at[1, number]),
                    ]
                )
            )
    return copies


def fold_own(copies, ground_ref, depth_ref, rows_ref, sides_ref, ground_out, surface_out):
    height, width = ground_ref.shape
    groups = height // SUBS
    tiles = width // (SUBS * LANES)
    last_tile = width // LANES - 1
    pieces = len(copies) // groups
    part = width // pieces
    size = (tiles + 1) * SUBS
    place, places = chain_place()
    col, cols = lax.axis_index("cols"), lax.axis_size("cols")
    sub, lane = position()
    marks = side_marks(sides_ref)
    edges = [[] for _ in range(groups)]
    for group in range(groups):
        rows = pl.ds(group * SUBS, SUBS)
        for tile in range(last_tile + 1):
            if tile * LANES % part == 0:
                wait_all(copies[group * pieces + tile * LANES // part])
            columns = pl.ds(tile * LANES, LANES)
            ground = ground_ref[rows, columns]
            surface = ground + depth_ref[rows, columns]
            outlets = []
            if group == 0:
                outlets.append((rows_ref[0:1, columns] == 1) & (sub == 0) & (place == 0))
            if group == groups - 1:
                outlets.append(
                    (rows_ref[1:2, columns] == 1) & (sub == SUBS - 1) & (place == places - 1)
                )
            if tile == 0:
                outlets.append(
                    (marks[0][group * SUBS : (group + 1) * SUBS] > 0.5) & (lane == 0) & (col == 0)
                )
            if tile == last_tile:
                outlets.append(
                    (marks[1][group * SUBS : (group + 1) * SUBS] > 0.5)
                    & (lane == LANES - 1)
                    & (col == cols - 1)
                )
            for outlet in outlets:
                surface = jnp.where(outlet, ground, surface)
            chunk, slot = tile // tiles, tile % tiles
            start = (HALO + group * SUBS) * size + slot * SUBS + chunk
            ground_out[pl.ds(start, SUBS, stride=size), :] = ground
            surface_out[pl.ds(start, SUBS, stride=size), :] = surface
            if tile in (0, last_tile):
                edges[group].append((ground, surface))
    return edges


def strips_of(rows_ref, tiles):
    start = (2 * HALO - 1) * tiles * SUBS
    return [[(rows_ref, start + (2 * parity + kind) * HALO) for parity in range(2)] for kind in range(2)]


def append_kernel(even_ref, odd_ref, *refs):
    height = even_ref.shape[0] // 2
    place, _ = chain_place()
    top = place % 2 == 0
    for out_ref, is_top in zip(refs[2:], (top, jnp.logical_not(top))):
        tiles = (out_ref.shape[0] - 4 * HALO) // ((2 * HALO - 1) * SUBS)
        for kind, starts in enumerate(strips_of(out_ref, tiles)):
            rows = pl.ds(aligned(kind * height + jnp.where(is_top, 0, height - HALO)), HALO)
            for source, (_, start) in zip((even_ref, odd_ref), starts):
                out_ref[pl.ds(start, HALO), :] = source[rows, :]


def unpack_rows(rows_ref, first, is_top, present, ground_ref, surface_ref, tiles):
    packed = tiles * SUBS
    size = packed + SUBS
    bases = (jnp.where(is_top, HALO - 1, 0), jnp.where(is_top, 0, HALO - 1))
    for base, out_ref, strips in zip(bases, (ground_ref, surface_ref), strips_of(rows_ref, tiles)):

        def body(row, carry):
            values = [
                jnp.where(present, rows_ref[register(base + row, slot, packed), :], unreached)
                for slot in range(tiles)
            ]
            for slot in range(tiles):
                out_ref[register(first + row, slot, size), :] = values[slot]
            fill_seam(out_ref, first + row, values[0], values[-1], strips, row, present, tiles)
            return carry

        lax.fori_loop(0, HALO, body, 0, unroll=4)


def fill_seam(out_ref, row, first_tile, last_tile, strips, strip_row, present, tiles):
    col, cols = lax.axis_index("cols"), lax.axis_size("cols")
    sub, lane = position()
    rightward = col % 2 == 0
    even, odd = [ref[pl.ds(start + strip_row, 1), :] for ref, start in strips]
    after = jnp.where(present & (col < cols - 1), jnp.where(rightward, even, odd), unreached)
    before = jnp.where(present & (col > 0), jnp.where(rightward, odd, even), unreached)
    after = jnp.where(sub == SUBS - 1, after, pltpu.roll(first_tile, SUBS - 1, 0))
    before = jnp.where(sub == 0, before, pltpu.roll(last_tile, 1, 0))
    out_ref[register(row, tiles, (tiles + 1) * SUBS), :] = jnp.where(lane < LANES // 2, after, before)


def relax_rows(source, target, ground, first, count, ring):
    size = ring * SUBS
    _, lane = position()
    at_first = lane == 0
    at_last = lane == LANES - 1
    order = [ring - 1] + list(range(ring - 1))
    made = {}

    def make(pair, slot):
        row = first + 2 * pair
        values = [source[register(row + step, slot, size), :] for step in range(-1, 3)]
        both = jnp.minimum(values[1], values[2])
        for one, column in enumerate((jnp.minimum(values[0], both), jnp.minimum(both, values[3]))):
            made[pair, one, slot] = (column, pltpu.roll(column, 1, 1), pltpu.roll(column, LANES - 1, 1))

    def finish(pair, slot):
        for one in range(2):
            row = first + 2 * pair + one
            before, here, after = [made[pair, one, (slot + step) % ring] for step in (-1, 0, 1)]
            from_left = jnp.where(at_first, before[1], here[1])
            from_right = jnp.where(at_last, after[2], here[2])
            lowest = jnp.minimum(jnp.minimum(from_left, from_right), here[0])
            where = register(row, slot, size)
            raised = jnp.minimum(source[where, :], lowest + rise_step)
            target[where, :] = jnp.maximum(ground[where, :], raised)

    makes = [(pair, slot) for pair in range(count // 2) for slot in order]
    finishes = [(pair, slot) for pair in range(count // 2) for slot in range(ring)]
    done = 0
    for number, item in enumerate(makes):
        make(*item)
        if number >= AHEAD:
            finish(*finishes[done])
            done += 1
    for item in finishes[done:]:
        finish(*item)


def hop_counts(links_ref, hops_ref, needed):
    tiles, degree = links_ref.shape
    links = links_ref[...]
    number = lax.broadcasted_iota(jnp.int32, (tiles, tiles), 1)
    linked = links[:, 0:1] == number
    for edge in range(1, degree):
        linked = linked | (links[:, edge : edge + 1] == number)
    linked = linked.astype(jnp.float32)
    tile = lax.broadcasted_iota(jnp.int32, (tiles, LANES), 0)
    lane = lax.broadcasted_iota(jnp.int32, (tiles, LANES), 1)
    reached = jnp.zeros((tiles, LANES), jnp.float32)
    for index, wanted in enumerate(needed):
        reached = jnp.where((lane == index) & (tile == wanted), 1.0, reached)
    hops = jnp.where(reached > 0.5, 0.0, float(ROUNDS + 1))
    for hop in range(1, ROUNDS + 1):
        reached = lax.dot_general(
            linked, reached, (((0,), (0,)), ((), ())), preferred_element_type=jnp.float32
        )
        reached = jnp.where(reached > 0.5, 1.0, 0.0)
        hops = jnp.minimum(hops, jnp.where(reached > 0.5, float(hop), float(ROUNDS + 1)))
    for index in range(len(needed)):
        hops_ref[pl.ds(index * tiles, tiles), :] = jnp.broadcast_to(
            hops[:, index : index + 1], (tiles, LANES)
        )


def needed_tiles():
    row, rows = lax.axis_index("rows"), lax.axis_size("rows")
    col, cols = lax.axis_index("cols"), lax.axis_size("cols")
    sub, subs = lax.axis_index("sub"), lax.axis_size("sub")
    above = jnp.maximum(jnp.where(sub == 0, row - 1, row), 0)
    below = jnp.minimum(jnp.where(sub == subs - 1, row + 1, row), rows - 1)
    left = jnp.maximum(col - 1, 0)
    right = jnp.minimum(col + 1, cols - 1)
    return [r * cols + c for r in (above, row, below) for c in (left, col, right)]


def hops_kernel(links_hbm, after_ref, hops_ref, links_ref, sem):
    links = pltpu.make_async_copy(links_hbm, links_ref, sem)
    links.start()
    links.wait()
    hop_counts(links_ref, hops_ref, needed_tiles())


def inner_kernel(height, tiles, near_ref, even_ref, odd_ref, *refs):
    ground_ref, surface_ref, other_ref = refs[3:]
    ring = tiles + 1
    size = ring * SUBS
    place, places = chain_place()
    top = place % 2 == 0
    has_near = jnp.where(top, place < places - 1, place > 0)
    unpack_rows(
        near_ref,
        jnp.where(top, HALO + height, 0),
        jnp.logical_not(top),
        has_near,
        ground_ref,
        surface_ref,
        tiles,
    )
    for kind, out_ref in enumerate((ground_ref, surface_ref)):
        strips = [(ref, kind * height) for ref in (even_ref, odd_ref)]

        def body(row, carry, out_ref=out_ref, strips=strips):
            first_tile = out_ref[register(HALO + row, 0, size), :]
            last_tile = out_ref[register(HALO + row, tiles - 1, size), :]
            fill_seam(
                out_ref, HALO + row, first_tile, last_tile, strips, row, place >= 0, tiles
            )
            return carry

        lax.fori_loop(0, height, body, 0, unroll=4)
    buffers = (surface_ref, other_ref)
    for step in range(1, PASSES + 1):
        first = step + jnp.where(top, HALO, 0)
        count = height + HALO - 2 * step
        relax_rows(buffers[(step + 1) % 2], buffers[step % 2], ground_ref, first, count, ring)


def outer_kernel(height, tiles, far_ref, *refs):
    ground_ref, surface_ref, other_ref, level_ref, far_out, near_out = refs[3:9]
    ring = tiles + 1
    size = ring * SUBS
    place, places = chain_place()
    top = place % 2 == 0
    has_far = jnp.where(top, place > 0, place < places - 1)
    unpack_rows(
        far_ref,
        jnp.where(top, 0, HALO + height),
        top,
        has_far,
        ground_ref,
        surface_ref,
        tiles,
    )
    buffers = (surface_ref, other_ref)
    for step in range(1, PASSES + 1):
        first = jnp.where(top, step, HALO + height - step)
        relax_rows(buffers[(step + 1) % 2], buffers[step % 2], ground_ref, first, HALO, ring)
    low, high = HALO, HALO + height - FINAL
    for row in range(FINAL):
        for slot in range(ring):
            where = register(row, slot, size)
            far_out[where, :] = surface_ref[register(jnp.where(top, low, high) + row, slot, size), :]
            near_out[where, :] = surface_ref[register(jnp.where(top, high, low) + row, slot, size), :]
    band, bands = lax.axis_index("sub"), lax.axis_size("sub")
    sub, lane = position()

    def at(row, slot):
        return surface_ref[register(HALO + row, slot, size), :]

    first_cell = (sub == 0) & (lane == 0)
    last_cell = (sub == SUBS - 1) & (lane == LANES - 1)
    first_lows, last_lows, row_lows = [], [], []
    for row in range(height):
        first_lows.append(at(row, 0))
        last_lows.append(at(row, tiles - 1))
    for slot in range(tiles):
        row_lows.append(jnp.where(band == 0, at(0, slot), unreached))
        row_lows.append(jnp.where(band == bands - 1, at(height - 1, slot), unreached))
    lowest = jnp.minimum(
        least(row_lows),
        jnp.minimum(
            jnp.where(first_cell, least(first_lows), unreached),
            jnp.where(last_cell, least(last_lows), unreached),
        ),
    )
    lowest = jnp.min(jnp.min(lowest, axis=0, keepdims=True), axis=1, keepdims=True)
    level_ref[...] = jnp.broadcast_to(lowest, level_ref.shape)


def least(values):
    values = list(values)
    while len(values) > 1:
        values = [
            jnp.minimum(*values[number : number + 2]) if number + 1 < len(values) else values[number]
            for number in range(0, len(values), 2)
        ]
    return values[0]


def late_kernel(
    height, tiles, ground_ref, surface_ref, far_ref, near_ref, floors_ref, hops_ref, out_hbm,
    one_ref, two_ref, out_ref, sems,
):
    ring = tiles + 1
    size = ring * SUBS
    sub, lane = position()
    bands = lax.axis_size("sub")
    count = floors_ref.shape[0] // bands
    level = least(floors_ref[pl.ds(band, count, stride=bands), :] for band in range(bands))
    raised = [level]
    for hop in range(ROUNDS):
        raised.append(raised[-1] + hop_rise)
    ceilings = []
    for index in range(9):
        hops = hops_ref[pl.ds(index * count, count), :]
        lowest = jnp.full((count, LANES), unreached, jnp.float32)
        for hop in range(ROUNDS + 1):
            lowest = jnp.where(hops == float(hop), raised[hop], lowest)
        lowest = jnp.min(lowest, axis=0, keepdims=True) + spill_lift
        ceilings.append(jnp.broadcast_to(lowest, (SUBS, LANES)))
    pairs = []
    for region in range(3):
        left, middle, right = ceilings[3 * region : 3 * region + 3]
        seam = jnp.where(
            lane < LANES // 2,
            jnp.where(sub == SUBS - 1, right, middle),
            jnp.where(sub == 0, left, middle),
        )
        pairs.append((middle, seam))
    place, _ = chain_place()
    top = place % 2 == 0
    low, high = HALO - FINAL, HALO + height
    far_pair = [jnp.where(top, above, below) for above, below in zip(pairs[0], pairs[2])]
    near_pair = [jnp.where(top, below, above) for above, below in zip(pairs[0], pairs[2])]
    spans = (
        (surface_ref, HALO, HALO, height, pairs[1]),
        (near_ref, 0, jnp.where(top, high, low), FINAL, near_pair),
        (far_ref, 0, jnp.where(top, low, high), FINAL, far_pair),
    )
    for source, source_first, first, rows, (middle, seam) in spans:

        def body(row, carry):
            for slot in range(ring):
                value = source[register(source_first + row, slot, size), :]
                value = jnp.minimum(value, seam if slot == tiles else middle)
                where = register(first + row, slot, size)
                one_ref[where, :] = jnp.maximum(ground_ref[where, :], value)
            return carry

        lax.fori_loop(0, rows, body, 0, unroll=4)
    buffers = (one_ref, two_ref)
    for step in range(1, FINAL):
        first = HALO - FINAL + step
        relax_rows(
            buffers[(step + 1) % 2], buffers[step % 2], ground_ref, first, 2 * HALO + height - 2 * first, ring
        )
    source, target = buffers[(FINAL + 1) % 2], buffers[FINAL % 2]
    copies = []
    for group in range(height // SUBS):
        first = HALO + group * SUBS
        relax_rows(source, target, ground_ref, first, SUBS, ring)
        for tile in range(tiles * SUBS):
            chunk, slot = tile // tiles, tile % tiles
            out_ref[pl.ds(group * SUBS, SUBS), pl.ds(tile * LANES, LANES)] = target[
                pl.ds(first * size + slot * SUBS + chunk, SUBS, stride=size), :
            ]
        where = (pl.ds(group * SUBS, SUBS), slice(None))
        copies += start_all([pltpu.make_async_copy(out_ref.at[where], out_hbm.at[where], sems.at[group])])
    wait_all(copies)


def in_vmem(count):
    return [pl.BlockSpec(memory_space=pltpu.VMEM)] * count


def in_hbm(count):
    return [pl.BlockSpec(memory_space=pltpu.HBM)] * count


def per_device(elevation, fill_depth, edge_rows, edge_sides, adjacency):
    height, width = elevation.shape
    tiles = width // (SUBS * LANES)
    groups = height // SUBS
    f32 = jnp.float32
    packed = tiles * SUBS
    size = packed + SUBS
    tile_count = adjacency.shape[0]
    places = lax.axis_size(("rows", "sub"))
    cols, subs = lax.axis_size("cols"), lax.axis_size("sub")
    short = pl.CostEstimate(flops=1024, bytes_accessed=1024, transcendentals=0)
    limit = pltpu.CompilerParams(vmem_limit_bytes=24 << 20)
    arguments = [
        pltpu.with_memory_space_constraint(value, pltpu.HBM)
        for value in (elevation, fill_depth, edge_rows, edge_sides, adjacency)
    ]
    sent = pltpu.VMEM(((2 * HALO - 1) * packed + 4 * HALO, LANES), f32)
    strip = pltpu.VMEM((2 * height, LANES), f32)
    work = pltpu.VMEM(((height + 2 * HALO) * size, LANES), f32)
    far, near, even, odd, ground, surface = pl.pallas_call(
        edge_kernel,
        out_shape=[sent, sent, strip, strip, work, work],
        in_specs=in_hbm(4),
        out_specs=in_vmem(6),
        scratch_shapes=[
            pltpu.VMEM((height, width), f32),
            pltpu.VMEM((height, width), f32),
            pltpu.VMEM(edge_rows.shape, jnp.int32),
            pltpu.VMEM(edge_sides.shape, jnp.int32),
            pltpu.SemaphoreType.DMA((2, 4 * groups)),
            pltpu.SemaphoreType.DMA((2,)),
        ],
        compiler_params=limit,
        cost_estimate=short,
        name="edge_rows",
    )(*arguments[:4])

    near_pairs, far_pairs = [matching(places, first) for first in range(2)]
    ends = [(place, place) for place in range(places) if place not in dict(far_pairs)]
    groups_count = lax.axis_size("groups")
    part = places * cols
    far_all = []
    for group, other in closed(matching(groups_count, 0), groups_count):
        for chosen, target in ((far_pairs, group), (ends, other)):
            for source, arrival in cross(chosen, [(col, col) for col in range(cols)], cols, subs):
                far_all.append((group * part + source, target * part + arrival))
    device_axes = ("rows", "cols", "sub")

    strips = []
    for first, piece in enumerate((even, odd)):
        pairs = matching(cols, first)
        strips.append(lax.ppermute(piece, "cols", pairs) if pairs else piece)
    far, near = pl.pallas_call(
        append_kernel,
        out_shape=[sent, sent],
        in_specs=in_vmem(4),
        out_specs=in_vmem(2),
        input_output_aliases={2: 0, 3: 1},
        compiler_params=limit,
        cost_estimate=short,
        name="append_strips",
    )(*strips, far, near)
    far_rows = lax.ppermute(far, ("groups",) + device_axes, far_all)
    near_rows = lax.ppermute(near, ("rows", "sub"), near_pairs)
    hops = pl.pallas_call(
        hops_kernel,
        out_shape=pltpu.VMEM((9 * tile_count, LANES), f32),
        in_specs=in_hbm(1) + in_vmem(1),
        out_specs=pl.BlockSpec(memory_space=pltpu.VMEM),
        scratch_shapes=[pltpu.VMEM(adjacency.shape, jnp.int32), pltpu.SemaphoreType.DMA],
        compiler_params=limit,
        cost_estimate=short,
        name="tile_hops",
    )(arguments[4], even)

    def inner(*refs):
        inner_kernel(height, tiles, *refs)

    ground, surface, other = pl.pallas_call(
        inner,
        out_shape=[work, work, work],
        in_specs=in_vmem(6),
        out_specs=in_vmem(3),
        input_output_aliases={3: 0, 4: 1},
        compiler_params=limit,
        cost_estimate=short,
        name="inner_passes",
    )(near_rows, *strips, ground, surface, hops)

    def outer(far_ref, *refs):
        outer_kernel(height, tiles, far_ref, *refs)

    devices = lax.axis_size(device_axes)
    again = pltpu.VMEM((FINAL * size, LANES), f32)
    ground, surface, other, floors, far, near = pl.pallas_call(
        outer,
        out_shape=[work, work, work, pltpu.VMEM((devices, LANES), f32), again, again],
        in_specs=in_vmem(4),
        out_specs=in_vmem(6),
        input_output_aliases={1: 0, 2: 1, 3: 2},
        compiler_params=limit,
        cost_estimate=short,
        name="outer_passes",
    )(far_rows, ground, surface, other)

    far_rows = lax.ppermute(far, ("groups",) + device_axes, far_all)
    near_rows = lax.ppermute(near, ("rows", "sub"), near_pairs)
    floors = lax.all_to_all(floors, device_axes, 0, 0, tiled=True)

    def late(*refs):
        late_kernel(height, tiles, *refs)

    return pl.pallas_call(
        late,
        out_shape=jax.ShapeDtypeStruct((height, width), f32),
        in_specs=in_vmem(6),
        out_specs=pl.BlockSpec(memory_space=pltpu.HBM),
        scratch_shapes=[
            work,
            work,
            pltpu.VMEM((height, width), f32),
            pltpu.SemaphoreType.DMA((groups,)),
        ],
        compiler_params=limit,
        cost_estimate=short,
        name="final_passes",
    )(ground, surface, far_rows, near_rows, floors, hops)


def solution(mesh):
    placed = (
        P(("groups", "rows", "sub"), "cols"),
        P(("groups", "rows", "sub"), "cols"),
        P("groups", "cols"),
        P("groups", ("rows", "sub")),
        P("groups", None),
    )
    return jax.shard_map(
        per_device,
        mesh=mesh,
        in_specs=placed,
        out_specs=P(("groups", "rows", "sub"), "cols"),
        check_vma=False,
    )
```

```python
import functools

import jax
import jax.numpy as jnp
from jax import lax
from jax.experimental import pallas as pl
from jax.experimental.pallas import tpu as pltpu
from jax.sharding import PartitionSpec as P

PASSES = 8
FINAL = 4
ROUNDS = 4
HALO = PASSES
SUBS = 8
LANES = 128
AHEAD = 5

unreached = 1000000000.0
rise_step = 0.01
hop_rise = 0.05
spill_lift = 3.0


def matching(count, first):
    pairs = []
    for low in range(first, count - 1, 2):
        pairs += [(low, low + 1), (low + 1, low)]
    return pairs


def closed(pairs, count):
    used = {source for source, _ in pairs}
    return pairs + [(place, place) for place in range(count) if place not in used]


def cross(row_pairs, col_pairs, cols, subs):
    def device(place, col):
        return (place // subs * cols + col) * subs + place % subs

    return [
        (device(row, col), device(row_to, col_to))
        for row, row_to in row_pairs
        for col, col_to in col_pairs
    ]


def chain_place():
    subs = lax.axis_size("sub")
    return lax.axis_index("rows") * subs + lax.axis_index("sub"), lax.axis_size("rows") * subs


def position():
    sub = lax.broadcasted_iota(jnp.int32, (SUBS, LANES), 0)
    lane = lax.broadcasted_iota(jnp.int32, (SUBS, LANES), 1)
    return sub, lane


def aligned(start):
    return start if isinstance(start, int) else pl.multiple_of(start, SUBS)


def rows_at(first, count, size):
    return pl.ds(aligned(first * size), count * size)


def register(row, slot, size):
    return pl.ds(aligned(row * size + slot * SUBS), SUBS)


def side_marks(sides_ref):
    height = sides_ref.shape[1]
    square = (height, height)
    diagonal = lax.broadcasted_iota(jnp.int32, square, 0) == lax.broadcasted_iota(jnp.int32, square, 1)
    marks = sides_ref[...].astype(jnp.float32)
    return [
        jnp.sum(jnp.where(diagonal, marks[side : side + 1, :], 0.0), axis=1, keepdims=True)
        for side in range(2)
    ]


def start_all(copies):
    for copy in copies:
        copy.start()
    return copies


def wait_all(copies):
    for copy in copies:
        copy.wait()


def edge_kernel(
    ground_hbm, depth_hbm, rows_hbm, sides_hbm, links_hbm,
    far_ref, near_ref, even_ref, odd_ref, ground_out, surface_out, links_ref,
    ground_ref, depth_ref, rows_ref, sides_ref, sems, small_sems,
):
    height, width = ground_hbm.shape
    tiles = width // (SUBS * LANES)
    small = [
        pltpu.make_async_copy(rows_hbm, rows_ref, small_sems.at[0]),
        pltpu.make_async_copy(sides_hbm, sides_ref, small_sems.at[1]),
        pltpu.make_async_copy(links_hbm, links_ref, small_sems.at[2]),
    ]
    start_all(small[1:])
    copies = start_own(ground_hbm, depth_hbm, ground_ref, depth_ref, sems)
    start_all(small[:1])
    wait_all(small)
    edges = fold_own(copies, ground_ref, depth_ref, rows_ref, sides_ref, ground_out, surface_out)
    place, _ = chain_place()
    top = place % 2 == 0
    size, packed = (tiles + 1) * SUBS, tiles * SUBS
    for out_ref, is_top in ((far_ref, top), (near_ref, jnp.logical_not(top))):
        first = HALO + jnp.where(is_top, 0, height - HALO)
        bases = (jnp.where(is_top, 0, HALO - 1), jnp.where(is_top, HALO - 1, 0))
        for source, base in zip((ground_out, surface_out), bases):
            for row in range(HALO):
                for slot in range(tiles):
                    out_ref[register(base + row, slot, packed), :] = source[register(first + row, slot, size), :]
    rightward = lax.axis_index("cols") % 2 == 0
    for group, values in enumerate(edges):
        for kind in range(2):
            rows = pl.ds(kind * height + group * SUBS, SUBS)
            even_ref[rows, :] = jnp.where(rightward, values[1][kind], values[0][kind])
            odd_ref[rows, :] = jnp.where(rightward, values[0][kind], values[1][kind])


def start_own(ground_hbm, depth_hbm, ground_ref, depth_ref, sems):
    height, width = ground_hbm.shape
    groups = height // SUBS
    pieces = sems.shape[1] // groups
    part = width // pieces
    copies = []
    for group in range(groups):
        for piece in range(pieces):
            where = (pl.ds(group * SUBS, SUBS), pl.ds(piece * part, part))
            number = group * pieces + piece
            copies.append(
                start_all(
                    [
                        pltpu.make_async_copy(ground_hbm.at[where], ground_ref.at[where], sems.at[0, number]),
                        pltpu.make_async_copy(depth_hbm.at[where], depth_ref.at[where], sems.at[1, number]),
                    ]
                )
            )
    return copies


def fold_own(copies, ground_ref, depth_ref, rows_ref, sides_ref, ground_out, surface_out):
    height, width = ground_ref.shape
    groups = height // SUBS
    tiles = width // (SUBS * LANES)
    last_tile = width // LANES - 1
    pieces = len(copies) // groups
    part = width // pieces
    size = (tiles + 1) * SUBS
    place, places = chain_place()
    col, cols = lax.axis_index("cols"), lax.axis_size("cols")
    sub, lane = position()
    marks = side_marks(sides_ref)
    edges = [[] for _ in range(groups)]
    for group in range(groups):
        rows = pl.ds(group * SUBS, SUBS)
        for tile in range(last_tile + 1):
            if tile * LANES % part == 0:
                wait_all(copies[group * pieces + tile * LANES // part])
            columns = pl.ds(tile * LANES, LANES)
            ground = ground_ref[rows, columns]
            surface = ground + depth_ref[rows, columns]
            outlets = []
            if group == 0:
                outlets.append((rows_ref[0:1, columns] == 1) & (sub == 0) & (place == 0))
            if group == groups - 1:
                outlets.append(
                    (rows_ref[1:2, columns] == 1) & (sub == SUBS - 1) & (place == places - 1)
                )
            if tile == 0:
                outlets.append(
                    (marks[0][group * SUBS : (group + 1) * SUBS] > 0.5) & (lane == 0) & (col == 0)
                )
            if tile == last_tile:
                outlets.append(
                    (marks[1][group * SUBS : (group + 1) * SUBS] > 0.5)
                    & (lane == LANES - 1)
                    & (col == cols - 1)
                )
            for outlet in outlets:
                surface = jnp.where(outlet, ground, surface)
            chunk, slot = tile // tiles, tile % tiles
            start = (HALO + group * SUBS) * size + slot * SUBS + chunk
            ground_out[pl.ds(start, SUBS, stride=size), :] = ground
            surface_out[pl.ds(start, SUBS, stride=size), :] = surface
            if tile in (0, last_tile):
                edges[group].append((ground, surface))
    return edges


def unpack_rows(rows_ref, first, is_top, present, strip_refs, strip_rows, ground_ref, surface_ref, tiles):
    packed = tiles * SUBS
    size = packed + SUBS
    bases = (jnp.where(is_top, HALO - 1, 0), jnp.where(is_top, 0, HALO - 1))
    for base, out_ref, strip_row in zip(bases, (ground_ref, surface_ref), strip_rows):

        def body(row, carry):
            values = [
                jnp.where(present, rows_ref[register(base + row, slot, packed), :], unreached)
                for slot in range(tiles)
            ]
            for slot in range(tiles):
                out_ref[register(first + row, slot, size), :] = values[slot]
            fill_seam(out_ref, first + row, values[0], values[-1], strip_refs, strip_row + row, present, tiles)
            return carry

        lax.fori_loop(0, HALO, body, 0, unroll=4)


def fill_seam(out_ref, row, first_tile, last_tile, strip_refs, strip_row, present, tiles):
    col, cols = lax.axis_index("cols"), lax.axis_size("cols")
    sub, lane = position()
    rightward = col % 2 == 0
    even, odd = [ref[pl.ds(strip_row, 1), :] for ref in strip_refs]
    after = jnp.where(present & (col < cols - 1), jnp.where(rightward, even, odd), unreached)
    before = jnp.where(present & (col > 0), jnp.where(rightward, odd, even), unreached)
    after = jnp.where(sub == SUBS - 1, after, pltpu.roll(first_tile, SUBS - 1, 0))
    before = jnp.where(sub == 0, before, pltpu.roll(last_tile, 1, 0))
    out_ref[register(row, tiles, (tiles + 1) * SUBS), :] = jnp.where(lane < LANES // 2, after, before)


def relax_passes(passes, ground, ring):
    size = ring * SUBS
    _, lane = position()
    at_first = lane == 0
    at_last = lane == LANES - 1
    order = [ring - 1] + list(range(ring - 1))
    made = {}

    def make(number, pair, slot):
        source, _, first, _, _ = passes[number]
        row = first + 2 * pair
        values = [source[register(row + step, slot, size), :] for step in range(-1, 3)]
        both = jnp.minimum(values[1], values[2])
        for one, column in enumerate((jnp.minimum(values[0], both), jnp.minimum(both, values[3]))):
            rolled = pltpu.roll(column, 1, 1), pltpu.roll(column, LANES - 1, 1)
            made[number, pair, one, slot] = (column, *rolled)

    def finish(number, pair, slot):
        source, target, first, _, _ = passes[number]
        for one in range(2):
            row = first + 2 * pair + one
            before, here, after = [made[number, pair, one, (slot + step) % ring] for step in (-1, 0, 1)]
            from_left = jnp.where(at_first, before[1], here[1])
            from_right = jnp.where(at_last, after[2], here[2])
            lowest = jnp.minimum(jnp.minimum(from_left, from_right), here[0])
            where = register(row, slot, size)
            raised = jnp.minimum(source[where, :], lowest + rise_step)
            target[where, :] = jnp.maximum(ground[where, :], raised)

    def items(slots):
        return [
            (number, pair, slot)
            for number, (_, _, _, count, _) in enumerate(passes)
            for pair in range(count // 2)
            for slot in slots
        ]

    makes, finishes = items(order), items(range(ring))
    for number in range(len(makes) + AHEAD):
        if number < len(makes):
            make(*makes[number])
        if number >= AHEAD:
            done = finishes[number - AHEAD]
            finish(*done)
            _, _, _, count, then = passes[done[0]]
            if then is not None and done[1:] == (count // 2 - 1, ring - 1):
                then()


def hop_counts(links_ref, hops_ref, needed):
    tiles, degree = links_ref.shape
    links = links_ref[...]
    number = lax.broadcasted_iota(jnp.int32, (tiles, tiles), 1)
    linked = links[:, 0:1] == number
    for edge in range(1, degree):
        linked = linked | (links[:, edge : edge + 1] == number)
    linked = linked.astype(jnp.float32)
    tile = lax.broadcasted_iota(jnp.int32, (tiles, LANES), 0)
    lane = lax.broadcasted_iota(jnp.int32, (tiles, LANES), 1)
    reached = jnp.zeros((tiles, LANES), jnp.float32)
    for index, wanted in enumerate(needed):
        reached = jnp.where((lane == index) & (tile == wanted), 1.0, reached)
    hops = jnp.where(reached > 0.5, 0.0, float(ROUNDS + 1))
    for hop in range(1, ROUNDS + 1):
        reached = lax.dot_general(
            linked, reached, (((0,), (0,)), ((), ())), preferred_element_type=jnp.float32
        )
        reached = jnp.where(reached > 0.5, 1.0, 0.0)
        hops = jnp.minimum(hops, jnp.where(reached > 0.5, float(hop), float(ROUNDS + 1)))
    for index in range(len(needed)):
        hops_ref[pl.ds(index * tiles, tiles), :] = jnp.broadcast_to(
            hops[:, index : index + 1], (tiles, LANES)
        )


def needed_tiles():
    row, rows = lax.axis_index("rows"), lax.axis_size("rows")
    col, cols = lax.axis_index("cols"), lax.axis_size("cols")
    sub, subs = lax.axis_index("sub"), lax.axis_size("sub")
    above = jnp.maximum(jnp.where(sub == 0, row - 1, row), 0)
    below = jnp.minimum(jnp.where(sub == subs - 1, row + 1, row), rows - 1)
    left = jnp.maximum(col - 1, 0)
    right = jnp.minimum(col + 1, cols - 1)
    return [r * cols + c for r in (above, row, below) for c in (left, col, right)]


def hops_kernel(links_ref, hops_ref):
    hop_counts(links_ref, hops_ref, needed_tiles())


def inner_kernel(height, tiles, near_ref, own_even_ref, own_odd_ref, near_even_ref, near_odd_ref, *refs):
    ground_ref, surface_ref, other_ref = refs[3:]
    own_strips, near_strips = (own_even_ref, own_odd_ref), (near_even_ref, near_odd_ref)
    ring = tiles + 1
    size = ring * SUBS
    place, places = chain_place()
    top = place % 2 == 0
    has_near = jnp.where(top, place < places - 1, place > 0)
    unpack_rows(
        near_ref,
        jnp.where(top, HALO + height, 0),
        jnp.logical_not(top),
        has_near,
        near_strips,
        [kind * height + jnp.where(top, 0, height - HALO) for kind in range(2)],
        ground_ref,
        surface_ref,
        tiles,
    )
    for kind, out_ref in enumerate((ground_ref, surface_ref)):

        def body(row, carry):
            first_tile = out_ref[register(HALO + row, 0, size), :]
            last_tile = out_ref[register(HALO + row, tiles - 1, size), :]
            fill_seam(
                out_ref, HALO + row, first_tile, last_tile, own_strips, kind * height + row, place >= 0, tiles
            )
            return carry

        lax.fori_loop(0, height, body, 0, unroll=4)
    buffers = (surface_ref, other_ref)
    passes = []
    for step in range(1, PASSES + 1):
        first = step + jnp.where(top, HALO, 0)
        passes.append((buffers[(step + 1) % 2], buffers[step % 2], first, height + HALO - 2 * step, None))
    relax_passes(passes, ground_ref, ring)


def outer_kernel(height, tiles, far_ref, even_ref, odd_ref, *refs):
    ground_ref, surface_ref, other_ref, level_ref, far_out, near_out = refs[3:9]
    ring = tiles + 1
    size = ring * SUBS
    place, places = chain_place()
    top = place % 2 == 0
    has_far = jnp.where(top, place > 0, place < places - 1)
    unpack_rows(
        far_ref,
        jnp.where(top, 0, HALO + height),
        top,
        has_far,
        (even_ref, odd_ref),
        [kind * height + jnp.where(top, height - HALO, 0) for kind in range(2)],
        ground_ref,
        surface_ref,
        tiles,
    )
    buffers = (surface_ref, other_ref)
    passes = []
    for step in range(1, PASSES + 1):
        first = jnp.where(top, step, HALO + height - step)
        passes.append((buffers[(step + 1) % 2], buffers[step % 2], first, HALO, None))
    relax_passes(passes, ground_ref, ring)
    low, high = HALO, HALO + height - FINAL
    for row in range(FINAL):
        for slot in range(ring):
            where = register(row, slot, size)
            far_out[where, :] = surface_ref[register(jnp.where(top, low, high) + row, slot, size), :]
            near_out[where, :] = surface_ref[register(jnp.where(top, high, low) + row, slot, size), :]
    band, bands = lax.axis_index("sub"), lax.axis_size("sub")
    sub, lane = position()

    def at(row, slot):
        return surface_ref[register(HALO + row, slot, size), :]

    first_cell = (sub == 0) & (lane == 0)
    last_cell = (sub == SUBS - 1) & (lane == LANES - 1)
    first_lows, last_lows, row_lows = [], [], []
    for row in range(height):
        first_lows.append(at(row, 0))
        last_lows.append(at(row, tiles - 1))
    for slot in range(tiles):
        row_lows.append(jnp.where(band == 0, at(0, slot), unreached))
        row_lows.append(jnp.where(band == bands - 1, at(height - 1, slot), unreached))
    lowest = jnp.minimum(
        least(row_lows),
        jnp.minimum(
            jnp.where(first_cell, least(first_lows), unreached),
            jnp.where(last_cell, least(last_lows), unreached),
        ),
    )
    lowest = jnp.min(jnp.min(lowest, axis=0, keepdims=True), axis=1, keepdims=True)
    level_ref[...] = jnp.broadcast_to(lowest, level_ref.shape)


def least(values):
    values = list(values)
    while len(values) > 1:
        values = [
            jnp.minimum(*values[number : number + 2]) if number + 1 < len(values) else values[number]
            for number in range(0, len(values), 2)
        ]
    return values[0]


def late_kernel(
    height, tiles, ground_ref, surface_ref, far_ref, near_ref, floors_ref, hops_ref, out_hbm,
    one_ref, two_ref, out_ref, sems,
):
    ring = tiles + 1
    size = ring * SUBS
    sub, lane = position()
    bands = lax.axis_size("sub")
    count = floors_ref.shape[0] // bands
    level = least(floors_ref[pl.ds(band, count, stride=bands), :] for band in range(bands))
    raised = [level]
    for hop in range(ROUNDS):
        raised.append(raised[-1] + hop_rise)
    ceilings = []
    for index in range(9):
        hops = hops_ref[pl.ds(index * count, count), :]
        lowest = jnp.full((count, LANES), unreached, jnp.float32)
        for hop in range(ROUNDS + 1):
            lowest = jnp.where(hops == float(hop), raised[hop], lowest)
        lowest = jnp.min(lowest, axis=0, keepdims=True) + spill_lift
        ceilings.append(jnp.broadcast_to(lowest, (SUBS, LANES)))
    pairs = []
    for region in range(3):
        left, middle, right = ceilings[3 * region : 3 * region + 3]
        seam = jnp.where(
            lane < LANES // 2,
            jnp.where(sub == SUBS - 1, right, middle),
            jnp.where(sub == 0, left, middle),
        )
        pairs.append((middle, seam))
    place, _ = chain_place()
    top = place % 2 == 0
    low, high = HALO - FINAL, HALO + height
    far_pair = [jnp.where(top, above, below) for above, below in zip(pairs[0], pairs[2])]
    near_pair = [jnp.where(top, below, above) for above, below in zip(pairs[0], pairs[2])]
    spans = (
        (surface_ref, HALO, HALO, height, pairs[1]),
        (near_ref, 0, jnp.where(top, high, low), FINAL, near_pair),
        (far_ref, 0, jnp.where(top, low, high), FINAL, far_pair),
    )
    for source, source_first, first, rows, (middle, seam) in spans:

        def body(row, carry):
            for slot in range(ring):
                value = source[register(source_first + row, slot, size), :]
                value = jnp.minimum(value, seam if slot == tiles else middle)
                where = register(first + row, slot, size)
                one_ref[where, :] = jnp.maximum(ground_ref[where, :], value)
            return carry

        lax.fori_loop(0, rows, body, 0, unroll=4)
    buffers = (one_ref, two_ref)
    passes = []
    for step in range(1, FINAL):
        first = HALO - FINAL + step
        count = 2 * HALO + height - 2 * first
        passes.append((buffers[(step + 1) % 2], buffers[step % 2], first, count, None))
    source, target = buffers[(FINAL + 1) % 2], buffers[FINAL % 2]
    copies = []

    def unfold(group):
        first = HALO + group * SUBS
        for tile in range(tiles * SUBS):
            chunk, slot = tile // tiles, tile % tiles
            out_ref[pl.ds(group * SUBS, SUBS), pl.ds(tile * LANES, LANES)] = target[
                pl.ds(first * size + slot * SUBS + chunk, SUBS, stride=size), :
            ]
        where = (pl.ds(group * SUBS, SUBS), slice(None))
        copies.extend(start_all([pltpu.make_async_copy(out_ref.at[where], out_hbm.at[where], sems.at[group])]))

    for group in range(height // SUBS):
        first = HALO + group * SUBS
        passes.append((source, target, first, SUBS, functools.partial(unfold, group)))
    relax_passes(passes, ground_ref, ring)
    wait_all(copies)


def in_vmem(count):
    return [pl.BlockSpec(memory_space=pltpu.VMEM)] * count


def in_hbm(count):
    return [pl.BlockSpec(memory_space=pltpu.HBM)] * count


def per_device(elevation, fill_depth, edge_rows, edge_sides, adjacency):
    height, width = elevation.shape
    tiles = width // (SUBS * LANES)
    groups = height // SUBS
    f32 = jnp.float32
    packed = tiles * SUBS
    size = packed + SUBS
    tile_count = adjacency.shape[0]
    places = lax.axis_size(("rows", "sub"))
    cols, subs = lax.axis_size("cols"), lax.axis_size("sub")
    short = pl.CostEstimate(flops=1024, bytes_accessed=1024, transcendentals=0)
    limit = pltpu.CompilerParams(vmem_limit_bytes=24 << 20)
    arguments = [
        pltpu.with_memory_space_constraint(value, pltpu.HBM)
        for value in (elevation, fill_depth, edge_rows, edge_sides, adjacency)
    ]
    sent = pltpu.VMEM(((2 * HALO - 1) * packed, LANES), f32)
    strip = pltpu.VMEM((2 * height, LANES), f32)
    work = pltpu.VMEM(((height + 2 * HALO) * size, LANES), f32)
    far, near, even, odd, ground, surface, links = pl.pallas_call(
        edge_kernel,
        out_shape=[sent, sent, strip, strip, work, work, pltpu.VMEM(adjacency.shape, jnp.int32)],
        in_specs=in_hbm(5),
        out_specs=in_vmem(7),
        scratch_shapes=[
            pltpu.VMEM((height, width), f32),
            pltpu.VMEM((height, width), f32),
            pltpu.VMEM(edge_rows.shape, jnp.int32),
            pltpu.VMEM(edge_sides.shape, jnp.int32),
            pltpu.SemaphoreType.DMA((2, 4 * groups)),
            pltpu.SemaphoreType.DMA((3,)),
        ],
        compiler_params=limit,
        cost_estimate=short,
        name="edge_rows",
    )(*arguments)

    near_pairs, far_pairs = [matching(places, first) for first in range(2)]
    stay = [(place, place) for place in range(places)]
    ends = [(place, place) for place in range(places) if place not in dict(far_pairs)]
    groups_count = lax.axis_size("groups")
    part = places * cols
    far_all = []
    for group, other in closed(matching(groups_count, 0), groups_count):
        for chosen, target in ((far_pairs, group), (ends, other)):
            for source, arrival in cross(chosen, [(col, col) for col in range(cols)], cols, subs):
                far_all.append((group * part + source, target * part + arrival))
    device_axes = ("rows", "cols", "sub")

    def swap_strips(pieces, row_pairs):
        arrived = []
        for first, piece in enumerate(pieces):
            pairs = cross(row_pairs, matching(cols, first), cols, subs)
            arrived.append(lax.ppermute(piece, device_axes, pairs) if pairs else piece)
        return arrived

    far_strips = swap_strips((even, odd), far_pairs + ends)
    far_rows = lax.ppermute(far, ("groups",) + device_axes, far_all)
    near_rows = lax.ppermute(near, ("rows", "sub"), near_pairs)
    strips = swap_strips((even, odd), stay) + swap_strips((even, odd), near_pairs)

    hops = pl.pallas_call(
        hops_kernel,
        out_shape=pltpu.VMEM((9 * tile_count, LANES), f32),
        in_specs=in_vmem(1),
        out_specs=pl.BlockSpec(memory_space=pltpu.VMEM),
        compiler_params=limit,
        cost_estimate=short,
        name="tile_hops",
    )(links)

    def inner(*refs):
        inner_kernel(height, tiles, *refs)

    ground, surface, other = pl.pallas_call(
        inner,
        out_shape=[work, work, work],
        in_specs=in_vmem(8),
        out_specs=in_vmem(3),
        input_output_aliases={5: 0, 6: 1},
        compiler_params=limit,
        cost_estimate=short,
        name="inner_passes",
    )(near_rows, *strips, ground, surface, hops)

    def outer(far_ref, *refs):
        outer_kernel(height, tiles, far_ref, *refs)

    devices = lax.axis_size(device_axes)
    again = pltpu.VMEM((FINAL * size, LANES), f32)
    ground, surface, other, floors, far, near = pl.pallas_call(
        outer,
        out_shape=[work, work, work, pltpu.VMEM((devices, LANES), f32), again, again],
        in_specs=in_vmem(6),
        out_specs=in_vmem(6),
        input_output_aliases={3: 0, 4: 1, 5: 2},
        compiler_params=limit,
        cost_estimate=short,
        name="outer_passes",
    )(far_rows, *far_strips, ground, surface, other)

    far_rows = lax.ppermute(far, ("groups",) + device_axes, far_all)
    near_rows = lax.ppermute(near, ("rows", "sub"), near_pairs)
    floors = lax.all_to_all(floors, device_axes, 0, 0, tiled=True)

    def late(*refs):
        late_kernel(height, tiles, *refs)

    return pl.pallas_call(
        late,
        out_shape=jax.ShapeDtypeStruct((height, width), f32),
        in_specs=in_vmem(6),
        out_specs=pl.BlockSpec(memory_space=pltpu.HBM),
        scratch_shapes=[
            work,
            work,
            pltpu.VMEM((height, width), f32),
            pltpu.SemaphoreType.DMA((groups,)),
        ],
        compiler_params=limit,
        cost_estimate=short,
        name="final_passes",
    )(ground, surface, far_rows, near_rows, floors, hops)


def solution(mesh):
    placed = (
        P(("groups", "rows", "sub"), "cols"),
        P(("groups", "rows", "sub"), "cols"),
        P("groups", "cols"),
        P("groups", ("rows", "sub")),
        P("groups", None),
    )
    return jax.shard_map(
        per_device,
        mesh=mesh,
        in_specs=placed,
        out_specs=P(("groups", "rows", "sub"), "cols"),
        check_vma=False,
    )
```

```python
import functools

import jax
import jax.numpy as jnp
from jax import lax
from jax.experimental import pallas as pl
from jax.experimental.pallas import tpu as pltpu
from jax.sharding import PartitionSpec as P

PASSES = 8
FINAL = 4
ROUNDS = 4
HALO = PASSES
SUBS = 8
LANES = 128
AHEAD = 5

unreached = 1000000000.0
rise_step = 0.01
hop_rise = 0.05
spill_lift = 3.0


def matching(count, first):
    pairs = []
    for low in range(first, count - 1, 2):
        pairs += [(low, low + 1), (low + 1, low)]
    return pairs


def closed(pairs, count):
    used = {source for source, _ in pairs}
    return pairs + [(place, place) for place in range(count) if place not in used]


def cross(row_pairs, col_pairs, cols, subs):
    def device(place, col):
        return (place // subs * cols + col) * subs + place % subs

    return [
        (device(row, col), device(row_to, col_to))
        for row, row_to in row_pairs
        for col, col_to in col_pairs
    ]


def chain_place():
    subs = lax.axis_size("sub")
    return lax.axis_index("rows") * subs + lax.axis_index("sub"), lax.axis_size("rows") * subs


def position():
    sub = lax.broadcasted_iota(jnp.int32, (SUBS, LANES), 0)
    lane = lax.broadcasted_iota(jnp.int32, (SUBS, LANES), 1)
    return sub, lane


def aligned(start):
    return start if isinstance(start, int) else pl.multiple_of(start, SUBS)


def rows_at(first, count, size):
    return pl.ds(aligned(first * size), count * size)


def register(row, slot, size):
    return pl.ds(aligned(row * size + slot * SUBS), SUBS)


def side_marks(sides_ref):
    height = sides_ref.shape[1]
    square = (height, height)
    diagonal = lax.broadcasted_iota(jnp.int32, square, 0) == lax.broadcasted_iota(jnp.int32, square, 1)
    marks = sides_ref[...].astype(jnp.float32)
    return [
        jnp.sum(jnp.where(diagonal, marks[side : side + 1, :], 0.0), axis=1, keepdims=True)
        for side in range(2)
    ]


def start_all(copies):
    for copy in copies:
        copy.start()
    return copies


def wait_all(copies):
    for copy in copies:
        copy.wait()


def edge_kernel(
    ground_hbm, depth_hbm, rows_hbm, sides_hbm, links_hbm,
    far_ref, near_ref, even_ref, odd_ref, ground_out, surface_out, links_ref,
    ground_ref, depth_ref, rows_ref, sides_ref, sems, small_sems,
):
    height, width = ground_hbm.shape
    tiles = width // (SUBS * LANES)
    small = [
        pltpu.make_async_copy(rows_hbm, rows_ref, small_sems.at[0]),
        pltpu.make_async_copy(sides_hbm, sides_ref, small_sems.at[1]),
        pltpu.make_async_copy(links_hbm, links_ref, small_sems.at[2]),
    ]
    start_all(small[1:])
    copies = start_own(ground_hbm, depth_hbm, ground_ref, depth_ref, sems)
    start_all(small[:1])
    wait_all(small)
    edges = fold_own(copies, ground_ref, depth_ref, rows_ref, sides_ref, ground_out, surface_out)
    place, _ = chain_place()
    top = place % 2 == 0
    size, packed = (tiles + 1) * SUBS, tiles * SUBS
    for out_ref, is_top in ((far_ref, top), (near_ref, jnp.logical_not(top))):
        first = HALO + jnp.where(is_top, 0, height - HALO)
        bases = (jnp.where(is_top, 0, HALO - 1), jnp.where(is_top, HALO - 1, 0))
        for source, base in zip((ground_out, surface_out), bases):
            for row in range(HALO):
                for slot in range(tiles):
                    out_ref[register(base + row, slot, packed), :] = source[register(first + row, slot, size), :]
    rightward = lax.axis_index("cols") % 2 == 0
    for group, values in enumerate(edges):
        for kind in range(2):
            rows = pl.ds(kind * height + group * SUBS, SUBS)
            even_ref[rows, :] = jnp.where(rightward, values[1][kind], values[0][kind])
            odd_ref[rows, :] = jnp.where(rightward, values[0][kind], values[1][kind])


def start_own(ground_hbm, depth_hbm, ground_ref, depth_ref, sems):
    height, width = ground_hbm.shape
    groups = height // SUBS
    pieces = sems.shape[1] // groups
    part = width // pieces
    copies = []
    for group in range(groups):
        for piece in range(pieces):
            where = (pl.ds(group * SUBS, SUBS), pl.ds(piece * part, part))
            number = group * pieces + piece
            copies.append(
                start_all(
                    [
                        pltpu.make_async_copy(ground_hbm.at[where], ground_ref.at[where], sems.at[0, number]),
                        pltpu.make_async_copy(depth_hbm.at[where], depth_ref.at[where], sems.at[1, number]),
                    ]
                )
            )
    return copies


def fold_own(copies, ground_ref, depth_ref, rows_ref, sides_ref, ground_out, surface_out):
    height, width = ground_ref.shape
    groups = height // SUBS
    tiles = width // (SUBS * LANES)
    last_tile = width // LANES - 1
    pieces = len(copies) // groups
    part = width // pieces
    size = (tiles + 1) * SUBS
    place, places = chain_place()
    col, cols = lax.axis_index("cols"), lax.axis_size("cols")
    sub, lane = position()
    marks = side_marks(sides_ref)
    edges = [[] for _ in range(groups)]
    for group in range(groups):
        rows = pl.ds(group * SUBS, SUBS)
        for tile in range(last_tile + 1):
            if tile * LANES % part == 0:
                wait_all(copies[group * pieces + tile * LANES // part])
            columns = pl.ds(tile * LANES, LANES)
            ground = ground_ref[rows, columns]
            surface = ground + depth_ref[rows, columns]
            outlets = []
            if group == 0:
                outlets.append((rows_ref[0:1, columns] == 1) & (sub == 0) & (place == 0))
            if group == groups - 1:
                outlets.append(
                    (rows_ref[1:2, columns] == 1) & (sub == SUBS - 1) & (place == places - 1)
                )
            if tile == 0:
                outlets.append(
                    (marks[0][group * SUBS : (group + 1) * SUBS] > 0.5) & (lane == 0) & (col == 0)
                )
            if tile == last_tile:
                outlets.append(
                    (marks[1][group * SUBS : (group + 1) * SUBS] > 0.5)
                    & (lane == LANES - 1)
                    & (col == cols - 1)
                )
            for outlet in outlets:
                surface = jnp.where(outlet, ground, surface)
            chunk, slot = tile // tiles, tile % tiles
            start = (HALO + group * SUBS) * size + slot * SUBS + chunk
            ground_out[pl.ds(start, SUBS, stride=size), :] = ground
            surface_out[pl.ds(start, SUBS, stride=size), :] = surface
            if tile in (0, last_tile):
                edges[group].append((ground, surface))
    return edges


def unpack_rows(rows_ref, first, is_top, present, strip_refs, strip_rows, ground_ref, surface_ref, tiles):
    packed = tiles * SUBS
    size = packed + SUBS
    bases = (jnp.where(is_top, HALO - 1, 0), jnp.where(is_top, 0, HALO - 1))
    for base, out_ref, strip_row in zip(bases, (ground_ref, surface_ref), strip_rows):
        for row in range(HALO):
            values = [
                jnp.where(present, rows_ref[register(base + row, slot, packed), :], unreached)
                for slot in range(tiles)
            ]
            for slot in range(tiles):
                out_ref[register(first + row, slot, size), :] = values[slot]
            fill_seam(out_ref, first + row, values[0], values[-1], strip_refs, strip_row + row, present, tiles)


def fill_seam(out_ref, row, first_tile, last_tile, strip_refs, strip_row, present, tiles):
    col, cols = lax.axis_index("cols"), lax.axis_size("cols")
    sub, lane = position()
    rightward = col % 2 == 0
    even, odd = [ref[pl.ds(strip_row, 1), :] for ref in strip_refs]
    after = jnp.where(present & (col < cols - 1), jnp.where(rightward, even, odd), unreached)
    before = jnp.where(present & (col > 0), jnp.where(rightward, odd, even), unreached)
    after = jnp.where(sub == SUBS - 1, after, pltpu.roll(first_tile, SUBS - 1, 0))
    before = jnp.where(sub == 0, before, pltpu.roll(last_tile, 1, 0))
    out_ref[register(row, tiles, (tiles + 1) * SUBS), :] = jnp.where(lane < LANES // 2, after, before)


def relax_passes(passes, ground, ring):
    size = ring * SUBS
    _, lane = position()
    at_first = lane == 0
    at_last = lane == LANES - 1
    order = [ring - 1] + list(range(ring - 1))
    made = {}

    def make(number, pair, slot):
        source, _, first, _, _ = passes[number]
        row = first + 2 * pair
        values = [source[register(row + step, slot, size), :] for step in range(-1, 3)]
        both = jnp.minimum(values[1], values[2])
        for one, column in enumerate((jnp.minimum(values[0], both), jnp.minimum(both, values[3]))):
            rolled = pltpu.roll(column, 1, 1), pltpu.roll(column, LANES - 1, 1)
            made[number, pair, one, slot] = (column, *rolled)

    def finish(number, pair, slot):
        source, target, first, _, _ = passes[number]
        for one in range(2):
            row = first + 2 * pair + one
            before, here, after = [made[number, pair, one, (slot + step) % ring] for step in (-1, 0, 1)]
            from_left = jnp.where(at_first, before[1], here[1])
            from_right = jnp.where(at_last, after[2], here[2])
            lowest = jnp.minimum(jnp.minimum(from_left, from_right), here[0])
            where = register(row, slot, size)
            raised = jnp.minimum(source[where, :], lowest + rise_step)
            target[where, :] = jnp.maximum(ground[where, :], raised)

    def items(slots):
        return [
            (number, pair, slot)
            for number, (_, _, _, count, _) in enumerate(passes)
            for pair in range(count // 2)
            for slot in slots
        ]

    makes, finishes = items(order), items(range(ring))
    for number in range(len(makes) + AHEAD):
        if number < len(makes):
            make(*makes[number])
        if number >= AHEAD:
            done = finishes[number - AHEAD]
            finish(*done)
            _, _, _, count, then = passes[done[0]]
            if then is not None and done[1:] == (count // 2 - 1, ring - 1):
                then()


def hop_counts(links_ref, hops_ref, needed):
    tiles, degree = links_ref.shape
    links = links_ref[...]
    number = lax.broadcasted_iota(jnp.int32, (tiles, tiles), 1)
    linked = links[:, 0:1] == number
    for edge in range(1, degree):
        linked = linked | (links[:, edge : edge + 1] == number)
    linked = linked.astype(jnp.float32)
    tile = lax.broadcasted_iota(jnp.int32, (tiles, LANES), 0)
    lane = lax.broadcasted_iota(jnp.int32, (tiles, LANES), 1)
    reached = jnp.zeros((tiles, LANES), jnp.float32)
    for index, wanted in enumerate(needed):
        reached = jnp.where((lane == index) & (tile == wanted), 1.0, reached)
    hops = jnp.where(reached > 0.5, 0.0, float(ROUNDS + 1))
    for hop in range(1, ROUNDS + 1):
        reached = lax.dot_general(
            linked, reached, (((0,), (0,)), ((), ())), preferred_element_type=jnp.float32
        )
        reached = jnp.where(reached > 0.5, 1.0, 0.0)
        hops = jnp.minimum(hops, jnp.where(reached > 0.5, float(hop), float(ROUNDS + 1)))
    for index in range(len(needed)):
        hops_ref[pl.ds(index * tiles, tiles), :] = jnp.broadcast_to(
            hops[:, index : index + 1], (tiles, LANES)
        )


def needed_tiles():
    row, rows = lax.axis_index("rows"), lax.axis_size("rows")
    col, cols = lax.axis_index("cols"), lax.axis_size("cols")
    sub, subs = lax.axis_index("sub"), lax.axis_size("sub")
    above = jnp.maximum(jnp.where(sub == 0, row - 1, row), 0)
    below = jnp.minimum(jnp.where(sub == subs - 1, row + 1, row), rows - 1)
    left = jnp.maximum(col - 1, 0)
    right = jnp.minimum(col + 1, cols - 1)
    return [r * cols + c for r in (above, row, below) for c in (left, col, right)]


def hops_kernel(links_ref, hops_ref):
    hop_counts(links_ref, hops_ref, needed_tiles())


def inner_kernel(height, tiles, near_ref, own_even_ref, own_odd_ref, near_even_ref, near_odd_ref, *refs):
    ground_ref, surface_ref, other_ref = refs[3:]
    own_strips, near_strips = (own_even_ref, own_odd_ref), (near_even_ref, near_odd_ref)
    ring = tiles + 1
    size = ring * SUBS
    place, places = chain_place()
    top = place % 2 == 0
    has_near = jnp.where(top, place < places - 1, place > 0)
    unpack_rows(
        near_ref,
        jnp.where(top, HALO + height, 0),
        jnp.logical_not(top),
        has_near,
        near_strips,
        [kind * height + jnp.where(top, 0, height - HALO) for kind in range(2)],
        ground_ref,
        surface_ref,
        tiles,
    )
    for kind, out_ref in enumerate((ground_ref, surface_ref)):
        for row in range(height):
            first_tile = out_ref[register(HALO + row, 0, size), :]
            last_tile = out_ref[register(HALO + row, tiles - 1, size), :]
            fill_seam(
                out_ref, HALO + row, first_tile, last_tile, own_strips, kind * height + row, place >= 0, tiles
            )
    buffers = (surface_ref, other_ref)
    passes = []
    for step in range(1, PASSES + 1):
        first = step + jnp.where(top, HALO, 0)
        passes.append((buffers[(step + 1) % 2], buffers[step % 2], first, height + HALO - 2 * step, None))
    relax_passes(passes, ground_ref, ring)


def outer_kernel(height, tiles, far_ref, even_ref, odd_ref, *refs):
    ground_ref, surface_ref, other_ref, level_ref, far_out, near_out = refs[3:9]
    ring = tiles + 1
    size = ring * SUBS
    place, places = chain_place()
    top = place % 2 == 0
    has_far = jnp.where(top, place > 0, place < places - 1)
    unpack_rows(
        far_ref,
        jnp.where(top, 0, HALO + height),
        top,
        has_far,
        (even_ref, odd_ref),
        [kind * height + jnp.where(top, height - HALO, 0) for kind in range(2)],
        ground_ref,
        surface_ref,
        tiles,
    )
    buffers = (surface_ref, other_ref)
    passes = []
    for step in range(1, PASSES + 1):
        first = jnp.where(top, step, HALO + height - step)
        passes.append((buffers[(step + 1) % 2], buffers[step % 2], first, HALO, None))
    relax_passes(passes, ground_ref, ring)
    low, high = HALO, HALO + height - FINAL
    for row in range(FINAL):
        for slot in range(ring):
            where = register(row, slot, size)
            far_out[where, :] = surface_ref[register(jnp.where(top, low, high) + row, slot, size), :]
            near_out[where, :] = surface_ref[register(jnp.where(top, high, low) + row, slot, size), :]
    band, bands = lax.axis_index("sub"), lax.axis_size("sub")
    sub, lane = position()

    def at(row, slot):
        return surface_ref[register(HALO + row, slot, size), :]

    first_cell = (sub == 0) & (lane == 0)
    last_cell = (sub == SUBS - 1) & (lane == LANES - 1)
    first_lows, last_lows, row_lows = [], [], []
    for row in range(height):
        first_lows.append(at(row, 0))
        last_lows.append(at(row, tiles - 1))
    for slot in range(tiles):
        row_lows.append(jnp.where(band == 0, at(0, slot), unreached))
        row_lows.append(jnp.where(band == bands - 1, at(height - 1, slot), unreached))
    lowest = jnp.minimum(
        least(row_lows),
        jnp.minimum(
            jnp.where(first_cell, least(first_lows), unreached),
            jnp.where(last_cell, least(last_lows), unreached),
        ),
    )
    lowest = jnp.min(jnp.min(lowest, axis=0, keepdims=True), axis=1, keepdims=True)
    level_ref[...] = jnp.broadcast_to(lowest, level_ref.shape)


def least(values):
    values = list(values)
    while len(values) > 1:
        values = [
            jnp.minimum(*values[number : number + 2]) if number + 1 < len(values) else values[number]
            for number in range(0, len(values), 2)
        ]
    return values[0]


def late_kernel(
    height, tiles, ground_ref, surface_ref, far_ref, near_ref, floors_ref, hops_ref, out_hbm,
    one_ref, two_ref, out_ref, sems,
):
    ring = tiles + 1
    size = ring * SUBS
    sub, lane = position()
    bands = lax.axis_size("sub")
    count = floors_ref.shape[0] // bands
    level = least(floors_ref[pl.ds(band, count, stride=bands), :] for band in range(bands))
    raised = [level]
    for hop in range(ROUNDS):
        raised.append(raised[-1] + hop_rise)
    ceilings = []
    for index in range(9):
        hops = hops_ref[pl.ds(index * count, count), :]
        lowest = jnp.full((count, LANES), unreached, jnp.float32)
        for hop in range(ROUNDS + 1):
            lowest = jnp.where(hops == float(hop), raised[hop], lowest)
        lowest = jnp.min(lowest, axis=0, keepdims=True) + spill_lift
        ceilings.append(jnp.broadcast_to(lowest, (SUBS, LANES)))
    pairs = []
    for region in range(3):
        left, middle, right = ceilings[3 * region : 3 * region + 3]
        seam = jnp.where(
            lane < LANES // 2,
            jnp.where(sub == SUBS - 1, right, middle),
            jnp.where(sub == 0, left, middle),
        )
        pairs.append((middle, seam))
    place, _ = chain_place()
    top = place % 2 == 0
    low, high = HALO - FINAL, HALO + height
    far_pair = [jnp.where(top, above, below) for above, below in zip(pairs[0], pairs[2])]
    near_pair = [jnp.where(top, below, above) for above, below in zip(pairs[0], pairs[2])]
    spans = (
        (surface_ref, HALO, HALO, height, pairs[1]),
        (near_ref, 0, jnp.where(top, high, low), FINAL, near_pair),
        (far_ref, 0, jnp.where(top, low, high), FINAL, far_pair),
    )
    for source, source_first, first, rows, (middle, seam) in spans:
        for row in range(rows):
            for slot in range(ring):
                value = source[register(source_first + row, slot, size), :]
                value = jnp.minimum(value, seam if slot == tiles else middle)
                where = register(first + row, slot, size)
                one_ref[where, :] = jnp.maximum(ground_ref[where, :], value)
    buffers = (one_ref, two_ref)
    passes = []
    for step in range(1, FINAL):
        first = HALO - FINAL + step
        count = 2 * HALO + height - 2 * first
        passes.append((buffers[(step + 1) % 2], buffers[step % 2], first, count, None))
    source, target = buffers[(FINAL + 1) % 2], buffers[FINAL % 2]
    copies = []

    def unfold(group):
        first = HALO + group * SUBS
        for tile in range(tiles * SUBS):
            chunk, slot = tile // tiles, tile % tiles
            out_ref[pl.ds(group * SUBS, SUBS), pl.ds(tile * LANES, LANES)] = target[
                pl.ds(first * size + slot * SUBS + chunk, SUBS, stride=size), :
            ]
        where = (pl.ds(group * SUBS, SUBS), slice(None))
        copies.extend(start_all([pltpu.make_async_copy(out_ref.at[where], out_hbm.at[where], sems.at[group])]))

    for group in range(height // SUBS):
        first = HALO + group * SUBS
        passes.append((source, target, first, SUBS, functools.partial(unfold, group)))
    relax_passes(passes, ground_ref, ring)
    wait_all(copies)


def in_vmem(count):
    return [pl.BlockSpec(memory_space=pltpu.VMEM)] * count


def in_hbm(count):
    return [pl.BlockSpec(memory_space=pltpu.HBM)] * count


def per_device(elevation, fill_depth, edge_rows, edge_sides, adjacency):
    height, width = elevation.shape
    tiles = width // (SUBS * LANES)
    groups = height // SUBS
    f32 = jnp.float32
    packed = tiles * SUBS
    size = packed + SUBS
    tile_count = adjacency.shape[0]
    places = lax.axis_size(("rows", "sub"))
    cols, subs = lax.axis_size("cols"), lax.axis_size("sub")
    short = pl.CostEstimate(flops=1024, bytes_accessed=1024, transcendentals=0)
    limit = pltpu.CompilerParams(vmem_limit_bytes=24 << 20)
    arguments = [
        pltpu.with_memory_space_constraint(value, pltpu.HBM)
        for value in (elevation, fill_depth, edge_rows, edge_sides, adjacency)
    ]
    sent = pltpu.VMEM(((2 * HALO - 1) * packed, LANES), f32)
    strip = pltpu.VMEM((2 * height, LANES), f32)
    work = pltpu.VMEM(((height + 2 * HALO) * size, LANES), f32)
    far, near, even, odd, ground, surface, links = pl.pallas_call(
        edge_kernel,
        out_shape=[sent, sent, strip, strip, work, work, pltpu.VMEM(adjacency.shape, jnp.int32)],
        in_specs=in_hbm(5),
        out_specs=in_vmem(7),
        scratch_shapes=[
            pltpu.VMEM((height, width), f32),
            pltpu.VMEM((height, width), f32),
            pltpu.VMEM(edge_rows.shape, jnp.int32),
            pltpu.VMEM(edge_sides.shape, jnp.int32),
            pltpu.SemaphoreType.DMA((2, 4 * groups)),
            pltpu.SemaphoreType.DMA((3,)),
        ],
        compiler_params=limit,
        cost_estimate=short,
        name="edge_rows",
    )(*arguments)

    near_pairs, far_pairs = [matching(places, first) for first in range(2)]
    stay = [(place, place) for place in range(places)]
    ends = [(place, place) for place in range(places) if place not in dict(far_pairs)]
    groups_count = lax.axis_size("groups")
    part = places * cols
    far_all = []
    for group, other in closed(matching(groups_count, 0), groups_count):
        for chosen, target in ((far_pairs, group), (ends, other)):
            for source, arrival in cross(chosen, [(col, col) for col in range(cols)], cols, subs):
                far_all.append((group * part + source, target * part + arrival))
    device_axes = ("rows", "cols", "sub")

    def swap_strips(pieces, row_pairs):
        arrived = []
        for first, piece in enumerate(pieces):
            pairs = cross(row_pairs, matching(cols, first), cols, subs)
            arrived.append(lax.ppermute(piece, device_axes, pairs) if pairs else piece)
        return arrived

    far_strips = swap_strips((even, odd), far_pairs + ends)
    far_rows = lax.ppermute(far, ("groups",) + device_axes, far_all)
    near_rows = lax.ppermute(near, ("rows", "sub"), near_pairs)
    strips = swap_strips((even, odd), stay) + swap_strips((even, odd), near_pairs)

    hops = pl.pallas_call(
        hops_kernel,
        out_shape=pltpu.VMEM((9 * tile_count, LANES), f32),
        in_specs=in_vmem(1),
        out_specs=pl.BlockSpec(memory_space=pltpu.VMEM),
        compiler_params=limit,
        cost_estimate=short,
        name="tile_hops",
    )(links)

    def inner(*refs):
        inner_kernel(height, tiles, *refs)

    ground, surface, other = pl.pallas_call(
        inner,
        out_shape=[work, work, work],
        in_specs=in_vmem(8),
        out_specs=in_vmem(3),
        input_output_aliases={5: 0, 6: 1},
        compiler_params=limit,
        cost_estimate=short,
        name="inner_passes",
    )(near_rows, *strips, ground, surface, hops)

    def outer(far_ref, *refs):
        outer_kernel(height, tiles, far_ref, *refs)

    devices = lax.axis_size(device_axes)
    again = pltpu.VMEM((FINAL * size, LANES), f32)
    ground, surface, other, floors, far, near = pl.pallas_call(
        outer,
        out_shape=[work, work, work, pltpu.VMEM((devices, LANES), f32), again, again],
        in_specs=in_vmem(6),
        out_specs=in_vmem(6),
        input_output_aliases={3: 0, 4: 1, 5: 2},
        compiler_params=limit,
        cost_estimate=short,
        name="outer_passes",
    )(far_rows, *far_strips, ground, surface, other)

    far_rows = lax.ppermute(far, ("groups",) + device_axes, far_all)
    near_rows = lax.ppermute(near, ("rows", "sub"), near_pairs)
    floors = lax.all_to_all(floors, device_axes, 0, 0, tiled=True)

    def late(*refs):
        late_kernel(height, tiles, *refs)

    return pl.pallas_call(
        late,
        out_shape=jax.ShapeDtypeStruct((height, width), f32),
        in_specs=in_vmem(6),
        out_specs=pl.BlockSpec(memory_space=pltpu.HBM),
        scratch_shapes=[
            work,
            work,
            pltpu.VMEM((height, width), f32),
            pltpu.SemaphoreType.DMA((groups,)),
        ],
        compiler_params=limit,
        cost_estimate=short,
        name="final_passes",
    )(ground, surface, far_rows, near_rows, floors, hops)


def solution(mesh):
    placed = (
        P(("groups", "rows", "sub"), "cols"),
        P(("groups", "rows", "sub"), "cols"),
        P("groups", "cols"),
        P("groups", ("rows", "sub")),
        P("groups", None),
    )
    return jax.shard_map(
        per_device,
        mesh=mesh,
        in_specs=placed,
        out_specs=P(("groups", "rows", "sub"), "cols"),
        check_vma=False,
    )
```

```python
import functools

import jax
import jax.numpy as jnp
from jax import lax
from jax.experimental import pallas as pl
from jax.experimental.pallas import tpu as pltpu
from jax.sharding import PartitionSpec as P

PASSES = 8
FINAL = 4
ROUNDS = 4
HALO = PASSES
SUBS = 8
LANES = 128
AHEAD = 5

unreached = 1000000000.0
rise_step = 0.01
hop_rise = 0.05
spill_lift = 3.0


def matching(count, first):
    pairs = []
    for low in range(first, count - 1, 2):
        pairs += [(low, low + 1), (low + 1, low)]
    return pairs


def closed(pairs, count):
    used = {source for source, _ in pairs}
    return pairs + [(place, place) for place in range(count) if place not in used]


def cross(row_pairs, col_pairs, cols, subs):
    def device(place, col):
        return (place // subs * cols + col) * subs + place % subs

    return [
        (device(row, col), device(row_to, col_to))
        for row, row_to in row_pairs
        for col, col_to in col_pairs
    ]


def chain_place():
    subs = lax.axis_size("sub")
    return lax.axis_index("rows") * subs + lax.axis_index("sub"), lax.axis_size("rows") * subs


def position():
    sub = lax.broadcasted_iota(jnp.int32, (SUBS, LANES), 0)
    lane = lax.broadcasted_iota(jnp.int32, (SUBS, LANES), 1)
    return sub, lane


def aligned(start):
    return start if isinstance(start, int) else pl.multiple_of(start, SUBS)


def rows_at(first, count, size):
    return pl.ds(aligned(first * size), count * size)


def register(row, slot, size):
    return pl.ds(aligned(row * size + slot * SUBS), SUBS)


def side_marks(sides_ref):
    height = sides_ref.shape[1]
    square = (height, height)
    diagonal = lax.broadcasted_iota(jnp.int32, square, 0) == lax.broadcasted_iota(jnp.int32, square, 1)
    marks = sides_ref[...].astype(jnp.float32)
    return [
        jnp.sum(jnp.where(diagonal, marks[side : side + 1, :], 0.0), axis=1, keepdims=True)
        for side in range(2)
    ]


def start_all(copies):
    for copy in copies:
        copy.start()
    return copies


def wait_all(copies):
    for copy in copies:
        copy.wait()


def edge_kernel(
    ground_hbm, depth_hbm, rows_hbm, sides_hbm, links_hbm,
    far_ref, near_ref, even_ref, odd_ref, ground_out, surface_out, links_ref,
    ground_ref, depth_ref, rows_ref, sides_ref, sems, small_sems,
):
    height, width = ground_hbm.shape
    tiles = width // (SUBS * LANES)
    small = [
        pltpu.make_async_copy(rows_hbm, rows_ref, small_sems.at[0]),
        pltpu.make_async_copy(sides_hbm, sides_ref, small_sems.at[1]),
        pltpu.make_async_copy(links_hbm, links_ref, small_sems.at[2]),
    ]
    start_all(small[1:])
    copies = start_own(ground_hbm, depth_hbm, ground_ref, depth_ref, sems)
    start_all(small[:1])
    wait_all(small)
    edges = fold_own(copies, ground_ref, depth_ref, rows_ref, sides_ref, ground_out, surface_out)
    place, _ = chain_place()
    top = place % 2 == 0
    size, packed = (tiles + 1) * SUBS, tiles * SUBS
    for out_ref, is_top in ((far_ref, top), (near_ref, jnp.logical_not(top))):
        first = HALO + jnp.where(is_top, 0, height - HALO)
        bases = (jnp.where(is_top, 0, HALO - 1), jnp.where(is_top, HALO - 1, 0))
        for source, base in zip((ground_out, surface_out), bases):
            for row in range(HALO):
                for slot in range(tiles):
                    out_ref[register(base + row, slot, packed), :] = source[register(first + row, slot, size), :]
    rightward = lax.axis_index("cols") % 2 == 0
    for group, values in enumerate(edges):
        for kind in range(2):
            rows = pl.ds(kind * height + group * SUBS, SUBS)
            even_ref[rows, :] = jnp.where(rightward, values[1][kind], values[0][kind])
            odd_ref[rows, :] = jnp.where(rightward, values[0][kind], values[1][kind])


def start_own(ground_hbm, depth_hbm, ground_ref, depth_ref, sems):
    pieces = sems.shape[1]
    part = ground_hbm.shape[1] // pieces
    copies = []
    for piece in range(pieces):
        where = (slice(None), pl.ds(piece * part, part))
        copies.append(
            start_all(
                [
                    pltpu.make_async_copy(ground_hbm.at[where], ground_ref.at[where], sems.at[0, piece]),
                    pltpu.make_async_copy(depth_hbm.at[where], depth_ref.at[where], sems.at[1, piece]),
                ]
            )
        )
    return copies


def fold_own(copies, ground_ref, depth_ref, rows_ref, sides_ref, ground_out, surface_out):
    height, width = ground_ref.shape
    groups = height // SUBS
    tiles = width // (SUBS * LANES)
    last_tile = width // LANES - 1
    part = width // len(copies)
    size = (tiles + 1) * SUBS
    place, places = chain_place()
    col, cols = lax.axis_index("cols"), lax.axis_size("cols")
    sub, lane = position()
    marks = side_marks(sides_ref)
    edges = [[] for _ in range(groups)]
    for tile in range(last_tile + 1):
        if tile * LANES % part == 0:
            wait_all(copies[tile * LANES // part])
        columns = pl.ds(tile * LANES, LANES)
        for group in range(groups):
            rows = pl.ds(group * SUBS, SUBS)
            ground = ground_ref[rows, columns]
            surface = ground + depth_ref[rows, columns]
            outlets = []
            if group == 0:
                outlets.append((rows_ref[0:1, columns] == 1) & (sub == 0) & (place == 0))
            if group == groups - 1:
                outlets.append(
                    (rows_ref[1:2, columns] == 1) & (sub == SUBS - 1) & (place == places - 1)
                )
            if tile == 0:
                outlets.append(
                    (marks[0][group * SUBS : (group + 1) * SUBS] > 0.5) & (lane == 0) & (col == 0)
                )
            if tile == last_tile:
                outlets.append(
                    (marks[1][group * SUBS : (group + 1) * SUBS] > 0.5)
                    & (lane == LANES - 1)
                    & (col == cols - 1)
                )
            for outlet in outlets:
                surface = jnp.where(outlet, ground, surface)
            chunk, slot = tile // tiles, tile % tiles
            start = (HALO + group * SUBS) * size + slot * SUBS + chunk
            ground_out[pl.ds(start, SUBS, stride=size), :] = ground
            surface_out[pl.ds(start, SUBS, stride=size), :] = surface
            if tile in (0, last_tile):
                edges[group].append((ground, surface))
    return edges


def unpack_rows(rows_ref, first, is_top, present, strip_refs, strip_rows, ground_ref, surface_ref, tiles):
    packed = tiles * SUBS
    size = packed + SUBS
    bases = (jnp.where(is_top, HALO - 1, 0), jnp.where(is_top, 0, HALO - 1))
    for base, out_ref, strip_row in zip(bases, (ground_ref, surface_ref), strip_rows):
        for row in range(HALO):
            values = [
                jnp.where(present, rows_ref[register(base + row, slot, packed), :], unreached)
                for slot in range(tiles)
            ]
            for slot in range(tiles):
                out_ref[register(first + row, slot, size), :] = values[slot]
            fill_seam(out_ref, first + row, values[0], values[-1], strip_refs, strip_row + row, present, tiles)


def fill_seam(out_ref, row, first_tile, last_tile, strip_refs, strip_row, present, tiles):
    col, cols = lax.axis_index("cols"), lax.axis_size("cols")
    sub, lane = position()
    rightward = col % 2 == 0
    even, odd = [ref[pl.ds(strip_row, 1), :] for ref in strip_refs]
    after = jnp.where(present & (col < cols - 1), jnp.where(rightward, even, odd), unreached)
    before = jnp.where(present & (col > 0), jnp.where(rightward, odd, even), unreached)
    after = jnp.where(sub == SUBS - 1, after, pltpu.roll(first_tile, SUBS - 1, 0))
    before = jnp.where(sub == 0, before, pltpu.roll(last_tile, 1, 0))
    out_ref[register(row, tiles, (tiles + 1) * SUBS), :] = jnp.where(lane < LANES // 2, after, before)


def relax_passes(passes, ground, ring, ahead=AHEAD):
    size = ring * SUBS
    _, lane = position()
    at_first = lane == 0
    at_last = lane == LANES - 1
    order = [ring - 1] + list(range(ring - 1))
    made = {}

    def make(number, pair, slot):
        source, _, first, _, _ = passes[number]
        row = first + 2 * pair
        values = [source[register(row + step, slot, size), :] for step in range(-1, 3)]
        both = jnp.minimum(values[1], values[2])
        for one, column in enumerate((jnp.minimum(values[0], both), jnp.minimum(both, values[3]))):
            rolled = pltpu.roll(column, 1, 1), pltpu.roll(column, LANES - 1, 1)
            made[number, pair, one, slot] = (column, *rolled)

    def finish(number, pair, slot):
        source, target, first, _, _ = passes[number]
        for one in range(2):
            row = first + 2 * pair + one
            before, here, after = [made[number, pair, one, (slot + step) % ring] for step in (-1, 0, 1)]
            from_left = jnp.where(at_first, before[1], here[1])
            from_right = jnp.where(at_last, after[2], here[2])
            lowest = jnp.minimum(jnp.minimum(from_left, from_right), here[0])
            where = register(row, slot, size)
            raised = jnp.minimum(source[where, :], lowest + rise_step)
            target[where, :] = jnp.maximum(ground[where, :], raised)

    def items(slots):
        return [
            (number, pair, slot)
            for number, (_, _, _, count, _) in enumerate(passes)
            for pair in range(count // 2)
            for slot in slots
        ]

    makes, finishes = items(order), items(range(ring))
    for number in range(len(makes) + ahead):
        if number < len(makes):
            make(*makes[number])
        if number >= ahead:
            done = finishes[number - ahead]
            finish(*done)
            _, _, _, count, then = passes[done[0]]
            if then is not None and done[1:] == (count // 2 - 1, ring - 1):
                then()


def hop_counts(links_ref, hops_ref, needed):
    tiles, degree = links_ref.shape
    links = links_ref[...]
    number = lax.broadcasted_iota(jnp.int32, (tiles, tiles), 1)
    linked = links[:, 0:1] == number
    for edge in range(1, degree):
        linked = linked | (links[:, edge : edge + 1] == number)
    linked = linked.astype(jnp.float32)
    tile = lax.broadcasted_iota(jnp.int32, (tiles, LANES), 0)
    lane = lax.broadcasted_iota(jnp.int32, (tiles, LANES), 1)
    reached = jnp.zeros((tiles, LANES), jnp.float32)
    for index, wanted in enumerate(needed):
        reached = jnp.where((lane == index) & (tile == wanted), 1.0, reached)
    hops = jnp.where(reached > 0.5, 0.0, float(ROUNDS + 1))
    for hop in range(1, ROUNDS + 1):
        reached = lax.dot_general(
            linked, reached, (((0,), (0,)), ((), ())), preferred_element_type=jnp.float32
        )
        reached = jnp.where(reached > 0.5, 1.0, 0.0)
        hops = jnp.minimum(hops, jnp.where(reached > 0.5, float(hop), float(ROUNDS + 1)))
    for index in range(len(needed)):
        hops_ref[pl.ds(index * tiles, tiles), :] = jnp.broadcast_to(
            hops[:, index : index + 1], (tiles, LANES)
        )


def needed_tiles():
    row, rows = lax.axis_index("rows"), lax.axis_size("rows")
    col, cols = lax.axis_index("cols"), lax.axis_size("cols")
    sub, subs = lax.axis_index("sub"), lax.axis_size("sub")
    above = jnp.maximum(jnp.where(sub == 0, row - 1, row), 0)
    below = jnp.minimum(jnp.where(sub == subs - 1, row + 1, row), rows - 1)
    left = jnp.maximum(col - 1, 0)
    right = jnp.minimum(col + 1, cols - 1)
    return [r * cols + c for r in (above, row, below) for c in (left, col, right)]


def hops_kernel(links_ref, hops_ref):
    hop_counts(links_ref, hops_ref, needed_tiles())


def inner_kernel(height, tiles, near_ref, own_even_ref, own_odd_ref, near_even_ref, near_odd_ref, *refs):
    ground_ref, surface_ref, other_ref = refs[3:]
    own_strips, near_strips = (own_even_ref, own_odd_ref), (near_even_ref, near_odd_ref)
    ring = tiles + 1
    size = ring * SUBS
    place, places = chain_place()
    top = place % 2 == 0
    has_near = jnp.where(top, place < places - 1, place > 0)
    unpack_rows(
        near_ref,
        jnp.where(top, HALO + height, 0),
        jnp.logical_not(top),
        has_near,
        near_strips,
        [kind * height + jnp.where(top, 0, height - HALO) for kind in range(2)],
        ground_ref,
        surface_ref,
        tiles,
    )
    for kind, out_ref in enumerate((ground_ref, surface_ref)):
        for row in range(height):
            first_tile = out_ref[register(HALO + row, 0, size), :]
            last_tile = out_ref[register(HALO + row, tiles - 1, size), :]
            fill_seam(
                out_ref, HALO + row, first_tile, last_tile, own_strips, kind * height + row, place >= 0, tiles
            )
    buffers = (surface_ref, other_ref)
    passes = []
    for step in range(1, PASSES + 1):
        first = step + jnp.where(top, HALO, 0)
        passes.append((buffers[(step + 1) % 2], buffers[step % 2], first, height + HALO - 2 * step, None))
    relax_passes(passes, ground_ref, ring)


def outer_kernel(height, tiles, far_ref, even_ref, odd_ref, *refs):
    ground_ref, surface_ref, other_ref, level_ref, far_out, near_out = refs[3:9]
    ring = tiles + 1
    size = ring * SUBS
    place, places = chain_place()
    top = place % 2 == 0
    has_far = jnp.where(top, place > 0, place < places - 1)
    unpack_rows(
        far_ref,
        jnp.where(top, 0, HALO + height),
        top,
        has_far,
        (even_ref, odd_ref),
        [kind * height + jnp.where(top, height - HALO, 0) for kind in range(2)],
        ground_ref,
        surface_ref,
        tiles,
    )
    buffers = (surface_ref, other_ref)

    def two_passes(pair, carry):
        passes = []
        for step in range(1, 3):
            first = jnp.where(top, step + 2 * pair, HALO + height - step - 2 * pair)
            passes.append((buffers[(step + 1) % 2], buffers[step % 2], first, HALO, None))
        relax_passes(passes, ground_ref, ring)
        return carry

    lax.fori_loop(0, PASSES // 2, two_passes, 0)
    low, high = HALO, HALO + height - FINAL
    for row in range(FINAL):
        for slot in range(ring):
            where = register(row, slot, size)
            far_out[where, :] = surface_ref[register(jnp.where(top, low, high) + row, slot, size), :]
            near_out[where, :] = surface_ref[register(jnp.where(top, high, low) + row, slot, size), :]
    band, bands = lax.axis_index("sub"), lax.axis_size("sub")
    sub, lane = position()

    def at(row, slot):
        return surface_ref[register(HALO + row, slot, size), :]

    first_cell = (sub == 0) & (lane == 0)
    last_cell = (sub == SUBS - 1) & (lane == LANES - 1)
    first_lows, last_lows, row_lows = [], [], []
    for row in range(height):
        first_lows.append(at(row, 0))
        last_lows.append(at(row, tiles - 1))
    for slot in range(tiles):
        row_lows.append(jnp.where(band == 0, at(0, slot), unreached))
        row_lows.append(jnp.where(band == bands - 1, at(height - 1, slot), unreached))
    lowest = jnp.minimum(
        least(row_lows),
        jnp.minimum(
            jnp.where(first_cell, least(first_lows), unreached),
            jnp.where(last_cell, least(last_lows), unreached),
        ),
    )
    lowest = jnp.min(jnp.min(lowest, axis=0, keepdims=True), axis=1, keepdims=True)
    level_ref[...] = jnp.broadcast_to(lowest, level_ref.shape)


def least(values):
    values = list(values)
    while len(values) > 1:
        values = [
            jnp.minimum(*values[number : number + 2]) if number + 1 < len(values) else values[number]
            for number in range(0, len(values), 2)
        ]
    return values[0]


def late_kernel(
    height, tiles, ground_ref, surface_ref, far_ref, near_ref, floors_ref, hops_ref, out_hbm,
    one_ref, two_ref, out_ref, sems,
):
    ring = tiles + 1
    size = ring * SUBS
    sub, lane = position()
    bands = lax.axis_size("sub")
    count = floors_ref.shape[0] // bands
    level = least(floors_ref[pl.ds(band, count, stride=bands), :] for band in range(bands))
    raised = [level]
    for hop in range(ROUNDS):
        raised.append(raised[-1] + hop_rise)
    ceilings = []
    for index in range(9):
        hops = hops_ref[pl.ds(index * count, count), :]
        lowest = jnp.full((count, LANES), unreached, jnp.float32)
        for hop in range(ROUNDS + 1):
            lowest = jnp.where(hops == float(hop), raised[hop], lowest)
        lowest = jnp.min(lowest, axis=0, keepdims=True) + spill_lift
        ceilings.append(jnp.broadcast_to(lowest, (SUBS, LANES)))
    pairs = []
    for region in range(3):
        left, middle, right = ceilings[3 * region : 3 * region + 3]
        seam = jnp.where(
            lane < LANES // 2,
            jnp.where(sub == SUBS - 1, right, middle),
            jnp.where(sub == 0, left, middle),
        )
        pairs.append((middle, seam))
    place, _ = chain_place()
    top = place % 2 == 0
    low, high = HALO - FINAL, HALO + height
    far_pair = [jnp.where(top, above, below) for above, below in zip(pairs[0], pairs[2])]
    near_pair = [jnp.where(top, below, above) for above, below in zip(pairs[0], pairs[2])]
    spans = (
        (surface_ref, HALO, HALO, height, pairs[1]),
        (near_ref, 0, jnp.where(top, high, low), FINAL, near_pair),
        (far_ref, 0, jnp.where(top, low, high), FINAL, far_pair),
    )
    for source, source_first, first, rows, (middle, seam) in spans:
        for row in range(rows):
            for slot in range(ring):
                value = source[register(source_first + row, slot, size), :]
                value = jnp.minimum(value, seam if slot == tiles else middle)
                where = register(first + row, slot, size)
                one_ref[where, :] = jnp.maximum(ground_ref[where, :], value)
    buffers = (one_ref, two_ref)
    passes = []
    for step in range(1, FINAL):
        first = HALO - FINAL + step
        count = 2 * HALO + height - 2 * first
        passes.append((buffers[(step + 1) % 2], buffers[step % 2], first, count, None))
    source, target = buffers[(FINAL + 1) % 2], buffers[FINAL % 2]
    copies = []

    def unfold(group):
        first = HALO + group * SUBS
        for tile in range(tiles * SUBS):
            chunk, slot = tile // tiles, tile % tiles
            out_ref[pl.ds(group * SUBS, SUBS), pl.ds(tile * LANES, LANES)] = target[
                pl.ds(first * size + slot * SUBS + chunk, SUBS, stride=size), :
            ]
        where = (pl.ds(group * SUBS, SUBS), slice(None))
        copies.extend(start_all([pltpu.make_async_copy(out_ref.at[where], out_hbm.at[where], sems.at[group])]))

    for group in range(height // SUBS):
        first = HALO + group * SUBS
        passes.append((source, target, first, SUBS, functools.partial(unfold, group)))
    relax_passes(passes, ground_ref, ring, 9)
    wait_all(copies)


def in_vmem(count):
    return [pl.BlockSpec(memory_space=pltpu.VMEM)] * count


def in_hbm(count):
    return [pl.BlockSpec(memory_space=pltpu.HBM)] * count


def per_device(elevation, fill_depth, edge_rows, edge_sides, adjacency):
    height, width = elevation.shape
    tiles = width // (SUBS * LANES)
    groups = height // SUBS
    f32 = jnp.float32
    packed = tiles * SUBS
    size = packed + SUBS
    tile_count = adjacency.shape[0]
    places = lax.axis_size(("rows", "sub"))
    cols, subs = lax.axis_size("cols"), lax.axis_size("sub")
    short = pl.CostEstimate(flops=1024, bytes_accessed=1024, transcendentals=0)
    limit = pltpu.CompilerParams(vmem_limit_bytes=24 << 20)
    arguments = [
        pltpu.with_memory_space_constraint(value, pltpu.HBM)
        for value in (elevation, fill_depth, edge_rows, edge_sides, adjacency)
    ]
    sent = pltpu.VMEM(((2 * HALO - 1) * packed, LANES), f32)
    strip = pltpu.VMEM((2 * height, LANES), f32)
    work = pltpu.VMEM(((height + 2 * HALO) * size, LANES), f32)
    far, near, even, odd, ground, surface, links = pl.pallas_call(
        edge_kernel,
        out_shape=[sent, sent, strip, strip, work, work, pltpu.VMEM(adjacency.shape, jnp.int32)],
        in_specs=in_hbm(5),
        out_specs=in_vmem(7),
        scratch_shapes=[
            pltpu.VMEM((height, width), f32),
            pltpu.VMEM((height, width), f32),
            pltpu.VMEM(edge_rows.shape, jnp.int32),
            pltpu.VMEM(edge_sides.shape, jnp.int32),
            pltpu.SemaphoreType.DMA((2, 4)),
            pltpu.SemaphoreType.DMA((3,)),
        ],
        compiler_params=limit,
        cost_estimate=short,
        name="edge_rows",
    )(*arguments)

    near_pairs, far_pairs = [matching(places, first) for first in range(2)]
    stay = [(place, place) for place in range(places)]
    ends = [(place, place) for place in range(places) if place not in dict(far_pairs)]
    groups_count = lax.axis_size("groups")
    part = places * cols
    far_all = []
    for group, other in closed(matching(groups_count, 0), groups_count):
        for chosen, target in ((far_pairs, group), (ends, other)):
            for source, arrival in cross(chosen, [(col, col) for col in range(cols)], cols, subs):
                far_all.append((group * part + source, target * part + arrival))
    device_axes = ("rows", "cols", "sub")

    def swap_strips(pieces, row_pairs):
        arrived = []
        for first, piece in enumerate(pieces):
            pairs = cross(row_pairs, matching(cols, first), cols, subs)
            arrived.append(lax.ppermute(piece, device_axes, pairs) if pairs else piece)
        return arrived

    far_strips = swap_strips((even, odd), far_pairs + ends)
    far_rows = lax.ppermute(far, ("groups",) + device_axes, far_all)
    near_rows = lax.ppermute(near, ("rows", "sub"), near_pairs)
    strips = swap_strips((even, odd), stay) + swap_strips((even, odd), near_pairs)

    hops = pl.pallas_call(
        hops_kernel,
        out_shape=pltpu.VMEM((9 * tile_count, LANES), f32),
        in_specs=in_vmem(1),
        out_specs=pl.BlockSpec(memory_space=pltpu.VMEM),
        compiler_params=limit,
        cost_estimate=short,
        name="tile_hops",
    )(links)

    def inner(*refs):
        inner_kernel(height, tiles, *refs)

    ground, surface, other = pl.pallas_call(
        inner,
        out_shape=[work, work, work],
        in_specs=in_vmem(8),
        out_specs=in_vmem(3),
        input_output_aliases={5: 0, 6: 1},
        compiler_params=limit,
        cost_estimate=short,
        name="inner_passes",
    )(near_rows, *strips, ground, surface, hops)

    def outer(far_ref, *refs):
        outer_kernel(height, tiles, far_ref, *refs)

    devices = lax.axis_size(device_axes)
    again = pltpu.VMEM((FINAL * size, LANES), f32)
    ground, surface, other, floors, far, near = pl.pallas_call(
        outer,
        out_shape=[work, work, work, pltpu.VMEM((devices, LANES), f32), again, again],
        in_specs=in_vmem(6),
        out_specs=in_vmem(6),
        input_output_aliases={3: 0, 4: 1, 5: 2},
        compiler_params=limit,
        cost_estimate=short,
        name="outer_passes",
    )(far_rows, *far_strips, ground, surface, other)

    far_rows = lax.ppermute(far, ("groups",) + device_axes, far_all)
    near_rows = lax.ppermute(near, ("rows", "sub"), near_pairs)
    floors = lax.all_to_all(floors, device_axes, 0, 0, tiled=True)

    def late(*refs):
        late_kernel(height, tiles, *refs)

    return pl.pallas_call(
        late,
        out_shape=jax.ShapeDtypeStruct((height, width), f32),
        in_specs=in_vmem(6),
        out_specs=pl.BlockSpec(memory_space=pltpu.HBM),
        scratch_shapes=[
            work,
            work,
            pltpu.VMEM((height, width), f32),
            pltpu.SemaphoreType.DMA((groups,)),
        ],
        compiler_params=limit,
        cost_estimate=short,
        name="final_passes",
    )(ground, surface, far_rows, near_rows, floors, hops)


def solution(mesh):
    placed = (
        P(("groups", "rows", "sub"), "cols"),
        P(("groups", "rows", "sub"), "cols"),
        P("groups", "cols"),
        P("groups", ("rows", "sub")),
        P("groups", None),
    )
    return jax.shard_map(
        per_device,
        mesh=mesh,
        in_specs=placed,
        out_specs=P(("groups", "rows", "sub"), "cols"),
        check_vma=False,
    )
```

```python
import functools

import jax
import jax.numpy as jnp
from jax import lax
from jax.experimental import pallas as pl
from jax.experimental.pallas import tpu as pltpu
from jax.sharding import PartitionSpec as P

PASSES = 8
FINAL = 4
ROUNDS = 4
HALO = PASSES
SUBS = 8
LANES = 128
AHEAD = 5

unreached = 1000000000.0
rise_step = 0.01
hop_rise = 0.05
spill_lift = 3.0


def matching(count, first):
    pairs = []
    for low in range(first, count - 1, 2):
        pairs += [(low, low + 1), (low + 1, low)]
    return pairs


def closed(pairs, count):
    used = {source for source, _ in pairs}
    return pairs + [(place, place) for place in range(count) if place not in used]


def cross(row_pairs, col_pairs, cols, subs):
    def device(place, col):
        return (place // subs * cols + col) * subs + place % subs

    return [
        (device(row, col), device(row_to, col_to))
        for row, row_to in row_pairs
        for col, col_to in col_pairs
    ]


def chain_place():
    subs = lax.axis_size("sub")
    return lax.axis_index("rows") * subs + lax.axis_index("sub"), lax.axis_size("rows") * subs


def position():
    sub = lax.broadcasted_iota(jnp.int32, (SUBS, LANES), 0)
    lane = lax.broadcasted_iota(jnp.int32, (SUBS, LANES), 1)
    return sub, lane


def aligned(start):
    return start if isinstance(start, int) else pl.multiple_of(start, SUBS)


def rows_at(first, count, size):
    return pl.ds(aligned(first * size), count * size)


def register(row, slot, size):
    return pl.ds(aligned(row * size + slot * SUBS), SUBS)


def side_marks(sides_ref):
    height = sides_ref.shape[1]
    square = (height, height)
    diagonal = lax.broadcasted_iota(jnp.int32, square, 0) == lax.broadcasted_iota(jnp.int32, square, 1)
    marks = sides_ref[...].astype(jnp.float32)
    return [
        jnp.sum(jnp.where(diagonal, marks[side : side + 1, :], 0.0), axis=1, keepdims=True)
        for side in range(2)
    ]


def start_all(copies):
    for copy in copies:
        copy.start()
    return copies


def wait_all(copies):
    for copy in copies:
        copy.wait()


def edge_kernel(
    ground_hbm, depth_hbm, rows_hbm, sides_hbm, links_hbm,
    far_ref, near_ref, even_ref, odd_ref, ground_out, surface_out, links_ref,
    ground_ref, depth_ref, rows_ref, sides_ref, sems, small_sems,
):
    height, width = ground_hbm.shape
    tiles = width // (SUBS * LANES)
    small = [
        pltpu.make_async_copy(rows_hbm, rows_ref, small_sems.at[0]),
        pltpu.make_async_copy(sides_hbm, sides_ref, small_sems.at[1]),
        pltpu.make_async_copy(links_hbm, links_ref, small_sems.at[2]),
    ]
    start_all(small[1:])
    copies = start_own(ground_hbm, depth_hbm, ground_ref, depth_ref, sems)
    start_all(small[:1])
    wait_all(small)
    edges = fold_own(copies, ground_ref, depth_ref, rows_ref, sides_ref, ground_out, surface_out)
    place, _ = chain_place()
    top = place % 2 == 0
    size, packed = (tiles + 1) * SUBS, tiles * SUBS
    for out_ref, is_top in ((far_ref, top), (near_ref, jnp.logical_not(top))):
        first = HALO + jnp.where(is_top, 0, height - HALO)
        bases = (jnp.where(is_top, 0, HALO - 1), jnp.where(is_top, HALO - 1, 0))
        for source, base in zip((ground_out, surface_out), bases):
            for row in range(HALO):
                for slot in range(tiles):
                    out_ref[register(base + row, slot, packed), :] = source[register(first + row, slot, size), :]
    rightward = lax.axis_index("cols") % 2 == 0
    for group, values in enumerate(edges):
        for kind in range(2):
            rows = pl.ds(kind * height + group * SUBS, SUBS)
            even_ref[rows, :] = jnp.where(rightward, values[1][kind], values[0][kind])
            odd_ref[rows, :] = jnp.where(rightward, values[0][kind], values[1][kind])


def start_own(ground_hbm, depth_hbm, ground_ref, depth_ref, sems):
    pieces = sems.shape[1]
    part = ground_hbm.shape[1] // pieces
    copies = []
    for piece in range(pieces):
        where = (slice(None), pl.ds(piece * part, part))
        copies.append(
            start_all(
                [
                    pltpu.make_async_copy(ground_hbm.at[where], ground_ref.at[where], sems.at[0, piece]),
                    pltpu.make_async_copy(depth_hbm.at[where], depth_ref.at[where], sems.at[1, piece]),
                ]
            )
        )
    return copies


def fold_own(copies, ground_ref, depth_ref, rows_ref, sides_ref, ground_out, surface_out):
    height, width = ground_ref.shape
    groups = height // SUBS
    tiles = width // (SUBS * LANES)
    last_tile = width // LANES - 1
    part = width // len(copies)
    size = (tiles + 1) * SUBS
    place, places = chain_place()
    col, cols = lax.axis_index("cols"), lax.axis_size("cols")
    sub, lane = position()
    marks = side_marks(sides_ref)
    edges = [[] for _ in range(groups)]
    for tile in range(last_tile + 1):
        if tile * LANES % part == 0:
            wait_all(copies[tile * LANES // part])
        columns = pl.ds(tile * LANES, LANES)
        for group in range(groups):
            rows = pl.ds(group * SUBS, SUBS)
            ground = ground_ref[rows, columns]
            surface = ground + depth_ref[rows, columns]
            outlets = []
            if group == 0:
                outlets.append((rows_ref[0:1, columns] == 1) & (sub == 0) & (place == 0))
            if group == groups - 1:
                outlets.append(
                    (rows_ref[1:2, columns] == 1) & (sub == SUBS - 1) & (place == places - 1)
                )
            if tile == 0:
                outlets.append(
                    (marks[0][group * SUBS : (group + 1) * SUBS] > 0.5) & (lane == 0) & (col == 0)
                )
            if tile == last_tile:
                outlets.append(
                    (marks[1][group * SUBS : (group + 1) * SUBS] > 0.5)
                    & (lane == LANES - 1)
                    & (col == cols - 1)
                )
            for outlet in outlets:
                surface = jnp.where(outlet, ground, surface)
            chunk, slot = tile // tiles, tile % tiles
            start = (HALO + group * SUBS) * size + slot * SUBS + chunk
            ground_out[pl.ds(start, SUBS, stride=size), :] = ground
            surface_out[pl.ds(start, SUBS, stride=size), :] = surface
            if tile in (0, last_tile):
                edges[group].append((ground, surface))
    return edges


def unpack_rows(rows_ref, first, is_top, present, strip_refs, strip_rows, ground_ref, surface_ref, tiles):
    packed = tiles * SUBS
    size = packed + SUBS
    bases = (jnp.where(is_top, HALO - 1, 0), jnp.where(is_top, 0, HALO - 1))
    for base, out_ref, strip_row in zip(bases, (ground_ref, surface_ref), strip_rows):
        for row in range(HALO):
            values = [
                jnp.where(present, rows_ref[register(base + row, slot, packed), :], unreached)
                for slot in range(tiles)
            ]
            for slot in range(tiles):
                out_ref[register(first + row, slot, size), :] = values[slot]
            fill_seam(out_ref, first + row, values[0], values[-1], strip_refs, strip_row + row, present, tiles)


def fill_seam(out_ref, row, first_tile, last_tile, strip_refs, strip_row, present, tiles):
    col, cols = lax.axis_index("cols"), lax.axis_size("cols")
    sub, lane = position()
    rightward = col % 2 == 0
    even, odd = [ref[pl.ds(strip_row, 1), :] for ref in strip_refs]
    after = jnp.where(present & (col < cols - 1), jnp.where(rightward, even, odd), unreached)
    before = jnp.where(present & (col > 0), jnp.where(rightward, odd, even), unreached)
    after = jnp.where(sub == SUBS - 1, after, pltpu.roll(first_tile, SUBS - 1, 0))
    before = jnp.where(sub == 0, before, pltpu.roll(last_tile, 1, 0))
    out_ref[register(row, tiles, (tiles + 1) * SUBS), :] = jnp.where(lane < LANES // 2, after, before)


def relax_passes(passes, ground, ring):
    size = ring * SUBS
    _, lane = position()
    at_first = lane == 0
    at_last = lane == LANES - 1
    order = [ring - 1] + list(range(ring - 1))
    made = {}

    def make(number, pair, slot):
        source, _, first, _, _ = passes[number]
        row = first + 2 * pair
        values = [source[register(row + step, slot, size), :] for step in range(-1, 3)]
        both = jnp.minimum(values[1], values[2])
        for one, column in enumerate((jnp.minimum(values[0], both), jnp.minimum(both, values[3]))):
            rolled = pltpu.roll(column, 1, 1), pltpu.roll(column, LANES - 1, 1)
            made[number, pair, one, slot] = (column, *rolled, values[1 + one])

    def finish(number, pair, slot):
        _, target, first, _, _ = passes[number]
        for one in range(2):
            row = first + 2 * pair + one
            before, here, after = [made[number, pair, one, (slot + step) % ring] for step in (-1, 0, 1)]
            from_left = jnp.where(at_first, before[1], here[1])
            from_right = jnp.where(at_last, after[2], here[2])
            lowest = jnp.minimum(jnp.minimum(from_left, from_right), here[0])
            where = register(row, slot, size)
            raised = jnp.minimum(here[3], lowest + rise_step)
            target[where, :] = jnp.maximum(ground[where, :], raised)

    def items(slots):
        return [
            (number, pair, slot)
            for number, (_, _, _, count, _) in enumerate(passes)
            for pair in range(count // 2)
            for slot in slots
        ]

    makes, finishes = items(order), items(range(ring))
    for number in range(len(makes) + AHEAD):
        if number < len(makes):
            make(*makes[number])
        if number >= AHEAD:
            done = finishes[number - AHEAD]
            finish(*done)
            _, _, _, count, then = passes[done[0]]
            if then is not None and done[1:] == (count // 2 - 1, ring - 1):
                then()


def hop_counts(links_ref, hops_ref, needed):
    tiles, degree = links_ref.shape
    links = links_ref[...]
    number = lax.broadcasted_iota(jnp.int32, (tiles, tiles), 1)
    linked = links[:, 0:1] == number
    for edge in range(1, degree):
        linked = linked | (links[:, edge : edge + 1] == number)
    linked = linked.astype(jnp.float32)
    tile = lax.broadcasted_iota(jnp.int32, (tiles, LANES), 0)
    lane = lax.broadcasted_iota(jnp.int32, (tiles, LANES), 1)
    reached = jnp.zeros((tiles, LANES), jnp.float32)
    for index, wanted in enumerate(needed):
        reached = jnp.where((lane == index) & (tile == wanted), 1.0, reached)
    hops = jnp.where(reached > 0.5, 0.0, float(ROUNDS + 1))
    for hop in range(1, ROUNDS + 1):
        reached = lax.dot_general(
            linked, reached, (((0,), (0,)), ((), ())), preferred_element_type=jnp.float32
        )
        reached = jnp.where(reached > 0.5, 1.0, 0.0)
        hops = jnp.minimum(hops, jnp.where(reached > 0.5, float(hop), float(ROUNDS + 1)))
    for index in range(len(needed)):
        hops_ref[pl.ds(index * tiles, tiles), :] = jnp.broadcast_to(
            hops[:, index : index + 1], (tiles, LANES)
        )


def needed_tiles():
    row, rows = lax.axis_index("rows"), lax.axis_size("rows")
    col, cols = lax.axis_index("cols"), lax.axis_size("cols")
    sub, subs = lax.axis_index("sub"), lax.axis_size("sub")
    above = jnp.maximum(jnp.where(sub == 0, row - 1, row), 0)
    below = jnp.minimum(jnp.where(sub == subs - 1, row + 1, row), rows - 1)
    left = jnp.maximum(col - 1, 0)
    right = jnp.minimum(col + 1, cols - 1)
    return [r * cols + c for r in (above, row, below) for c in (left, col, right)]


def hops_kernel(links_ref, hops_ref):
    hop_counts(links_ref, hops_ref, needed_tiles())


def inner_kernel(height, tiles, near_ref, own_even_ref, own_odd_ref, near_even_ref, near_odd_ref, *refs):
    ground_ref, surface_ref, other_ref = refs[3:]
    own_strips, near_strips = (own_even_ref, own_odd_ref), (near_even_ref, near_odd_ref)
    ring = tiles + 1
    size = ring * SUBS
    place, places = chain_place()
    top = place % 2 == 0
    has_near = jnp.where(top, place < places - 1, place > 0)
    unpack_rows(
        near_ref,
        jnp.where(top, HALO + height, 0),
        jnp.logical_not(top),
        has_near,
        near_strips,
        [kind * height + jnp.where(top, 0, height - HALO) for kind in range(2)],
        ground_ref,
        surface_ref,
        tiles,
    )
    for kind, out_ref in enumerate((ground_ref, surface_ref)):
        for row in range(height):
            first_tile = out_ref[register(HALO + row, 0, size), :]
            last_tile = out_ref[register(HALO + row, tiles - 1, size), :]
            fill_seam(
                out_ref, HALO + row, first_tile, last_tile, own_strips, kind * height + row, place >= 0, tiles
            )
    buffers = (surface_ref, other_ref)
    passes = []
    for step in range(1, PASSES + 1):
        first = step + jnp.where(top, HALO, 0)
        passes.append((buffers[(step + 1) % 2], buffers[step % 2], first, height + HALO - 2 * step, None))
    relax_passes(passes, ground_ref, ring)


def outer_kernel(height, tiles, far_ref, even_ref, odd_ref, *refs):
    ground_ref, surface_ref, other_ref, level_ref, far_out, near_out = refs[3:9]
    ring = tiles + 1
    size = ring * SUBS
    place, places = chain_place()
    top = place % 2 == 0
    has_far = jnp.where(top, place > 0, place < places - 1)
    unpack_rows(
        far_ref,
        jnp.where(top, 0, HALO + height),
        top,
        has_far,
        (even_ref, odd_ref),
        [kind * height + jnp.where(top, height - HALO, 0) for kind in range(2)],
        ground_ref,
        surface_ref,
        tiles,
    )
    buffers = (surface_ref, other_ref)
    passes = []
    for step in range(1, PASSES + 1):
        first = jnp.where(top, step, HALO + height - step)
        passes.append((buffers[(step + 1) % 2], buffers[step % 2], first, HALO, None))
    relax_passes(passes, ground_ref, ring)
    low, high = HALO, HALO + height - FINAL
    for row in range(FINAL):
        for slot in range(ring):
            where = register(row, slot, size)
            far_out[where, :] = surface_ref[register(jnp.where(top, low, high) + row, slot, size), :]
            near_out[where, :] = surface_ref[register(jnp.where(top, high, low) + row, slot, size), :]
    band, bands = lax.axis_index("sub"), lax.axis_size("sub")
    sub, lane = position()

    def at(row, slot):
        return surface_ref[register(HALO + row, slot, size), :]

    first_cell = (sub == 0) & (lane == 0)
    last_cell = (sub == SUBS - 1) & (lane == LANES - 1)
    first_lows, last_lows, row_lows = [], [], []
    for row in range(height):
        first_lows.append(at(row, 0))
        last_lows.append(at(row, tiles - 1))
    for slot in range(tiles):
        row_lows.append(jnp.where(band == 0, at(0, slot), unreached))
        row_lows.append(jnp.where(band == bands - 1, at(height - 1, slot), unreached))
    lowest = jnp.minimum(
        least(row_lows),
        jnp.minimum(
            jnp.where(first_cell, least(first_lows), unreached),
            jnp.where(last_cell, least(last_lows), unreached),
        ),
    )
    lowest = jnp.min(jnp.min(lowest, axis=0, keepdims=True), axis=1, keepdims=True)
    level_ref[...] = jnp.broadcast_to(lowest, level_ref.shape)


def least(values):
    values = list(values)
    while len(values) > 1:
        values = [
            jnp.minimum(*values[number : number + 2]) if number + 1 < len(values) else values[number]
            for number in range(0, len(values), 2)
        ]
    return values[0]


def late_kernel(
    height, tiles, ground_ref, surface_ref, far_ref, near_ref, floors_ref, hops_ref, out_hbm,
    one_ref, two_ref, out_ref, sems,
):
    ring = tiles + 1
    size = ring * SUBS
    sub, lane = position()
    bands = lax.axis_size("sub")
    count = floors_ref.shape[0] // bands
    level = least(floors_ref[pl.ds(band, count, stride=bands), :] for band in range(bands))
    raised = [level]
    for hop in range(ROUNDS):
        raised.append(raised[-1] + hop_rise)
    ceilings = []
    for index in range(9):
        hops = hops_ref[pl.ds(index * count, count), :]
        lowest = jnp.full((count, LANES), unreached, jnp.float32)
        for hop in range(ROUNDS + 1):
            lowest = jnp.where(hops == float(hop), raised[hop], lowest)
        lowest = jnp.min(lowest, axis=0, keepdims=True) + spill_lift
        ceilings.append(jnp.broadcast_to(lowest, (SUBS, LANES)))
    pairs = []
    for region in range(3):
        left, middle, right = ceilings[3 * region : 3 * region + 3]
        seam = jnp.where(
            lane < LANES // 2,
            jnp.where(sub == SUBS - 1, right, middle),
            jnp.where(sub == 0, left, middle),
        )
        pairs.append((middle, seam))
    place, _ = chain_place()
    top = place % 2 == 0
    low, high = HALO - FINAL, HALO + height
    far_pair = [jnp.where(top, above, below) for above, below in zip(pairs[0], pairs[2])]
    near_pair = [jnp.where(top, below, above) for above, below in zip(pairs[0], pairs[2])]
    spans = (
        (surface_ref, HALO, HALO, height, pairs[1]),
        (near_ref, 0, jnp.where(top, high, low), FINAL, near_pair),
        (far_ref, 0, jnp.where(top, low, high), FINAL, far_pair),
    )
    for source, source_first, first, rows, (middle, seam) in spans:
        for row in range(rows):
            for slot in range(ring):
                value = source[register(source_first + row, slot, size), :]
                value = jnp.minimum(value, seam if slot == tiles else middle)
                where = register(first + row, slot, size)
                one_ref[where, :] = jnp.maximum(ground_ref[where, :], value)
    buffers = (one_ref, two_ref)
    passes = []
    for step in range(1, FINAL):
        first = HALO - FINAL + step
        count = 2 * HALO + height - 2 * first
        passes.append((buffers[(step + 1) % 2], buffers[step % 2], first, count, None))
    source, target = buffers[(FINAL + 1) % 2], buffers[FINAL % 2]
    copies = []

    def unfold(group):
        first = HALO + group * SUBS
        for tile in range(tiles * SUBS):
            chunk, slot = tile // tiles, tile % tiles
            out_ref[pl.ds(group * SUBS, SUBS), pl.ds(tile * LANES, LANES)] = target[
                pl.ds(first * size + slot * SUBS + chunk, SUBS, stride=size), :
            ]
        where = (pl.ds(group * SUBS, SUBS), slice(None))
        copies.extend(start_all([pltpu.make_async_copy(out_ref.at[where], out_hbm.at[where], sems.at[group])]))

    for group in range(height // SUBS):
        first = HALO + group * SUBS
        passes.append((source, target, first, SUBS, functools.partial(unfold, group)))
    relax_passes(passes, ground_ref, ring)
    wait_all(copies)


def in_vmem(count):
    return [pl.BlockSpec(memory_space=pltpu.VMEM)] * count


def in_hbm(count):
    return [pl.BlockSpec(memory_space=pltpu.HBM)] * count


def per_device(elevation, fill_depth, edge_rows, edge_sides, adjacency):
    height, width = elevation.shape
    tiles = width // (SUBS * LANES)
    groups = height // SUBS
    f32 = jnp.float32
    packed = tiles * SUBS
    size = packed + SUBS
    tile_count = adjacency.shape[0]
    places = lax.axis_size(("rows", "sub"))
    cols, subs = lax.axis_size("cols"), lax.axis_size("sub")
    short = pl.CostEstimate(flops=1024, bytes_accessed=1024, transcendentals=0)
    limit = pltpu.CompilerParams(vmem_limit_bytes=24 << 20)
    arguments = [
        pltpu.with_memory_space_constraint(value, pltpu.HBM)
        for value in (elevation, fill_depth, edge_rows, edge_sides, adjacency)
    ]
    sent = pltpu.VMEM(((2 * HALO - 1) * packed, LANES), f32)
    strip = pltpu.VMEM((2 * height, LANES), f32)
    work = pltpu.VMEM(((height + 2 * HALO) * size, LANES), f32)
    far, near, even, odd, ground, surface, links = pl.pallas_call(
        edge_kernel,
        out_shape=[sent, sent, strip, strip, work, work, pltpu.VMEM(adjacency.shape, jnp.int32)],
        in_specs=in_hbm(5),
        out_specs=in_vmem(7),
        scratch_shapes=[
            pltpu.VMEM((height, width), f32),
            pltpu.VMEM((height, width), f32),
            pltpu.VMEM(edge_rows.shape, jnp.int32),
            pltpu.VMEM(edge_sides.shape, jnp.int32),
            pltpu.SemaphoreType.DMA((2, 4)),
            pltpu.SemaphoreType.DMA((3,)),
        ],
        compiler_params=limit,
        cost_estimate=short,
        name="edge_rows",
    )(*arguments)

    near_pairs, far_pairs = [matching(places, first) for first in range(2)]
    stay = [(place, place) for place in range(places)]
    ends = [(place, place) for place in range(places) if place not in dict(far_pairs)]
    groups_count = lax.axis_size("groups")
    part = places * cols
    far_all = []
    for group, other in closed(matching(groups_count, 0), groups_count):
        for chosen, target in ((far_pairs, group), (ends, other)):
            for source, arrival in cross(chosen, [(col, col) for col in range(cols)], cols, subs):
                far_all.append((group * part + source, target * part + arrival))
    device_axes = ("rows", "cols", "sub")

    def swap_strips(pieces, row_pairs):
        arrived = []
        for first, piece in enumerate(pieces):
            pairs = cross(row_pairs, matching(cols, first), cols, subs)
            arrived.append(lax.ppermute(piece, device_axes, pairs) if pairs else piece)
        return arrived

    far_strips = swap_strips((even, odd), far_pairs + ends)
    far_rows = lax.ppermute(far, ("groups",) + device_axes, far_all)
    near_rows = lax.ppermute(near, ("rows", "sub"), near_pairs)
    strips = swap_strips((even, odd), stay) + swap_strips((even, odd), near_pairs)

    hops = pl.pallas_call(
        hops_kernel,
        out_shape=pltpu.VMEM((9 * tile_count, LANES), f32),
        in_specs=in_vmem(1),
        out_specs=pl.BlockSpec(memory_space=pltpu.VMEM),
        compiler_params=limit,
        cost_estimate=short,
        name="tile_hops",
    )(links)

    def inner(*refs):
        inner_kernel(height, tiles, *refs)

    ground, surface, other = pl.pallas_call(
        inner,
        out_shape=[work, work, work],
        in_specs=in_vmem(8),
        out_specs=in_vmem(3),
        input_output_aliases={5: 0, 6: 1},
        compiler_params=limit,
        cost_estimate=short,
        name="inner_passes",
    )(near_rows, *strips, ground, surface, hops)

    def outer(far_ref, *refs):
        outer_kernel(height, tiles, far_ref, *refs)

    devices = lax.axis_size(device_axes)
    again = pltpu.VMEM((FINAL * size, LANES), f32)
    ground, surface, other, floors, far, near = pl.pallas_call(
        outer,
        out_shape=[work, work, work, pltpu.VMEM((devices, LANES), f32), again, again],
        in_specs=in_vmem(6),
        out_specs=in_vmem(6),
        input_output_aliases={3: 0, 4: 1, 5: 2},
        compiler_params=limit,
        cost_estimate=short,
        name="outer_passes",
    )(far_rows, *far_strips, ground, surface, other)

    far_rows = lax.ppermute(far, ("groups",) + device_axes, far_all)
    near_rows = lax.ppermute(near, ("rows", "sub"), near_pairs)
    floors = lax.all_to_all(floors, device_axes, 0, 0, tiled=True)

    def late(*refs):
        late_kernel(height, tiles, *refs)

    return pl.pallas_call(
        late,
        out_shape=jax.ShapeDtypeStruct((height, width), f32),
        in_specs=in_vmem(6),
        out_specs=pl.BlockSpec(memory_space=pltpu.HBM),
        scratch_shapes=[
            work,
            work,
            pltpu.VMEM((height, width), f32),
            pltpu.SemaphoreType.DMA((groups,)),
        ],
        compiler_params=limit,
        cost_estimate=short,
        name="final_passes",
    )(ground, surface, far_rows, near_rows, floors, hops)


def solution(mesh):
    placed = (
        P(("groups", "rows", "sub"), "cols"),
        P(("groups", "rows", "sub"), "cols"),
        P("groups", "cols"),
        P("groups", ("rows", "sub")),
        P("groups", None),
    )
    return jax.shard_map(
        per_device,
        mesh=mesh,
        in_specs=placed,
        out_specs=P(("groups", "rows", "sub"), "cols"),
        check_vma=False,
    )
```

```python
import functools

import jax
import jax.numpy as jnp
from jax import lax
from jax.experimental import pallas as pl
from jax.experimental.pallas import tpu as pltpu
from jax.sharding import PartitionSpec as P

PASSES = 8
FINAL = 4
ROUNDS = 4
HALO = PASSES
SUBS = 8
LANES = 128
WANTED = 16
AHEAD = 5

unreached = 1000000000.0
rise_step = 0.01
hop_rise = 0.05
spill_lift = 3.0


def matching(count, first):
    pairs = []
    for low in range(first, count - 1, 2):
        pairs += [(low, low + 1), (low + 1, low)]
    return pairs


def closed(pairs, count):
    used = {source for source, _ in pairs}
    return pairs + [(place, place) for place in range(count) if place not in used]


def cross(row_pairs, col_pairs, cols, subs):
    def device(place, col):
        return (place // subs * cols + col) * subs + place % subs

    return [
        (device(row, col), device(row_to, col_to))
        for row, row_to in row_pairs
        for col, col_to in col_pairs
    ]


def chain_place():
    subs = lax.axis_size("sub")
    return lax.axis_index("rows") * subs + lax.axis_index("sub"), lax.axis_size("rows") * subs


def position():
    sub = lax.broadcasted_iota(jnp.int32, (SUBS, LANES), 0)
    lane = lax.broadcasted_iota(jnp.int32, (SUBS, LANES), 1)
    return sub, lane


def aligned(start):
    return start if isinstance(start, int) else pl.multiple_of(start, SUBS)


def rows_at(first, count, size):
    return pl.ds(aligned(first * size), count * size)


def register(row, slot, size):
    return pl.ds(aligned(row * size + slot * SUBS), SUBS)


def side_marks(sides_ref):
    height = sides_ref.shape[1]
    square = (height, height)
    diagonal = lax.broadcasted_iota(jnp.int32, square, 0) == lax.broadcasted_iota(jnp.int32, square, 1)
    marks = sides_ref[...].astype(jnp.float32)
    return [
        jnp.sum(jnp.where(diagonal, marks[side : side + 1, :], 0.0), axis=1, keepdims=True)
        for side in range(2)
    ]


def start_all(copies):
    for copy in copies:
        copy.start()
    return copies


def wait_all(copies):
    for copy in copies:
        copy.wait()


def edge_kernel(
    ground_hbm, depth_hbm, rows_hbm, sides_hbm, links_hbm,
    far_ref, near_ref, even_ref, odd_ref, ground_out, surface_out, links_ref,
    ground_ref, depth_ref, rows_ref, sides_ref, sems, small_sems,
):
    height, width = ground_hbm.shape
    tiles = width // (SUBS * LANES)
    small = [
        pltpu.make_async_copy(rows_hbm, rows_ref, small_sems.at[0]),
        pltpu.make_async_copy(sides_hbm, sides_ref, small_sems.at[1]),
        pltpu.make_async_copy(links_hbm, links_ref, small_sems.at[2]),
    ]
    start_all(small[1:])
    copies = start_own(ground_hbm, depth_hbm, ground_ref, depth_ref, sems)
    start_all(small[:1])
    wait_all(small)
    edges = fold_own(copies, ground_ref, depth_ref, rows_ref, sides_ref, ground_out, surface_out)
    place, _ = chain_place()
    top = place % 2 == 0
    size, packed = (tiles + 1) * SUBS, tiles * SUBS
    for out_ref, is_top in ((far_ref, top), (near_ref, jnp.logical_not(top))):
        first = HALO + jnp.where(is_top, 0, height - HALO)
        bases = (jnp.where(is_top, 0, HALO - 1), jnp.where(is_top, HALO - 1, 0))
        for source, base in zip((ground_out, surface_out), bases):
            for row in range(HALO):
                for slot in range(tiles):
                    out_ref[register(base + row, slot, packed), :] = source[register(first + row, slot, size), :]
    rightward = lax.axis_index("cols") % 2 == 0
    for group, values in enumerate(edges):
        for kind in range(2):
            rows = pl.ds(kind * height + group * SUBS, SUBS)
            even_ref[rows, :] = jnp.where(rightward, values[1][kind], values[0][kind])
            odd_ref[rows, :] = jnp.where(rightward, values[0][kind], values[1][kind])


def start_own(ground_hbm, depth_hbm, ground_ref, depth_ref, sems):
    pieces = sems.shape[1]
    part = ground_hbm.shape[1] // pieces
    copies = []
    for piece in range(pieces):
        where = (slice(None), pl.ds(piece * part, part))
        copies.append(
            start_all(
                [
                    pltpu.make_async_copy(ground_hbm.at[where], ground_ref.at[where], sems.at[0, piece]),
                    pltpu.make_async_copy(depth_hbm.at[where], depth_ref.at[where], sems.at[1, piece]),
                ]
            )
        )
    return copies


def fold_own(copies, ground_ref, depth_ref, rows_ref, sides_ref, ground_out, surface_out):
    height, width = ground_ref.shape
    groups = height // SUBS
    tiles = width // (SUBS * LANES)
    last_tile = width // LANES - 1
    part = width // len(copies)
    size = (tiles + 1) * SUBS
    place, places = chain_place()
    col, cols = lax.axis_index("cols"), lax.axis_size("cols")
    sub, lane = position()
    marks = side_marks(sides_ref)
    edges = [[] for _ in range(groups)]
    for tile in range(last_tile + 1):
        if tile * LANES % part == 0:
            wait_all(copies[tile * LANES // part])
        columns = pl.ds(tile * LANES, LANES)
        for group in range(groups):
            rows = pl.ds(group * SUBS, SUBS)
            ground = ground_ref[rows, columns]
            surface = ground + depth_ref[rows, columns]
            outlets = []
            if group == 0:
                outlets.append((rows_ref[0:1, columns] == 1) & (sub == 0) & (place == 0))
            if group == groups - 1:
                outlets.append(
                    (rows_ref[1:2, columns] == 1) & (sub == SUBS - 1) & (place == places - 1)
                )
            if tile == 0:
                outlets.append(
                    (marks[0][group * SUBS : (group + 1) * SUBS] > 0.5) & (lane == 0) & (col == 0)
                )
            if tile == last_tile:
                outlets.append(
                    (marks[1][group * SUBS : (group + 1) * SUBS] > 0.5)
                    & (lane == LANES - 1)
                    & (col == cols - 1)
                )
            for outlet in outlets:
                surface = jnp.where(outlet, ground, surface)
            chunk, slot = tile // tiles, tile % tiles
            start = (HALO + group * SUBS) * size + slot * SUBS + chunk
            ground_out[pl.ds(start, SUBS, stride=size), :] = ground
            surface_out[pl.ds(start, SUBS, stride=size), :] = surface
            if tile in (0, last_tile):
                edges[group].append((ground, surface))
    return edges


def unpack_rows(rows_ref, first, is_top, present, strip_refs, strip_rows, ground_ref, surface_ref, tiles):
    packed = tiles * SUBS
    size = packed + SUBS
    bases = (jnp.where(is_top, HALO - 1, 0), jnp.where(is_top, 0, HALO - 1))
    for base, out_ref, strip_row in zip(bases, (ground_ref, surface_ref), strip_rows):
        for row in range(HALO):
            values = [
                jnp.where(present, rows_ref[register(base + row, slot, packed), :], unreached)
                for slot in range(tiles)
            ]
            for slot in range(tiles):
                out_ref[register(first + row, slot, size), :] = values[slot]
            fill_seam(out_ref, first + row, values[0], values[-1], strip_refs, strip_row + row, present, tiles)


def fill_seam(out_ref, row, first_tile, last_tile, strip_refs, strip_row, present, tiles):
    col, cols = lax.axis_index("cols"), lax.axis_size("cols")
    sub, lane = position()
    rightward = col % 2 == 0
    even, odd = [ref[pl.ds(strip_row, 1), :] for ref in strip_refs]
    after = jnp.where(present & (col < cols - 1), jnp.where(rightward, even, odd), unreached)
    before = jnp.where(present & (col > 0), jnp.where(rightward, odd, even), unreached)
    after = jnp.where(sub == SUBS - 1, after, pltpu.roll(first_tile, SUBS - 1, 0))
    before = jnp.where(sub == 0, before, pltpu.roll(last_tile, 1, 0))
    out_ref[register(row, tiles, (tiles + 1) * SUBS), :] = jnp.where(lane < LANES // 2, after, before)


def relax_passes(passes, ground, ring):
    size = ring * SUBS
    _, lane = position()
    at_first = lane == 0
    at_last = lane == LANES - 1
    order = [ring - 1] + list(range(ring - 1))
    made = {}

    def make(number, pair, slot):
        source, _, first, _, _ = passes[number]
        row = first + 2 * pair
        values = [source[register(row + step, slot, size), :] for step in range(-1, 3)]
        both = jnp.minimum(values[1], values[2])
        for one, column in enumerate((jnp.minimum(values[0], both), jnp.minimum(both, values[3]))):
            rolled = pltpu.roll(column, 1, 1), pltpu.roll(column, LANES - 1, 1)
            made[number, pair, one, slot] = (column, *rolled, values[1 + one])

    def finish(number, pair, slot):
        _, target, first, _, _ = passes[number]
        for one in range(2):
            row = first + 2 * pair + one
            before, here, after = [made[number, pair, one, (slot + step) % ring] for step in (-1, 0, 1)]
            from_left = jnp.where(at_first, before[1], here[1])
            from_right = jnp.where(at_last, after[2], here[2])
            lowest = jnp.minimum(jnp.minimum(from_left, from_right), here[0])
            where = register(row, slot, size)
            raised = jnp.minimum(here[3], lowest + rise_step)
            target[where, :] = jnp.maximum(ground[where, :], raised)

    def items(slots):
        return [
            (number, pair, slot)
            for number, (_, _, _, count, _) in enumerate(passes)
            for pair in range(count // 2)
            for slot in slots
        ]

    makes, finishes = items(order), items(range(ring))
    for number in range(len(makes) + AHEAD):
        if number < len(makes):
            make(*makes[number])
        if number >= AHEAD:
            done = finishes[number - AHEAD]
            finish(*done)
            _, _, _, count, then = passes[done[0]]
            if then is not None and done[1:] == (count // 2 - 1, ring - 1):
                then()


def hop_counts(links_ref, hops_ref, needed):
    tiles, degree = links_ref.shape
    links = links_ref[...]
    number = lax.broadcasted_iota(jnp.int32, (tiles, tiles), 1)
    linked = links[:, 0:1] == number
    for edge in range(1, degree):
        linked = linked | (links[:, edge : edge + 1] == number)
    linked = linked.astype(jnp.float32)
    index = lax.broadcasted_iota(jnp.int32, (WANTED, tiles), 0)
    tile = lax.broadcasted_iota(jnp.int32, (WANTED, tiles), 1)
    reached = jnp.zeros((WANTED, tiles), jnp.float32)
    for number, wanted in enumerate(needed):
        reached = jnp.where((index == number) & (tile == wanted), 1.0, reached)
    hops = jnp.where(reached > 0.5, 0.0, float(ROUNDS + 1))
    for hop in range(1, ROUNDS + 1):
        reached = jnp.dot(reached, linked, preferred_element_type=jnp.float32)
        reached = jnp.where(reached > 0.5, 1.0, 0.0)
        hops = jnp.minimum(hops, jnp.where(reached > 0.5, float(hop), float(ROUNDS + 1)))
    for number in range(tiles):
        hops_ref[pl.ds(number * WANTED, WANTED), :] = jnp.broadcast_to(
            hops[:, number : number + 1], (WANTED, LANES)
        )


def needed_tiles():
    row, rows = lax.axis_index("rows"), lax.axis_size("rows")
    col, cols = lax.axis_index("cols"), lax.axis_size("cols")
    sub, subs = lax.axis_index("sub"), lax.axis_size("sub")
    above = jnp.maximum(jnp.where(sub == 0, row - 1, row), 0)
    below = jnp.minimum(jnp.where(sub == subs - 1, row + 1, row), rows - 1)
    left = jnp.maximum(col - 1, 0)
    right = jnp.minimum(col + 1, cols - 1)
    return [r * cols + c for r in (above, row, below) for c in (left, col, right)]


def hops_kernel(links_ref, hops_ref):
    hop_counts(links_ref, hops_ref, needed_tiles())


def copy_rows(source, first, target, ring):
    for row in range(FINAL):
        for slot in range(ring):
            target[register(row, slot, ring * SUBS), :] = source[register(first + row, slot, ring * SUBS), :]


def inner_kernel(height, tiles, near_ref, own_even_ref, own_odd_ref, near_even_ref, near_odd_ref, *refs):
    ground_ref, surface_ref, other_ref, near_out = refs[3:]
    own_strips, near_strips = (own_even_ref, own_odd_ref), (near_even_ref, near_odd_ref)
    ring = tiles + 1
    size = ring * SUBS
    place, places = chain_place()
    top = place % 2 == 0
    has_near = jnp.where(top, place < places - 1, place > 0)
    unpack_rows(
        near_ref,
        jnp.where(top, HALO + height, 0),
        jnp.logical_not(top),
        has_near,
        near_strips,
        [kind * height + jnp.where(top, 0, height - HALO) for kind in range(2)],
        ground_ref,
        surface_ref,
        tiles,
    )
    for kind, out_ref in enumerate((ground_ref, surface_ref)):
        for row in range(height):
            first_tile = out_ref[register(HALO + row, 0, size), :]
            last_tile = out_ref[register(HALO + row, tiles - 1, size), :]
            fill_seam(
                out_ref, HALO + row, first_tile, last_tile, own_strips, kind * height + row, place >= 0, tiles
            )
    buffers = (surface_ref, other_ref)
    passes = []
    for step in range(1, PASSES + 1):
        first = step + jnp.where(top, HALO, 0)
        passes.append((buffers[(step + 1) % 2], buffers[step % 2], first, height + HALO - 2 * step, None))
    relax_passes(passes, ground_ref, ring)
    copy_rows(surface_ref, jnp.where(top, HALO + height - FINAL, HALO), near_out, ring)


def outer_kernel(height, tiles, far_ref, even_ref, odd_ref, *refs):
    ground_ref, surface_ref, other_ref, level_ref, far_out = refs[3:8]
    ring = tiles + 1
    size = ring * SUBS
    place, places = chain_place()
    top = place % 2 == 0
    has_far = jnp.where(top, place > 0, place < places - 1)
    unpack_rows(
        far_ref,
        jnp.where(top, 0, HALO + height),
        top,
        has_far,
        (even_ref, odd_ref),
        [kind * height + jnp.where(top, height - HALO, 0) for kind in range(2)],
        ground_ref,
        surface_ref,
        tiles,
    )
    buffers = (surface_ref, other_ref)
    passes = []
    for step in range(1, PASSES + 1):
        first = jnp.where(top, step, HALO + height - step)
        passes.append((buffers[(step + 1) % 2], buffers[step % 2], first, HALO, None))
    relax_passes(passes, ground_ref, ring)
    copy_rows(surface_ref, jnp.where(top, HALO, HALO + height - FINAL), far_out, ring)
    band, bands = lax.axis_index("sub"), lax.axis_size("sub")
    sub, lane = position()

    def at(row, slot):
        return surface_ref[register(HALO + row, slot, size), :]

    first_cell = (sub == 0) & (lane == 0)
    last_cell = (sub == SUBS - 1) & (lane == LANES - 1)
    first_lows, last_lows, row_lows = [], [], []
    for row in range(height):
        first_lows.append(at(row, 0))
        last_lows.append(at(row, tiles - 1))
    for slot in range(tiles):
        row_lows.append(jnp.where(band == 0, at(0, slot), unreached))
        row_lows.append(jnp.where(band == bands - 1, at(height - 1, slot), unreached))
    lowest = jnp.minimum(
        least(row_lows),
        jnp.minimum(
            jnp.where(first_cell, least(first_lows), unreached),
            jnp.where(last_cell, least(last_lows), unreached),
        ),
    )
    lowest = jnp.min(jnp.min(lowest, axis=0, keepdims=True), axis=1, keepdims=True)
    level_ref[...] = jnp.broadcast_to(lowest, level_ref.shape)


def least(values):
    values = list(values)
    while len(values) > 1:
        values = [
            jnp.minimum(*values[number : number + 2]) if number + 1 < len(values) else values[number]
            for number in range(0, len(values), 2)
        ]
    return values[0]


def late_kernel(
    height, tiles, ground_ref, surface_ref, far_ref, near_ref, floors_ref, hops_ref, out_hbm,
    one_ref, two_ref, out_ref, ceilings_ref, sems,
):
    ring = tiles + 1
    size = ring * SUBS
    sub, lane = position()
    bands = lax.axis_size("sub")
    offers = []
    for tile in range(floors_ref.shape[0] // bands):
        raised = [least(floors_ref[pl.ds(tile * bands + band, 1), :] for band in range(bands))]
        for hop in range(ROUNDS):
            raised.append(raised[-1] + hop_rise)
        hops = hops_ref[pl.ds(tile * WANTED, WANTED), :]
        offer = jnp.full((WANTED, LANES), unreached, jnp.float32)
        for hop in range(ROUNDS + 1):
            offer = jnp.where(hops == float(hop), raised[hop], offer)
        offers.append(offer)
    ceilings_ref[...] = least(offers) + spill_lift
    ceilings = [jnp.broadcast_to(ceilings_ref[pl.ds(index, 1), :], (SUBS, LANES)) for index in range(9)]
    pairs = []
    for region in range(3):
        left, middle, right = ceilings[3 * region : 3 * region + 3]
        seam = jnp.where(
            lane < LANES // 2,
            jnp.where(sub == SUBS - 1, right, middle),
            jnp.where(sub == 0, left, middle),
        )
        pairs.append((middle, seam))
    place, _ = chain_place()
    top = place % 2 == 0
    low, high = HALO - FINAL, HALO + height
    far_pair = [jnp.where(top, above, below) for above, below in zip(pairs[0], pairs[2])]
    near_pair = [jnp.where(top, below, above) for above, below in zip(pairs[0], pairs[2])]
    spans = (
        (surface_ref, HALO, HALO, height, pairs[1]),
        (near_ref, 0, jnp.where(top, high, low), FINAL, near_pair),
        (far_ref, 0, jnp.where(top, low, high), FINAL, far_pair),
    )
    for source, source_first, first, rows, (middle, seam) in spans:
        for row in range(rows):
            for slot in range(ring):
                value = source[register(source_first + row, slot, size), :]
                value = jnp.minimum(value, seam if slot == tiles else middle)
                where = register(first + row, slot, size)
                one_ref[where, :] = jnp.maximum(ground_ref[where, :], value)
    buffers = (one_ref, two_ref)
    passes = []
    for step in range(1, FINAL):
        first = HALO - FINAL + step
        count = 2 * HALO + height - 2 * first
        passes.append((buffers[(step + 1) % 2], buffers[step % 2], first, count, None))
    source, target = buffers[(FINAL + 1) % 2], buffers[FINAL % 2]
    copies = []

    def unfold(group):
        first = HALO + group * SUBS
        half = tiles * SUBS // 2
        for tile in range(tiles * SUBS):
            chunk, slot = tile // tiles, tile % tiles
            out_ref[pl.ds(group * SUBS, SUBS), pl.ds(tile * LANES, LANES)] = target[
                pl.ds(first * size + slot * SUBS + chunk, SUBS, stride=size), :
            ]
            if tile % half == half - 1:
                side = tile // half
                where = (pl.ds(group * SUBS, SUBS), pl.ds(side * half * LANES, half * LANES))
                copy = pltpu.make_async_copy(out_ref.at[where], out_hbm.at[where], sems.at[group, side])
                copies.extend(start_all([copy]))

    for group in range(height // SUBS):
        first = HALO + group * SUBS
        passes.append((source, target, first, SUBS, functools.partial(unfold, group)))
    relax_passes(passes, ground_ref, ring)
    wait_all(copies)


def in_vmem(count):
    return [pl.BlockSpec(memory_space=pltpu.VMEM)] * count


def in_hbm(count):
    return [pl.BlockSpec(memory_space=pltpu.HBM)] * count


def per_device(elevation, fill_depth, edge_rows, edge_sides, adjacency):
    height, width = elevation.shape
    tiles = width // (SUBS * LANES)
    groups = height // SUBS
    f32 = jnp.float32
    packed = tiles * SUBS
    size = packed + SUBS
    tile_count = adjacency.shape[0]
    places = lax.axis_size(("rows", "sub"))
    cols, subs = lax.axis_size("cols"), lax.axis_size("sub")
    short = pl.CostEstimate(flops=1024, bytes_accessed=1024, transcendentals=0)
    limit = pltpu.CompilerParams(vmem_limit_bytes=24 << 20)
    arguments = [
        pltpu.with_memory_space_constraint(value, pltpu.HBM)
        for value in (elevation, fill_depth, edge_rows, edge_sides, adjacency)
    ]
    sent = pltpu.VMEM(((2 * HALO - 1) * packed, LANES), f32)
    strip = pltpu.VMEM((2 * height, LANES), f32)
    work = pltpu.VMEM(((height + 2 * HALO) * size, LANES), f32)
    far, near, even, odd, ground, surface, links = pl.pallas_call(
        edge_kernel,
        out_shape=[sent, sent, strip, strip, work, work, pltpu.VMEM(adjacency.shape, jnp.int32)],
        in_specs=in_hbm(5),
        out_specs=in_vmem(7),
        scratch_shapes=[
            pltpu.VMEM((height, width), f32),
            pltpu.VMEM((height, width), f32),
            pltpu.VMEM(edge_rows.shape, jnp.int32),
            pltpu.VMEM(edge_sides.shape, jnp.int32),
            pltpu.SemaphoreType.DMA((2, 4)),
            pltpu.SemaphoreType.DMA((3,)),
        ],
        compiler_params=limit,
        cost_estimate=short,
        name="edge_rows",
    )(*arguments)

    near_pairs, far_pairs = [matching(places, first) for first in range(2)]
    stay = [(place, place) for place in range(places)]
    ends = [(place, place) for place in range(places) if place not in dict(far_pairs)]
    groups_count = lax.axis_size("groups")
    part = places * cols
    far_all = []
    for group, other in closed(matching(groups_count, 0), groups_count):
        for chosen, target in ((far_pairs, group), (ends, other)):
            for source, arrival in cross(chosen, [(col, col) for col in range(cols)], cols, subs):
                far_all.append((group * part + source, target * part + arrival))
    device_axes = ("rows", "cols", "sub")

    def swap_strips(pieces, row_pairs):
        arrived = []
        for first, piece in enumerate(pieces):
            pairs = cross(row_pairs, matching(cols, first), cols, subs)
            arrived.append(lax.ppermute(piece, device_axes, pairs) if pairs else piece)
        return arrived

    far_strips = swap_strips((even, odd), far_pairs + ends)
    far_rows = lax.ppermute(far, ("groups",) + device_axes, far_all)
    near_rows = lax.ppermute(near, ("rows", "sub"), near_pairs)
    strips = swap_strips((even, odd), stay) + swap_strips((even, odd), near_pairs)

    hops = pl.pallas_call(
        hops_kernel,
        out_shape=pltpu.VMEM((WANTED * tile_count, LANES), f32),
        in_specs=in_vmem(1),
        out_specs=pl.BlockSpec(memory_space=pltpu.VMEM),
        compiler_params=limit,
        cost_estimate=short,
        name="tile_hops",
    )(links)

    def inner(*refs):
        inner_kernel(height, tiles, *refs)

    again = pltpu.VMEM((FINAL * size, LANES), f32)
    ground, surface, other, near = pl.pallas_call(
        inner,
        out_shape=[work, work, work, again],
        in_specs=in_vmem(8),
        out_specs=in_vmem(4),
        input_output_aliases={5: 0, 6: 1},
        compiler_params=limit,
        cost_estimate=short,
        name="inner_passes",
    )(near_rows, *strips, ground, surface, hops)

    def outer(far_ref, *refs):
        outer_kernel(height, tiles, far_ref, *refs)

    devices = lax.axis_size(device_axes)
    ground, surface, other, floors, far = pl.pallas_call(
        outer,
        out_shape=[work, work, work, pltpu.VMEM((devices, LANES), f32), again],
        in_specs=in_vmem(6),
        out_specs=in_vmem(5),
        input_output_aliases={3: 0, 4: 1, 5: 2},
        compiler_params=limit,
        cost_estimate=short,
        name="outer_passes",
    )(far_rows, *far_strips, ground, surface, other)

    far_rows = lax.ppermute(far, ("groups",) + device_axes, far_all)
    near_rows = lax.ppermute(near, ("rows", "sub"), near_pairs)
    floors = lax.all_to_all(floors, device_axes, 0, 0, tiled=True)

    def late(*refs):
        late_kernel(height, tiles, *refs)

    return pl.pallas_call(
        late,
        out_shape=jax.ShapeDtypeStruct((height, width), f32),
        in_specs=in_vmem(6),
        out_specs=pl.BlockSpec(memory_space=pltpu.HBM),
        scratch_shapes=[
            work,
            work,
            pltpu.VMEM((height, width), f32),
            pltpu.VMEM((WANTED, LANES), f32),
            pltpu.SemaphoreType.DMA((groups, 2)),
        ],
        compiler_params=limit,
        cost_estimate=short,
        name="final_passes",
    )(ground, surface, far_rows, near_rows, floors, hops)


def solution(mesh):
    placed = (
        P(("groups", "rows", "sub"), "cols"),
        P(("groups", "rows", "sub"), "cols"),
        P("groups", "cols"),
        P("groups", ("rows", "sub")),
        P("groups", None),
    )
    return jax.shard_map(
        per_device,
        mesh=mesh,
        in_specs=placed,
        out_specs=P(("groups", "rows", "sub"), "cols"),
        check_vma=False,
    )
```

```python
import functools

import jax
import jax.numpy as jnp
from jax import lax
from jax.experimental import pallas as pl
from jax.experimental.pallas import tpu as pltpu
from jax.sharding import PartitionSpec as P

PASSES = 8
FINAL = 4
ROUNDS = 4
HALO = PASSES
SUBS = 8
LANES = 128
WANTED = 16
SKEW = SUBS + 1
AHEAD = 5

unreached = 1000000000.0
rise_step = 0.01
hop_rise = 0.05
spill_lift = 3.0


def matching(count, first):
    pairs = []
    for low in range(first, count - 1, 2):
        pairs += [(low, low + 1), (low + 1, low)]
    return pairs


def closed(pairs, count):
    used = {source for source, _ in pairs}
    return pairs + [(place, place) for place in range(count) if place not in used]


def cross(row_pairs, col_pairs, cols, subs):
    def device(place, col):
        return (place // subs * cols + col) * subs + place % subs

    return [
        (device(row, col), device(row_to, col_to))
        for row, row_to in row_pairs
        for col, col_to in col_pairs
    ]


def chain_place():
    subs = lax.axis_size("sub")
    return lax.axis_index("rows") * subs + lax.axis_index("sub"), lax.axis_size("rows") * subs


def position():
    sub = lax.broadcasted_iota(jnp.int32, (SUBS, LANES), 0)
    lane = lax.broadcasted_iota(jnp.int32, (SUBS, LANES), 1)
    return sub, lane


def aligned(start):
    return start if isinstance(start, int) else pl.multiple_of(start, SUBS)


def rows_at(first, count, size):
    return pl.ds(aligned(first * size), count * size)


def register(row, slot, size):
    return pl.ds(aligned(row * size + slot * SUBS), SUBS)


def side_marks(sides_ref):
    height = sides_ref.shape[1]
    square = (height, height)
    diagonal = lax.broadcasted_iota(jnp.int32, square, 0) == lax.broadcasted_iota(jnp.int32, square, 1)
    marks = sides_ref[...].astype(jnp.float32)
    return [
        jnp.sum(jnp.where(diagonal, marks[side : side + 1, :], 0.0), axis=1, keepdims=True)
        for side in range(2)
    ]


def start_all(copies):
    for copy in copies:
        copy.start()
    return copies


def wait_all(copies):
    for copy in copies:
        copy.wait()


def edge_kernel(
    ground_hbm, depth_hbm, rows_hbm, sides_hbm, links_hbm,
    far_ref, near_ref, even_ref, odd_ref, ground_out, surface_out, links_ref,
    ground_ref, depth_ref, rows_ref, sides_ref, stage_ref, sems, small_sems,
):
    height, width = ground_hbm.shape
    tiles = width // (SUBS * LANES)
    small = [
        pltpu.make_async_copy(rows_hbm, rows_ref, small_sems.at[0]),
        pltpu.make_async_copy(sides_hbm, sides_ref, small_sems.at[1]),
        pltpu.make_async_copy(links_hbm, links_ref, small_sems.at[2]),
    ]
    start_all(small[1:])
    copies = start_own(ground_hbm, depth_hbm, ground_ref, depth_ref, sems)
    start_all(small[:1])
    wait_all(small)
    edges = fold_own(copies, ground_ref, depth_ref, rows_ref, sides_ref, ground_out, surface_out, stage_ref)
    place, _ = chain_place()
    top = place % 2 == 0
    size, packed = (tiles + 1) * SUBS, tiles * SUBS
    for out_ref, is_top in ((far_ref, top), (near_ref, jnp.logical_not(top))):
        first = HALO + jnp.where(is_top, 0, height - HALO)
        bases = (jnp.where(is_top, 0, HALO - 1), jnp.where(is_top, HALO - 1, 0))
        for source, base in zip((ground_out, surface_out), bases):
            for row in range(HALO):
                for slot in range(tiles):
                    out_ref[register(base + row, slot, packed), :] = source[register(first + row, slot, size), :]
    rightward = lax.axis_index("cols") % 2 == 0
    for group, values in enumerate(edges):
        for kind in range(2):
            rows = pl.ds(kind * height + group * SUBS, SUBS)
            even_ref[rows, :] = jnp.where(rightward, values[1][kind], values[0][kind])
            odd_ref[rows, :] = jnp.where(rightward, values[0][kind], values[1][kind])


def start_own(ground_hbm, depth_hbm, ground_ref, depth_ref, sems):
    pieces = sems.shape[1]
    part = ground_hbm.shape[1] // pieces
    copies = []
    for piece in range(pieces):
        where = (slice(None), pl.ds(piece * part, part))
        copies.append(
            start_all(
                [
                    pltpu.make_async_copy(ground_hbm.at[where], ground_ref.at[where], sems.at[0, piece]),
                    pltpu.make_async_copy(depth_hbm.at[where], depth_ref.at[where], sems.at[1, piece]),
                ]
            )
        )
    return copies


def staged(base, slot, number):
    return pl.ds(base + (slot * SUBS + number) * SKEW, SUBS)


def across(base, slot, number):
    return pl.ds(base + slot * SUBS * SKEW + number, SUBS, stride=SKEW)


def fold_own(copies, ground_ref, depth_ref, rows_ref, sides_ref, ground_out, surface_out, stage_ref):
    height, width = ground_ref.shape
    groups = height // SUBS
    tiles = width // (SUBS * LANES)
    last_tile = width // LANES - 1
    part = width // len(copies)
    size = (tiles + 1) * SUBS
    place, places = chain_place()
    col, cols = lax.axis_index("cols"), lax.axis_size("cols")
    sub, lane = position()
    marks = side_marks(sides_ref)
    edges = [[] for _ in range(groups)]
    for tile in range(last_tile + 1):
        if tile * LANES % part == 0:
            wait_all(copies[tile * LANES // part])
        columns = pl.ds(tile * LANES, LANES)
        for group in range(groups):
            rows = pl.ds(group * SUBS, SUBS)
            ground = ground_ref[rows, columns]
            surface = ground + depth_ref[rows, columns]
            outlets = []
            if group == 0:
                outlets.append((rows_ref[0:1, columns] == 1) & (sub == 0) & (place == 0))
            if group == groups - 1:
                outlets.append(
                    (rows_ref[1:2, columns] == 1) & (sub == SUBS - 1) & (place == places - 1)
                )
            if tile == 0:
                outlets.append(
                    (marks[0][group * SUBS : (group + 1) * SUBS] > 0.5) & (lane == 0) & (col == 0)
                )
            if tile == last_tile:
                outlets.append(
                    (marks[1][group * SUBS : (group + 1) * SUBS] > 0.5)
                    & (lane == LANES - 1)
                    & (col == cols - 1)
                )
            for outlet in outlets:
                surface = jnp.where(outlet, ground, surface)
            chunk, slot = tile // tiles, tile % tiles
            for kind, value in enumerate((ground, surface)):
                stage_ref[staged((group * 2 + kind) * tiles * SUBS * SKEW, slot, chunk), :] = value
            if tile in (0, last_tile):
                edges[group].append((ground, surface))
    for group in range(groups):
        for kind, out_ref in enumerate((ground_out, surface_out)):
            base = (group * 2 + kind) * tiles * SUBS * SKEW
            for slot in range(tiles):
                for row in range(SUBS):
                    where = register(HALO + group * SUBS + row, slot, size)
                    out_ref[where, :] = stage_ref[across(base, slot, row), :]
    return edges


def unpack_rows(rows_ref, first, is_top, present, strip_refs, strip_rows, ground_ref, surface_ref, tiles):
    packed = tiles * SUBS
    size = packed + SUBS
    bases = (jnp.where(is_top, HALO - 1, 0), jnp.where(is_top, 0, HALO - 1))
    for base, out_ref, strip_row in zip(bases, (ground_ref, surface_ref), strip_rows):
        for row in range(HALO):
            values = [
                jnp.where(present, rows_ref[register(base + row, slot, packed), :], unreached)
                for slot in range(tiles)
            ]
            for slot in range(tiles):
                out_ref[register(first + row, slot, size), :] = values[slot]
            fill_seam(out_ref, first + row, values[0], values[-1], strip_refs, strip_row + row, present, tiles)


def fill_seam(out_ref, row, first_tile, last_tile, strip_refs, strip_row, present, tiles):
    col, cols = lax.axis_index("cols"), lax.axis_size("cols")
    sub, lane = position()
    rightward = col % 2 == 0
    even, odd = [ref[pl.ds(strip_row, 1), :] for ref in strip_refs]
    after = jnp.where(present & (col < cols - 1), jnp.where(rightward, even, odd), unreached)
    before = jnp.where(present & (col > 0), jnp.where(rightward, odd, even), unreached)
    after = jnp.where(sub == SUBS - 1, after, pltpu.roll(first_tile, SUBS - 1, 0))
    before = jnp.where(sub == 0, before, pltpu.roll(last_tile, 1, 0))
    out_ref[register(row, tiles, (tiles + 1) * SUBS), :] = jnp.where(lane < LANES // 2, after, before)


def relax_passes(passes, ground, ring):
    size = ring * SUBS
    _, lane = position()
    at_first = lane == 0
    at_last = lane == LANES - 1
    order = [ring - 1] + list(range(ring - 1))
    made = {}

    def make(number, pair, slot):
        source, _, first, _, _ = passes[number]
        row = first + 2 * pair
        values = [source[register(row + step, slot, size), :] for step in range(-1, 3)]
        both = jnp.minimum(values[1], values[2])
        for one, column in enumerate((jnp.minimum(values[0], both), jnp.minimum(both, values[3]))):
            rolled = pltpu.roll(column, 1, 1), pltpu.roll(column, LANES - 1, 1)
            made[number, pair, one, slot] = (column, *rolled, values[1 + one])

    def finish(number, pair, slot):
        _, target, first, _, _ = passes[number]
        for one in range(2):
            row = first + 2 * pair + one
            before, here, after = [made[number, pair, one, (slot + step) % ring] for step in (-1, 0, 1)]
            from_left = jnp.where(at_first, before[1], here[1])
            from_right = jnp.where(at_last, after[2], here[2])
            lowest = jnp.minimum(jnp.minimum(from_left, from_right), here[0])
            where = register(row, slot, size)
            raised = jnp.minimum(here[3], lowest + rise_step)
            target[where, :] = jnp.maximum(ground[where, :], raised)

    def items(slots):
        return [
            (number, pair, slot)
            for number, (_, _, _, count, _) in enumerate(passes)
            for pair in range(count // 2)
            for slot in slots
        ]

    makes, finishes = items(order), items(range(ring))
    for number in range(len(makes) + AHEAD):
        if number < len(makes):
            make(*makes[number])
        if number >= AHEAD:
            done = finishes[number - AHEAD]
            finish(*done)
            _, _, _, count, then = passes[done[0]]
            if then is not None and done[1:] == (count // 2 - 1, ring - 1):
                then()


def hop_counts(links_ref, hops_ref, needed):
    tiles, degree = links_ref.shape
    links = links_ref[...]
    number = lax.broadcasted_iota(jnp.int32, (tiles, tiles), 1)
    linked = links[:, 0:1] == number
    for edge in range(1, degree):
        linked = linked | (links[:, edge : edge + 1] == number)
    linked = linked.astype(jnp.float32)
    index = lax.broadcasted_iota(jnp.int32, (WANTED, tiles), 0)
    tile = lax.broadcasted_iota(jnp.int32, (WANTED, tiles), 1)
    reached = jnp.zeros((WANTED, tiles), jnp.float32)
    for number, wanted in enumerate(needed):
        reached = jnp.where((index == number) & (tile == wanted), 1.0, reached)
    hops = jnp.where(reached > 0.5, 0.0, float(ROUNDS + 1))
    for hop in range(1, ROUNDS + 1):
        reached = jnp.dot(reached, linked, preferred_element_type=jnp.float32)
        reached = jnp.where(reached > 0.5, 1.0, 0.0)
        hops = jnp.minimum(hops, jnp.where(reached > 0.5, float(hop), float(ROUNDS + 1)))
    for number in range(tiles):
        hops_ref[pl.ds(number * WANTED, WANTED), :] = jnp.broadcast_to(
            hops[:, number : number + 1], (WANTED, LANES)
        )


def needed_tiles():
    row, rows = lax.axis_index("rows"), lax.axis_size("rows")
    col, cols = lax.axis_index("cols"), lax.axis_size("cols")
    sub, subs = lax.axis_index("sub"), lax.axis_size("sub")
    above = jnp.maximum(jnp.where(sub == 0, row - 1, row), 0)
    below = jnp.minimum(jnp.where(sub == subs - 1, row + 1, row), rows - 1)
    left = jnp.maximum(col - 1, 0)
    right = jnp.minimum(col + 1, cols - 1)
    return [r * cols + c for r in (above, row, below) for c in (left, col, right)]


def hops_kernel(links_ref, hops_ref):
    hop_counts(links_ref, hops_ref, needed_tiles())


def copy_rows(source, first, target, ring):
    for row in range(FINAL):
        for slot in range(ring):
            target[register(row, slot, ring * SUBS), :] = source[register(first + row, slot, ring * SUBS), :]


def inner_kernel(height, tiles, near_ref, own_even_ref, own_odd_ref, near_even_ref, near_odd_ref, *refs):
    ground_ref, surface_ref, other_ref, near_out = refs[3:]
    own_strips, near_strips = (own_even_ref, own_odd_ref), (near_even_ref, near_odd_ref)
    ring = tiles + 1
    size = ring * SUBS
    place, places = chain_place()
    top = place % 2 == 0
    has_near = jnp.where(top, place < places - 1, place > 0)
    unpack_rows(
        near_ref,
        jnp.where(top, HALO + height, 0),
        jnp.logical_not(top),
        has_near,
        near_strips,
        [kind * height + jnp.where(top, 0, height - HALO) for kind in range(2)],
        ground_ref,
        surface_ref,
        tiles,
    )
    for kind, out_ref in enumerate((ground_ref, surface_ref)):
        for row in range(height):
            first_tile = out_ref[register(HALO + row, 0, size), :]
            last_tile = out_ref[register(HALO + row, tiles - 1, size), :]
            fill_seam(
                out_ref, HALO + row, first_tile, last_tile, own_strips, kind * height + row, place >= 0, tiles
            )
    buffers = (surface_ref, other_ref)
    passes = []
    for step in range(1, PASSES + 1):
        first = step + jnp.where(top, HALO, 0)
        passes.append((buffers[(step + 1) % 2], buffers[step % 2], first, height + HALO - 2 * step, None))
    relax_passes(passes, ground_ref, ring)
    copy_rows(surface_ref, jnp.where(top, HALO + height - FINAL, HALO), near_out, ring)


def outer_kernel(height, tiles, far_ref, even_ref, odd_ref, *refs):
    ground_ref, surface_ref, other_ref, level_ref, far_out = refs[3:8]
    ring = tiles + 1
    size = ring * SUBS
    place, places = chain_place()
    top = place % 2 == 0
    has_far = jnp.where(top, place > 0, place < places - 1)
    unpack_rows(
        far_ref,
        jnp.where(top, 0, HALO + height),
        top,
        has_far,
        (even_ref, odd_ref),
        [kind * height + jnp.where(top, height - HALO, 0) for kind in range(2)],
        ground_ref,
        surface_ref,
        tiles,
    )
    buffers = (surface_ref, other_ref)
    passes = []
    for step in range(1, PASSES + 1):
        first = jnp.where(top, step, HALO + height - step)
        passes.append((buffers[(step + 1) % 2], buffers[step % 2], first, HALO, None))
    relax_passes(passes, ground_ref, ring)
    copy_rows(surface_ref, jnp.where(top, HALO, HALO + height - FINAL), far_out, ring)
    band, bands = lax.axis_index("sub"), lax.axis_size("sub")
    sub, lane = position()

    def at(row, slot):
        return surface_ref[register(HALO + row, slot, size), :]

    first_cell = (sub == 0) & (lane == 0)
    last_cell = (sub == SUBS - 1) & (lane == LANES - 1)
    first_lows, last_lows, row_lows = [], [], []
    for row in range(height):
        first_lows.append(at(row, 0))
        last_lows.append(at(row, tiles - 1))
    for slot in range(tiles):
        row_lows.append(jnp.where(band == 0, at(0, slot), unreached))
        row_lows.append(jnp.where(band == bands - 1, at(height - 1, slot), unreached))
    lowest = jnp.minimum(
        least(row_lows),
        jnp.minimum(
            jnp.where(first_cell, least(first_lows), unreached),
            jnp.where(last_cell, least(last_lows), unreached),
        ),
    )
    lowest = jnp.min(jnp.min(lowest, axis=0, keepdims=True), axis=1, keepdims=True)
    level_ref[...] = jnp.broadcast_to(lowest, level_ref.shape)


def least(values):
    values = list(values)
    while len(values) > 1:
        values = [
            jnp.minimum(*values[number : number + 2]) if number + 1 < len(values) else values[number]
            for number in range(0, len(values), 2)
        ]
    return values[0]


def late_kernel(
    height, tiles, ground_ref, surface_ref, far_ref, near_ref, floors_ref, hops_ref, out_hbm,
    one_ref, two_ref, out_ref, ceilings_ref, stage_ref, sems,
):
    ring = tiles + 1
    size = ring * SUBS
    sub, lane = position()
    bands = lax.axis_size("sub")
    offers = []
    for tile in range(floors_ref.shape[0] // bands):
        raised = [least(floors_ref[pl.ds(tile * bands + band, 1), :] for band in range(bands))]
        for hop in range(ROUNDS):
            raised.append(raised[-1] + hop_rise)
        hops = hops_ref[pl.ds(tile * WANTED, WANTED), :]
        offer = jnp.full((WANTED, LANES), unreached, jnp.float32)
        for hop in range(ROUNDS + 1):
            offer = jnp.where(hops == float(hop), raised[hop], offer)
        offers.append(offer)
    ceilings_ref[...] = least(offers) + spill_lift
    ceilings = [jnp.broadcast_to(ceilings_ref[pl.ds(index, 1), :], (SUBS, LANES)) for index in range(9)]
    pairs = []
    for region in range(3):
        left, middle, right = ceilings[3 * region : 3 * region + 3]
        seam = jnp.where(
            lane < LANES // 2,
            jnp.where(sub == SUBS - 1, right, middle),
            jnp.where(sub == 0, left, middle),
        )
        pairs.append((middle, seam))
    place, _ = chain_place()
    top = place % 2 == 0
    low, high = HALO - FINAL, HALO + height
    far_pair = [jnp.where(top, above, below) for above, below in zip(pairs[0], pairs[2])]
    near_pair = [jnp.where(top, below, above) for above, below in zip(pairs[0], pairs[2])]
    spans = (
        (surface_ref, HALO, HALO, height, pairs[1]),
        (near_ref, 0, jnp.where(top, high, low), FINAL, near_pair),
        (far_ref, 0, jnp.where(top, low, high), FINAL, far_pair),
    )
    for source, source_first, first, rows, (middle, seam) in spans:
        for row in range(rows):
            for slot in range(ring):
                value = source[register(source_first + row, slot, size), :]
                value = jnp.minimum(value, seam if slot == tiles else middle)
                where = register(first + row, slot, size)
                one_ref[where, :] = jnp.maximum(ground_ref[where, :], value)
    buffers = (one_ref, two_ref)
    passes = []
    for step in range(1, FINAL):
        first = HALO - FINAL + step
        count = 2 * HALO + height - 2 * first
        passes.append((buffers[(step + 1) % 2], buffers[step % 2], first, count, None))
    source, target = buffers[(FINAL + 1) % 2], buffers[FINAL % 2]
    copies = []

    def unfold(group):
        first = HALO + group * SUBS
        half = tiles * SUBS // 2
        for slot in range(tiles):
            for row in range(SUBS):
                stage_ref[staged(0, slot, row), :] = target[register(first + row, slot, size), :]
        for tile in range(tiles * SUBS):
            chunk, slot = tile // tiles, tile % tiles
            columns = pl.ds(tile * LANES, LANES)
            out_ref[pl.ds(group * SUBS, SUBS), columns] = stage_ref[across(0, slot, chunk), :]
            if tile % half == half - 1:
                side = tile // half
                where = (pl.ds(group * SUBS, SUBS), pl.ds(side * half * LANES, half * LANES))
                copy = pltpu.make_async_copy(out_ref.at[where], out_hbm.at[where], sems.at[group, side])
                copies.extend(start_all([copy]))

    for group in range(height // SUBS):
        first = HALO + group * SUBS
        passes.append((source, target, first, SUBS, functools.partial(unfold, group)))
    relax_passes(passes, ground_ref, ring)
    wait_all(copies)


def in_vmem(count):
    return [pl.BlockSpec(memory_space=pltpu.VMEM)] * count


def in_hbm(count):
    return [pl.BlockSpec(memory_space=pltpu.HBM)] * count


def per_device(elevation, fill_depth, edge_rows, edge_sides, adjacency):
    height, width = elevation.shape
    tiles = width // (SUBS * LANES)
    groups = height // SUBS
    f32 = jnp.float32
    packed = tiles * SUBS
    size = packed + SUBS
    tile_count = adjacency.shape[0]
    places = lax.axis_size(("rows", "sub"))
    cols, subs = lax.axis_size("cols"), lax.axis_size("sub")
    short = pl.CostEstimate(flops=1024, bytes_accessed=1024, transcendentals=0)
    limit = pltpu.CompilerParams(vmem_limit_bytes=24 << 20)
    arguments = [
        pltpu.with_memory_space_constraint(value, pltpu.HBM)
        for value in (elevation, fill_depth, edge_rows, edge_sides, adjacency)
    ]
    sent = pltpu.VMEM(((2 * HALO - 1) * packed, LANES), f32)
    strip = pltpu.VMEM((2 * height, LANES), f32)
    work = pltpu.VMEM(((height + 2 * HALO) * size, LANES), f32)
    far, near, even, odd, ground, surface, links = pl.pallas_call(
        edge_kernel,
        out_shape=[sent, sent, strip, strip, work, work, pltpu.VMEM(adjacency.shape, jnp.int32)],
        in_specs=in_hbm(5),
        out_specs=in_vmem(7),
        scratch_shapes=[
            pltpu.VMEM((height, width), f32),
            pltpu.VMEM((height, width), f32),
            pltpu.VMEM(edge_rows.shape, jnp.int32),
            pltpu.VMEM(edge_sides.shape, jnp.int32),
            pltpu.VMEM((2 * groups * packed * SKEW, LANES), f32),
            pltpu.SemaphoreType.DMA((2, 4)),
            pltpu.SemaphoreType.DMA((3,)),
        ],
        compiler_params=limit,
        cost_estimate=short,
        name="edge_rows",
    )(*arguments)

    near_pairs, far_pairs = [matching(places, first) for first in range(2)]
    stay = [(place, place) for place in range(places)]
    ends = [(place, place) for place in range(places) if place not in dict(far_pairs)]
    groups_count = lax.axis_size("groups")
    part = places * cols
    far_all = []
    for group, other in closed(matching(groups_count, 0), groups_count):
        for chosen, target in ((far_pairs, group), (ends, other)):
            for source, arrival in cross(chosen, [(col, col) for col in range(cols)], cols, subs):
                far_all.append((group * part + source, target * part + arrival))
    device_axes = ("rows", "cols", "sub")

    def swap_strips(pieces, row_pairs):
        arrived = []
        for first, piece in enumerate(pieces):
            pairs = cross(row_pairs, matching(cols, first), cols, subs)
            arrived.append(lax.ppermute(piece, device_axes, pairs) if pairs else piece)
        return arrived

    far_strips = swap_strips((even, odd), far_pairs + ends)
    far_rows = lax.ppermute(far, ("groups",) + device_axes, far_all)
    near_rows = lax.ppermute(near, ("rows", "sub"), near_pairs)
    strips = swap_strips((even, odd), stay) + swap_strips((even, odd), near_pairs)

    hops = pl.pallas_call(
        hops_kernel,
        out_shape=pltpu.VMEM((WANTED * tile_count, LANES), f32),
        in_specs=in_vmem(1),
        out_specs=pl.BlockSpec(memory_space=pltpu.VMEM),
        compiler_params=limit,
        cost_estimate=short,
        name="tile_hops",
    )(links)

    def inner(*refs):
        inner_kernel(height, tiles, *refs)

    again = pltpu.VMEM((FINAL * size, LANES), f32)
    ground, surface, other, near = pl.pallas_call(
        inner,
        out_shape=[work, work, work, again],
        in_specs=in_vmem(8),
        out_specs=in_vmem(4),
        input_output_aliases={5: 0, 6: 1},
        compiler_params=limit,
        cost_estimate=short,
        name="inner_passes",
    )(near_rows, *strips, ground, surface, hops)

    def outer(far_ref, *refs):
        outer_kernel(height, tiles, far_ref, *refs)

    devices = lax.axis_size(device_axes)
    ground, surface, other, floors, far = pl.pallas_call(
        outer,
        out_shape=[work, work, work, pltpu.VMEM((devices, LANES), f32), again],
        in_specs=in_vmem(6),
        out_specs=in_vmem(5),
        input_output_aliases={3: 0, 4: 1, 5: 2},
        compiler_params=limit,
        cost_estimate=short,
        name="outer_passes",
    )(far_rows, *far_strips, ground, surface, other)

    far_rows = lax.ppermute(far, ("groups",) + device_axes, far_all)
    near_rows = lax.ppermute(near, ("rows", "sub"), near_pairs)
    floors = lax.all_to_all(floors, device_axes, 0, 0, tiled=True)

    def late(*refs):
        late_kernel(height, tiles, *refs)

    return pl.pallas_call(
        late,
        out_shape=jax.ShapeDtypeStruct((height, width), f32),
        in_specs=in_vmem(6),
        out_specs=pl.BlockSpec(memory_space=pltpu.HBM),
        scratch_shapes=[
            work,
            work,
            pltpu.VMEM((height, width), f32),
            pltpu.VMEM((WANTED, LANES), f32),
            pltpu.VMEM((packed * SKEW, LANES), f32),
            pltpu.SemaphoreType.DMA((groups, 2)),
        ],
        compiler_params=limit,
        cost_estimate=short,
        name="final_passes",
    )(ground, surface, far_rows, near_rows, floors, hops)


def solution(mesh):
    placed = (
        P(("groups", "rows", "sub"), "cols"),
        P(("groups", "rows", "sub"), "cols"),
        P("groups", "cols"),
        P("groups", ("rows", "sub")),
        P("groups", None),
    )
    return jax.shard_map(
        per_device,
        mesh=mesh,
        in_specs=placed,
        out_specs=P(("groups", "rows", "sub"), "cols"),
        check_vma=False,
    )
```

```python
import functools

import jax
import jax.numpy as jnp
from jax import lax
from jax.experimental import pallas as pl
from jax.experimental.pallas import tpu as pltpu
from jax.sharding import PartitionSpec as P

PASSES = 8
FINAL = 4
ROUNDS = 4
HALO = PASSES
SUBS = 8
LANES = 128
WANTED = 16
SKEW = SUBS + 1
AHEAD = 5

unreached = 1000000000.0
rise_step = 0.01
hop_rise = 0.05
spill_lift = 3.0


def matching(count, first):
    pairs = []
    for low in range(first, count - 1, 2):
        pairs += [(low, low + 1), (low + 1, low)]
    return pairs


def closed(pairs, count):
    used = {source for source, _ in pairs}
    return pairs + [(place, place) for place in range(count) if place not in used]


def cross(row_pairs, col_pairs, cols, subs):
    def device(place, col):
        return (place // subs * cols + col) * subs + place % subs

    return [
        (device(row, col), device(row_to, col_to))
        for row, row_to in row_pairs
        for col, col_to in col_pairs
    ]


def chain_place():
    subs = lax.axis_size("sub")
    return lax.axis_index("rows") * subs + lax.axis_index("sub"), lax.axis_size("rows") * subs


def position():
    sub = lax.broadcasted_iota(jnp.int32, (SUBS, LANES), 0)
    lane = lax.broadcasted_iota(jnp.int32, (SUBS, LANES), 1)
    return sub, lane


def aligned(start):
    return start if isinstance(start, int) else pl.multiple_of(start, SUBS)


def rows_at(first, count, size):
    return pl.ds(aligned(first * size), count * size)


def register(row, slot, size):
    return pl.ds(aligned(row * size + slot * SUBS), SUBS)


def side_marks(sides_ref):
    height = sides_ref.shape[1]
    square = (height, height)
    diagonal = lax.broadcasted_iota(jnp.int32, square, 0) == lax.broadcasted_iota(jnp.int32, square, 1)
    marks = sides_ref[...].astype(jnp.float32)
    return [
        jnp.sum(jnp.where(diagonal, marks[side : side + 1, :], 0.0), axis=1, keepdims=True)
        for side in range(2)
    ]


def start_all(copies):
    for copy in copies:
        copy.start()
    return copies


def wait_all(copies):
    for copy in copies:
        copy.wait()


def edge_kernel(
    ground_hbm, depth_hbm, rows_hbm, sides_hbm, links_hbm,
    far_ref, near_low_ref, near_high_ref, even_ref, odd_ref, ground_out, surface_out, links_ref,
    ground_ref, depth_ref, rows_ref, sides_ref, stage_ref, sems, small_sems,
):
    height, width = ground_hbm.shape
    tiles = width // (SUBS * LANES)
    small = [
        pltpu.make_async_copy(rows_hbm, rows_ref, small_sems.at[0]),
        pltpu.make_async_copy(sides_hbm, sides_ref, small_sems.at[1]),
        pltpu.make_async_copy(links_hbm, links_ref, small_sems.at[2]),
    ]
    start_all(small[1:])
    copies = start_own(ground_hbm, depth_hbm, ground_ref, depth_ref, sems)
    start_all(small[:1])
    wait_all(small)
    edges = fold_own(copies, ground_ref, depth_ref, rows_ref, sides_ref, ground_out, surface_out, stage_ref)
    place, _ = chain_place()
    top = place % 2 == 0
    size = (tiles + 1) * SUBS
    for out_refs, is_top in (((far_ref,), top), ((near_low_ref, near_high_ref), jnp.logical_not(top))):
        share = tiles // len(out_refs)
        first = HALO + jnp.where(is_top, 0, height - HALO)
        bases = (jnp.where(is_top, 0, HALO - 1), jnp.where(is_top, HALO - 1, 0))
        for source, base in zip((ground_out, surface_out), bases):
            for row in range(HALO):
                for slot in range(tiles):
                    where = register(base + row, slot % share, share * SUBS)
                    out_refs[slot // share][where, :] = source[register(first + row, slot, size), :]
    rightward = lax.axis_index("cols") % 2 == 0
    for group, values in enumerate(edges):
        for kind in range(2):
            rows = pl.ds(kind * height + group * SUBS, SUBS)
            even_ref[rows, :] = jnp.where(rightward, values[1][kind], values[0][kind])
            odd_ref[rows, :] = jnp.where(rightward, values[0][kind], values[1][kind])


def start_own(ground_hbm, depth_hbm, ground_ref, depth_ref, sems):
    pieces = sems.shape[1]
    part = ground_hbm.shape[1] // pieces
    copies = []
    for piece in range(pieces):
        where = (slice(None), pl.ds(piece * part, part))
        copies.append(
            start_all(
                [
                    pltpu.make_async_copy(ground_hbm.at[where], ground_ref.at[where], sems.at[0, piece]),
                    pltpu.make_async_copy(depth_hbm.at[where], depth_ref.at[where], sems.at[1, piece]),
                ]
            )
        )
    return copies


def staged(base, slot, number):
    return pl.ds(base + (slot * SUBS + number) * SKEW, SUBS)


def across(base, slot, number):
    return pl.ds(base + slot * SUBS * SKEW + number, SUBS, stride=SKEW)


def fold_own(copies, ground_ref, depth_ref, rows_ref, sides_ref, ground_out, surface_out, stage_ref):
    height, width = ground_ref.shape
    groups = height // SUBS
    tiles = width // (SUBS * LANES)
    last_tile = width // LANES - 1
    part = width // len(copies)
    size = (tiles + 1) * SUBS
    place, places = chain_place()
    col, cols = lax.axis_index("cols"), lax.axis_size("cols")
    sub, lane = position()
    marks = side_marks(sides_ref)
    edges = [[] for _ in range(groups)]
    for tile in range(last_tile + 1):
        if tile * LANES % part == 0:
            wait_all(copies[tile * LANES // part])
        columns = pl.ds(tile * LANES, LANES)
        for group in range(groups):
            rows = pl.ds(group * SUBS, SUBS)
            ground = ground_ref[rows, columns]
            surface = ground + depth_ref[rows, columns]
            outlets = []
            if group == 0:
                outlets.append((rows_ref[0:1, columns] == 1) & (sub == 0) & (place == 0))
            if group == groups - 1:
                outlets.append(
                    (rows_ref[1:2, columns] == 1) & (sub == SUBS - 1) & (place == places - 1)
                )
            if tile == 0:
                outlets.append(
                    (marks[0][group * SUBS : (group + 1) * SUBS] > 0.5) & (lane == 0) & (col == 0)
                )
            if tile == last_tile:
                outlets.append(
                    (marks[1][group * SUBS : (group + 1) * SUBS] > 0.5)
                    & (lane == LANES - 1)
                    & (col == cols - 1)
                )
            for outlet in outlets:
                surface = jnp.where(outlet, ground, surface)
            chunk, slot = tile // tiles, tile % tiles
            for kind, value in enumerate((ground, surface)):
                stage_ref[staged((group * 2 + kind) * tiles * SUBS * SKEW, slot, chunk), :] = value
            if tile in (0, last_tile):
                edges[group].append((ground, surface))
    for group in range(groups):
        for kind, out_ref in enumerate((ground_out, surface_out)):
            base = (group * 2 + kind) * tiles * SUBS * SKEW
            for slot in range(tiles):
                for row in range(SUBS):
                    where = register(HALO + group * SUBS + row, slot, size)
                    out_ref[where, :] = stage_ref[across(base, slot, row), :]
    return edges


def unpack_rows(rows_refs, first, is_top, present, strip_refs, strip_rows, ground_ref, surface_ref, tiles):
    share = tiles // len(rows_refs)
    size = (tiles + 1) * SUBS
    bases = (jnp.where(is_top, HALO - 1, 0), jnp.where(is_top, 0, HALO - 1))
    for base, out_ref, strip_row in zip(bases, (ground_ref, surface_ref), strip_rows):
        for row in range(HALO):
            values = [
                jnp.where(
                    present, rows_refs[slot // share][register(base + row, slot % share, share * SUBS), :], unreached
                )
                for slot in range(tiles)
            ]
            for slot in range(tiles):
                out_ref[register(first + row, slot, size), :] = values[slot]
            fill_seam(out_ref, first + row, values[0], values[-1], strip_refs, strip_row + row, present, tiles)


def fill_seam(out_ref, row, first_tile, last_tile, strip_refs, strip_row, present, tiles):
    col, cols = lax.axis_index("cols"), lax.axis_size("cols")
    sub, lane = position()
    rightward = col % 2 == 0
    even, odd = [ref[pl.ds(strip_row, 1), :] for ref in strip_refs]
    after = jnp.where(present & (col < cols - 1), jnp.where(rightward, even, odd), unreached)
    before = jnp.where(present & (col > 0), jnp.where(rightward, odd, even), unreached)
    after = jnp.where(sub == SUBS - 1, after, pltpu.roll(first_tile, SUBS - 1, 0))
    before = jnp.where(sub == 0, before, pltpu.roll(last_tile, 1, 0))
    out_ref[register(row, tiles, (tiles + 1) * SUBS), :] = jnp.where(lane < LANES // 2, after, before)


def relax_passes(passes, ground, ring):
    size = ring * SUBS
    _, lane = position()
    at_first = lane == 0
    at_last = lane == LANES - 1
    order = [ring - 1] + list(range(ring - 1))
    made = {}

    def make(number, pair, slot):
        source, _, first, _, _ = passes[number]
        row = first + 2 * pair
        values = [source[register(row + step, slot, size), :] for step in range(-1, 3)]
        both = jnp.minimum(values[1], values[2])
        for one, column in enumerate((jnp.minimum(values[0], both), jnp.minimum(both, values[3]))):
            rolled = pltpu.roll(column, 1, 1), pltpu.roll(column, LANES - 1, 1)
            made[number, pair, one, slot] = (column, *rolled, values[1 + one])

    def finish(number, pair, slot):
        _, target, first, _, _ = passes[number]
        for one in range(2):
            row = first + 2 * pair + one
            before, here, after = [made[number, pair, one, (slot + step) % ring] for step in (-1, 0, 1)]
            from_left = jnp.where(at_first, before[1], here[1])
            from_right = jnp.where(at_last, after[2], here[2])
            lowest = jnp.minimum(jnp.minimum(from_left, from_right), here[0])
            where = register(row, slot, size)
            raised = jnp.minimum(here[3], lowest + rise_step)
            target[where, :] = jnp.maximum(ground[where, :], raised)

    def items(slots):
        return [
            (number, pair, slot)
            for number, (_, _, _, count, _) in enumerate(passes)
            for pair in range(count // 2)
            for slot in slots
        ]

    makes, finishes = items(order), items(range(ring))
    for number in range(len(makes) + AHEAD):
        if number < len(makes):
            make(*makes[number])
        if number >= AHEAD:
            done = finishes[number - AHEAD]
            finish(*done)
            _, _, _, count, then = passes[done[0]]
            if then is not None and done[1:] == (count // 2 - 1, ring - 1):
                then()


def hop_counts(links_ref, hops_ref, needed):
    tiles, degree = links_ref.shape
    links = links_ref[...]
    number = lax.broadcasted_iota(jnp.int32, (tiles, tiles), 1)
    linked = links[:, 0:1] == number
    for edge in range(1, degree):
        linked = linked | (links[:, edge : edge + 1] == number)
    linked = linked.astype(jnp.float32)
    index = lax.broadcasted_iota(jnp.int32, (WANTED, tiles), 0)
    tile = lax.broadcasted_iota(jnp.int32, (WANTED, tiles), 1)
    reached = jnp.zeros((WANTED, tiles), jnp.float32)
    for number, wanted in enumerate(needed):
        reached = jnp.where((index == number) & (tile == wanted), 1.0, reached)
    hops = jnp.where(reached > 0.5, 0.0, float(ROUNDS + 1))
    for hop in range(1, ROUNDS + 1):
        reached = jnp.dot(reached, linked, preferred_element_type=jnp.float32)
        reached = jnp.where(reached > 0.5, 1.0, 0.0)
        hops = jnp.minimum(hops, jnp.where(reached > 0.5, float(hop), float(ROUNDS + 1)))
    for number in range(tiles):
        hops_ref[pl.ds(number * WANTED, WANTED), :] = jnp.broadcast_to(
            hops[:, number : number + 1], (WANTED, LANES)
        )


def needed_tiles():
    row, rows = lax.axis_index("rows"), lax.axis_size("rows")
    col, cols = lax.axis_index("cols"), lax.axis_size("cols")
    sub, subs = lax.axis_index("sub"), lax.axis_size("sub")
    above = jnp.maximum(jnp.where(sub == 0, row - 1, row), 0)
    below = jnp.minimum(jnp.where(sub == subs - 1, row + 1, row), rows - 1)
    left = jnp.maximum(col - 1, 0)
    right = jnp.minimum(col + 1, cols - 1)
    return [r * cols + c for r in (above, row, below) for c in (left, col, right)]


def hops_kernel(links_ref, hops_ref):
    hop_counts(links_ref, hops_ref, needed_tiles())


def copy_rows(source, first, target, ring):
    for row in range(FINAL):
        for slot in range(ring):
            target[register(row, slot, ring * SUBS), :] = source[register(first + row, slot, ring * SUBS), :]


def inner_kernel(height, tiles, near_low_ref, near_high_ref, own_even_ref, own_odd_ref, near_even_ref, near_odd_ref, *refs):
    ground_ref, surface_ref, other_ref, near_out = refs[3:]
    own_strips, near_strips = (own_even_ref, own_odd_ref), (near_even_ref, near_odd_ref)
    ring = tiles + 1
    size = ring * SUBS
    place, places = chain_place()
    top = place % 2 == 0
    has_near = jnp.where(top, place < places - 1, place > 0)
    unpack_rows(
        (near_low_ref, near_high_ref),
        jnp.where(top, HALO + height, 0),
        jnp.logical_not(top),
        has_near,
        near_strips,
        [kind * height + jnp.where(top, 0, height - HALO) for kind in range(2)],
        ground_ref,
        surface_ref,
        tiles,
    )
    for kind, out_ref in enumerate((ground_ref, surface_ref)):
        for row in range(height):
            first_tile = out_ref[register(HALO + row, 0, size), :]
            last_tile = out_ref[register(HALO + row, tiles - 1, size), :]
            fill_seam(
                out_ref, HALO + row, first_tile, last_tile, own_strips, kind * height + row, place >= 0, tiles
            )
    buffers = (surface_ref, other_ref)
    passes = []
    for step in range(1, PASSES + 1):
        first = step + jnp.where(top, HALO, 0)
        passes.append((buffers[(step + 1) % 2], buffers[step % 2], first, height + HALO - 2 * step, None))
    relax_passes(passes, ground_ref, ring)
    copy_rows(surface_ref, jnp.where(top, HALO + height - FINAL, HALO), near_out, ring)


def outer_kernel(height, tiles, far_ref, even_ref, odd_ref, *refs):
    ground_ref, surface_ref, other_ref, level_ref, far_out = refs[3:8]
    ring = tiles + 1
    size = ring * SUBS
    place, places = chain_place()
    top = place % 2 == 0
    has_far = jnp.where(top, place > 0, place < places - 1)
    unpack_rows(
        (far_ref,),
        jnp.where(top, 0, HALO + height),
        top,
        has_far,
        (even_ref, odd_ref),
        [kind * height + jnp.where(top, height - HALO, 0) for kind in range(2)],
        ground_ref,
        surface_ref,
        tiles,
    )
    buffers = (surface_ref, other_ref)
    passes = []
    for step in range(1, PASSES + 1):
        first = jnp.where(top, step, HALO + height - step)
        passes.append((buffers[(step + 1) % 2], buffers[step % 2], first, HALO, None))
    relax_passes(passes, ground_ref, ring)
    copy_rows(surface_ref, jnp.where(top, HALO, HALO + height - FINAL), far_out, ring)
    band, bands = lax.axis_index("sub"), lax.axis_size("sub")
    sub, lane = position()

    def at(row, slot):
        return surface_ref[register(HALO + row, slot, size), :]

    first_cell = (sub == 0) & (lane == 0)
    last_cell = (sub == SUBS - 1) & (lane == LANES - 1)
    first_lows, last_lows, row_lows = [], [], []
    for row in range(height):
        first_lows.append(at(row, 0))
        last_lows.append(at(row, tiles - 1))
    for slot in range(tiles):
        row_lows.append(jnp.where(band == 0, at(0, slot), unreached))
        row_lows.append(jnp.where(band == bands - 1, at(height - 1, slot), unreached))
    lowest = jnp.minimum(
        least(row_lows),
        jnp.minimum(
            jnp.where(first_cell, least(first_lows), unreached),
            jnp.where(last_cell, least(last_lows), unreached),
        ),
    )
    lowest = jnp.min(jnp.min(lowest, axis=0, keepdims=True), axis=1, keepdims=True)
    level_ref[...] = jnp.broadcast_to(lowest, level_ref.shape)


def least(values):
    values = list(values)
    while len(values) > 1:
        values = [
            jnp.minimum(*values[number : number + 2]) if number + 1 < len(values) else values[number]
            for number in range(0, len(values), 2)
        ]
    return values[0]


def late_kernel(
    height, tiles, ground_ref, surface_ref, far_ref, near_ref, floors_ref, hops_ref, out_hbm,
    one_ref, two_ref, out_ref, ceilings_ref, stage_ref, sems,
):
    ring = tiles + 1
    size = ring * SUBS
    sub, lane = position()
    bands = lax.axis_size("sub")
    offers = []
    for tile in range(floors_ref.shape[0] // bands):
        raised = [least(floors_ref[pl.ds(tile * bands + band, 1), :] for band in range(bands))]
        for hop in range(ROUNDS):
            raised.append(raised[-1] + hop_rise)
        hops = hops_ref[pl.ds(tile * WANTED, WANTED), :]
        offer = jnp.full((WANTED, LANES), unreached, jnp.float32)
        for hop in range(ROUNDS + 1):
            offer = jnp.where(hops == float(hop), raised[hop], offer)
        offers.append(offer)
    ceilings_ref[...] = least(offers) + spill_lift
    ceilings = [jnp.broadcast_to(ceilings_ref[pl.ds(index, 1), :], (SUBS, LANES)) for index in range(9)]
    pairs = []
    for region in range(3):
        left, middle, right = ceilings[3 * region : 3 * region + 3]
        seam = jnp.where(
            lane < LANES // 2,
            jnp.where(sub == SUBS - 1, right, middle),
            jnp.where(sub == 0, left, middle),
        )
        pairs.append((middle, seam))
    place, _ = chain_place()
    top = place % 2 == 0
    low, high = HALO - FINAL, HALO + height
    far_pair = [jnp.where(top, above, below) for above, below in zip(pairs[0], pairs[2])]
    near_pair = [jnp.where(top, below, above) for above, below in zip(pairs[0], pairs[2])]
    spans = (
        (surface_ref, HALO, HALO, height, pairs[1]),
        (near_ref, 0, jnp.where(top, high, low), FINAL, near_pair),
        (far_ref, 0, jnp.where(top, low, high), FINAL, far_pair),
    )
    for source, source_first, first, rows, (middle, seam) in spans:
        for row in range(rows):
            for slot in range(ring):
                value = source[register(source_first + row, slot, size), :]
                value = jnp.minimum(value, seam if slot == tiles else middle)
                where = register(first + row, slot, size)
                one_ref[where, :] = jnp.maximum(ground_ref[where, :], value)
    buffers = (one_ref, two_ref)
    passes = []
    for step in range(1, FINAL):
        first = HALO - FINAL + step
        count = 2 * HALO + height - 2 * first
        passes.append((buffers[(step + 1) % 2], buffers[step % 2], first, count, None))
    source, target = buffers[(FINAL + 1) % 2], buffers[FINAL % 2]
    copies = []

    def unfold(group):
        first = HALO + group * SUBS
        half = tiles * SUBS // 2
        for slot in range(tiles):
            for row in range(SUBS):
                stage_ref[staged(0, slot, row), :] = target[register(first + row, slot, size), :]
        for tile in range(tiles * SUBS):
            chunk, slot = tile // tiles, tile % tiles
            columns = pl.ds(tile * LANES, LANES)
            out_ref[pl.ds(group * SUBS, SUBS), columns] = stage_ref[across(0, slot, chunk), :]
            if tile % half == half - 1:
                side = tile // half
                where = (pl.ds(group * SUBS, SUBS), pl.ds(side * half * LANES, half * LANES))
                copy = pltpu.make_async_copy(out_ref.at[where], out_hbm.at[where], sems.at[group, side])
                copies.extend(start_all([copy]))

    for group in range(height // SUBS):
        first = HALO + group * SUBS
        passes.append((source, target, first, SUBS, functools.partial(unfold, group)))
    relax_passes(passes, ground_ref, ring)
    wait_all(copies)


def in_vmem(count):
    return [pl.BlockSpec(memory_space=pltpu.VMEM)] * count


def in_hbm(count):
    return [pl.BlockSpec(memory_space=pltpu.HBM)] * count


def per_device(elevation, fill_depth, edge_rows, edge_sides, adjacency):
    height, width = elevation.shape
    tiles = width // (SUBS * LANES)
    groups = height // SUBS
    f32 = jnp.float32
    packed = tiles * SUBS
    size = packed + SUBS
    tile_count = adjacency.shape[0]
    places = lax.axis_size(("rows", "sub"))
    cols, subs = lax.axis_size("cols"), lax.axis_size("sub")
    short = pl.CostEstimate(flops=1024, bytes_accessed=1024, transcendentals=0)
    limit = pltpu.CompilerParams(vmem_limit_bytes=24 << 20)
    arguments = [
        pltpu.with_memory_space_constraint(value, pltpu.HBM)
        for value in (elevation, fill_depth, edge_rows, edge_sides, adjacency)
    ]
    sent = pltpu.VMEM(((2 * HALO - 1) * packed, LANES), f32)
    strip = pltpu.VMEM((2 * height, LANES), f32)
    work = pltpu.VMEM(((height + 2 * HALO) * size, LANES), f32)
    half = pltpu.VMEM(((2 * HALO - 1) * packed // 2, LANES), f32)
    far, near_low, near_high, even, odd, ground, surface, links = pl.pallas_call(
        edge_kernel,
        out_shape=[sent, half, half, strip, strip, work, work, pltpu.VMEM(adjacency.shape, jnp.int32)],
        in_specs=in_hbm(5),
        out_specs=in_vmem(8),
        scratch_shapes=[
            pltpu.VMEM((height, width), f32),
            pltpu.VMEM((height, width), f32),
            pltpu.VMEM(edge_rows.shape, jnp.int32),
            pltpu.VMEM(edge_sides.shape, jnp.int32),
            pltpu.VMEM((2 * groups * packed * SKEW, LANES), f32),
            pltpu.SemaphoreType.DMA((2, 4)),
            pltpu.SemaphoreType.DMA((3,)),
        ],
        compiler_params=limit,
        cost_estimate=short,
        name="edge_rows",
    )(*arguments)

    near_pairs, far_pairs = [matching(places, first) for first in range(2)]
    stay = [(place, place) for place in range(places)]
    ends = [(place, place) for place in range(places) if place not in dict(far_pairs)]
    groups_count = lax.axis_size("groups")
    part = places * cols
    far_all = []
    for group, other in closed(matching(groups_count, 0), groups_count):
        for chosen, target in ((far_pairs, group), (ends, other)):
            for source, arrival in cross(chosen, [(col, col) for col in range(cols)], cols, subs):
                far_all.append((group * part + source, target * part + arrival))
    device_axes = ("rows", "cols", "sub")

    def swap_strips(pieces, row_pairs):
        arrived = []
        for first, piece in enumerate(pieces):
            pairs = cross(row_pairs, matching(cols, first), cols, subs)
            arrived.append(lax.ppermute(piece, device_axes, pairs) if pairs else piece)
        return arrived

    far_strips = swap_strips((even, odd), far_pairs + ends)
    far_rows = lax.ppermute(far, ("groups",) + device_axes, far_all)
    near_rows = [lax.ppermute(part, ("rows", "sub"), near_pairs) for part in (near_low, near_high)]
    strips = swap_strips((even, odd), stay) + swap_strips((even, odd), near_pairs)

    hops = pl.pallas_call(
        hops_kernel,
        out_shape=pltpu.VMEM((WANTED * tile_count, LANES), f32),
        in_specs=in_vmem(1),
        out_specs=pl.BlockSpec(memory_space=pltpu.VMEM),
        compiler_params=limit,
        cost_estimate=short,
        name="tile_hops",
    )(links)

    def inner(*refs):
        inner_kernel(height, tiles, *refs)

    again = pltpu.VMEM((FINAL * size, LANES), f32)
    ground, surface, other, near = pl.pallas_call(
        inner,
        out_shape=[work, work, work, again],
        in_specs=in_vmem(9),
        out_specs=in_vmem(4),
        input_output_aliases={6: 0, 7: 1},
        compiler_params=limit,
        cost_estimate=short,
        name="inner_passes",
    )(*near_rows, *strips, ground, surface, hops)

    def outer(far_ref, *refs):
        outer_kernel(height, tiles, far_ref, *refs)

    devices = lax.axis_size(device_axes)
    ground, surface, other, floors, far = pl.pallas_call(
        outer,
        out_shape=[work, work, work, pltpu.VMEM((devices, LANES), f32), again],
        in_specs=in_vmem(6),
        out_specs=in_vmem(5),
        input_output_aliases={3: 0, 4: 1, 5: 2},
        compiler_params=limit,
        cost_estimate=short,
        name="outer_passes",
    )(far_rows, *far_strips, ground, surface, other)

    far_rows = lax.ppermute(far, ("groups",) + device_axes, far_all)
    near_rows = lax.ppermute(near, ("rows", "sub"), near_pairs)
    floors = lax.all_to_all(floors, device_axes, 0, 0, tiled=True)

    def late(*refs):
        late_kernel(height, tiles, *refs)

    return pl.pallas_call(
        late,
        out_shape=jax.ShapeDtypeStruct((height, width), f32),
        in_specs=in_vmem(6),
        out_specs=pl.BlockSpec(memory_space=pltpu.HBM),
        scratch_shapes=[
            work,
            work,
            pltpu.VMEM((height, width), f32),
            pltpu.VMEM((WANTED, LANES), f32),
            pltpu.VMEM((packed * SKEW, LANES), f32),
            pltpu.SemaphoreType.DMA((groups, 2)),
        ],
        compiler_params=limit,
        cost_estimate=short,
        name="final_passes",
    )(ground, surface, far_rows, near_rows, floors, hops)


def solution(mesh):
    placed = (
        P(("groups", "rows", "sub"), "cols"),
        P(("groups", "rows", "sub"), "cols"),
        P("groups", "cols"),
        P("groups", ("rows", "sub")),
        P("groups", None),
    )
    return jax.shard_map(
        per_device,
        mesh=mesh,
        in_specs=placed,
        out_specs=P(("groups", "rows", "sub"), "cols"),
        check_vma=False,
    )
```

```python
import functools

import jax
import jax.numpy as jnp
from jax import lax
from jax.experimental import pallas as pl
from jax.experimental.pallas import tpu as pltpu
from jax.sharding import PartitionSpec as P

PASSES = 8
FINAL = 4
ROUNDS = 4
HALO = PASSES
SUBS = 8
LANES = 128
WANTED = 16
SKEW = SUBS + 1
AHEAD = 5

unreached = 1000000000.0
rise_step = 0.01
hop_rise = 0.05
spill_lift = 3.0


def matching(count, first):
    pairs = []
    for low in range(first, count - 1, 2):
        pairs += [(low, low + 1), (low + 1, low)]
    return pairs


def closed(pairs, count):
    used = {source for source, _ in pairs}
    return pairs + [(place, place) for place in range(count) if place not in used]


def cross(row_pairs, col_pairs, cols, subs):
    def device(place, col):
        return (place // subs * cols + col) * subs + place % subs

    return [
        (device(row, col), device(row_to, col_to))
        for row, row_to in row_pairs
        for col, col_to in col_pairs
    ]


def chain_place():
    subs = lax.axis_size("sub")
    return lax.axis_index("rows") * subs + lax.axis_index("sub"), lax.axis_size("rows") * subs


def position():
    sub = lax.broadcasted_iota(jnp.int32, (SUBS, LANES), 0)
    lane = lax.broadcasted_iota(jnp.int32, (SUBS, LANES), 1)
    return sub, lane


def aligned(start):
    return start if isinstance(start, int) else pl.multiple_of(start, SUBS)


def rows_at(first, count, size):
    return pl.ds(aligned(first * size), count * size)


def register(row, slot, size):
    return pl.ds(aligned(row * size + slot * SUBS), SUBS)


def side_marks(sides_ref):
    height = sides_ref.shape[1]
    square = (height, height)
    diagonal = lax.broadcasted_iota(jnp.int32, square, 0) == lax.broadcasted_iota(jnp.int32, square, 1)
    marks = sides_ref[...].astype(jnp.float32)
    return [
        jnp.sum(jnp.where(diagonal, marks[side : side + 1, :], 0.0), axis=1, keepdims=True)
        for side in range(2)
    ]


def start_all(copies):
    for copy in copies:
        copy.start()
    return copies


def wait_all(copies):
    for copy in copies:
        copy.wait()


def edge_kernel(
    ground_hbm, depth_hbm, rows_hbm, sides_hbm, links_hbm,
    far_ref, near_ref, even_ref, odd_ref, ground_out, surface_out, links_ref,
    ground_ref, depth_ref, rows_ref, sides_ref, stage_ref, sems, small_sems,
):
    height, width = ground_hbm.shape
    tiles = width // (SUBS * LANES)
    small = [
        pltpu.make_async_copy(rows_hbm, rows_ref, small_sems.at[0]),
        pltpu.make_async_copy(sides_hbm, sides_ref, small_sems.at[1]),
        pltpu.make_async_copy(links_hbm, links_ref, small_sems.at[2]),
    ]
    start_all(small[1:])
    copies = start_own(ground_hbm, depth_hbm, ground_ref, depth_ref, sems)
    start_all(small[:1])
    wait_all(small)
    edges = fold_own(copies, ground_ref, depth_ref, rows_ref, sides_ref, ground_out, surface_out, stage_ref)
    place, _ = chain_place()
    top = place % 2 == 0
    size, packed = (tiles + 1) * SUBS, tiles * SUBS
    for out_ref, is_top in ((far_ref, top), (near_ref, jnp.logical_not(top))):
        first = HALO + jnp.where(is_top, 0, height - HALO)
        bases = (jnp.where(is_top, 0, HALO - 1), jnp.where(is_top, HALO - 1, 0))
        for source, base in zip((ground_out, surface_out), bases):
            for row in range(HALO):
                for slot in range(tiles):
                    out_ref[register(base + row, slot, packed), :] = source[register(first + row, slot, size), :]
    rightward = lax.axis_index("cols") % 2 == 0
    for group, values in enumerate(edges):
        for kind in range(2):
            rows = pl.ds(kind * height + group * SUBS, SUBS)
            even_ref[rows, :] = jnp.where(rightward, values[1][kind], values[0][kind])
            odd_ref[rows, :] = jnp.where(rightward, values[0][kind], values[1][kind])


def start_own(ground_hbm, depth_hbm, ground_ref, depth_ref, sems):
    pieces = sems.shape[1]
    part = ground_hbm.shape[1] // pieces
    copies = []
    for piece in range(pieces):
        where = (slice(None), pl.ds(piece * part, part))
        copies.append(
            start_all(
                [
                    pltpu.make_async_copy(ground_hbm.at[where], ground_ref.at[where], sems.at[0, piece]),
                    pltpu.make_async_copy(depth_hbm.at[where], depth_ref.at[where], sems.at[1, piece]),
                ]
            )
        )
    return copies


def staged(base, slot, number):
    return pl.ds(base + (slot * SUBS + number) * SKEW, SUBS)


def across(base, slot, number):
    return pl.ds(base + slot * SUBS * SKEW + number, SUBS, stride=SKEW)


def fold_own(copies, ground_ref, depth_ref, rows_ref, sides_ref, ground_out, surface_out, stage_ref):
    height, width = ground_ref.shape
    groups = height // SUBS
    tiles = width // (SUBS * LANES)
    last_tile = width // LANES - 1
    part = width // len(copies)
    size = (tiles + 1) * SUBS
    place, places = chain_place()
    col, cols = lax.axis_index("cols"), lax.axis_size("cols")
    sub, lane = position()
    marks = side_marks(sides_ref)
    edges = [[] for _ in range(groups)]
    for tile in range(last_tile + 1):
        if tile * LANES % part == 0:
            wait_all(copies[tile * LANES // part])
        columns = pl.ds(tile * LANES, LANES)
        for group in range(groups):
            rows = pl.ds(group * SUBS, SUBS)
            ground = ground_ref[rows, columns]
            surface = ground + depth_ref[rows, columns]
            outlets = []
            if group == 0:
                outlets.append((rows_ref[0:1, columns] == 1) & (sub == 0) & (place == 0))
            if group == groups - 1:
                outlets.append(
                    (rows_ref[1:2, columns] == 1) & (sub == SUBS - 1) & (place == places - 1)
                )
            if tile == 0:
                outlets.append(
                    (marks[0][group * SUBS : (group + 1) * SUBS] > 0.5) & (lane == 0) & (col == 0)
                )
            if tile == last_tile:
                outlets.append(
                    (marks[1][group * SUBS : (group + 1) * SUBS] > 0.5)
                    & (lane == LANES - 1)
                    & (col == cols - 1)
                )
            for outlet in outlets:
                surface = jnp.where(outlet, ground, surface)
            chunk, slot = tile // tiles, tile % tiles
            for kind, value in enumerate((ground, surface)):
                stage_ref[staged((group * 2 + kind) * tiles * SUBS * SKEW, slot, chunk), :] = value
            if tile in (0, last_tile):
                edges[group].append((ground, surface))
    for group in range(groups):
        for kind, out_ref in enumerate((ground_out, surface_out)):
            base = (group * 2 + kind) * tiles * SUBS * SKEW
            for slot in range(tiles):
                for row in range(SUBS):
                    where = register(HALO + group * SUBS + row, slot, size)
                    out_ref[where, :] = stage_ref[across(base, slot, row), :]
    return edges


def unpack_rows(rows_ref, first, is_top, present, strip_refs, strip_rows, ground_ref, surface_ref, tiles):
    packed = tiles * SUBS
    size = packed + SUBS
    bases = (jnp.where(is_top, HALO - 1, 0), jnp.where(is_top, 0, HALO - 1))
    for base, out_ref, strip_row in zip(bases, (ground_ref, surface_ref), strip_rows):
        for row in range(HALO):
            values = [
                jnp.where(present, rows_ref[register(base + row, slot, packed), :], unreached)
                for slot in range(tiles)
            ]
            for slot in range(tiles):
                out_ref[register(first + row, slot, size), :] = values[slot]
            fill_seam(out_ref, first + row, values[0], values[-1], strip_refs, strip_row + row, present, tiles)


def fill_seam(out_ref, row, first_tile, last_tile, strip_refs, strip_row, present, tiles):
    col, cols = lax.axis_index("cols"), lax.axis_size("cols")
    sub, lane = position()
    rightward = col % 2 == 0
    even, odd = [ref[pl.ds(strip_row, 1), :] for ref in strip_refs]
    after = jnp.where(present & (col < cols - 1), jnp.where(rightward, even, odd), unreached)
    before = jnp.where(present & (col > 0), jnp.where(rightward, odd, even), unreached)
    after = jnp.where(sub == SUBS - 1, after, pltpu.roll(first_tile, SUBS - 1, 0))
    before = jnp.where(sub == 0, before, pltpu.roll(last_tile, 1, 0))
    out_ref[register(row, tiles, (tiles + 1) * SUBS), :] = jnp.where(lane < LANES // 2, after, before)


def relax_passes(passes, ground, ring):
    size = ring * SUBS
    _, lane = position()
    at_first = lane == 0
    at_last = lane == LANES - 1
    order = [ring - 1] + list(range(ring - 1))
    made = {}

    def make(number, pair, slot):
        source, _, first, _, _ = passes[number]
        row = first + 2 * pair
        values = [source[register(row + step, slot, size), :] for step in range(-1, 3)]
        both = jnp.minimum(values[1], values[2])
        for one, column in enumerate((jnp.minimum(values[0], both), jnp.minimum(both, values[3]))):
            rolled = pltpu.roll(column, 1, 1), pltpu.roll(column, LANES - 1, 1)
            made[number, pair, one, slot] = (column, *rolled, values[1 + one])

    def finish(number, pair, slot):
        _, target, first, _, _ = passes[number]
        for one in range(2):
            row = first + 2 * pair + one
            before, here, after = [made[number, pair, one, (slot + step) % ring] for step in (-1, 0, 1)]
            from_left = jnp.where(at_first, before[1], here[1])
            from_right = jnp.where(at_last, after[2], here[2])
            lowest = jnp.minimum(jnp.minimum(from_left, from_right), here[0])
            where = register(row, slot, size)
            raised = jnp.minimum(here[3], lowest + rise_step)
            target[where, :] = jnp.maximum(ground[where, :], raised)

    def items(slots):
        return [
            (number, pair, slot)
            for number, (_, _, _, count, _) in enumerate(passes)
            for pair in range(count // 2)
            for slot in slots
        ]

    makes, finishes = items(order), items(range(ring))
    for number in range(len(makes) + AHEAD):
        if number < len(makes):
            make(*makes[number])
        if number >= AHEAD:
            done = finishes[number - AHEAD]
            finish(*done)
            _, _, _, count, then = passes[done[0]]
            if then is not None and done[1:] == (count // 2 - 1, ring - 1):
                then()


def hop_counts(links_ref, hops_ref, needed):
    tiles, degree = links_ref.shape
    links = links_ref[...]
    number = lax.broadcasted_iota(jnp.int32, (tiles, tiles), 1)
    linked = links[:, 0:1] == number
    for edge in range(1, degree):
        linked = linked | (links[:, edge : edge + 1] == number)
    linked = linked.astype(jnp.float32)
    index = lax.broadcasted_iota(jnp.int32, (WANTED, tiles), 0)
    tile = lax.broadcasted_iota(jnp.int32, (WANTED, tiles), 1)
    reached = jnp.zeros((WANTED, tiles), jnp.float32)
    for number, wanted in enumerate(needed):
        reached = jnp.where((index == number) & (tile == wanted), 1.0, reached)
    hops = jnp.where(reached > 0.5, 0.0, float(ROUNDS + 1))
    for hop in range(1, ROUNDS + 1):
        reached = jnp.dot(reached, linked, preferred_element_type=jnp.float32)
        reached = jnp.where(reached > 0.5, 1.0, 0.0)
        hops = jnp.minimum(hops, jnp.where(reached > 0.5, float(hop), float(ROUNDS + 1)))
    for number in range(tiles):
        hops_ref[pl.ds(number * WANTED, WANTED), :] = jnp.broadcast_to(
            hops[:, number : number + 1], (WANTED, LANES)
        )


def needed_tiles():
    row, rows = lax.axis_index("rows"), lax.axis_size("rows")
    col, cols = lax.axis_index("cols"), lax.axis_size("cols")
    sub, subs = lax.axis_index("sub"), lax.axis_size("sub")
    above = jnp.maximum(jnp.where(sub == 0, row - 1, row), 0)
    below = jnp.minimum(jnp.where(sub == subs - 1, row + 1, row), rows - 1)
    left = jnp.maximum(col - 1, 0)
    right = jnp.minimum(col + 1, cols - 1)
    return [r * cols + c for r in (above, row, below) for c in (left, col, right)]


def hops_kernel(links_ref, hops_ref):
    hop_counts(links_ref, hops_ref, needed_tiles())


def copy_rows(source, first, target, ring):
    for row in range(FINAL):
        for slot in range(ring):
            target[register(row, slot, ring * SUBS), :] = source[register(first + row, slot, ring * SUBS), :]


def inner_kernel(height, tiles, near_ref, own_even_ref, own_odd_ref, near_even_ref, near_odd_ref, *refs):
    ground_ref, surface_ref, other_ref, near_out = refs[3:]
    own_strips, near_strips = (own_even_ref, own_odd_ref), (near_even_ref, near_odd_ref)
    ring = tiles + 1
    size = ring * SUBS
    place, places = chain_place()
    top = place % 2 == 0
    has_near = jnp.where(top, place < places - 1, place > 0)
    unpack_rows(
        near_ref,
        jnp.where(top, HALO + height, 0),
        jnp.logical_not(top),
        has_near,
        near_strips,
        [kind * height + jnp.where(top, 0, height - HALO) for kind in range(2)],
        ground_ref,
        surface_ref,
        tiles,
    )
    for kind, out_ref in enumerate((ground_ref, surface_ref)):
        for row in range(height):
            first_tile = out_ref[register(HALO + row, 0, size), :]
            last_tile = out_ref[register(HALO + row, tiles - 1, size), :]
            fill_seam(
                out_ref, HALO + row, first_tile, last_tile, own_strips, kind * height + row, place >= 0, tiles
            )
    buffers = (surface_ref, other_ref)
    passes = []
    for step in range(1, PASSES + 1):
        first = step + jnp.where(top, HALO, 0)
        passes.append((buffers[(step + 1) % 2], buffers[step % 2], first, height + HALO - 2 * step, None))
    relax_passes(passes, ground_ref, ring)
    copy_rows(surface_ref, jnp.where(top, HALO + height - FINAL, HALO), near_out, ring)


def outer_kernel(height, tiles, far_ref, even_ref, odd_ref, *refs):
    ground_ref, surface_ref, other_ref, level_ref, far_out = refs[3:8]
    ring = tiles + 1
    size = ring * SUBS
    place, places = chain_place()
    top = place % 2 == 0
    has_far = jnp.where(top, place > 0, place < places - 1)
    unpack_rows(
        far_ref,
        jnp.where(top, 0, HALO + height),
        top,
        has_far,
        (even_ref, odd_ref),
        [kind * height + jnp.where(top, height - HALO, 0) for kind in range(2)],
        ground_ref,
        surface_ref,
        tiles,
    )
    buffers = (surface_ref, other_ref)
    passes = []
    for step in range(1, PASSES + 1):
        first = jnp.where(top, step, HALO + height - step)
        passes.append((buffers[(step + 1) % 2], buffers[step % 2], first, HALO, None))
    relax_passes(passes, ground_ref, ring)
    copy_rows(surface_ref, jnp.where(top, HALO, HALO + height - FINAL), far_out, ring)
    band, bands = lax.axis_index("sub"), lax.axis_size("sub")
    sub, lane = position()

    def at(row, slot):
        return surface_ref[register(HALO + row, slot, size), :]

    first_cell = (sub == 0) & (lane == 0)
    last_cell = (sub == SUBS - 1) & (lane == LANES - 1)
    first_lows, last_lows, row_lows = [], [], []
    for row in range(height):
        first_lows.append(at(row, 0))
        last_lows.append(at(row, tiles - 1))
    for slot in range(tiles):
        row_lows.append(jnp.where(band == 0, at(0, slot), unreached))
        row_lows.append(jnp.where(band == bands - 1, at(height - 1, slot), unreached))
    lowest = jnp.minimum(
        least(row_lows),
        jnp.minimum(
            jnp.where(first_cell, least(first_lows), unreached),
            jnp.where(last_cell, least(last_lows), unreached),
        ),
    )
    lowest = jnp.min(jnp.min(lowest, axis=0, keepdims=True), axis=1, keepdims=True)
    level_ref[...] = jnp.broadcast_to(lowest, level_ref.shape)


def least(values):
    values = list(values)
    while len(values) > 1:
        values = [
            jnp.minimum(*values[number : number + 2]) if number + 1 < len(values) else values[number]
            for number in range(0, len(values), 2)
        ]
    return values[0]


def late_kernel(
    height, tiles, ground_ref, surface_ref, far_ref, near_ref, floors_ref, hops_ref, out_hbm,
    one_ref, two_ref, out_ref, ceilings_ref, stage_ref, sems,
):
    ring = tiles + 1
    size = ring * SUBS
    sub, lane = position()
    bands = lax.axis_size("sub")
    offers = []
    for tile in range(floors_ref.shape[0] // bands):
        raised = [least(floors_ref[pl.ds(tile * bands + band, 1), :] for band in range(bands))]
        for hop in range(ROUNDS):
            raised.append(raised[-1] + hop_rise)
        hops = hops_ref[pl.ds(tile * WANTED, WANTED), :]
        offer = jnp.full((WANTED, LANES), unreached, jnp.float32)
        for hop in range(ROUNDS + 1):
            offer = jnp.where(hops == float(hop), raised[hop], offer)
        offers.append(offer)
    ceilings_ref[...] = least(offers) + spill_lift
    ceilings = [jnp.broadcast_to(ceilings_ref[pl.ds(index, 1), :], (SUBS, LANES)) for index in range(9)]
    pairs = []
    for region in range(3):
        left, middle, right = ceilings[3 * region : 3 * region + 3]
        seam = jnp.where(
            lane < LANES // 2,
            jnp.where(sub == SUBS - 1, right, middle),
            jnp.where(sub == 0, left, middle),
        )
        pairs.append((middle, seam))
    place, _ = chain_place()
    top = place % 2 == 0
    low, high = HALO - FINAL, HALO + height
    far_pair = [jnp.where(top, above, below) for above, below in zip(pairs[0], pairs[2])]
    near_pair = [jnp.where(top, below, above) for above, below in zip(pairs[0], pairs[2])]
    spans = (
        (surface_ref, HALO, HALO, height, pairs[1]),
        (near_ref, 0, jnp.where(top, high, low), FINAL, near_pair),
        (far_ref, 0, jnp.where(top, low, high), FINAL, far_pair),
    )
    for source, source_first, first, rows, (middle, seam) in spans:
        for row in range(rows):
            for slot in range(ring):
                value = source[register(source_first + row, slot, size), :]
                value = jnp.minimum(value, seam if slot == tiles else middle)
                where = register(first + row, slot, size)
                one_ref[where, :] = jnp.maximum(ground_ref[where, :], value)
    buffers = (one_ref, two_ref)
    passes = []
    for step in range(1, FINAL):
        first = HALO - FINAL + step
        count = 2 * HALO + height - 2 * first
        passes.append((buffers[(step + 1) % 2], buffers[step % 2], first, count, None))
    source, target = buffers[(FINAL + 1) % 2], buffers[FINAL % 2]
    copies = []

    def unfold(group):
        first = HALO + group * SUBS
        half = tiles * SUBS // 2
        for slot in range(tiles):
            for row in range(SUBS):
                stage_ref[staged(0, slot, row), :] = target[register(first + row, slot, size), :]
        for tile in range(tiles * SUBS):
            chunk, slot = tile // tiles, tile % tiles
            columns = pl.ds(tile * LANES, LANES)
            out_ref[pl.ds(group * SUBS, SUBS), columns] = stage_ref[across(0, slot, chunk), :]
            if tile % half == half - 1:
                side = tile // half
                where = (pl.ds(group * SUBS, SUBS), pl.ds(side * half * LANES, half * LANES))
                copy = pltpu.make_async_copy(out_ref.at[where], out_hbm.at[where], sems.at[group, side])
                copies.extend(start_all([copy]))

    for group in range(height // SUBS):
        first = HALO + group * SUBS
        passes.append((source, target, first, SUBS, functools.partial(unfold, group)))
    relax_passes(passes, ground_ref, ring)
    wait_all(copies)


def in_vmem(count):
    return [pl.BlockSpec(memory_space=pltpu.VMEM)] * count


def in_hbm(count):
    return [pl.BlockSpec(memory_space=pltpu.HBM)] * count


def per_device(elevation, fill_depth, edge_rows, edge_sides, adjacency):
    height, width = elevation.shape
    tiles = width // (SUBS * LANES)
    groups = height // SUBS
    f32 = jnp.float32
    packed = tiles * SUBS
    size = packed + SUBS
    tile_count = adjacency.shape[0]
    places = lax.axis_size(("rows", "sub"))
    cols, subs = lax.axis_size("cols"), lax.axis_size("sub")
    short = pl.CostEstimate(flops=1024, bytes_accessed=1024, transcendentals=0)
    limit = pltpu.CompilerParams(vmem_limit_bytes=24 << 20)
    arguments = [
        pltpu.with_memory_space_constraint(value, pltpu.HBM)
        for value in (elevation, fill_depth, edge_rows, edge_sides, adjacency)
    ]
    sent = pltpu.VMEM(((2 * HALO - 1) * packed, LANES), f32)
    strip = pltpu.VMEM((2 * height, LANES), f32)
    work = pltpu.VMEM(((height + 2 * HALO) * size, LANES), f32)
    far, near, even, odd, ground, surface, links = pl.pallas_call(
        edge_kernel,
        out_shape=[sent, sent, strip, strip, work, work, pltpu.VMEM(adjacency.shape, jnp.int32)],
        in_specs=in_hbm(5),
        out_specs=in_vmem(7),
        scratch_shapes=[
            pltpu.VMEM((height, width), f32),
            pltpu.VMEM((height, width), f32),
            pltpu.VMEM(edge_rows.shape, jnp.int32),
            pltpu.VMEM(edge_sides.shape, jnp.int32),
            pltpu.VMEM((2 * groups * packed * SKEW, LANES), f32),
            pltpu.SemaphoreType.DMA((2, 2)),
            pltpu.SemaphoreType.DMA((3,)),
        ],
        compiler_params=limit,
        cost_estimate=short,
        name="edge_rows",
    )(*arguments)

    near_pairs, far_pairs = [matching(places, first) for first in range(2)]
    stay = [(place, place) for place in range(places)]
    ends = [(place, place) for place in range(places) if place not in dict(far_pairs)]
    groups_count = lax.axis_size("groups")
    part = places * cols
    far_all = []
    for group, other in closed(matching(groups_count, 0), groups_count):
        for chosen, target in ((far_pairs, group), (ends, other)):
            for source, arrival in cross(chosen, [(col, col) for col in range(cols)], cols, subs):
                far_all.append((group * part + source, target * part + arrival))
    device_axes = ("rows", "cols", "sub")

    def swap_strips(pieces, row_pairs):
        arrived = []
        for first, piece in enumerate(pieces):
            pairs = cross(row_pairs, matching(cols, first), cols, subs)
            arrived.append(lax.ppermute(piece, device_axes, pairs) if pairs else piece)
        return arrived

    far_strips = swap_strips((even, odd), far_pairs + ends)
    far_rows = lax.ppermute(far, ("groups",) + device_axes, far_all)
    near_rows = lax.ppermute(near, ("rows", "sub"), near_pairs)
    strips = swap_strips((even, odd), stay) + swap_strips((even, odd), near_pairs)

    hops = pl.pallas_call(
        hops_kernel,
        out_shape=pltpu.VMEM((WANTED * tile_count, LANES), f32),
        in_specs=in_vmem(1),
        out_specs=pl.BlockSpec(memory_space=pltpu.VMEM),
        compiler_params=limit,
        cost_estimate=short,
        name="tile_hops",
    )(links)

    def inner(*refs):
        inner_kernel(height, tiles, *refs)

    again = pltpu.VMEM((FINAL * size, LANES), f32)
    ground, surface, other, near = pl.pallas_call(
        inner,
        out_shape=[work, work, work, again],
        in_specs=in_vmem(8),
        out_specs=in_vmem(4),
        input_output_aliases={5: 0, 6: 1},
        compiler_params=limit,
        cost_estimate=short,
        name="inner_passes",
    )(near_rows, *strips, ground, surface, hops)

    def outer(far_ref, *refs):
        outer_kernel(height, tiles, far_ref, *refs)

    devices = lax.axis_size(device_axes)
    ground, surface, other, floors, far = pl.pallas_call(
        outer,
        out_shape=[work, work, work, pltpu.VMEM((devices, LANES), f32), again],
        in_specs=in_vmem(6),
        out_specs=in_vmem(5),
        input_output_aliases={3: 0, 4: 1, 5: 2},
        compiler_params=limit,
        cost_estimate=short,
        name="outer_passes",
    )(far_rows, *far_strips, ground, surface, other)

    far_rows = lax.ppermute(far, ("groups",) + device_axes, far_all)
    near_rows = lax.ppermute(near, ("rows", "sub"), near_pairs)
    floors = lax.all_to_all(floors, device_axes, 0, 0, tiled=True)

    def late(*refs):
        late_kernel(height, tiles, *refs)

    return pl.pallas_call(
        late,
        out_shape=jax.ShapeDtypeStruct((height, width), f32),
        in_specs=in_vmem(6),
        out_specs=pl.BlockSpec(memory_space=pltpu.HBM),
        scratch_shapes=[
            work,
            work,
            pltpu.VMEM((height, width), f32),
            pltpu.VMEM((WANTED, LANES), f32),
            pltpu.VMEM((packed * SKEW, LANES), f32),
            pltpu.SemaphoreType.DMA((groups, 2)),
        ],
        compiler_params=limit,
        cost_estimate=short,
        name="final_passes",
    )(ground, surface, far_rows, near_rows, floors, hops)


def solution(mesh):
    placed = (
        P(("groups", "rows", "sub"), "cols"),
        P(("groups", "rows", "sub"), "cols"),
        P("groups", "cols"),
        P("groups", ("rows", "sub")),
        P("groups", None),
    )
    return jax.shard_map(
        per_device,
        mesh=mesh,
        in_specs=placed,
        out_specs=P(("groups", "rows", "sub"), "cols"),
        check_vma=False,
    )
```
